32 devices in a mesh: grp: 4 (over x, core), vocab: 8 (over z, y).
Axes of the slice: x: 2, y: 2, z: 4, core: 2. Of those that a mesh axis runs over, the one named last changes fastest.
Arguments:
- hidden: bfloat16 [512, 3584], P('grp'), may hold values from -300 to 300
- token_ids: int32 [512], P('grp'), may hold values from 0 to 16383
- serving: int32 [512], replicated, may hold values from 0 to 511, each once
- head_weight: bfloat16 [3584, 16384], P(None, ('grp', 'vocab')), may hold values from -0.3125 to 0.3125
- teacher_logits: bfloat16 [512, 4, 4096], P('grp', None, 'vocab'), may hold values from -300 to 300
Outputs:
- grad_hidden: float32 [512, 3584], P(('grp', 'vocab'))
- grad_head: bfloat16 [3584, 16384], P(None, ('grp', 'vocab'))
The draws below stay inside these ranges and needn't reach their ends.
All inputs are finite; a program needn't handle non-finite values.
Results may differ from the reference program's by a relative error of at most 0.012.
Values may be sent and summed in bfloat16 or wider, within the bound.
No kernel may reach another device: no remote copies, remote signals or barrier semaphores. Data moves between devices by JAX's collectives and lax.ppermute only.
A program may use at most 128 MiB of HBM per device.

```python
import math
import jax
import jax.numpy as jnp
import numpy as np
from jax import lax

DS = 3584
VOCAB_DEV = 512
GRPS = 4
ROWS_ALL = 512
VOCAB = 16384
VQ = 4096
N_VOCAB = 8


def shared_directions(key):
    return jax.random.normal(jax.random.fold_in(key, 5), (3, DS), jnp.float32) / math.sqrt(DS)


def draw_hidden(key, part):
    directions = shared_directions(key)
    key = jax.random.fold_in(key, 11)
    key_base, key_scale, key_load = jax.random.split(key, 3)
    scales = jnp.exp(jax.random.uniform(key_scale, (ROWS_ALL, 1), jnp.float32, math.log(0.5), math.log(5.0)))
    loads = 2.0 * jax.random.normal(key_load, (ROWS_ALL, 3), jnp.float32)
    along = loads[:, 0:1] * directions[0][None, :] + loads[:, 1:2] * directions[1][None, :] + loads[:, 2:3] * directions[2][None, :]
    base = jax.random.normal(key_base, (ROWS_ALL, DS), jnp.float32)
    values = jnp.clip((base + along) * scales, -30.0, 30.0)
    return values.astype(jnp.bfloat16)


def draw_head_weight(key, part):
    directions = shared_directions(key)
    key = jax.random.fold_in(key, 37)
    key_noise, key_center, key_coef = jax.random.split(key, 3)
    unit = 3.0 / math.sqrt(DS)
    coefs = jax.random.normal(key_coef, (3, VOCAB), jnp.float32)
    noise = jax.random.normal(key_noise, (DS, VOCAB), jnp.float32)
    center = jax.random.normal(key_center, (DS, 1), jnp.float32)
    values = unit * (noise + center) + directions[0][:, None] * coefs[0][None, :] + directions[1][:, None] * coefs[1][None, :] + directions[2][:, None] * coefs[2][None, :]
    return jnp.clip(values, -0.3125, 0.3125).astype(jnp.bfloat16)


def draw_teacher_logits(key, part):
    key = jax.random.fold_in(key, 23)
    key_base, key_scale = jax.random.split(key)
    scales = jnp.exp(jax.random.uniform(key_scale, (ROWS_ALL, 1, 1), jnp.float32, 0.0, math.log(3.0)))
    base = jax.random.normal(key_base, (ROWS_ALL, GRPS, VQ), jnp.float32)
    values = jnp.clip(base * 3.0 * scales, -40.0, 40.0)
    return values.astype(jnp.bfloat16)


def place_ends(result, rng, least, largest):
    place = [jax.random.randint(jax.random.fold_in(rng, axis), (), 0, length) for axis, length in enumerate(result.shape)]
    main_axis = result.shape.index(max(result.shape))
    beside = place[:main_axis] + [(place[main_axis] + 1) % result.shape[main_axis]] + place[main_axis + 1:]
    return result.at[tuple(place)].set(least).at[tuple(beside)].set(largest)


def rank_bounds(number_of, slope):
    weights = [(1 << 20) // math.isqrt(standing ** slope) + 1 for standing in range(1, number_of + 1)]
    spread = 1 + sum(weights) // (1 << 30)
    return np.cumsum(np.array([max(1, weight // spread) for weight in weights]))


def ranked_ids(stream_key, shape, count, lean):
    table = rank_bounds(count, lean)
    ticket = jax.random.randint(jax.random.fold_in(stream_key, 1), shape, 0, int(table[count - 1]))
    grade = jnp.searchsorted(jnp.asarray(table, jnp.int32), ticket, side="right")
    return jax.random.permutation(jax.random.fold_in(stream_key, 2), count)[grade].astype(jnp.int32)


def setup_inputs(seed: int = 0) -> dict:
    arg_keys = jax.random.split(jax.random.key(seed), 6)
    return {
        "hidden": draw_hidden(jax.random.fold_in(arg_keys[5], 71), 0),
        "token_ids": place_ends(ranked_ids(arg_keys[1], (ROWS_ALL,), VOCAB, 2), jax.random.fold_in(arg_keys[1], 3), 0, VOCAB - 1).astype(jnp.int32),
        "serving": jax.random.permutation(arg_keys[2], ROWS_ALL).astype(jnp.int32),
        "head_weight": draw_head_weight(jax.random.fold_in(arg_keys[5], 71), 0),
        "teacher_logits": draw_teacher_logits(jax.random.fold_in(arg_keys[5], 71), 0),
    }


smoothing_divisor = 2.0
imitation_mixing_coefficient = 0.5
objective_scaling_factor = 32.0


def reference(hidden, token_ids, serving, head_weight, teacher_logits):
    rows_all = hidden.shape[0]
    mentor_activations = teacher_logits.reshape(rows_all, VOCAB)[serving].astype(jnp.float32)
    logits = jnp.dot(hidden, head_weight, preferred_element_type=jnp.float32)
    student_peak = jnp.max(logits, axis=1, keepdims=True)
    mentor_peak_activation = jnp.max(mentor_activations, axis=1, keepdims=True)
    shifted_pupil_activations = logits - student_peak
    mentor_shifted_activations = (mentor_activations - mentor_peak_activation) / smoothing_divisor
    sum_hard = jnp.sum(jnp.exp(shifted_pupil_activations), axis=1, keepdims=True)
    mentor_component_accumulated = jnp.sum(jnp.exp(shifted_pupil_activations / smoothing_divisor), axis=1, keepdims=True)
    mentor_exponential_summed = jnp.sum(jnp.exp(mentor_shifted_activations), axis=1, keepdims=True)
    columns = jnp.arange(VOCAB, dtype=jnp.int32)
    labels = (token_ids[:, None] == columns[None, :]).astype(jnp.float32)
    mentor_match_component = jnp.exp(shifted_pupil_activations / smoothing_divisor) / mentor_component_accumulated - jnp.exp(mentor_shifted_activations) / mentor_exponential_summed
    ground_truth_component = jnp.exp(shifted_pupil_activations) / sum_hard - labels
    activation_derivative = (objective_scaling_factor * (imitation_mixing_coefficient * smoothing_divisor * mentor_match_component + (1.0 - imitation_mixing_coefficient) * ground_truth_component)).astype(jnp.bfloat16)
    grad_hidden = lax.dot_general(activation_derivative, head_weight, (((1,), (1,)), ((), ())), preferred_element_type=jnp.float32)
    blocks = GRPS * N_VOCAB
    grad_blocks = activation_derivative.reshape(rows_all, blocks, VOCAB_DEV).transpose(1, 0, 2)
    hidden_t = hidden.T

    def one_block(block):
        return jnp.dot(hidden_t, block, preferred_element_type=jnp.float32).astype(jnp.bfloat16)

    grad_head = lax.map(one_block, grad_blocks).transpose(1, 0, 2).reshape(DS, VOCAB)
    return grad_hidden, grad_head
```

```python
import jax
import jax.numpy as jnp
from jax import lax
from jax.sharding import PartitionSpec as P

BF16 = jnp.bfloat16
F32 = jnp.float32


def swap(value, axis, mask):
    count = lax.axis_size(axis)
    return lax.ppermute(value, axis, [(i, i ^ mask) for i in range(count)])


def body(hidden, token_ids, serving, head_weight, teacher_logits):
    groups = lax.axis_size("grp")
    shards = lax.axis_size("vocab")
    me_g = lax.axis_index("grp")
    me_v = lax.axis_index("vocab")
    per = hidden.shape[0]
    depth = hidden.shape[1]
    cols = head_weight.shape[1]

    arrived = lax.all_to_all(teacher_logits, "grp", split_axis=1, concat_axis=0, tiled=True)
    from_x = swap(hidden, "grp", 2)
    from_core = swap(hidden, "grp", 1)
    from_diag = swap(from_x, "grp", 1)
    ids_x = swap(token_ids, "grp", 2)
    ids_pair = jnp.concatenate([token_ids, ids_x])
    ids_core = swap(ids_pair, "grp", 1)
    ids = jnp.concatenate([token_ids, ids_core[:per], ids_x, ids_core[per:]])
    rows = [hidden, from_core, from_x, from_diag]

    order = me_g ^ jnp.arange(groups, dtype=jnp.int32)
    serving_rel = serving.reshape(groups, per)[order].reshape(-1)
    aligned = arrived.reshape(groups * per, cols)[serving_rel].astype(F32)

    logits = jnp.concatenate(
        [jnp.dot(block, head_weight, preferred_element_type=F32) for block in rows]
    )
    peak = jnp.max(logits, axis=1)
    tpeak = jnp.max(aligned, axis=1)
    shifted = logits - peak[:, None]
    tshifted = (aligned - tpeak[:, None]) * 0.5
    stats = jnp.stack(
        [
            peak,
            jnp.sum(jnp.exp(shifted), axis=1),
            jnp.sum(jnp.exp(shifted * 0.5), axis=1),
            tpeak,
            jnp.sum(jnp.exp(tshifted), axis=1),
        ]
    )
    stats = stats.reshape(5, groups, per).swapaxes(0, 1)[order]
    everyone = lax.all_to_all(
        jnp.broadcast_to(stats[None], (groups * shards,) + stats.shape),
        ("grp", "vocab"),
        split_axis=0,
        concat_axis=0,
        tiled=True,
    )
    everyone = everyone[:, order]
    peaks, hards, softs, tpeaks, tsums = [
        everyone[:, :, k].reshape(groups * shards, groups * per) for k in range(5)
    ]
    top = jnp.max(peaks, axis=0)
    ttop = jnp.max(tpeaks, axis=0)
    hard = jnp.sum(hards * jnp.exp(peaks - top), axis=0)
    soft = jnp.sum(softs * jnp.exp((peaks - top) * 0.5), axis=0)
    tsum = jnp.sum(tsums * jnp.exp((tpeaks - ttop) * 0.5), axis=0)

    first = (me_g * shards + me_v) * cols
    columns = first + jnp.arange(cols, dtype=jnp.int32)
    labels = (ids[:, None] == columns[None, :]).astype(F32)
    moved = logits - top[:, None]
    grad = (
        32.0
        * (
            jnp.exp(moved * 0.5) / soft[:, None]
            - jnp.exp((aligned - ttop[:, None]) * 0.5) / tsum[:, None]
            + 0.5 * (jnp.exp(moved) / hard[:, None] - labels)
        )
    ).astype(BF16)

    blocks = grad.reshape(groups, per, cols)

    def back(j):
        return lax.dot_general(
            blocks[j], head_weight, (((1,), (1,)), ((), ())), preferred_element_type=F32
        )

    far = swap(back(3).astype(BF16), "grp", 1)
    near = swap(back(1).astype(BF16), "grp", 1)
    across = swap((back(2) + far.astype(F32)).astype(BF16), "grp", 2)
    mine = (back(0) + near.astype(F32) + across.astype(F32)).astype(BF16)
    parts = lax.all_to_all(
        mine.reshape(shards, per // shards, depth), "vocab", split_axis=0, concat_axis=0, tiled=True
    )
    grad_hidden = jnp.sum(parts.astype(F32), axis=0)

    grad_head = lax.dot_general(
        jnp.concatenate(rows),
        grad,
        (((0,), (0,)), ((), ())),
        preferred_element_type=F32,
    ).astype(BF16)
    return (grad_hidden, grad_head)


def solution(mesh):
    placed = (P("grp", None), P("grp"), P(), P(None, ("grp", "vocab")), P("grp", None, "vocab"))
    return jax.shard_map(
        body,
        mesh=mesh,
        in_specs=placed,
        out_specs=(P(("grp", "vocab"), None), P(None, ("grp", "vocab"))),
        check_vma=False,
    )
```

```python
import jax
import jax.numpy as jnp
from jax import lax
from jax.experimental import pallas as pl
from jax.experimental.pallas import tpu as pltpu
from jax.sharding import PartitionSpec as P

BF16 = jnp.bfloat16
F32 = jnp.float32
AXES = ("grp", "vocab")
VMEM = pl.BlockSpec(memory_space=pltpu.VMEM)
SMEM = pl.BlockSpec(memory_space=pltpu.SMEM)
ANY = pl.BlockSpec(memory_space=pl.ANY)
PARAMS = pltpu.CompilerParams(vmem_limit_bytes=40 * 2**20)
STAT_ROWS = 8


def columns_to_rows(columns):
    count = columns[0].shape[0]
    lane = lax.broadcasted_iota(jnp.int32, (count, 128), 1)
    wide = jnp.zeros((count, 128), F32)
    for k, column in enumerate(columns):
        wide = jnp.where(lane == k, column, wide)
    return wide.T[:STAT_ROWS]


def teacher_kernel(me_ref, serving_ref, arrived_ref, aligned_ref, stats_ref):
    me = me_ref[0]
    groups, _, per = serving_ref.shape
    total = arrived_ref.shape[0]
    for j in range(groups):
        wanted = serving_ref[me ^ j]
        pick = (lax.broadcasted_iota(jnp.int32, (total, per), 0) == wanted).astype(BF16)
        rows = lax.dot_general(
            pick, arrived_ref[...], (((0,), (0,)), ((), ())), preferred_element_type=F32
        )
        aligned_ref[j] = rows.astype(BF16)
        peak = jnp.max(rows, axis=1, keepdims=True)
        part = jnp.sum(jnp.exp((rows - peak) * 0.5), axis=1, keepdims=True)
        stats_ref[:, j * per : (j + 1) * per] = columns_to_rows([peak, part])


def teacher_rows(me, serving, arrived, groups):
    total, cols = arrived.shape
    per = total // groups
    return pl.pallas_call(
        teacher_kernel,
        out_shape=(
            jax.ShapeDtypeStruct((groups, per, cols), BF16),
            jax.ShapeDtypeStruct((STAT_ROWS, total), F32),
        ),
        in_specs=[SMEM, VMEM, VMEM],
        out_specs=(VMEM, VMEM),
        compiler_params=PARAMS,
        cost_estimate=pl.CostEstimate(
            flops=2 * total * total * cols, bytes_accessed=2 * total * cols * 2, transcendentals=total * cols
        ),
        name="teacher_rows",
    )(me, serving.reshape(groups, 1, per), arrived)


def place_copies(pieces, places, full, sems):
    copies = []
    for k, (piece, place) in enumerate(zip(pieces, places)):
        count = piece.shape[0]
        start = place if isinstance(place, int) else pl.multiple_of(place, 16)
        copy = pltpu.make_async_copy(piece, full.at[pl.ds(start, count)], sems.at[k])
        copy.start()
        copies.append(copy)
    return copies


def logits_kernel(spots, splits, *refs):
    n = len(spots)
    at_ref, pieces, (w_ref, logits_ref, stats_ref, full, weights, sems, wsems) = (
        refs[0],
        refs[1 : 1 + n],
        refs[1 + n :],
    )
    places = [spot if isinstance(spot, int) else at_ref[spot[0]] for spot in spots]
    copies = place_copies(pieces, places, full, sems)
    depth = w_ref.shape[0]
    step = depth // splits
    wcopies = []
    for c in range(splits):
        part = pl.ds(c * step, step)
        copy = pltpu.make_async_copy(w_ref.at[part], weights.at[part], wsems.at[c])
        copy.start()
        wcopies.append(copy)
    for copy in copies:
        copy.wait()
    total = None
    for c in range(splits):
        wcopies[c].wait()
        term = jnp.dot(
            full[:, c * step : (c + 1) * step],
            weights[c * step : (c + 1) * step, :],
            preferred_element_type=F32,
        )
        total = term if total is None else total + term
    logits_ref[...] = total
    peak = jnp.max(total, axis=1, keepdims=True)
    soft = jnp.exp((total - peak) * 0.5)
    stats_ref[...] = columns_to_rows(
        [
            peak,
            jnp.sum(soft * soft, axis=1, keepdims=True),
            jnp.sum(soft, axis=1, keepdims=True),
        ]
    )


def student_logits(at, pieces, spots, head_weight):
    depth, cols = head_weight.shape
    rows = sum(piece.shape[0] for piece in pieces)
    splits = 7 if depth % (7 * 128) == 0 else 1
    return pl.pallas_call(
        lambda *refs: logits_kernel(spots, splits, *refs),
        out_shape=(
            jax.ShapeDtypeStruct((rows, cols), F32),
            jax.ShapeDtypeStruct((STAT_ROWS, rows), F32),
        ),
        in_specs=[SMEM] + [ANY] * (len(pieces) + 1),
        out_specs=(VMEM, VMEM),
        scratch_shapes=[
            pltpu.VMEM((rows, depth), BF16),
            pltpu.VMEM((depth, cols), BF16),
            pltpu.SemaphoreType.DMA((len(pieces),)),
            pltpu.SemaphoreType.DMA((splits,)),
        ],
        compiler_params=PARAMS,
        cost_estimate=pl.CostEstimate(
            flops=2 * rows * depth * cols,
            bytes_accessed=(rows + cols) * depth * 2 + rows * cols * 4,
            transcendentals=rows * cols,
        ),
        name="student_logits",
    )(at, *pieces, head_weight)


def back_kernel(chunk, at_ref, top_ref, low_ref, aligned_ref, stats_ref, w_ref, grad_ref, back_ref, mixed, weights, wsem):
    copy = pltpu.make_async_copy(w_ref, weights, wsem)
    copy.start()
    first = at_ref[0]
    flip = at_ref[1]
    per, cols = top_ref.shape
    turn = (
        lax.broadcasted_iota(jnp.int32, (per, per), 1)
        == (lax.broadcasted_iota(jnp.int32, (per, per), 0) ^ flip)
    ).astype(BF16)
    column = first + lax.broadcasted_iota(jnp.int32, (per, cols), 1)
    for k, logits_ref in enumerate((top_ref, low_ref)):
        stats = jnp.concatenate([stats_ref[k, 0], jnp.zeros((128 - STAT_ROWS, per), F32)]).T
        peak, hard, soft, tpeak, tsum, ids = [stats[:, i : i + 1] for i in range(6)]
        half = jnp.exp((logits_ref[...] - peak) * 0.5)
        taught = jnp.exp((aligned_ref[k, 0].astype(F32) - tpeak) * 0.5)
        label = jnp.where(column == ids.astype(jnp.int32), 16.0, 0.0)
        grad = (half * (32.0 / soft) - taught * (32.0 / tsum)) + (half * half * (16.0 / hard) - label)
        grad = grad.astype(BF16)
        grad_ref[k] = grad
        mixed[k * per : (k + 1) * per, :] = jnp.dot(turn, grad, preferred_element_type=F32).astype(BF16)
    copy.wait()
    depth = weights.shape[0]
    rows = mixed[...]
    for c in range(depth // chunk):
        part = slice(c * chunk, (c + 1) * chunk)
        out = lax.dot_general(
            rows, weights[part, :], (((1,), (1,)), ((), ())), preferred_element_type=F32
        ).astype(BF16)
        back_ref[0, :, part] = out[:per]
        back_ref[1, :, part] = out[per:]


def back_rows(at, near, far, aligned, stats, head_weight, which):
    depth, cols = head_weight.shape
    per = near.shape[0] // 2
    chunk = 512 if depth % 512 == 0 else depth
    paired = lambda i: (0, which, 0, 0)
    return pl.pallas_call(
        lambda *refs: back_kernel(chunk, *refs),
        grid=(1,),
        out_shape=(
            jax.ShapeDtypeStruct((2, per, cols), BF16),
            jax.ShapeDtypeStruct((2, per, depth), BF16),
        ),
        in_specs=[
            SMEM,
            pl.BlockSpec((per, cols), lambda i: (which, 0)),
            pl.BlockSpec((per, cols), lambda i: (which, 0)),
            pl.BlockSpec((2, 1, per, cols), paired),
            pl.BlockSpec((2, 1, STAT_ROWS, per), paired),
            ANY,
        ],
        out_specs=(
            pl.BlockSpec((2, per, cols), lambda i: (0, 0, 0)),
            pl.BlockSpec((2, per, depth), lambda i: (0, 0, 0)),
        ),
        scratch_shapes=[
            pltpu.VMEM((2 * per, cols), BF16),
            pltpu.VMEM((depth, cols), BF16),
            pltpu.SemaphoreType.DMA,
        ],
        compiler_params=PARAMS,
        cost_estimate=pl.CostEstimate(
            flops=4 * per * depth * cols,
            bytes_accessed=depth * cols * 2 + 4 * per * depth,
            transcendentals=4 * per * cols,
        ),
        name="back_rows",
    )(at, near, far, aligned, stats, head_weight)


def head_kernel(spots, *refs):
    n = len(spots)
    at_ref, pieces, (even_ref, odd_ref, out_ref, full, sems) = refs[0], refs[1 : 1 + n], refs[1 + n :]
    step = pl.program_id(0)

    @pl.when(step == 0)
    def _():
        places = [spot if isinstance(spot, int) else at_ref[spot[0]] for spot in spots]
        for copy in place_copies(pieces, places, full, sems):
            copy.wait()

    tile = out_ref.shape[0]
    part = pl.ds(pl.multiple_of(step * tile, tile), tile)
    grads = jnp.concatenate([even_ref[0], odd_ref[0], even_ref[1], odd_ref[1]])
    out_ref[...] = lax.dot_general(
        full[:, part], grads, (((0,), (0,)), ((), ())), preferred_element_type=F32
    ).astype(BF16)


def head_gradient(at, pieces, spots, even, odd):
    depth = pieces[0].shape[1]
    rows = sum(piece.shape[0] for piece in pieces)
    _, per, cols = even.shape
    tile = 512 if depth % 512 == 0 else depth
    whole = pl.BlockSpec((2, per, cols), lambda i: (0, 0, 0))
    return pl.pallas_call(
        lambda *refs: head_kernel(spots, *refs),
        grid=(depth // tile,),
        out_shape=jax.ShapeDtypeStruct((depth, cols), BF16),
        in_specs=[SMEM] + [ANY] * len(pieces) + [whole, whole],
        out_specs=pl.BlockSpec((tile, cols), lambda i: (i, 0)),
        scratch_shapes=[
            pltpu.VMEM((rows, depth), BF16),
            pltpu.SemaphoreType.DMA((len(pieces),)),
        ],
        compiler_params=PARAMS,
        cost_estimate=pl.CostEstimate(
            flops=2 * rows * depth * cols,
            bytes_accessed=(rows + cols) * depth * 2 + rows * cols * 2,
            transcendentals=0,
        ),
        name="head_gradient",
    )(at, *pieces, even, odd)


def flip_groups(stats, mask):
    groups = stats.shape[1]
    return jnp.stack([stats[:, j ^ mask] for j in range(groups)], axis=1)


def merge(parts):
    peak, tpeak = parts[0][0], parts[0][3]
    ids = parts[0][5]
    for part in parts[1:]:
        peak, tpeak = jnp.maximum(peak, part[0]), jnp.maximum(tpeak, part[3])
        ids = jnp.maximum(ids, part[5])
    hard = soft = tsum = 0.0
    for part in parts:
        shrink = jnp.exp((part[0] - peak) * 0.5)
        hard = hard + part[1] * (shrink * shrink)
        soft = soft + part[2] * shrink
        tsum = tsum + part[4] * jnp.exp((part[3] - tpeak) * 0.5)
    return jnp.stack([peak, hard, soft, tpeak, tsum, ids])


def body(hidden, token_ids, serving, head_weight, teacher_logits):
    groups = lax.axis_size("grp")
    shards = lax.axis_size("vocab")
    me_g = lax.axis_index("grp")
    me_v = lax.axis_index("vocab")
    per, depth = hidden.shape
    cols = head_weight.shape[1]
    owned = per // shards
    CORE, X = shards, 2 * shards
    Y, W = 1, 2
    count = groups * shards

    def swap(value, mask):
        return lax.ppermute(value, AXES, [(i, i ^ mask) for i in range(count)])

    quarter_rows = per // 4
    half_rows = quarter_rows // 2
    quarter = me_v & 3
    x0 = swap(lax.dynamic_slice_in_dim(hidden, quarter * quarter_rows, quarter_rows, 0), X)
    from_core = swap(hidden, CORE)
    arrived = lax.all_to_all(teacher_logits, "grp", split_axis=1, concat_axis=0, tiled=True)
    x1 = swap(x0, Y)
    x2 = swap(x0, W)
    x3a = swap(x2[:half_rows], Y)
    x3b = swap(x1[half_rows:], W)
    xs = [x0, x1, x2, x3a, x3b]
    ds = [swap(piece, CORE) for piece in xs]
    starts = [
        (quarter ^ k) * quarter_rows + extra
        for k, extra in ((0, 0), (1, 0), (2, 0), (3, 0), (3, half_rows))
    ]
    late_at = jnp.stack([s for s in starts] + [per + s for s in starts]).astype(jnp.int32)
    all_at = late_at + 2 * per
    late = xs + ds
    late_spots = [(k,) for k in range(10)]

    near_logits, near_stats = student_logits(late_at, [hidden, from_core], [0, per], head_weight)
    aligned, tstats = teacher_rows(
        me_g.astype(jnp.int32).reshape(1), serving, arrived.reshape(groups * per, cols), groups
    )
    far_logits, far_stats = student_logits(late_at, late, late_spots, head_weight)

    mine = jnp.concatenate([near_stats[:3], far_stats[:3]], axis=1)
    ids = jnp.concatenate([token_ids.astype(F32), jnp.zeros(((groups - 1) * per,), F32)])
    stats = jnp.concatenate([mine, tstats[:2], ids[None]]).reshape(6, groups, per)
    stats = merge([stats, flip_groups(swap(stats, CORE), 1)])
    stats = merge(
        [
            stats,
            flip_groups(swap(stats, X), 2),
            swap(stats, Y),
            flip_groups(swap(stats, X + Y), 2),
        ]
    )
    mask = W
    while mask < shards:
        masks = [mask, 2 * mask, 3 * mask] if 2 * mask < shards else [mask]
        stats = merge([stats] + [swap(stats, m) for m in masks])
        mask *= 4
    stats = jnp.concatenate([stats, jnp.zeros((STAT_ROWS - 6, groups, per), F32)])
    stats = stats.swapaxes(0, 1).reshape(2, 2, STAT_ROWS, per)

    at = jnp.stack([(me_g * shards + me_v) * cols, me_v * owned]).astype(jnp.int32)
    pairs = aligned.reshape(2, 2, per, cols)
    odd, away = back_rows(at, near_logits, far_logits, pairs, stats, head_weight, 1)
    recv = swap(away, CORE)
    even, keep = back_rows(at, near_logits, far_logits, pairs, stats, head_weight, 0)

    bits = shards.bit_length() - 1
    shape = (2,) * (1 + bits) + (owned, depth)
    held = [keep.reshape(shape), recv.reshape(shape)]
    masks = {0: X}
    for b in range(bits):
        masks[1 + b] = shards >> (1 + b)
    ydim, wdim = bits, bits - 1
    units = depth // 128
    third = units // 3
    edges = [0, third * 128, 2 * third * 128, depth]
    orders = [(0, ydim, wdim), (ydim, wdim, 0), (wdim, 0, ydim)]
    parts = []
    for p, order in enumerate(orders):
        terms = [h[..., edges[p] : edges[p + 1]] for h in held]
        for dim in order:
            sent = sum(lax.index_in_dim(t, 1, dim).astype(F32) for t in terms).astype(BF16)
            got = swap(sent, masks[dim])
            terms = [lax.index_in_dim(t, 0, dim) for t in terms] + [got]
        parts.append(terms)
    parts = [
        sum(t.astype(F32) for t in terms) for terms in parts
    ]
    total = jnp.concatenate(parts, axis=-1)
    for dim in range(1, wdim):
        got = swap(lax.index_in_dim(total, 1, dim).astype(BF16), masks[dim])
        total = lax.index_in_dim(total, 0, dim) + got.astype(F32)
    grad_hidden = total.reshape(owned, depth)

    grad_head = head_gradient(
        all_at, [hidden, from_core] + late, [0, per] + late_spots, even, odd
    )
    return (grad_hidden, grad_head)


def solution(mesh):
    placed = (P("grp", None), P("grp"), P(), P(None, ("grp", "vocab")), P("grp", None, "vocab"))
    return jax.shard_map(
        body,
        mesh=mesh,
        in_specs=placed,
        out_specs=(P(("grp", "vocab"), None), P(None, ("grp", "vocab"))),
        check_vma=False,
    )
```

```python
import jax
import jax.numpy as jnp
from jax import lax
from jax.experimental import pallas as pl
from jax.experimental.pallas import tpu as pltpu
from jax.sharding import PartitionSpec as P

BF16 = jnp.bfloat16
F32 = jnp.float32
AXES = ("grp", "vocab")
VMEM = pl.BlockSpec(memory_space=pltpu.VMEM)
SMEM = pl.BlockSpec(memory_space=pltpu.SMEM)
HBM = pl.BlockSpec(memory_space=pltpu.HBM)
PARAMS = pltpu.CompilerParams(vmem_limit_bytes=40 * 2**20)
STAT_ROWS = 8


def columns_to_rows(columns):
    count = columns[0].shape[0]
    lane = lax.broadcasted_iota(jnp.int32, (count, 128), 1)
    wide = jnp.zeros((count, 128), F32)
    for k, column in enumerate(columns):
        wide = jnp.where(lane == k, column, wide)
    return wide.T[:STAT_ROWS]


def teacher_kernel(me_ref, serving_ref, arrived_ref, aligned_ref, stats_ref):
    me = me_ref[0]
    groups, _, per = serving_ref.shape
    total = arrived_ref.shape[0]
    for j in range(groups):
        wanted = serving_ref[me ^ j]
        pick = (lax.broadcasted_iota(jnp.int32, (total, per), 0) == wanted).astype(BF16)
        rows = lax.dot_general(
            pick, arrived_ref[...], (((0,), (0,)), ((), ())), preferred_element_type=F32
        )
        aligned_ref[j] = rows.astype(BF16)
        peak = jnp.max(rows, axis=1, keepdims=True)
        part = jnp.sum(jnp.exp((rows - peak) * 0.5), axis=1, keepdims=True)
        stats_ref[:, j * per : (j + 1) * per] = columns_to_rows([peak, part])


def teacher_rows(me, serving, arrived, groups):
    total, cols = arrived.shape
    per = total // groups
    return pl.pallas_call(
        teacher_kernel,
        out_shape=(
            jax.ShapeDtypeStruct((groups, per, cols), BF16),
            jax.ShapeDtypeStruct((STAT_ROWS, total), F32),
        ),
        in_specs=[SMEM, VMEM, VMEM],
        out_specs=(VMEM, VMEM),
        compiler_params=PARAMS,
        cost_estimate=pl.CostEstimate(
            flops=2 * total * total * cols, bytes_accessed=2 * total * cols * 2, transcendentals=total * cols
        ),
        name="teacher_rows",
    )(me, serving.reshape(groups, 1, per), arrived)


def place_copies(pieces, places, full, sems):
    copies = []
    for k, (piece, place) in enumerate(zip(pieces, places)):
        count = piece.shape[0]
        start = place if isinstance(place, int) else pl.multiple_of(place, 16)
        copy = pltpu.make_async_copy(piece, full.at[pl.ds(start, count)], sems.at[k])
        copy.start()
        copies.append(copy)
    return copies


def logits_kernel(spots, splits, *refs):
    n = len(spots)
    at_ref, pieces, rest = refs[0], refs[1 : 1 + n], refs[1 + n :]
    w_ref, logits_ref, stats_ref, rows_ref, full, weights, sems, wsems, osem = rest
    places = [spot if isinstance(spot, int) else at_ref[spot[0]] for spot in spots]
    copies = place_copies(pieces, places, full, sems)
    depth = w_ref.shape[0]
    step = depth // splits
    wcopies = []
    for c in range(splits):
        part = pl.ds(c * step, step)
        copy = pltpu.make_async_copy(w_ref.at[part], weights.at[part], wsems.at[c])
        copy.start()
        wcopies.append(copy)
    for copy in copies:
        copy.wait()
    out = pltpu.make_async_copy(full, rows_ref, osem)
    out.start()
    total = None
    for c in range(splits):
        wcopies[c].wait()
        term = jnp.dot(
            full[:, c * step : (c + 1) * step],
            weights[c * step : (c + 1) * step, :],
            preferred_element_type=F32,
        )
        total = term if total is None else total + term
    logits_ref[...] = total
    peak = jnp.max(total, axis=1, keepdims=True)
    soft = jnp.exp((total - peak) * 0.5)
    stats_ref[...] = columns_to_rows(
        [
            peak,
            jnp.sum(soft * soft, axis=1, keepdims=True),
            jnp.sum(soft, axis=1, keepdims=True),
        ]
    )
    out.wait()


def student_logits(at, pieces, spots, head_weight):
    depth, cols = head_weight.shape
    rows = sum(piece.shape[0] for piece in pieces)
    splits = 7 if depth % (7 * 128) == 0 else 1
    return pl.pallas_call(
        lambda *refs: logits_kernel(spots, splits, *refs),
        out_shape=(
            jax.ShapeDtypeStruct((rows, cols), F32),
            jax.ShapeDtypeStruct((STAT_ROWS, rows), F32),
            jax.ShapeDtypeStruct((rows, depth), BF16),
        ),
        in_specs=[SMEM] + [HBM] * (len(pieces) + 1),
        out_specs=(VMEM, VMEM, HBM),
        scratch_shapes=[
            pltpu.VMEM((rows, depth), BF16),
            pltpu.VMEM((depth, cols), BF16),
            pltpu.SemaphoreType.DMA((len(pieces),)),
            pltpu.SemaphoreType.DMA((splits,)),
            pltpu.SemaphoreType.DMA,
        ],
        compiler_params=PARAMS,
        cost_estimate=pl.CostEstimate(
            flops=2 * rows * depth * cols,
            bytes_accessed=(rows + cols) * depth * 2 + rows * cols * 4,
            transcendentals=rows * cols,
        ),
        name="student_logits",
    )(at, *pieces, head_weight)


def back_kernel(chunk, at_ref, top_ref, low_ref, aligned_ref, stats_ref, w_ref, grad_ref, back_ref, mixed, weights, wsems):
    depth = weights.shape[0]
    copies = []
    for c in range(depth // chunk):
        part = pl.ds(c * chunk, chunk)
        copy = pltpu.make_async_copy(w_ref.at[part], weights.at[part], wsems.at[c])
        copy.start()
        copies.append(copy)
    first = at_ref[0]
    flip = at_ref[1]
    per, cols = top_ref.shape
    turn = (
        lax.broadcasted_iota(jnp.int32, (per, per), 1)
        == (lax.broadcasted_iota(jnp.int32, (per, per), 0) ^ flip)
    ).astype(BF16)
    column = first + lax.broadcasted_iota(jnp.int32, (per, cols), 1)
    for k, logits_ref in enumerate((top_ref, low_ref)):
        stats = jnp.concatenate([stats_ref[k], jnp.zeros((128 - STAT_ROWS, per), F32)]).T
        peak, hard, soft, tpeak, tsum, ids = [stats[:, i : i + 1] for i in range(6)]
        half = jnp.exp((logits_ref[...] - peak) * 0.5)
        taught = jnp.exp((aligned_ref[k, 0].astype(F32) - tpeak) * 0.5)
        label = jnp.where(column == ids.astype(jnp.int32), 16.0, 0.0)
        grad = (half * (32.0 / soft) - taught * (32.0 / tsum)) + (half * half * (16.0 / hard) - label)
        grad = grad.astype(BF16)
        grad_ref[k] = grad
        mixed[k * per : (k + 1) * per, :] = jnp.dot(turn, grad, preferred_element_type=F32).astype(BF16)
    rows = mixed[...]
    for c in range(depth // chunk):
        part = slice(c * chunk, (c + 1) * chunk)
        copies[c].wait()
        out = lax.dot_general(
            rows, weights[part, :], (((1,), (1,)), ((), ())), preferred_element_type=F32
        ).astype(BF16)
        back_ref[0, :, part] = out[:per]
        back_ref[1, :, part] = out[per:]


def back_rows(at, near, far, aligned, stats, head_weight, which):
    depth, cols = head_weight.shape
    per = near.shape[0] // 2
    chunk = 512 if depth % 512 == 0 else depth
    paired = lambda i: (0, which, 0, 0)
    return pl.pallas_call(
        lambda *refs: back_kernel(chunk, *refs),
        grid=(1,),
        out_shape=(
            jax.ShapeDtypeStruct((2, per, cols), BF16),
            jax.ShapeDtypeStruct((2, per, depth), BF16),
        ),
        in_specs=[
            SMEM,
            pl.BlockSpec((per, cols), lambda i: (which, 0)),
            pl.BlockSpec((per, cols), lambda i: (which, 0)),
            pl.BlockSpec((2, 1, per, cols), paired),
            pl.BlockSpec((2, STAT_ROWS, per), lambda i: (0, 0, which)),
            HBM,
        ],
        out_specs=(
            pl.BlockSpec((2, per, cols), lambda i: (0, 0, 0)),
            pl.BlockSpec((2, per, depth), lambda i: (0, 0, 0)),
        ),
        scratch_shapes=[
            pltpu.VMEM((2 * per, cols), BF16),
            pltpu.VMEM((depth, cols), BF16),
            pltpu.SemaphoreType.DMA((depth // chunk,)),
        ],
        compiler_params=PARAMS,
        cost_estimate=pl.CostEstimate(
            flops=4 * per * depth * cols,
            bytes_accessed=depth * cols * 2 + 4 * per * depth,
            transcendentals=4 * per * cols,
        ),
        name="back_rows",
    )(at, near, far, aligned, stats, head_weight)


def head_kernel(near_ref, far_ref, even_ref, odd_ref, out_ref, grads):
    @pl.when(pl.program_id(0) == 0)
    def _():
        per = even_ref.shape[1]
        for k, block in enumerate((even_ref[0], odd_ref[0], even_ref[1], odd_ref[1])):
            grads[k * per : (k + 1) * per, :] = block

    rows = jnp.concatenate([near_ref[...], far_ref[...]])
    out_ref[...] = lax.dot_general(
        rows, grads[...], (((0,), (0,)), ((), ())), preferred_element_type=F32
    ).astype(BF16)


def head_gradient(near, far, even, odd):
    rows, depth = near.shape
    _, per, cols = even.shape
    tile = 512 if depth % 512 == 0 else depth
    whole = pl.BlockSpec((2, per, cols), lambda i: (0, 0, 0))
    slab = pl.BlockSpec((rows, tile), lambda i: (0, i))
    return pl.pallas_call(
        head_kernel,
        grid=(depth // tile,),
        out_shape=jax.ShapeDtypeStruct((depth, cols), BF16),
        in_specs=[slab, slab, whole, whole],
        out_specs=pl.BlockSpec((tile, cols), lambda i: (i, 0)),
        scratch_shapes=[pltpu.VMEM((4 * per, cols), BF16)],
        compiler_params=PARAMS,
        cost_estimate=pl.CostEstimate(
            flops=4 * rows * depth * cols,
            bytes_accessed=(2 * rows + cols) * depth * 2 + 2 * rows * cols * 2,
            transcendentals=0,
        ),
        name="head_gradient",
    )(near, far, even, odd)


def merge_rows(a, b):
    top = jnp.maximum(a, b)
    peak, tpeak = top[0:1], top[3:4]
    shrink = []
    for part in (a, b):
        s = jnp.exp((part[0:1] - peak) * 0.5)
        t = jnp.exp((part[3:4] - tpeak) * 0.5)
        shrink.append((part[1:2] * (s * s), part[2:3] * s, part[4:5] * t))
    hard, soft, tsum = [p + q for p, q in zip(*shrink)]
    return jnp.concatenate([peak, hard, soft, tpeak, tsum, top[5:]])


def merge_kernel(order, mine_ref, got_ref, out_ref):
    per = mine_ref.shape[2]
    for p in range(2):
        for i in range(2):
            here = (p, slice(None), slice(i * per // 2, (i + 1) * per // 2))
            q, j = order(p, i)
            there = (q, slice(None), slice(j * per // 2, (j + 1) * per // 2))
            out_ref[here] = merge_rows(mine_ref[here], got_ref[there])


def merge(mine, got, mask):
    order = lambda p, i: (p ^ (mask >> 1), i ^ (mask & 1))
    return pl.pallas_call(
        lambda *refs: merge_kernel(order, *refs),
        out_shape=jax.ShapeDtypeStruct(mine.shape, F32),
        in_specs=[VMEM, VMEM],
        out_specs=VMEM,
        cost_estimate=pl.CostEstimate(flops=0, bytes_accessed=3 * mine.size * 4, transcendentals=0),
        name="merge_stats",
    )(mine, got)


def gather_kernel(near_ref, far_ref, tstats_ref, ids_ref, out_ref):
    per2 = near_ref.shape[1]
    per = per2 // 2
    for p, ref in enumerate((near_ref, far_ref)):
        out_ref[p, 0:3, :] = ref[0:3, :]
        out_ref[p, 3:5, :] = tstats_ref[0:2, p * per2 : (p + 1) * per2]
        out_ref[p, 5:8, :] = jnp.zeros((3, per2), F32)
    out_ref[0, 5:6, 0:per] = ids_ref[...].astype(F32)


def first_stats(near, far, tstats, ids):
    return pl.pallas_call(
        gather_kernel,
        out_shape=jax.ShapeDtypeStruct((2,) + near.shape, F32),
        in_specs=[VMEM] * 4,
        out_specs=VMEM,
        cost_estimate=pl.CostEstimate(flops=0, bytes_accessed=2 * near.size * 8, transcendentals=0),
        name="first_stats",
    )(near, far, tstats, ids.reshape(1, -1))


def body(hidden, token_ids, serving, head_weight, teacher_logits):
    groups = lax.axis_size("grp")
    shards = lax.axis_size("vocab")
    me_g = lax.axis_index("grp")
    me_v = lax.axis_index("vocab")
    per, depth = hidden.shape
    cols = head_weight.shape[1]
    owned = per // shards
    CORE, X = shards, 2 * shards
    Y, W = 1, 2
    count = groups * shards

    def swap(value, mask):
        return lax.ppermute(value, AXES, [(i, i ^ mask) for i in range(count)])

    quarter_rows = per // 4
    quarter = me_v & 3
    starts = [(quarter ^ k) * quarter_rows for k in range(4)]
    first = lax.dynamic_slice_in_dim(hidden, starts[0], quarter_rows, 0)
    second = lax.dynamic_slice_in_dim(hidden, starts[3], quarter_rows, 0)
    x0 = swap(first, X)
    x3 = swap(second, X)
    from_core = swap(hidden, CORE)
    arrived = lax.all_to_all(teacher_logits, "grp", split_axis=1, concat_axis=0, tiled=True)
    x1 = swap(x0, Y)
    x2 = swap(x0, W)
    late_at = jnp.stack(starts + [per + s for s in starts]).astype(jnp.int32)
    near_logits, near_stats, near_rows = student_logits(
        late_at, [hidden, from_core], [0, per], head_weight
    )
    aligned, tstats = teacher_rows(
        me_g.astype(jnp.int32).reshape(1), serving, arrived.reshape(groups * per, cols), groups
    )
    x1, near_logits = lax.optimization_barrier((x1, near_logits))
    xs = [x0, x1, x2, x3]
    ds = [swap(piece, CORE) for piece in xs]
    far_logits, far_stats, far_rows = student_logits(
        late_at, xs + ds, [(k,) for k in range(8)], head_weight
    )

    stats = first_stats(near_stats, far_stats, tstats, token_ids)
    stats = merge(stats, swap(stats, CORE), 1)
    stats = merge(stats, swap(stats, X), 2)
    mask = Y
    while mask < shards:
        stats = merge(stats, swap(stats, mask), 0)
        mask *= 2

    at = jnp.stack([(me_g * shards + me_v) * cols, me_v * owned]).astype(jnp.int32)
    pairs = aligned.reshape(2, 2, per, cols)
    odd, away = back_rows(at, near_logits, far_logits, pairs, stats, head_weight, 1)
    recv = swap(away, CORE)
    even, keep = back_rows(at, near_logits, far_logits, pairs, stats, head_weight, 0)

    bits = shards.bit_length() - 1
    shape = (2,) * (1 + bits) + (owned, depth)
    held = [keep.reshape(shape), recv.reshape(shape)]
    masks = {0: X}
    for b in range(bits):
        masks[1 + b] = shards >> (1 + b)
    ydim, wdim = bits, bits - 1
    units = depth // 128
    third = units // 3
    edges = [0, third * 128, 2 * third * 128, depth]
    orders = [(0, ydim, wdim), (ydim, wdim, 0), (wdim, 0, ydim)]
    parts = [[h[..., edges[p] : edges[p + 1]] for h in held] for p in range(3)]
    grad_head = None
    for stage in range(3):
        sents = [
            sum(lax.index_in_dim(t, 1, orders[p][stage]).astype(F32) for t in parts[p]).astype(BF16)
            for p in range(3)
        ]
        gots = [swap(sents[p], masks[orders[p][stage]]) for p in range(3)]
        if stage == 0:
            grad_head = head_gradient(near_rows, far_rows, even, odd)
            grad_head, *gots = lax.optimization_barrier((grad_head, *gots))
        for p in range(3):
            parts[p] = [lax.index_in_dim(t, 0, orders[p][stage]) for t in parts[p]] + [gots[p]]
    total = jnp.concatenate([sum(t.astype(F32) for t in terms) for terms in parts], axis=-1)
    for dim in range(1, wdim):
        got = swap(lax.index_in_dim(total, 1, dim).astype(BF16), masks[dim])
        total = lax.index_in_dim(total, 0, dim) + got.astype(F32)
    return (total.reshape(owned, depth), grad_head)


def solution(mesh):
    placed = (P("grp", None), P("grp"), P(), P(None, ("grp", "vocab")), P("grp", None, "vocab"))
    return jax.shard_map(
        body,
        mesh=mesh,
        in_specs=placed,
        out_specs=(P(("grp", "vocab"), None), P(None, ("grp", "vocab"))),
        check_vma=False,
    )
```

```python
import jax
import jax.numpy as jnp
from jax import lax
from jax.experimental import pallas as pl
from jax.experimental.pallas import tpu as pltpu
from jax.sharding import PartitionSpec as P

BF16 = jnp.bfloat16
F32 = jnp.float32
AXES = ("grp", "vocab")
VMEM = pl.BlockSpec(memory_space=pltpu.VMEM)
SMEM = pl.BlockSpec(memory_space=pltpu.SMEM)
STAT_ROWS = 8
MIB = 2**20


def params(mib):
    return pltpu.CompilerParams(vmem_limit_bytes=mib * MIB)


def cost(flops, nbytes, exps=0):
    return pl.CostEstimate(flops=flops, bytes_accessed=nbytes, transcendentals=exps)


def shape(dims, dtype):
    return jax.ShapeDtypeStruct(dims, dtype)


def columns_to_rows(columns):
    count = columns[0].shape[0]
    lane = lax.broadcasted_iota(jnp.int32, (count, 128), 1)
    wide = jnp.zeros((count, 128), F32)
    for k, column in enumerate(columns):
        wide = jnp.where(lane == k, column, wide)
    return wide.T[:STAT_ROWS]


def teacher_kernel(at_ref, serving_ref, a0, a1, a2, a3, aligned_ref, stats_ref):
    me, core = at_ref[0], at_ref[1]
    _, per, cols = a0.shape
    for j in range(2):
        wanted = serving_ref[me ^ (2 * j)]
        sums = [0.0, 0.0]
        for k, arrived in enumerate((a0, a1, a2, a3)):
            row = lax.broadcasted_iota(jnp.int32, (per, per), 0) + (me ^ k) * per
            pick = (row == wanted).astype(BF16)
            for c in range(2):
                sums[c] += lax.dot_general(
                    pick, arrived[core ^ c], (((0,), (0,)), ((), ())), preferred_element_type=F32
                )
        peak = jnp.maximum(*[jnp.max(s, axis=1, keepdims=True) for s in sums])
        total = sum(jnp.sum(jnp.exp((s - peak) * 0.5), axis=1, keepdims=True) for s in sums)
        for c in range(2):
            aligned_ref[j, :, c * cols : (c + 1) * cols] = sums[c].astype(BF16)
        stats_ref[j] = columns_to_rows([peak, total])


def teacher_rows(at, serving, arrived):
    _, per, cols = arrived[0].shape
    groups = serving.shape[0] // per
    return pl.pallas_call(
        teacher_kernel,
        out_shape=(shape((2, per, 2 * cols), BF16), shape((2, STAT_ROWS, per), F32)),
        in_specs=[SMEM] + [VMEM] * 5,
        out_specs=(VMEM, VMEM),
        compiler_params=params(10),
        cost_estimate=cost(32 * per * per * cols, 12 * per * cols * 2, 4 * per * cols),
        name="teacher_rows",
    )(at, serving.reshape(groups, 1, per), *arrived)


def logits_of(rows, own_ref, other_ref, logits_ref):
    cols = own_ref.shape[1]
    a = jnp.dot(rows, own_ref[...], preferred_element_type=F32)
    b = jnp.dot(rows, other_ref[...], preferred_element_type=F32)
    logits_ref[:, :cols] = a
    logits_ref[:, cols:] = b
    peak = jnp.maximum(jnp.max(a, axis=1, keepdims=True), jnp.max(b, axis=1, keepdims=True))
    a = jnp.exp((a - peak) * 0.5)
    b = jnp.exp((b - peak) * 0.5)
    hard = jnp.sum(a * a, axis=1, keepdims=True) + jnp.sum(b * b, axis=1, keepdims=True)
    soft = jnp.sum(a, axis=1, keepdims=True) + jnp.sum(b, axis=1, keepdims=True)
    return columns_to_rows([peak, hard, soft])


def near_kernel(rows_ref, own_ref, other_ref, logits_ref, stats_ref):
    stats_ref[...] = logits_of(rows_ref[...], own_ref, other_ref, logits_ref)


def near_logits(rows, own, other):
    per, depth = rows.shape
    cols = own.shape[1]
    return pl.pallas_call(
        near_kernel,
        out_shape=(shape((per, 2 * cols), F32), shape((STAT_ROWS, per), F32)),
        in_specs=[VMEM] * 3,
        out_specs=(VMEM, VMEM),
        compiler_params=params(16),
        cost_estimate=cost(4 * per * depth * cols, (per + 2 * cols) * depth * 2, 2 * per * cols),
        name="near_logits",
    )(rows, own, other)


def far_kernel(spots_ref, x0, x1, x2, x3, own_ref, other_ref, near_ref, taught_ref, ids_ref, logits_ref, rows_ref, out_ref):
    count = x0.shape[0]
    for k, piece in enumerate((x0, x1, x2, x3)):
        rows_ref[pl.ds(pl.multiple_of(spots_ref[k], 16), count), :] = piece[...]
    stats = logits_of(rows_ref[...], own_ref, other_ref, logits_ref)
    per = rows_ref.shape[0]
    for j, student in enumerate((near_ref[...], stats)):
        out_ref[j, 0:3, :] = student[0:3]
        out_ref[j, 3:5, :] = taught_ref[j, 0:2, :]
        out_ref[j, 5:8, :] = jnp.zeros((3, per), F32)
    out_ref[0, 5:6, :] = ids_ref[...].astype(F32)


def far_logits(spots, pieces, own, other, near_stats, taught, ids):
    depth, cols = own.shape
    per = sum(piece.shape[0] for piece in pieces)
    return pl.pallas_call(
        far_kernel,
        out_shape=(
            shape((per, 2 * cols), F32),
            shape((per, depth), BF16),
            shape((2, STAT_ROWS, per), F32),
        ),
        in_specs=[SMEM] + [VMEM] * 9,
        out_specs=(VMEM, VMEM, VMEM),
        compiler_params=params(20),
        cost_estimate=cost(4 * per * depth * cols, (per + 2 * cols) * depth * 2, 2 * per * cols),
        name="far_logits",
    )(spots, *pieces, own, other, near_stats, taught, ids.reshape(1, per))


def merged(parts):
    top = parts[0]
    for part in parts[1:]:
        top = jnp.maximum(top, part)
    hard = soft = total = 0.0
    for part in parts:
        s = jnp.exp((part[0:1] - top[0:1]) * 0.5)
        t = jnp.exp((part[3:4] - top[3:4]) * 0.5)
        hard += part[1:2] * (s * s)
        soft += part[2:3] * s
        total += part[4:5] * t
    return top[0:1], hard, soft, top[3:4], total, top[5:]


def merge_kernel(flips, *refs):
    out_ref = refs[-1]
    for j in range(2):
        out_ref[j] = jnp.concatenate(merged([ref[j ^ f] for ref, f in zip(refs, flips)]))


def merge(parts, flips):
    return pl.pallas_call(
        lambda *refs: merge_kernel(flips, *refs),
        out_shape=shape(parts[0].shape, F32),
        in_specs=[VMEM] * len(parts),
        out_specs=VMEM,
        compiler_params=params(2),
        cost_estimate=cost(0, 5 * parts[0].size * 4),
        name="merge_stats",
    )(*parts)


def picker(bit, side, flip, total):
    row = lax.broadcasted_iota(jnp.int32, (total // 2, total), 0)
    low = row & ((1 << bit) - 1)
    row = ((row >> bit) << (bit + 1)) + (side << bit) + low
    return (lax.broadcasted_iota(jnp.int32, (total // 2, total), 1) == (row ^ flip)).astype(BF16)


def push_back(bits, edges, side, flip, own, other, wown_ref, wother_ref, out_refs):
    for p, out_ref in enumerate(out_refs):
        pick = picker(bits[p], side, flip, own.shape[0])
        part = slice(edges[p], edges[p + 1])
        total = 0.0
        for grad, w_ref in ((own, wown_ref), (other, wother_ref)):
            rows = jnp.dot(pick, grad, preferred_element_type=F32).astype(BF16)
            total += lax.dot_general(
                rows, w_ref[part, :], (((1,), (1,)), ((), ())), preferred_element_type=F32
            )
        out_ref[...] = total.astype(out_ref.dtype)


def send_kernel(bits, edges, n, at_ref, *refs):
    stats_refs = refs[:n]
    near_ref, far_ref, aligned_ref, wown_ref, wother_ref = refs[n : n + 5]
    gown_ref, gother_ref = refs[n + 5 : n + 7]
    out_refs = refs[n + 7 :]
    flip = at_ref[0]
    per, wide = near_ref.shape
    cols = wide // 2
    for j, logits_ref in enumerate((near_ref, far_ref)):
        rows = merged([ref[j] for ref in stats_refs])
        stats = jnp.concatenate(rows + (jnp.zeros((128 - STAT_ROWS, per), F32),)).T
        peak, hard, soft, tpeak, total, ids = [stats[:, i : i + 1] for i in range(6)]
        ids = ids.astype(jnp.int32)
        hard, soft, total = 16.0 / hard, 32.0 / soft, 32.0 / total
        for c, g_ref in enumerate((gown_ref, gother_ref)):
            part = slice(c * cols, (c + 1) * cols)
            column = at_ref[1 + c] + lax.broadcasted_iota(jnp.int32, (per, cols), 1)
            half = jnp.exp((logits_ref[:, part] - peak) * 0.5)
            taught = jnp.exp((aligned_ref[j, :, part].astype(F32) - tpeak) * 0.5)
            label = jnp.where(column == ids, 16.0, 0.0)
            grad = (half * soft - taught * total) + (half * half * hard - label)
            g_ref[j * per : (j + 1) * per, :] = grad.astype(BF16)
    push_back(bits, edges, 1, flip, gown_ref[...], gother_ref[...], wown_ref, wother_ref, out_refs)


def keep_kernel(bits, edges, at_ref, gown_ref, gother_ref, wown_ref, wother_ref, *out_refs):
    push_back(bits, edges, 0, at_ref[0], gown_ref[...], gother_ref[...], wown_ref, wother_ref, out_refs)


def send_rows(at, stats, near, far, aligned, own, other, bits, edges):
    depth, cols = own.shape
    per = near.shape[0]
    outs = [shape((per, edges[p + 1] - edges[p]), BF16) for p in range(3)]
    got = pl.pallas_call(
        lambda *refs: send_kernel(bits, edges, len(stats), *refs),
        out_shape=[shape((2 * per, cols), BF16)] * 2 + outs,
        in_specs=[SMEM] + [VMEM] * (len(stats) + 5),
        out_specs=[VMEM] * 5,
        compiler_params=params(20),
        cost_estimate=cost(4 * per * depth * cols, 2 * cols * depth * 2, 4 * per * cols),
        name="send_rows",
    )(at, *stats, near, far, aligned, own, other)
    return got[0], got[1], got[2:]


def keep_rows(at, gown, gother, own, other, bits, edges):
    depth, cols = own.shape
    per = gown.shape[0] // 2
    outs = [shape((per, edges[p + 1] - edges[p]), F32) for p in range(3)]
    return pl.pallas_call(
        lambda *refs: keep_kernel(bits, edges, *refs),
        out_shape=outs,
        in_specs=[SMEM] + [VMEM] * 4,
        out_specs=[VMEM] * 3,
        compiler_params=params(20),
        cost_estimate=cost(4 * per * depth * cols, 2 * cols * depth * 2),
        name="keep_rows",
    )(at, gown, gother, own, other)


def head_kernel(r0, r1, r2, r3, mine_ref, theirs_ref, out_ref):
    rows = jnp.concatenate([r0[...], r1[...], r2[...], r3[...]])
    grads = jnp.concatenate([mine_ref[...], theirs_ref[...]])
    out_ref[...] = lax.dot_general(
        rows, grads, (((0,), (0,)), ((), ())), preferred_element_type=F32
    ).astype(BF16)


def head_gradient(rows, mine, theirs):
    per, depth = rows[0].shape
    cols = mine.shape[1]
    tile = 512 if depth % 512 == 0 else depth
    whole = pl.BlockSpec((2 * per, cols), lambda i: (0, 0))
    slab = pl.BlockSpec((per, tile), lambda i: (0, i))
    return pl.pallas_call(
        head_kernel,
        grid=(depth // tile,),
        out_shape=shape((depth, cols), BF16),
        in_specs=[slab] * 4 + [whole] * 2,
        out_specs=pl.BlockSpec((tile, cols), lambda i: (i, 0)),
        compiler_params=params(12),
        cost_estimate=cost(8 * per * depth * cols, (4 * per + cols) * depth * 2),
        name="head_gradient",
    )(*rows, mine, theirs)


def body(hidden, token_ids, serving, head_weight, teacher_logits):
    groups = lax.axis_size("grp")
    shards = lax.axis_size("vocab")
    me_g = lax.axis_index("grp")
    me_v = lax.axis_index("vocab")
    per, depth = hidden.shape
    cols = head_weight.shape[1]
    owned = per // shards
    CORE, X = shards, 2 * shards
    Y, W = 1, 2
    count = groups * shards

    def swap(value, mask):
        return lax.ppermute(value, AXES, [(i, i ^ mask) for i in range(count)])

    def tie(*values):
        return lax.optimization_barrier(values)

    def ints(*values):
        return jnp.stack([jnp.asarray(v, jnp.int32) for v in values])

    quarter_rows = per // 4
    quarter = me_v & 3
    starts = [(quarter ^ k) * quarter_rows for k in range(4)]
    x0 = swap(lax.dynamic_slice_in_dim(hidden, starts[0], quarter_rows, 0), X)
    other_weight = swap(head_weight, CORE)
    second = lax.dynamic_slice_in_dim(hidden, starts[3], quarter_rows, 0)
    chip = me_g >> 1
    kept = lax.dynamic_slice_in_dim(teacher_logits, 2 * chip, 2, 1).swapaxes(0, 1)
    gone = lax.dynamic_slice_in_dim(teacher_logits, 2 * (chip ^ 1), 2, 1).swapaxes(0, 1)
    x0, second, kept, gone, near_in = tie(x0, second, kept, gone, hidden)
    x1 = swap(x0, Y)
    x2 = swap(x0, W)
    x3 = swap(second, X)
    taught_x = swap(gone, X)
    taught_core = swap(kept, CORE)
    logits0, stats0 = near_logits(near_in, head_weight, other_weight)
    taught_far = swap(taught_x, CORE)
    aligned, taught_stats = teacher_rows(
        ints(me_g, me_g & 1), serving, [kept, taught_core, taught_x, taught_far]
    )
    logits1, x_rows, stats = far_logits(
        ints(*starts), [x0, x1, x2, x3], head_weight, other_weight, stats0, taught_stats, token_ids
    )

    stats = merge([stats, swap(stats, X), swap(stats, Y), swap(stats, X + Y)], (0, 1, 0, 1))
    core_rows = swap(hidden, CORE)
    stats, x_sent = tie(stats, x_rows)
    core_x_rows = swap(x_sent, CORE)
    mask = W
    while True:
        masks = [mask, 2 * mask, 3 * mask] if 2 * mask < shards else [mask]
        parts = [stats] + [swap(stats, m) for m in masks]
        mask *= 4
        if mask >= shards:
            break
        stats = merge(parts, (0,) * len(parts))

    bits = shards.bit_length() - 1
    masks = {0: X}
    for b in range(bits):
        masks[1 + b] = shards >> (1 + b)
    ydim, wdim = bits, bits - 1
    third = depth // 128 // 3 * 128
    edges = (0, third, 2 * third, depth)
    orders = [(0, ydim, wdim), (ydim, wdim, 0), (wdim, 0, ydim)]
    low = owned.bit_length() - 1
    row_bit = {0: low + bits, ydim: low, wdim: low + 1}
    first_bits = tuple(row_bit[order[0]] for order in orders)
    at = ints(
        me_v * owned, (me_g * shards + me_v) * cols, ((me_g ^ 1) * shards + me_v) * cols
    )
    gown, gother, sents = send_rows(
        at, parts, logits0, logits1, aligned, head_weight, other_weight, first_bits, edges
    )
    gots = [swap(sents[p], masks[orders[p][0]]) for p in range(3)]
    theirs = swap(gother, CORE)
    keeps = keep_rows(at, gown, gother, head_weight, other_weight, first_bits, edges)
    grad_head = head_gradient([hidden, x_rows, core_rows, core_x_rows], gown, theirs)
    grad_head, *gots = tie(grad_head, *gots)

    def folded(value, p):
        dims = [2] * (1 + bits)
        dims[orders[p][0]] = 1
        return value.reshape(*dims, owned, value.shape[-1])

    terms = [[folded(keeps[p], p), folded(gots[p], p)] for p in range(3)]
    for stage in (1, 2):
        sents = [
            sum(lax.index_in_dim(t, 1, orders[p][stage]).astype(F32) for t in terms[p]).astype(BF16)
            for p in range(3)
        ]
        gots = [swap(sents[p], masks[orders[p][stage]]) for p in range(3)]
        for p in range(3):
            terms[p] = [lax.index_in_dim(t, 0, orders[p][stage]) for t in terms[p]] + [gots[p]]
    total = jnp.concatenate([sum(t.astype(F32) for t in ts) for ts in terms], axis=-1)
    for dim in range(1, wdim):
        got = swap(lax.index_in_dim(total, 1, dim).astype(BF16), masks[dim])
        total = lax.index_in_dim(total, 0, dim) + got.astype(F32)
    return (total.reshape(owned, depth), grad_head)


def solution(mesh):
    placed = (P("grp", None), P("grp"), P(), P(None, ("grp", "vocab")), P("grp", None, "vocab"))
    return jax.shard_map(
        body,
        mesh=mesh,
        in_specs=placed,
        out_specs=(P(("grp", "vocab"), None), P(None, ("grp", "vocab"))),
        check_vma=False,
    )
```

```python
import jax
import jax.numpy as jnp
from jax import lax
from jax.experimental import pallas as pl
from jax.experimental.pallas import tpu as pltpu
from jax.sharding import PartitionSpec as P

BF16 = jnp.bfloat16
F32 = jnp.float32
AXES = ("grp", "vocab")
VMEM = pl.BlockSpec(memory_space=pltpu.VMEM)
SMEM = pl.BlockSpec(memory_space=pltpu.SMEM)
STAT_ROWS = 8
MIB = 2**20


def params(mib):
    return pltpu.CompilerParams(vmem_limit_bytes=mib * MIB)


def cost(flops, nbytes, exps=0):
    return pl.CostEstimate(flops=flops, bytes_accessed=nbytes, transcendentals=exps)


def shape(dims, dtype):
    return jax.ShapeDtypeStruct(dims, dtype)


def columns_to_rows(columns):
    count = columns[0].shape[0]
    lane = lax.broadcasted_iota(jnp.int32, (count, 128), 1)
    wide = jnp.zeros((count, 128), F32)
    for k, column in enumerate(columns):
        wide = jnp.where(lane == k, column, wide)
    return wide.T[:STAT_ROWS]


def taught_kernel(kept_ref, gone_ref, out_ref):
    parts = [ref[c].astype(F32) for ref in (kept_ref, gone_ref) for c in range(2)]
    top = parts[0]
    for part in parts[1:]:
        top = jnp.maximum(top, part)
    peak = jnp.max(top, axis=1, keepdims=True)
    total = sum(jnp.exp((part - peak) * 0.5) for part in parts)
    out_ref[...] = columns_to_rows([peak, jnp.sum(total, axis=1, keepdims=True)])


def taught_stats(kept, gone):
    _, per, cols = kept.shape
    return pl.pallas_call(
        taught_kernel,
        out_shape=shape((STAT_ROWS, per), F32),
        in_specs=[VMEM] * 2,
        out_specs=VMEM,
        compiler_params=params(6),
        cost_estimate=cost(0, 4 * per * cols * 2, 4 * per * cols),
        name="taught_stats",
    )(kept, gone)


def teacher_kernel(at_ref, serving_ref, a0, a1, a2, a3, aligned_ref):
    me, core = at_ref[0], at_ref[1]
    _, per, cols = a0.shape
    for j in range(2):
        wanted = serving_ref[me ^ (2 * j)]
        sums = [0.0, 0.0]
        for k, arrived in enumerate((a0, a1, a2, a3)):
            row = lax.broadcasted_iota(jnp.int32, (per, per), 0) + (me ^ k) * per
            pick = (row == wanted).astype(BF16)
            for c in range(2):
                sums[c] += lax.dot_general(
                    pick, arrived[core ^ c], (((0,), (0,)), ((), ())), preferred_element_type=F32
                )
        for c in range(2):
            aligned_ref[j, :, c * cols : (c + 1) * cols] = sums[c].astype(BF16)


def teacher_rows(at, serving, arrived):
    _, per, cols = arrived[0].shape
    return pl.pallas_call(
        teacher_kernel,
        out_shape=shape((2, per, 2 * cols), BF16),
        in_specs=[SMEM] + [VMEM] * 5,
        out_specs=VMEM,
        compiler_params=params(10),
        cost_estimate=cost(32 * per * per * cols, 12 * per * cols * 2),
        name="teacher_rows",
    )(at, serving, *arrived)


def student_stats(logits_ref, a, b):
    cols = a.shape[1]
    logits_ref[:, :cols] = a
    logits_ref[:, cols:] = b
    peak = jnp.max(jnp.maximum(a, b), axis=1, keepdims=True)
    a = jnp.exp((a - peak) * 0.5)
    b = jnp.exp((b - peak) * 0.5)
    hard = jnp.sum(a * a + b * b, axis=1, keepdims=True)
    soft = jnp.sum(a + b, axis=1, keepdims=True)
    return columns_to_rows([peak, hard, soft])


def near_kernel(splits, rows_ref, w_ref, other_ref, logits_ref, stats_ref, own_ref, sems):
    step = w_ref.shape[0] // splits
    copies = []
    for c in range(splits):
        part = pl.ds(c * step, step)
        copies.append(pltpu.make_async_copy(w_ref.at[part], own_ref.at[part], sems.at[c]))
        copies[c].start()
    b = jnp.dot(rows_ref[...], other_ref[...], preferred_element_type=F32)
    a = 0.0
    for c in range(splits):
        copies[c].wait()
        part = slice(c * step, (c + 1) * step)
        a += jnp.dot(rows_ref[:, part], own_ref[part, :], preferred_element_type=F32)
    stats_ref[...] = student_stats(logits_ref, a, b)


def near_logits(rows, own, other):
    per, depth = rows.shape
    cols = own.shape[1]
    splits = 2 if depth % 256 == 0 else 1
    return pl.pallas_call(
        lambda *refs: near_kernel(splits, *refs),
        out_shape=(
            shape((per, 2 * cols), F32),
            shape((STAT_ROWS, per), F32),
            shape((depth, cols), BF16),
        ),
        in_specs=[VMEM, pl.BlockSpec(memory_space=pl.ANY), VMEM],
        out_specs=(VMEM, VMEM, VMEM),
        scratch_shapes=[pltpu.SemaphoreType.DMA((splits,))],
        compiler_params=params(16),
        cost_estimate=cost(4 * per * depth * cols, (per + 2 * cols) * depth * 2, 2 * per * cols),
        name="near_logits",
    )(rows, own, other)


NOTHING = -3.0e38


def far_kernel(spots_ref, x0, x1, x2, x3, own_ref, other_ref, near_ref, taught_ref, taught_core_ref, ids_ref, logits_ref, rows_ref, out_ref):
    count = x0.shape[0]
    for k, piece in enumerate((x0, x1, x2, x3)):
        rows_ref[pl.ds(pl.multiple_of(spots_ref[k], 16), count), :] = piece[...]
    per = rows_ref.shape[0]
    a = jnp.dot(rows_ref[...], own_ref[...], preferred_element_type=F32)
    b = jnp.dot(rows_ref[...], other_ref[...], preferred_element_type=F32)
    out_ref[0, 0:3, :] = near_ref[0:3, :]
    out_ref[0, 3:4, :] = ids_ref[...].astype(F32)
    out_ref[0, 4:6, :] = taught_ref[0:2, :]
    out_ref[0, 6:8, :] = taught_core_ref[0:2, :]
    out_ref[1, 0:3, :] = student_stats(logits_ref, a, b)[0:3]
    row = lax.broadcasted_iota(jnp.int32, (5, per), 0)
    out_ref[1, 3:8, :] = jnp.where((row == 1) | (row == 3), NOTHING, 0.0)


def far_logits(spots, pieces, own, other, near_stats, taught, taught_core, ids):
    depth, cols = own.shape
    per = sum(piece.shape[0] for piece in pieces)
    return pl.pallas_call(
        far_kernel,
        out_shape=(
            shape((per, 2 * cols), F32),
            shape((per, depth), BF16),
            shape((2, STAT_ROWS, per), F32),
        ),
        in_specs=[SMEM] + [VMEM] * 10,
        out_specs=(VMEM, VMEM, VMEM),
        compiler_params=params(20),
        cost_estimate=cost(4 * per * depth * cols, (per + 2 * cols) * depth * 2, 2 * per * cols),
        name="far_logits",
    )(spots, *pieces, own, other, near_stats, taught, taught_core, ids)


def merged(parts):
    top = parts[0]
    for part in parts[1:]:
        top = jnp.maximum(top, part)
    hard = soft = taught0 = taught1 = 0.0
    for part in parts:
        shrink = jnp.exp((part - top) * 0.5)
        s = shrink[0:1]
        hard += part[1:2] * (s * s)
        soft += part[2:3] * s
        taught0 += part[5:6] * shrink[4:5]
        taught1 += part[7:8] * shrink[6:7]
    return top[0:1], hard, soft, top[3:4], top[4:5], taught0, top[6:7], taught1


def merge_kernel(flips, *refs):
    out_ref = refs[-1]
    for j in range(2):
        out_ref[j] = jnp.concatenate(merged([ref[j ^ f] for ref, f in zip(refs, flips)]))


def merge(parts, flips, held):
    return pl.pallas_call(
        lambda *refs: merge_kernel(flips, *refs),
        out_shape=shape(parts[0].shape, F32),
        in_specs=[VMEM] * (len(parts) + len(held)),
        out_specs=VMEM,
        compiler_params=params(6),
        cost_estimate=cost(0, 5 * parts[0].size * 4),
        name="merge_stats",
    )(*parts, *held)


def picker(bit, flip, total):
    half = total // 2
    row = lax.broadcasted_iota(jnp.int32, (total, total), 0)
    side = jnp.where(row < half, 1 << bit, 0)
    row = row & (half - 1)
    row = ((row >> bit) << (bit + 1)) + side + (row & ((1 << bit) - 1))
    return (lax.broadcasted_iota(jnp.int32, (total, total), 1) == (row ^ flip)).astype(BF16)


def back_kernel(bits, edges, n, at_ref, *refs):
    stats_refs = refs[:n]
    serving_ref, near_ref, far_ref, aligned_ref, wown_ref, wother_ref = refs[n : n + 6]
    gown_ref, gother_ref = refs[n + 6 : n + 8]
    send_refs, keep_refs = refs[n + 8 : n + 11], refs[n + 11 :]
    flip, me = at_ref[0], at_ref[3]
    per, wide = near_ref.shape
    cols = wide // 2
    stats = [merged([ref[j] for ref in stats_refs]) for j in range(2)]
    lane = lax.broadcasted_iota(jnp.int32, (per, per), 1)
    for j, logits_ref in enumerate((near_ref, far_ref)):
        rows = stats[j][:4] + (serving_ref[me ^ (2 * j)].astype(F32),)
        columns = jnp.concatenate(rows + (jnp.zeros((128 - len(rows), per), F32),)).T
        peak, hard, soft, ids, wanted = [columns[:, i : i + 1] for i in range(len(rows))]
        ids, wanted = ids.astype(jnp.int32), wanted.astype(jnp.int32)
        tpeak = total = 0.0
        for k in range(4):
            here = wanted - (me ^ k) * per == lane
            taught = stats[k // 2][4 + 2 * (k % 2) : 6 + 2 * (k % 2)]
            tpeak += jnp.sum(jnp.where(here, taught[0], 0.0), axis=1, keepdims=True)
            total += jnp.sum(jnp.where(here, taught[1], 0.0), axis=1, keepdims=True)
        hard, soft, total = 16.0 / hard, 32.0 / soft, 32.0 / total
        for c, g_ref in enumerate((gown_ref, gother_ref)):
            part = slice(c * cols, (c + 1) * cols)
            column = at_ref[1 + c] + lax.broadcasted_iota(jnp.int32, (per, cols), 1)
            half = jnp.exp((logits_ref[:, part] - peak) * 0.5)
            taught = jnp.exp((aligned_ref[j, :, part].astype(F32) - tpeak) * 0.5)
            label = jnp.where(column == ids, 16.0, 0.0)
            grad = (half * soft - taught * total) + (half * half * hard - label)
            g_ref[j * per : (j + 1) * per, :] = grad.astype(BF16)
    for p in range(3):
        pick = picker(bits[p], flip, 2 * per)
        part = slice(edges[p], edges[p + 1])
        back = 0.0
        for g_ref, w_ref in ((gown_ref, wown_ref), (gother_ref, wother_ref)):
            rows = jnp.dot(pick, g_ref[...], preferred_element_type=F32).astype(BF16)
            back += lax.dot_general(
                rows, w_ref[part, :], (((1,), (1,)), ((), ())), preferred_element_type=F32
            )
        send_refs[p][...] = back[:per].astype(BF16)
        keep_refs[p][...] = back[per:]


def back_rows(at, stats, serving, near, far, aligned, own, other, bits, edges):
    depth, cols = own.shape
    per = near.shape[0]
    sends = [shape((per, edges[p + 1] - edges[p]), BF16) for p in range(3)]
    keeps = [shape((per, edges[p + 1] - edges[p]), F32) for p in range(3)]
    got = pl.pallas_call(
        lambda *refs: back_kernel(bits, edges, len(stats), *refs),
        out_shape=[shape((2 * per, cols), BF16)] * 2 + sends + keeps,
        in_specs=[SMEM] + [VMEM] * (len(stats) + 6),
        out_specs=[VMEM] * 8,
        compiler_params=params(24),
        cost_estimate=cost(8 * per * depth * cols, 2 * cols * depth * 2, 4 * per * cols),
        name="back_rows",
    )(at, *stats, serving, near, far, aligned, own, other)
    return got[0], got[1], got[2:5], got[5:8]


def head_kernel(r0, r1, r2, r3, mine_ref, theirs_ref, out_ref):
    rows = jnp.concatenate([r0[...], r1[...], r2[...], r3[...]])
    grads = jnp.concatenate([mine_ref[...], theirs_ref[...]])
    out_ref[...] = lax.dot_general(
        rows, grads, (((0,), (0,)), ((), ())), preferred_element_type=F32
    ).astype(BF16)


def head_gradient(rows, mine, theirs):
    per, depth = rows[0].shape
    cols = mine.shape[1]
    tile = 512 if depth % 512 == 0 else depth
    whole = pl.BlockSpec((2 * per, cols), lambda i: (0, 0))
    slab = pl.BlockSpec((per, tile), lambda i: (0, i))
    return pl.pallas_call(
        head_kernel,
        grid=(depth // tile,),
        out_shape=shape((depth, cols), BF16),
        in_specs=[slab] * 4 + [whole] * 2,
        out_specs=pl.BlockSpec((tile, cols), lambda i: (i, 0)),
        compiler_params=params(12),
        cost_estimate=cost(8 * per * depth * cols, (4 * per + cols) * depth * 2),
        name="head_gradient",
    )(*rows, mine, theirs)


def body(hidden, token_ids, serving, head_weight, teacher_logits):
    groups = lax.axis_size("grp")
    shards = lax.axis_size("vocab")
    me_g = lax.axis_index("grp")
    me_v = lax.axis_index("vocab")
    per, depth = hidden.shape
    cols = head_weight.shape[1]
    owned = per // shards
    CORE, X = shards, 2 * shards
    Y, W = 1, 2
    count = groups * shards

    def swap(value, mask):
        return lax.ppermute(value, AXES, [(i, i ^ mask) for i in range(count)])

    def tie(*values):
        return lax.optimization_barrier(values)

    def ints(*values):
        return jnp.stack([jnp.asarray(v, jnp.int32) for v in values])

    quarter_rows = per // 4
    quarter = me_v & 3
    starts = [(quarter ^ k) * quarter_rows for k in range(4)]
    x0 = swap(lax.dynamic_slice_in_dim(hidden, starts[0], quarter_rows, 0), X)
    other_weight = swap(head_weight, CORE)
    second = lax.dynamic_slice_in_dim(hidden, starts[3], quarter_rows, 0)
    chip = me_g >> 1
    kept = lax.dynamic_slice_in_dim(teacher_logits, 2 * chip, 2, 1).swapaxes(0, 1)
    gone = lax.dynamic_slice_in_dim(teacher_logits, 2 * (chip ^ 1), 2, 1).swapaxes(0, 1)
    taught = taught_stats(kept, gone)
    taught_core = swap(taught, CORE)
    x0, second, near_in = tie(x0, second, hidden)
    x1 = swap(x0, Y)
    x2 = swap(x0, W)
    x3 = swap(second, X)
    logits0, stats0, own_weight = near_logits(near_in, head_weight, other_weight)
    x3, gone, logits0 = tie(x3, gone, logits0)
    logits1, x_rows, stats = far_logits(
        ints(*starts),
        [x0, x1, x2, x3],
        own_weight,
        other_weight,
        stats0,
        taught,
        taught_core,
        token_ids.reshape(1, per),
    )

    served = serving.reshape(groups, 1, per)
    taught_x = swap(gone, X)
    arrived = [kept, swap(kept, CORE), taught_x, swap(taught_x, CORE)]
    aligned = teacher_rows(ints(me_g, me_g & 1), served, arrived)

    held = [logits0, logits1]
    stats = merge([stats, swap(stats, X), swap(stats, Y), swap(stats, X + Y)], (0, 1, 0, 1), held)
    core_rows = swap(hidden, CORE)
    stats, x_sent = tie(stats, x_rows)
    core_x_rows = swap(x_sent, CORE)
    mask = W
    while True:
        masks = [mask, 2 * mask, 3 * mask] if 2 * mask < shards else [mask]
        parts = [stats] + [swap(stats, m) for m in masks]
        mask *= 4
        if mask >= shards:
            break
        stats = merge(parts, (0,) * len(parts), held)

    bits = shards.bit_length() - 1
    masks = {0: X}
    for b in range(bits):
        masks[1 + b] = shards >> (1 + b)
    ydim, wdim = bits, bits - 1
    third = depth // 128 // 3 * 128
    edges = (0, third, 2 * third, depth)
    orders = [(0, ydim, wdim), (ydim, wdim, 0), (wdim, 0, ydim)]
    low = owned.bit_length() - 1
    row_bit = {0: low + bits, ydim: low, wdim: low + 1}
    first_bits = tuple(row_bit[order[0]] for order in orders)
    at = ints(
        me_v * owned, (me_g * shards + me_v) * cols, ((me_g ^ 1) * shards + me_v) * cols, me_g
    )
    gown, gother, sents, keeps = back_rows(
        at, parts, served, logits0, logits1, aligned, own_weight, other_weight, first_bits, edges
    )
    gots = [swap(sents[p], masks[orders[p][0]]) for p in range(3)]
    theirs = swap(gother, CORE)
    grad_head = head_gradient([hidden, x_rows, core_rows, core_x_rows], gown, theirs)
    grad_head, *gots = tie(grad_head, *gots)

    def folded(value, p):
        dims = [2] * (1 + bits)
        dims[orders[p][0]] = 1
        return value.reshape(*dims, owned, value.shape[-1])

    terms = [[folded(keeps[p], p), folded(gots[p], p)] for p in range(3)]
    for stage in (1, 2):
        sents = [
            sum(lax.index_in_dim(t, 1, orders[p][stage]).astype(F32) for t in terms[p]).astype(BF16)
            for p in range(3)
        ]
        gots = [swap(sents[p], masks[orders[p][stage]]) for p in range(3)]
        for p in range(3):
            terms[p] = [lax.index_in_dim(t, 0, orders[p][stage]) for t in terms[p]] + [gots[p]]
    total = jnp.concatenate([sum(t.astype(F32) for t in ts) for ts in terms], axis=-1)
    for dim in range(1, wdim):
        got = swap(lax.index_in_dim(total, 1, dim).astype(BF16), masks[dim])
        total = lax.index_in_dim(total, 0, dim) + got.astype(F32)
    return (total.reshape(owned, depth), grad_head)


def solution(mesh):
    placed = (P("grp", None), P("grp"), P(), P(None, ("grp", "vocab")), P("grp", None, "vocab"))
    return jax.shard_map(
        body,
        mesh=mesh,
        in_specs=placed,
        out_specs=(P(("grp", "vocab"), None), P(None, ("grp", "vocab"))),
        check_vma=False,
    )
```

```python
import jax
import jax.numpy as jnp
from jax import lax
from jax.experimental import pallas as pl
from jax.experimental.pallas import tpu as pltpu
from jax.sharding import PartitionSpec as P

BF16 = jnp.bfloat16
F32 = jnp.float32
AXES = ("grp", "vocab")
VMEM = pl.BlockSpec(memory_space=pltpu.VMEM)
SMEM = pl.BlockSpec(memory_space=pltpu.SMEM)
STAT_ROWS = 8
MIB = 2**20


def params(mib):
    return pltpu.CompilerParams(vmem_limit_bytes=mib * MIB)


def cost(flops, nbytes, exps=0):
    return pl.CostEstimate(flops=flops, bytes_accessed=nbytes, transcendentals=exps)


def shape(dims, dtype):
    return jax.ShapeDtypeStruct(dims, dtype)


def columns_to_rows(columns):
    count = columns[0].shape[0]
    lane = lax.broadcasted_iota(jnp.int32, (count, 128), 1)
    wide = jnp.zeros((count, 128), F32)
    for k, column in enumerate(columns):
        wide = jnp.where(lane == k, column, wide)
    return wide.T[:STAT_ROWS]


def taught_kernel(kept_ref, gone_ref, out_ref):
    parts = [ref[c].astype(F32) for ref in (kept_ref, gone_ref) for c in range(2)]
    top = parts[0]
    for part in parts[1:]:
        top = jnp.maximum(top, part)
    peak = jnp.max(top, axis=1, keepdims=True)
    total = sum(jnp.exp((part - peak) * 0.5) for part in parts)
    out_ref[...] = columns_to_rows([peak, jnp.sum(total, axis=1, keepdims=True)])


def taught_stats(kept, gone):
    _, per, cols = kept.shape
    return pl.pallas_call(
        taught_kernel,
        out_shape=shape((STAT_ROWS, per), F32),
        in_specs=[VMEM] * 2,
        out_specs=VMEM,
        compiler_params=params(6),
        cost_estimate=cost(0, 4 * per * cols * 2, 4 * per * cols),
        name="taught_stats",
    )(kept, gone)


def teacher_kernel(at_ref, serving_ref, a0, a1, a2, a3, aligned_ref):
    me, core = at_ref[0], at_ref[1]
    _, per, cols = a0.shape
    for j in range(2):
        wanted = serving_ref[me ^ (2 * j)]
        sums = [0.0, 0.0]
        for k, arrived in enumerate((a0, a1, a2, a3)):
            row = lax.broadcasted_iota(jnp.int32, (per, per), 0) + (me ^ k) * per
            pick = (row == wanted).astype(BF16)
            for c in range(2):
                sums[c] += lax.dot_general(
                    pick, arrived[core ^ c], (((0,), (0,)), ((), ())), preferred_element_type=F32
                )
        for c in range(2):
            aligned_ref[j, :, c * cols : (c + 1) * cols] = sums[c].astype(BF16)


def teacher_rows(at, serving, arrived):
    _, per, cols = arrived[0].shape
    return pl.pallas_call(
        teacher_kernel,
        out_shape=shape((2, per, 2 * cols), BF16),
        in_specs=[SMEM] + [VMEM] * 5,
        out_specs=VMEM,
        compiler_params=params(10),
        cost_estimate=cost(32 * per * per * cols, 12 * per * cols * 2),
        name="teacher_rows",
    )(at, serving, *arrived)


def student_stats(logits):
    peak = jnp.max(logits, axis=1, keepdims=True)
    soft = jnp.exp((logits - peak) * 0.5)
    hard = jnp.sum(soft * soft, axis=1, keepdims=True)
    return columns_to_rows([peak, hard, jnp.sum(soft, axis=1, keepdims=True)])


def own_kernel(splits, rows_ref, w_ref, logits_ref, stats_ref, own_ref, sems):
    step = w_ref.shape[0] // splits
    copies = []
    for c in range(splits):
        part = pl.ds(c * step, step)
        copies.append(pltpu.make_async_copy(w_ref.at[part], own_ref.at[part], sems.at[c]))
        copies[c].start()
    logits = 0.0
    for c in range(splits):
        copies[c].wait()
        part = slice(c * step, (c + 1) * step)
        logits += jnp.dot(rows_ref[:, part], own_ref[part, :], preferred_element_type=F32)
    logits_ref[...] = logits
    stats_ref[...] = student_stats(logits)


def own_logits(rows, own):
    per, depth = rows.shape
    cols = own.shape[1]
    splits = 4 if depth % 512 == 0 else 1
    return pl.pallas_call(
        lambda *refs: own_kernel(splits, *refs),
        out_shape=(
            shape((per, cols), F32),
            shape((STAT_ROWS, per), F32),
            shape((depth, cols), BF16),
        ),
        in_specs=[VMEM, pl.BlockSpec(memory_space=pl.ANY)],
        out_specs=(VMEM, VMEM, VMEM),
        scratch_shapes=[pltpu.SemaphoreType.DMA((splits,))],
        compiler_params=params(10),
        cost_estimate=cost(2 * per * depth * cols, (per + 2 * cols) * depth * 2, per * cols),
        name="own_logits",
    )(rows, own)


def core_kernel(rows_ref, w_ref, held_ref, logits_ref, stats_ref):
    logits = jnp.dot(rows_ref[...], w_ref[...], preferred_element_type=F32)
    logits_ref[...] = logits
    stats_ref[...] = student_stats(logits)


def core_logits(rows, other, held):
    per, depth = rows.shape
    cols = other.shape[1]
    return pl.pallas_call(
        core_kernel,
        out_shape=(shape((per, cols), F32), shape((STAT_ROWS, per), F32)),
        in_specs=[VMEM] * 3,
        out_specs=(VMEM, VMEM),
        compiler_params=params(10),
        cost_estimate=cost(2 * per * depth * cols, (per + cols) * depth * 2, per * cols),
        name="core_logits",
    )(rows, other, held)


NOTHING = -3.0e38


def both(a, b):
    peak = jnp.maximum(a[0:1], b[0:1])
    ea, eb = jnp.exp((a[0:1] - peak) * 0.5), jnp.exp((b[0:1] - peak) * 0.5)
    return jnp.concatenate(
        [peak, a[1:2] * (ea * ea) + b[1:2] * (eb * eb), a[2:3] * ea + b[2:3] * eb]
    )


def far_kernel(spots_ref, x0, x1, x2, x3, own_ref, other_ref, stats_a, stats_b, taught_ref, taught_core_ref, ids_ref, a_ref, b_ref, rows_ref, out_ref):
    count = x0.shape[0]
    for k, piece in enumerate((x0, x1, x2, x3)):
        rows_ref[pl.ds(pl.multiple_of(spots_ref[k], 16), count), :] = piece[...]
    per = rows_ref.shape[0]
    a = jnp.dot(rows_ref[...], own_ref[...], preferred_element_type=F32)
    b = jnp.dot(rows_ref[...], other_ref[...], preferred_element_type=F32)
    a_ref[...] = a
    b_ref[...] = b
    out_ref[0, 0:3, :] = both(stats_a[...], stats_b[...])
    out_ref[0, 3:4, :] = ids_ref[...].astype(F32)
    out_ref[0, 4:6, :] = taught_ref[0:2, :]
    out_ref[0, 6:8, :] = taught_core_ref[0:2, :]
    out_ref[1, 0:3, :] = both(student_stats(a), student_stats(b))
    row = lax.broadcasted_iota(jnp.int32, (5, per), 0)
    out_ref[1, 3:8, :] = jnp.where((row == 1) | (row == 3), NOTHING, 0.0)


def far_logits(spots, pieces, own, other, stats_a, stats_b, taught, taught_core, ids):
    depth, cols = own.shape
    per = sum(piece.shape[0] for piece in pieces)
    return pl.pallas_call(
        far_kernel,
        out_shape=(
            shape((per, cols), F32),
            shape((per, cols), F32),
            shape((per, depth), BF16),
            shape((2, STAT_ROWS, per), F32),
        ),
        in_specs=[SMEM] + [VMEM] * 11,
        out_specs=(VMEM, VMEM, VMEM, VMEM),
        compiler_params=params(20),
        cost_estimate=cost(4 * per * depth * cols, (per + 2 * cols) * depth * 2, 2 * per * cols),
        name="far_logits",
    )(spots, *pieces, own, other, stats_a, stats_b, taught, taught_core, ids)


def merged(parts):
    top = parts[0]
    for part in parts[1:]:
        top = jnp.maximum(top, part)
    hard = soft = taught0 = taught1 = 0.0
    for part in parts:
        shrink = jnp.exp((part - top) * 0.5)
        s = shrink[0:1]
        hard += part[1:2] * (s * s)
        soft += part[2:3] * s
        taught0 += part[5:6] * shrink[4:5]
        taught1 += part[7:8] * shrink[6:7]
    return top[0:1], hard, soft, top[3:4], top[4:5], taught0, top[6:7], taught1


def merge_kernel(flips, *refs):
    out_ref = refs[-1]
    for j in range(2):
        out_ref[j] = jnp.concatenate(merged([ref[j ^ f] for ref, f in zip(refs, flips)]))


def merge(parts, flips, held):
    return pl.pallas_call(
        lambda *refs: merge_kernel(flips, *refs),
        out_shape=shape(parts[0].shape, F32),
        in_specs=[VMEM] * (len(parts) + len(held)),
        out_specs=VMEM,
        compiler_params=params(14),
        cost_estimate=cost(0, 5 * parts[0].size * 4),
        name="merge_stats",
    )(*parts, *held)


def picker(bit, flip, total):
    half = total // 2
    row = lax.broadcasted_iota(jnp.int32, (total, total), 0)
    side = jnp.where(row < half, 1 << bit, 0)
    row = row & (half - 1)
    row = ((row >> bit) << (bit + 1)) + side + (row & ((1 << bit) - 1))
    return (lax.broadcasted_iota(jnp.int32, (total, total), 1) == (row ^ flip)).astype(BF16)


def back_kernel(bits, edges, n, at_ref, *refs):
    stats_refs = refs[:n]
    logits_refs = refs[n : n + 4]
    serving_ref, aligned_ref, wown_ref, wother_ref = refs[n + 4 : n + 8]
    gown_ref, gother_ref = refs[n + 8 : n + 10]
    send_refs, keep_refs = refs[n + 10 : n + 13], refs[n + 13 :]
    flip, me = at_ref[0], at_ref[3]
    per, cols = logits_refs[0].shape
    stats = [merged([ref[j] for ref in stats_refs]) for j in range(2)]
    lane = lax.broadcasted_iota(jnp.int32, (per, per), 1)
    for j in range(2):
        rows = stats[j][:4] + (serving_ref[me ^ (2 * j)].astype(F32),)
        columns = jnp.concatenate(rows + (jnp.zeros((128 - len(rows), per), F32),)).T
        peak, hard, soft, ids, wanted = [columns[:, i : i + 1] for i in range(len(rows))]
        ids, wanted = ids.astype(jnp.int32), wanted.astype(jnp.int32)
        tpeak = total = 0.0
        for k in range(4):
            here = wanted - (me ^ k) * per == lane
            taught = stats[k // 2][4 + 2 * (k % 2) : 6 + 2 * (k % 2)]
            tpeak += jnp.sum(jnp.where(here, taught[0], 0.0), axis=1, keepdims=True)
            total += jnp.sum(jnp.where(here, taught[1], 0.0), axis=1, keepdims=True)
        hard, soft, total = 16.0 / hard, 32.0 / soft, 32.0 / total
        for c, g_ref in enumerate((gown_ref, gother_ref)):
            part = slice(c * cols, (c + 1) * cols)
            column = at_ref[1 + c] + lax.broadcasted_iota(jnp.int32, (per, cols), 1)
            half = jnp.exp((logits_refs[2 * j + c][...] - peak) * 0.5)
            taught = jnp.exp((aligned_ref[j, :, part].astype(F32) - tpeak) * 0.5)
            label = jnp.where(column == ids, 16.0, 0.0)
            grad = (half * soft - taught * total) + (half * half * hard - label)
            g_ref[j * per : (j + 1) * per, :] = grad.astype(BF16)
    for p in range(3):
        pick = picker(bits[p], flip, 2 * per)
        part = slice(edges[p], edges[p + 1])
        back = 0.0
        for g_ref, w_ref in ((gown_ref, wown_ref), (gother_ref, wother_ref)):
            rows = jnp.dot(pick, g_ref[...], preferred_element_type=F32).astype(BF16)
            back += lax.dot_general(
                w_ref[part, :], rows, (((1,), (1,)), ((), ())), preferred_element_type=F32
            )
        back = back.T
        send_refs[p][...] = back[:per].astype(BF16)
        keep_refs[p][...] = back[per:]


def back_rows(at, stats, logits, serving, aligned, own, other, bits, edges):
    depth, cols = own.shape
    per = logits[0].shape[0]
    sends = [shape((per, edges[p + 1] - edges[p]), BF16) for p in range(3)]
    keeps = [shape((per, edges[p + 1] - edges[p]), F32) for p in range(3)]
    got = pl.pallas_call(
        lambda *refs: back_kernel(bits, edges, len(stats), *refs),
        out_shape=[shape((2 * per, cols), BF16)] * 2 + sends + keeps,
        in_specs=[SMEM] + [VMEM] * (len(stats) + 8),
        out_specs=[VMEM] * 8,
        compiler_params=params(24),
        cost_estimate=cost(8 * per * depth * cols, 2 * cols * depth * 2, 4 * per * cols),
        name="back_rows",
    )(at, *stats, *logits, serving, aligned, own, other)
    return got[0], got[1], got[2:5], got[5:8]


def head_kernel(r0, r1, r2, r3, mine_ref, theirs_ref, out_ref):
    rows = jnp.concatenate([r0[...], r1[...], r2[...], r3[...]])
    grads = jnp.concatenate([mine_ref[...], theirs_ref[...]])
    out_ref[...] = lax.dot_general(
        rows, grads, (((0,), (0,)), ((), ())), preferred_element_type=F32
    ).astype(BF16)


def head_gradient(rows, mine, theirs):
    per, depth = rows[0].shape
    cols = mine.shape[1]
    tile = 512 if depth % 512 == 0 else depth
    whole = pl.BlockSpec((2 * per, cols), lambda i: (0, 0))
    slab = pl.BlockSpec((per, tile), lambda i: (0, i))
    return pl.pallas_call(
        head_kernel,
        grid=(depth // tile,),
        out_shape=shape((depth, cols), BF16),
        in_specs=[slab] * 4 + [whole] * 2,
        out_specs=pl.BlockSpec((tile, cols), lambda i: (i, 0)),
        compiler_params=params(12),
        cost_estimate=cost(8 * per * depth * cols, (4 * per + cols) * depth * 2),
        name="head_gradient",
    )(*rows, mine, theirs)


def body(hidden, token_ids, serving, head_weight, teacher_logits):
    groups = lax.axis_size("grp")
    shards = lax.axis_size("vocab")
    me_g = lax.axis_index("grp")
    me_v = lax.axis_index("vocab")
    per, depth = hidden.shape
    cols = head_weight.shape[1]
    owned = per // shards
    CORE, X = shards, 2 * shards
    Y, W = 1, 2
    count = groups * shards

    def swap(value, mask):
        return lax.ppermute(value, AXES, [(i, i ^ mask) for i in range(count)])

    def tie(*values):
        return lax.optimization_barrier(values)

    def ints(*values):
        return jnp.stack([jnp.asarray(v, jnp.int32) for v in values])

    quarter_rows = per // 4
    quarter = me_v & 3
    starts = [(quarter ^ k) * quarter_rows for k in range(4)]
    other_weight = swap(head_weight, CORE)
    first = lax.dynamic_slice_in_dim(hidden, starts[0], quarter_rows, 0)
    x0 = swap(first, X)
    _, rows, teacher = tie(first, hidden, teacher_logits)
    second = lax.dynamic_slice_in_dim(rows, starts[3], quarter_rows, 0)
    chip = me_g >> 1
    kept = lax.dynamic_slice_in_dim(teacher, 2 * chip, 2, 1).swapaxes(0, 1)
    gone = lax.dynamic_slice_in_dim(teacher, 2 * (chip ^ 1), 2, 1).swapaxes(0, 1)
    taught = taught_stats(kept, gone)
    near_a, stats_a, own_weight = own_logits(rows, head_weight)
    x0, second, kept, gone, taught, near_a, rows = tie(
        x0, second, kept, gone, taught, near_a, rows
    )
    x1 = swap(x0, Y)
    x2 = swap(x0, W)
    x3 = swap(second, X)
    taught_core = swap(taught, CORE)
    kept_core = swap(kept, CORE)
    near_b, stats_b = core_logits(rows, other_weight, x0)
    x1, x2, x3, gone, near_b, kept_core, taught_core = tie(
        x1, x2, x3, gone, near_b, kept_core, taught_core
    )
    taught_x = swap(gone, X)
    far_a, far_b, x_rows, stats = far_logits(
        ints(*starts),
        [x0, x1, x2, x3],
        own_weight,
        other_weight,
        stats_a,
        stats_b,
        taught,
        taught_core,
        token_ids.reshape(1, per),
    )

    served = serving.reshape(groups, 1, per)
    logits = [near_a, near_b, far_a, far_b]
    held = logits + [own_weight]
    stats = merge([stats, swap(stats, X), swap(stats, Y), swap(stats, X + Y)], (0, 1, 0, 1), held)
    _, taught_x, rows, x_sent = tie(stats, taught_x, rows, x_rows)
    core_rows = [swap(rows, CORE), swap(x_sent, CORE)]
    aligned = teacher_rows(
        ints(me_g, me_g & 1), served, [kept, kept_core, taught_x, swap(taught_x, CORE)]
    )
    aligned, *core_rows = tie(aligned, *core_rows)
    mask = W
    while True:
        masks = [mask, 2 * mask, 3 * mask] if 2 * mask < shards else [mask]
        parts = [stats] + [swap(stats, m) for m in masks]
        mask *= 4
        if mask >= shards:
            break
        stats = merge(parts, (0,) * len(parts), held)

    bits = shards.bit_length() - 1
    masks = {0: X}
    for b in range(bits):
        masks[1 + b] = shards >> (1 + b)
    ydim, wdim = bits, bits - 1
    third = depth // 128 // 3 * 128
    edges = (0, third, 2 * third, depth)
    orders = [(0, ydim, wdim), (ydim, wdim, 0), (wdim, 0, ydim)]
    low = owned.bit_length() - 1
    row_bit = {0: low + bits, ydim: low, wdim: low + 1}
    first_bits = tuple(row_bit[order[0]] for order in orders)
    at = ints(
        me_v * owned, (me_g * shards + me_v) * cols, ((me_g ^ 1) * shards + me_v) * cols, me_g
    )
    gown, gother, sents, keeps = back_rows(
        at, parts, logits, served, aligned, own_weight, other_weight, first_bits, edges
    )
    gots = [swap(sents[p], masks[orders[p][0]]) for p in range(3)]
    theirs = swap(gother, CORE)
    grad_head = head_gradient([hidden, x_rows] + core_rows, gown, theirs)
    grad_head, *gots = tie(grad_head, *gots)

    def folded(value, p):
        dims = [2] * (1 + bits)
        dims[orders[p][0]] = 1
        return value.reshape(*dims, owned, value.shape[-1])

    terms = [[folded(keeps[p], p), folded(gots[p], p)] for p in range(3)]
    for stage in (1, 2):
        sents = [
            sum(lax.index_in_dim(t, 1, orders[p][stage]).astype(F32) for t in terms[p]).astype(BF16)
            for p in range(3)
        ]
        gots = [swap(sents[p], masks[orders[p][stage]]) for p in range(3)]
        for p in range(3):
            terms[p] = [lax.index_in_dim(t, 0, orders[p][stage]) for t in terms[p]] + [gots[p]]
    total = jnp.concatenate([sum(t.astype(F32) for t in ts) for ts in terms], axis=-1)
    for dim in range(1, wdim):
        got = swap(lax.index_in_dim(total, 1, dim).astype(BF16), masks[dim])
        total = lax.index_in_dim(total, 0, dim) + got.astype(F32)
    return (total.reshape(owned, depth), grad_head)


def solution(mesh):
    placed = (P("grp", None), P("grp"), P(), P(None, ("grp", "vocab")), P("grp", None, "vocab"))
    return jax.shard_map(
        body,
        mesh=mesh,
        in_specs=placed,
        out_specs=(P(("grp", "vocab"), None), P(None, ("grp", "vocab"))),
        check_vma=False,
    )
```

```python
import jax
import jax.numpy as jnp
from jax import lax
from jax.experimental import pallas as pl
from jax.experimental.pallas import tpu as pltpu
from jax.sharding import PartitionSpec as P

BF16 = jnp.bfloat16
F32 = jnp.float32
AXES = ("grp", "vocab")
VMEM = pl.BlockSpec(memory_space=pltpu.VMEM)
SMEM = pl.BlockSpec(memory_space=pltpu.SMEM)
STAT_ROWS = 8
MIB = 2**20


def params(mib):
    return pltpu.CompilerParams(vmem_limit_bytes=mib * MIB)


def cost(flops, nbytes, exps=0):
    return pl.CostEstimate(flops=flops, bytes_accessed=nbytes, transcendentals=exps)


def shape(dims, dtype):
    return jax.ShapeDtypeStruct(dims, dtype)


def columns_to_rows(columns):
    count = columns[0].shape[0]
    lane = lax.broadcasted_iota(jnp.int32, (count, 128), 1)
    wide = jnp.zeros((count, 128), F32)
    for k, column in enumerate(columns):
        wide = jnp.where(lane == k, column, wide)
    return wide.T[:STAT_ROWS]


def taught_kernel(kept_ref, gone_ref, out_ref):
    parts = [ref[c].astype(F32) for ref in (kept_ref, gone_ref) for c in range(2)]
    top = parts[0]
    for part in parts[1:]:
        top = jnp.maximum(top, part)
    peak = jnp.max(top, axis=1, keepdims=True)
    total = sum(jnp.exp((part - peak) * 0.5) for part in parts)
    out_ref[...] = columns_to_rows([peak, jnp.sum(total, axis=1, keepdims=True)])


def taught_stats(kept, gone):
    _, per, cols = kept.shape
    return pl.pallas_call(
        taught_kernel,
        out_shape=shape((STAT_ROWS, per), F32),
        in_specs=[VMEM] * 2,
        out_specs=VMEM,
        compiler_params=params(4),
        cost_estimate=cost(0, 4 * per * cols * 2, 4 * per * cols),
        name="taught_stats",
    )(kept, gone)


def teacher_kernel(at_ref, serving_ref, a0, a1, a2, a3, aligned_ref):
    me, core = at_ref[0], at_ref[1]
    _, per, cols = a0.shape
    for j in range(2):
        wanted = serving_ref[me ^ (2 * j)]
        sums = [0.0, 0.0]
        for k, arrived in enumerate((a0, a1, a2, a3)):
            row = lax.broadcasted_iota(jnp.int32, (per, per), 0) + (me ^ k) * per
            pick = (row == wanted).astype(BF16)
            for c in range(2):
                sums[c] += lax.dot_general(
                    pick, arrived[core ^ c], (((0,), (0,)), ((), ())), preferred_element_type=F32
                )
        for c in range(2):
            aligned_ref[j, :, c * cols : (c + 1) * cols] = sums[c].astype(BF16)


def teacher_rows(at, serving, arrived):
    _, per, cols = arrived[0].shape
    return pl.pallas_call(
        teacher_kernel,
        out_shape=shape((2, per, 2 * cols), BF16),
        in_specs=[SMEM] + [VMEM] * 5,
        out_specs=VMEM,
        compiler_params=params(5),
        cost_estimate=cost(32 * per * per * cols, 12 * per * cols * 2),
        name="teacher_rows",
    )(at, serving, *arrived)


def student_stats(logits):
    peak = jnp.max(logits, axis=1, keepdims=True)
    soft = jnp.exp((logits - peak) * 0.5)
    hard = jnp.sum(soft * soft, axis=1, keepdims=True)
    return columns_to_rows([peak, hard, jnp.sum(soft, axis=1, keepdims=True)])


def own_kernel(splits, rows_ref, w_ref, logits_ref, stats_ref, own_ref, sems):
    step = w_ref.shape[0] // splits
    copies = []
    for c in range(splits):
        part = pl.ds(c * step, step)
        copies.append(pltpu.make_async_copy(w_ref.at[part], own_ref.at[part], sems.at[c]))
        copies[c].start()
    logits = 0.0
    for c in range(splits):
        copies[c].wait()
        part = slice(c * step, (c + 1) * step)
        logits += jnp.dot(rows_ref[:, part], own_ref[part, :], preferred_element_type=F32)
    logits_ref[...] = logits
    stats_ref[...] = student_stats(logits)


def own_logits(rows, own):
    per, depth = rows.shape
    cols = own.shape[1]
    splits = 4 if depth % 512 == 0 else 1
    return pl.pallas_call(
        lambda *refs: own_kernel(splits, *refs),
        out_shape=(
            shape((per, cols), F32),
            shape((STAT_ROWS, per), F32),
            shape((depth, cols), BF16),
        ),
        in_specs=[VMEM, pl.BlockSpec(memory_space=pl.ANY)],
        out_specs=(VMEM, VMEM, VMEM),
        scratch_shapes=[pltpu.SemaphoreType.DMA((splits,))],
        compiler_params=params(6),
        cost_estimate=cost(2 * per * depth * cols, (per + 2 * cols) * depth * 2, per * cols),
        name="own_logits",
    )(rows, own)


def core_kernel(rows_ref, w_ref, held_ref, logits_ref, stats_ref):
    logits = jnp.dot(rows_ref[...], w_ref[...], preferred_element_type=F32)
    logits_ref[...] = logits
    stats_ref[...] = student_stats(logits)


def core_logits(rows, other, held):
    per, depth = rows.shape
    cols = other.shape[1]
    return pl.pallas_call(
        core_kernel,
        out_shape=(shape((per, cols), F32), shape((STAT_ROWS, per), F32)),
        in_specs=[VMEM] * 3,
        out_specs=(VMEM, VMEM),
        compiler_params=params(6),
        cost_estimate=cost(2 * per * depth * cols, (per + cols) * depth * 2, per * cols),
        name="core_logits",
    )(rows, other, held)


NOTHING = -3.0e38


def both(a, b):
    peak = jnp.maximum(a[0:1], b[0:1])
    ea, eb = jnp.exp((a[0:1] - peak) * 0.5), jnp.exp((b[0:1] - peak) * 0.5)
    return jnp.concatenate(
        [peak, a[1:2] * (ea * ea) + b[1:2] * (eb * eb), a[2:3] * ea + b[2:3] * eb]
    )


def far_kernel(spots_ref, x0, x1, x2, x3, own_ref, other_ref, stats_a, stats_b, taught_ref, taught_core_ref, ids_ref, a_ref, b_ref, rows_ref, out_ref):
    count = x0.shape[0]
    for k, piece in enumerate((x0, x1, x2, x3)):
        rows_ref[pl.ds(pl.multiple_of(spots_ref[k], 16), count), :] = piece[...]
    per = rows_ref.shape[0]
    a = jnp.dot(rows_ref[...], own_ref[...], preferred_element_type=F32)
    b = jnp.dot(rows_ref[...], other_ref[...], preferred_element_type=F32)
    a_ref[...] = a
    b_ref[...] = b
    out_ref[0, 0:3, :] = both(stats_a[...], stats_b[...])
    out_ref[0, 3:4, :] = ids_ref[...].astype(F32)
    out_ref[0, 4:6, :] = taught_ref[0:2, :]
    out_ref[0, 6:8, :] = taught_core_ref[0:2, :]
    out_ref[1, 0:3, :] = both(student_stats(a), student_stats(b))
    row = lax.broadcasted_iota(jnp.int32, (5, per), 0)
    out_ref[1, 3:8, :] = jnp.where((row == 1) | (row == 3), NOTHING, 0.0)


def far_logits(spots, pieces, own, other, stats_a, stats_b, taught, taught_core, ids):
    depth, cols = own.shape
    per = sum(piece.shape[0] for piece in pieces)
    return pl.pallas_call(
        far_kernel,
        out_shape=(
            shape((per, cols), F32),
            shape((per, cols), F32),
            shape((per, depth), BF16),
            shape((2, STAT_ROWS, per), F32),
        ),
        in_specs=[SMEM] + [VMEM] * 11,
        out_specs=(VMEM, VMEM, VMEM, VMEM),
        compiler_params=params(11),
        cost_estimate=cost(4 * per * depth * cols, (per + 2 * cols) * depth * 2, 2 * per * cols),
        name="far_logits",
    )(spots, *pieces, own, other, stats_a, stats_b, taught, taught_core, ids)


def merged(parts):
    top = parts[0]
    for part in parts[1:]:
        top = jnp.maximum(top, part)
    hard = soft = taught0 = taught1 = 0.0
    for part in parts:
        shrink = jnp.exp((part - top) * 0.5)
        s = shrink[0:1]
        hard += part[1:2] * (s * s)
        soft += part[2:3] * s
        taught0 += part[5:6] * shrink[4:5]
        taught1 += part[7:8] * shrink[6:7]
    return top[0:1], hard, soft, top[3:4], top[4:5], taught0, top[6:7], taught1


def merge_kernel(flips, *refs):
    out_ref = refs[-1]
    for j in range(2):
        out_ref[j] = jnp.concatenate(merged([ref[j ^ f] for ref, f in zip(refs, flips)]))


def merge(parts, flips, held):
    return pl.pallas_call(
        lambda *refs: merge_kernel(flips, *refs),
        out_shape=shape(parts[0].shape, F32),
        in_specs=[VMEM] * (len(parts) + len(held)),
        out_specs=VMEM,
        compiler_params=params(6),
        cost_estimate=cost(0, 5 * parts[0].size * 4),
        name="merge_stats",
    )(*parts, *held)


def picker(bit, flip, total):
    half = total // 2
    row = lax.broadcasted_iota(jnp.int32, (total, total), 0)
    side = jnp.where(row < half, 1 << bit, 0)
    row = row & (half - 1)
    row = ((row >> bit) << (bit + 1)) + side + (row & ((1 << bit) - 1))
    return (lax.broadcasted_iota(jnp.int32, (total, total), 1) == (row ^ flip)).astype(BF16)


def back_kernel(bits, edges, n, at_ref, *refs):
    stats_refs = refs[:n]
    logits_refs = refs[n : n + 4]
    serving_ref, aligned_ref, wown_ref, wother_ref = refs[n + 4 : n + 8]
    gown_ref, gother_ref = refs[n + 8 : n + 10]
    send_refs, keep_refs = refs[n + 10 : n + 13], refs[n + 13 :]
    flip, me = at_ref[0], at_ref[3]
    per, cols = logits_refs[0].shape
    stats = [merged([ref[j] for ref in stats_refs]) for j in range(2)]
    lane = lax.broadcasted_iota(jnp.int32, (per, per), 1)
    for j in range(2):
        rows = stats[j][:4] + (serving_ref[me ^ (2 * j)].astype(F32),)
        columns = jnp.concatenate(rows + (jnp.zeros((128 - len(rows), per), F32),)).T
        peak, hard, soft, ids, wanted = [columns[:, i : i + 1] for i in range(len(rows))]
        ids, wanted = ids.astype(jnp.int32), wanted.astype(jnp.int32)
        tpeak = total = 0.0
        for k in range(4):
            here = wanted - (me ^ k) * per == lane
            taught = stats[k // 2][4 + 2 * (k % 2) : 6 + 2 * (k % 2)]
            tpeak += jnp.sum(jnp.where(here, taught[0], 0.0), axis=1, keepdims=True)
            total += jnp.sum(jnp.where(here, taught[1], 0.0), axis=1, keepdims=True)
        hard, soft, total = 16.0 / hard, 32.0 / soft, 32.0 / total
        for c, g_ref in enumerate((gown_ref, gother_ref)):
            part = slice(c * cols, (c + 1) * cols)
            column = at_ref[1 + c] + lax.broadcasted_iota(jnp.int32, (per, cols), 1)
            half = jnp.exp((logits_refs[2 * j + c][...] - peak) * 0.5)
            taught = jnp.exp((aligned_ref[j, :, part].astype(F32) - tpeak) * 0.5)
            label = jnp.where(column == ids, 16.0, 0.0)
            grad = (half * soft - taught * total) + (half * half * hard - label)
            g_ref[j * per : (j + 1) * per, :] = grad.astype(BF16)
    for p in range(3):
        pick = picker(bits[p], flip, 2 * per)
        part = slice(edges[p], edges[p + 1])
        back = 0.0
        for g_ref, w_ref in ((gown_ref, wown_ref), (gother_ref, wother_ref)):
            rows = jnp.dot(pick, g_ref[...], preferred_element_type=F32).astype(BF16)
            back += lax.dot_general(
                w_ref[part, :], rows, (((1,), (1,)), ((), ())), preferred_element_type=F32
            )
        back = back.T
        send_refs[p][...] = back[:per].astype(BF16)
        keep_refs[p][...] = back[per:]


def back_rows(at, stats, logits, serving, aligned, own, other, bits, edges):
    depth, cols = own.shape
    per = logits[0].shape[0]
    sends = [shape((per, edges[p + 1] - edges[p]), BF16) for p in range(3)]
    keeps = [shape((per, edges[p + 1] - edges[p]), F32) for p in range(3)]
    got = pl.pallas_call(
        lambda *refs: back_kernel(bits, edges, len(stats), *refs),
        out_shape=[shape((2 * per, cols), BF16)] * 2 + sends + keeps,
        in_specs=[SMEM] + [VMEM] * (len(stats) + 8),
        out_specs=[VMEM] * 8,
        compiler_params=params(18),
        cost_estimate=cost(8 * per * depth * cols, 2 * cols * depth * 2, 4 * per * cols),
        name="back_rows",
    )(at, *stats, *logits, serving, aligned, own, other)
    return got[0], got[1], got[2:5], got[5:8]


def head_kernel(r0, r1, r2, r3, mine_ref, theirs_ref, out_ref):
    rows = jnp.concatenate([r0[...], r1[...], r2[...], r3[...]])
    grads = jnp.concatenate([mine_ref[...], theirs_ref[...]])
    out_ref[...] = lax.dot_general(
        rows, grads, (((0,), (0,)), ((), ())), preferred_element_type=F32
    ).astype(BF16)


def head_gradient(rows, mine, theirs):
    per, depth = rows[0].shape
    cols = mine.shape[1]
    tile = 512 if depth % 512 == 0 else depth
    whole = pl.BlockSpec((2 * per, cols), lambda i: (0, 0))
    slab = pl.BlockSpec((per, tile), lambda i: (0, i))
    return pl.pallas_call(
        head_kernel,
        grid=(depth // tile,),
        out_shape=shape((depth, cols), BF16),
        in_specs=[slab] * 4 + [whole] * 2,
        out_specs=pl.BlockSpec((tile, cols), lambda i: (i, 0)),
        compiler_params=params(6),
        cost_estimate=cost(8 * per * depth * cols, (4 * per + cols) * depth * 2),
        name="head_gradient",
    )(*rows, mine, theirs)


def body(hidden, token_ids, serving, head_weight, teacher_logits):
    groups = lax.axis_size("grp")
    shards = lax.axis_size("vocab")
    me_g = lax.axis_index("grp")
    me_v = lax.axis_index("vocab")
    per, depth = hidden.shape
    cols = head_weight.shape[1]
    owned = per // shards
    CORE, X = shards, 2 * shards
    Y, W = 1, 2
    count = groups * shards

    def swap(value, mask):
        return lax.ppermute(value, AXES, [(i, i ^ mask) for i in range(count)])

    def tie(*values):
        return lax.optimization_barrier(values)

    def ints(*values):
        return jnp.stack([jnp.asarray(v, jnp.int32) for v in values])

    quarter_rows = per // 4
    quarter = me_v & 3
    starts = [(quarter ^ k) * quarter_rows for k in range(4)]
    other_weight = swap(head_weight, CORE)
    core_hidden = swap(hidden, CORE)
    first = lax.dynamic_slice_in_dim(hidden, starts[0], quarter_rows, 0)
    x0 = swap(first, X)
    _, rows, teacher = tie(first, hidden, teacher_logits)
    second = lax.dynamic_slice_in_dim(rows, starts[3], quarter_rows, 0)
    chip = me_g >> 1
    kept = lax.dynamic_slice_in_dim(teacher, 2 * chip, 2, 1).swapaxes(0, 1)
    gone = lax.dynamic_slice_in_dim(teacher, 2 * (chip ^ 1), 2, 1).swapaxes(0, 1)
    taught = taught_stats(kept, gone)
    near_a, stats_a, own_weight = own_logits(rows, head_weight)
    x0, second, kept, gone, taught, near_a, rows = tie(
        x0, second, kept, gone, taught, near_a, rows
    )
    x1 = swap(x0, Y)
    x2 = swap(x0, W)
    x3 = swap(second, X)
    taught_core = swap(taught, CORE)
    kept_core = swap(kept, CORE)
    near_b, stats_b = core_logits(rows, other_weight, x0)
    x1, x2, x3, gone, near_b, kept_core, core_hidden = tie(
        x1, x2, x3, gone, near_b, kept_core, core_hidden
    )
    taught_x = swap(gone, X)
    far_a, far_b, x_rows, stats = far_logits(
        ints(*starts),
        [x0, x1, x2, x3],
        own_weight,
        other_weight,
        stats_a,
        stats_b,
        taught,
        taught_core,
        token_ids.reshape(1, per),
    )

    served = serving.reshape(groups, 1, per)
    _, taught_x = tie(stats, taught_x)
    taught_far = swap(taught_x, CORE)
    logits = [near_a, near_b, far_a, far_b]
    held = logits + [own_weight]
    stats = merge([stats, swap(stats, X), swap(stats, Y), swap(stats, X + Y)], (0, 1, 0, 1), held)
    _, taught_far = tie(stats, taught_far)
    aligned = teacher_rows(
        ints(me_g, me_g & 1), served, [kept, kept_core, taught_x, taught_far]
    )
    core_x = swap(x_rows, CORE)
    mask = W
    while True:
        masks = [mask, 2 * mask, 3 * mask] if 2 * mask < shards else [mask]
        parts = [stats] + [swap(stats, m) for m in masks]
        mask *= 4
        if mask >= shards:
            break
        stats = merge(parts, (0,) * len(parts), held)

    bits = shards.bit_length() - 1
    masks = {0: X}
    for b in range(bits):
        masks[1 + b] = shards >> (1 + b)
    ydim, wdim = bits, bits - 1
    third = depth // 128 // 3 * 128
    edges = (0, third, 2 * third, depth)
    orders = [(0, ydim, wdim), (ydim, wdim, 0), (wdim, 0, ydim)]
    low = owned.bit_length() - 1
    row_bit = {0: low + bits, ydim: low, wdim: low + 1}
    first_bits = tuple(row_bit[order[0]] for order in orders)
    at = ints(
        me_v * owned, (me_g * shards + me_v) * cols, ((me_g ^ 1) * shards + me_v) * cols, me_g
    )
    gown, gother, sents, keeps = back_rows(
        at, parts, logits, served, aligned, own_weight, other_weight, first_bits, edges
    )
    gots = [swap(sents[p], masks[orders[p][0]]) for p in range(3)]
    theirs = swap(gother, CORE)
    grad_head = head_gradient([hidden, x_rows, core_hidden, core_x], gown, theirs)
    grad_head, *gots = tie(grad_head, *gots)

    def folded(value, p):
        dims = [2] * (1 + bits)
        dims[orders[p][0]] = 1
        return value.reshape(*dims, owned, value.shape[-1])

    terms = [[folded(keeps[p], p), folded(gots[p], p)] for p in range(3)]
    for stage in (1, 2):
        sents = [
            sum(lax.index_in_dim(t, 1, orders[p][stage]).astype(F32) for t in terms[p]).astype(BF16)
            for p in range(3)
        ]
        gots = [swap(sents[p], masks[orders[p][stage]]) for p in range(3)]
        for p in range(3):
            terms[p] = [lax.index_in_dim(t, 0, orders[p][stage]) for t in terms[p]] + [gots[p]]
    for dim in range(1, wdim):
        for p in range(3):
            sent = sum(lax.index_in_dim(t, 1, dim).astype(F32) for t in terms[p]).astype(BF16)
            terms[p] = [lax.index_in_dim(t, 0, dim) for t in terms[p]] + [swap(sent, masks[dim])]
    total = jnp.concatenate([sum(t.astype(F32) for t in ts) for ts in terms], axis=-1)
    return (total.reshape(owned, depth), grad_head)


def solution(mesh):
    placed = (P("grp", None), P("grp"), P(), P(None, ("grp", "vocab")), P("grp", None, "vocab"))
    return jax.shard_map(
        body,
        mesh=mesh,
        in_specs=placed,
        out_specs=(P(("grp", "vocab"), None), P(None, ("grp", "vocab"))),
        check_vma=False,
    )
```

```python
import jax
import jax.numpy as jnp
from jax import lax
from jax.experimental import pallas as pl
from jax.experimental.pallas import tpu as pltpu
from jax.sharding import PartitionSpec as P

BF16 = jnp.bfloat16
F32 = jnp.float32
AXES = ("grp", "vocab")
VMEM = pl.BlockSpec(memory_space=pltpu.VMEM)
SMEM = pl.BlockSpec(memory_space=pltpu.SMEM)
STAT_ROWS = 8
MIB = 2**20


def params(mib):
    return pltpu.CompilerParams(vmem_limit_bytes=mib * MIB)


def cost(flops, nbytes, exps=0):
    return pl.CostEstimate(flops=flops, bytes_accessed=nbytes, transcendentals=exps)


def shape(dims, dtype):
    return jax.ShapeDtypeStruct(dims, dtype)


def columns_to_rows(columns):
    count = columns[0].shape[0]
    lane = lax.broadcasted_iota(jnp.int32, (count, 128), 1)
    wide = jnp.zeros((count, 128), F32)
    for k, column in enumerate(columns):
        wide = jnp.where(lane == k, column, wide)
    return wide.T[:STAT_ROWS]


def taught_kernel(kept_ref, gone_ref, out_ref):
    parts = [ref[c].astype(F32) for ref in (kept_ref, gone_ref) for c in range(2)]
    top = parts[0]
    for part in parts[1:]:
        top = jnp.maximum(top, part)
    peak = jnp.max(top, axis=1, keepdims=True)
    total = sum(jnp.exp((part - peak) * 0.5) for part in parts)
    out_ref[...] = columns_to_rows([peak, jnp.sum(total, axis=1, keepdims=True)])


def taught_stats(kept, gone):
    _, per, cols = kept.shape
    return pl.pallas_call(
        taught_kernel,
        out_shape=shape((STAT_ROWS, per), F32),
        in_specs=[VMEM] * 2,
        out_specs=VMEM,
        compiler_params=params(4),
        cost_estimate=cost(0, 4 * per * cols * 2, 4 * per * cols),
        name="taught_stats",
    )(kept, gone)


def teacher_kernel(at_ref, serving_ref, a0, a1, a2, a3, aligned_ref):
    me, core = at_ref[0], at_ref[1]
    _, per, cols = a0.shape
    for j in range(2):
        wanted = serving_ref[me ^ (2 * j)]
        sums = [0.0, 0.0]
        for k, arrived in enumerate((a0, a1, a2, a3)):
            row = lax.broadcasted_iota(jnp.int32, (per, per), 0) + (me ^ k) * per
            pick = (row == wanted).astype(BF16)
            for c in range(2):
                sums[c] += lax.dot_general(
                    pick, arrived[core ^ c], (((0,), (0,)), ((), ())), preferred_element_type=F32
                )
        for c in range(2):
            aligned_ref[j, :, c * cols : (c + 1) * cols] = sums[c].astype(BF16)


def teacher_rows(at, serving, arrived):
    _, per, cols = arrived[0].shape
    return pl.pallas_call(
        teacher_kernel,
        out_shape=shape((2, per, 2 * cols), BF16),
        in_specs=[SMEM] + [VMEM] * 5,
        out_specs=VMEM,
        compiler_params=params(5),
        cost_estimate=cost(32 * per * per * cols, 12 * per * cols * 2),
        name="teacher_rows",
    )(at, serving, *arrived)


def student_stats(logits):
    peak = jnp.max(logits, axis=1, keepdims=True)
    soft = jnp.exp((logits - peak) * 0.5)
    hard = jnp.sum(soft * soft, axis=1, keepdims=True)
    return columns_to_rows([peak, hard, jnp.sum(soft, axis=1, keepdims=True)])


def own_kernel(splits, rows_ref, w_ref, logits_ref, stats_ref, own_ref, sems):
    step = w_ref.shape[0] // splits
    copies = []
    for c in range(splits):
        part = pl.ds(c * step, step)
        copies.append(pltpu.make_async_copy(w_ref.at[part], own_ref.at[part], sems.at[c]))
        copies[c].start()
    logits = 0.0
    for c in range(splits):
        copies[c].wait()
        part = slice(c * step, (c + 1) * step)
        logits += jnp.dot(rows_ref[:, part], own_ref[part, :], preferred_element_type=F32)
    logits_ref[...] = logits
    stats_ref[...] = student_stats(logits)


def own_logits(rows, own):
    per, depth = rows.shape
    cols = own.shape[1]
    splits = 4 if depth % 512 == 0 else 1
    return pl.pallas_call(
        lambda *refs: own_kernel(splits, *refs),
        out_shape=(
            shape((per, cols), F32),
            shape((STAT_ROWS, per), F32),
            shape((depth, cols), BF16),
        ),
        in_specs=[VMEM, pl.BlockSpec(memory_space=pl.ANY)],
        out_specs=(VMEM, VMEM, VMEM),
        scratch_shapes=[pltpu.SemaphoreType.DMA((splits,))],
        compiler_params=params(6),
        cost_estimate=cost(2 * per * depth * cols, (per + 2 * cols) * depth * 2, per * cols),
        name="own_logits",
    )(rows, own)


def core_kernel(rows_ref, w_ref, held_ref, logits_ref, stats_ref):
    logits = jnp.dot(rows_ref[...], w_ref[...], preferred_element_type=F32)
    logits_ref[...] = logits
    stats_ref[...] = student_stats(logits)


def core_logits(rows, other, held):
    per, depth = rows.shape
    cols = other.shape[1]
    return pl.pallas_call(
        core_kernel,
        out_shape=(shape((per, cols), F32), shape((STAT_ROWS, per), F32)),
        in_specs=[VMEM] * 3,
        out_specs=(VMEM, VMEM),
        compiler_params=params(6),
        cost_estimate=cost(2 * per * depth * cols, (per + cols) * depth * 2, per * cols),
        name="core_logits",
    )(rows, other, held)


NOTHING = -3.0e38


def both(a, b):
    peak = jnp.maximum(a[0:1], b[0:1])
    ea, eb = jnp.exp((a[0:1] - peak) * 0.5), jnp.exp((b[0:1] - peak) * 0.5)
    return jnp.concatenate(
        [peak, a[1:2] * (ea * ea) + b[1:2] * (eb * eb), a[2:3] * ea + b[2:3] * eb]
    )


def far_kernel(spots_ref, x0, x1, x2, x3, own_ref, other_ref, stats_a, stats_b, taught_ref, taught_core_ref, ids_ref, a_ref, b_ref, rows_ref, out_ref):
    count = x0.shape[0]
    for k, piece in enumerate((x0, x1, x2, x3)):
        rows_ref[pl.ds(pl.multiple_of(spots_ref[k], 16), count), :] = piece[...]
    per = rows_ref.shape[0]
    a = jnp.dot(rows_ref[...], own_ref[...], preferred_element_type=F32)
    b = jnp.dot(rows_ref[...], other_ref[...], preferred_element_type=F32)
    a_ref[...] = a
    b_ref[...] = b
    out_ref[0, 0:3, :] = both(stats_a[...], stats_b[...])
    out_ref[0, 3:4, :] = ids_ref[...].astype(F32)
    out_ref[0, 4:6, :] = taught_ref[0:2, :]
    out_ref[0, 6:8, :] = taught_core_ref[0:2, :]
    out_ref[1, 0:3, :] = both(student_stats(a), student_stats(b))
    row = lax.broadcasted_iota(jnp.int32, (5, per), 0)
    out_ref[1, 3:8, :] = jnp.where((row == 1) | (row == 3), NOTHING, 0.0)


def far_logits(spots, pieces, own, other, stats_a, stats_b, taught, taught_core, ids):
    depth, cols = own.shape
    per = sum(piece.shape[0] for piece in pieces)
    return pl.pallas_call(
        far_kernel,
        out_shape=(
            shape((per, cols), F32),
            shape((per, cols), F32),
            shape((per, depth), BF16),
            shape((2, STAT_ROWS, per), F32),
        ),
        in_specs=[SMEM] + [VMEM] * 11,
        out_specs=(VMEM, VMEM, VMEM, VMEM),
        compiler_params=params(11),
        cost_estimate=cost(4 * per * depth * cols, (per + 2 * cols) * depth * 2, 2 * per * cols),
        name="far_logits",
    )(spots, *pieces, own, other, stats_a, stats_b, taught, taught_core, ids)


def merged(parts):
    top = parts[0]
    for part in parts[1:]:
        top = jnp.maximum(top, part)
    hard = soft = taught0 = taught1 = 0.0
    for part in parts:
        shrink = jnp.exp((part - top) * 0.5)
        s = shrink[0:1]
        hard += part[1:2] * (s * s)
        soft += part[2:3] * s
        taught0 += part[5:6] * shrink[4:5]
        taught1 += part[7:8] * shrink[6:7]
    return top[0:1], hard, soft, top[3:4], top[4:5], taught0, top[6:7], taught1


def merge_kernel(flips, *refs):
    out_ref = refs[-1]
    for j in range(2):
        out_ref[j] = jnp.concatenate(merged([ref[j ^ f] for ref, f in zip(refs, flips)]))


def merge(parts, flips, held):
    return pl.pallas_call(
        lambda *refs: merge_kernel(flips, *refs),
        out_shape=shape(parts[0].shape, F32),
        in_specs=[VMEM] * (len(parts) + len(held)),
        out_specs=VMEM,
        compiler_params=params(6),
        cost_estimate=cost(0, 5 * parts[0].size * 4),
        name="merge_stats",
    )(*parts, *held)


def picker(bit, flip, total):
    half = total // 2
    row = lax.broadcasted_iota(jnp.int32, (total, total), 0)
    side = jnp.where(row < half, 1 << bit, 0)
    row = row & (half - 1)
    row = ((row >> bit) << (bit + 1)) + side + (row & ((1 << bit) - 1))
    return (lax.broadcasted_iota(jnp.int32, (total, total), 1) == (row ^ flip)).astype(BF16)


def back_kernel(bits, edges, n, at_ref, *refs):
    stats_refs = refs[:n]
    logits_refs = refs[n : n + 4]
    serving_ref, aligned_ref, wown_ref, wother_ref = refs[n + 4 : n + 8]
    gown_ref, gother_ref = refs[n + 8 : n + 10]
    send_refs, keep_refs = refs[n + 10 : n + 13], refs[n + 13 :]
    flip, me = at_ref[0], at_ref[3]
    per, cols = logits_refs[0].shape
    stats = [merged([ref[j] for ref in stats_refs]) for j in range(2)]
    lane = lax.broadcasted_iota(jnp.int32, (per, per), 1)
    for j in range(2):
        rows = stats[j][:4] + (serving_ref[me ^ (2 * j)].astype(F32),)
        columns = jnp.concatenate(rows + (jnp.zeros((128 - len(rows), per), F32),)).T
        peak, hard, soft, ids, wanted = [columns[:, i : i + 1] for i in range(len(rows))]
        ids, wanted = ids.astype(jnp.int32), wanted.astype(jnp.int32)
        tpeak = total = 0.0
        for k in range(4):
            here = wanted - (me ^ k) * per == lane
            taught = stats[k // 2][4 + 2 * (k % 2) : 6 + 2 * (k % 2)]
            tpeak += jnp.sum(jnp.where(here, taught[0], 0.0), axis=1, keepdims=True)
            total += jnp.sum(jnp.where(here, taught[1], 0.0), axis=1, keepdims=True)
        hard, soft, total = 16.0 / hard, 32.0 / soft, 32.0 / total
        for c, g_ref in enumerate((gown_ref, gother_ref)):
            part = slice(c * cols, (c + 1) * cols)
            column = at_ref[1 + c] + lax.broadcasted_iota(jnp.int32, (per, cols), 1)
            half = jnp.exp((logits_refs[2 * j + c][...] - peak) * 0.5)
            taught = jnp.exp((aligned_ref[j, :, part].astype(F32) - tpeak) * 0.5)
            label = jnp.where(column == ids, 16.0, 0.0)
            grad = (half * soft - taught * total) + (half * half * hard - label)
            g_ref[j * per : (j + 1) * per, :] = grad.astype(BF16)
    for p in range(3):
        pick = picker(bits[p], flip, 2 * per)
        part = slice(edges[p], edges[p + 1])
        back = 0.0
        for g_ref, w_ref in ((gown_ref, wown_ref), (gother_ref, wother_ref)):
            rows = jnp.dot(pick, g_ref[...], preferred_element_type=F32).astype(BF16)
            back += lax.dot_general(
                w_ref[part, :], rows, (((1,), (1,)), ((), ())), preferred_element_type=F32
            )
        back = back.T
        send_refs[p][...] = back[:per].astype(BF16)
        keep_refs[p][...] = back[per:]


def back_rows(at, stats, logits, serving, aligned, own, other, bits, edges):
    depth, cols = own.shape
    per = logits[0].shape[0]
    sends = [shape((per, edges[p + 1] - edges[p]), BF16) for p in range(3)]
    keeps = [shape((per, edges[p + 1] - edges[p]), F32) for p in range(3)]
    got = pl.pallas_call(
        lambda *refs: back_kernel(bits, edges, len(stats), *refs),
        out_shape=[shape((2 * per, cols), BF16)] * 2 + sends + keeps,
        in_specs=[SMEM] + [VMEM] * (len(stats) + 8),
        out_specs=[VMEM] * 8,
        compiler_params=params(18),
        cost_estimate=cost(8 * per * depth * cols, 2 * cols * depth * 2, 4 * per * cols),
        name="back_rows",
    )(at, *stats, *logits, serving, aligned, own, other)
    return got[0], got[1], got[2:5], got[5:8]


def head_kernel(r0, r1, r2, r3, mine_ref, theirs_ref, out_ref):
    rows = jnp.concatenate([r0[...], r1[...], r2[...], r3[...]])
    grads = jnp.concatenate([mine_ref[...], theirs_ref[...]])
    out_ref[...] = lax.dot_general(
        rows, grads, (((0,), (0,)), ((), ())), preferred_element_type=F32
    ).astype(BF16)


def head_gradient(rows, mine, theirs):
    per, depth = rows[0].shape
    cols = mine.shape[1]
    tile = 512 if depth % 512 == 0 else depth
    whole = pl.BlockSpec((2 * per, cols), lambda i: (0, 0))
    slab = pl.BlockSpec((per, tile), lambda i: (0, i))
    return pl.pallas_call(
        head_kernel,
        grid=(depth // tile,),
        out_shape=shape((depth, cols), BF16),
        in_specs=[slab] * 4 + [whole] * 2,
        out_specs=pl.BlockSpec((tile, cols), lambda i: (i, 0)),
        compiler_params=params(6),
        cost_estimate=cost(8 * per * depth * cols, (4 * per + cols) * depth * 2),
        name="head_gradient",
    )(*rows, mine, theirs)


def body(hidden, token_ids, serving, head_weight, teacher_logits):
    groups = lax.axis_size("grp")
    shards = lax.axis_size("vocab")
    me_g = lax.axis_index("grp")
    me_v = lax.axis_index("vocab")
    per, depth = hidden.shape
    cols = head_weight.shape[1]
    owned = per // shards
    CORE, X = shards, 2 * shards
    Y, W = 1, 2
    count = groups * shards

    def swap(value, mask):
        return lax.ppermute(value, AXES, [(i, i ^ mask) for i in range(count)])

    def tie(*values):
        return lax.optimization_barrier(values)

    def ints(*values):
        return jnp.stack([jnp.asarray(v, jnp.int32) for v in values])

    quarter_rows = per // 4
    quarter = me_v & 3
    starts = [(quarter ^ k) * quarter_rows for k in range(4)]
    chip = me_g >> 1
    spots = ints(*starts)
    at = ints(
        me_v * owned, (me_g * shards + me_v) * cols, ((me_g ^ 1) * shards + me_v) * cols, me_g
    )
    who = ints(me_g, me_g & 1)
    unsigned = [jnp.asarray(v, jnp.uint32) for v in (starts[0], starts[3], 2 * chip, 2 * (chip ^ 1))]
    rows, weight, spots, at, who, *unsigned = tie(hidden, head_weight, spots, at, who, *unsigned)
    zero = jnp.uint32(0)

    def cut(value, start, size, dim):
        indices = [start if d == dim else zero for d in range(value.ndim)]
        sizes = [size if d == dim else n for d, n in enumerate(value.shape)]
        return lax.dynamic_slice(value, indices, sizes)

    other_weight = swap(weight, CORE)
    core_hidden = swap(rows, CORE)
    first = cut(rows, unsigned[0], quarter_rows, 0)
    x0 = swap(first, X)
    _, rows, teacher = tie(first, rows, teacher_logits)
    second = cut(rows, unsigned[1], quarter_rows, 0)
    kept = cut(teacher, unsigned[2], 2, 1).swapaxes(0, 1)
    gone = cut(teacher, unsigned[3], 2, 1).swapaxes(0, 1)
    taught = taught_stats(kept, gone)
    near_a, stats_a, own_weight = own_logits(rows, head_weight)
    x0, second, kept, gone, taught, near_a, rows = tie(
        x0, second, kept, gone, taught, near_a, rows
    )
    x1 = swap(x0, Y)
    x2 = swap(x0, W)
    x3 = swap(second, X)
    taught_core = swap(taught, CORE)
    kept_core = swap(kept, CORE)
    near_b, stats_b = core_logits(rows, other_weight, x0)
    x1, x2, x3, gone, near_b, kept_core, taught_core = tie(
        x1, x2, x3, gone, near_b, kept_core, taught_core
    )
    spots, core_hidden = tie(spots, core_hidden)
    taught_x = swap(gone, X)
    far_a, far_b, x_rows, stats = far_logits(
        spots,
        [x0, x1, x2, x3],
        own_weight,
        other_weight,
        stats_a,
        stats_b,
        taught,
        taught_core,
        token_ids.reshape(1, per),
    )

    served = serving.reshape(groups, 1, per)
    _, taught_x = tie(stats, taught_x)
    taught_far = swap(taught_x, CORE)
    logits = [near_a, near_b, far_a, far_b]
    held = logits + [own_weight]
    stats = merge([stats, swap(stats, X), swap(stats, Y), swap(stats, X + Y)], (0, 1, 0, 1), held)
    _, taught_far = tie(stats, taught_far)
    aligned = teacher_rows(who, served, [kept, kept_core, taught_x, taught_far])
    core_x = swap(x_rows, CORE)
    mask = W
    while True:
        masks = [mask, 2 * mask, 3 * mask] if 2 * mask < shards else [mask]
        parts = [stats] + [swap(stats, m) for m in masks]
        mask *= 4
        if mask >= shards:
            break
        stats = merge(parts, (0,) * len(parts), held)

    bits = shards.bit_length() - 1
    masks = {0: X}
    for b in range(bits):
        masks[1 + b] = shards >> (1 + b)
    ydim, wdim = bits, bits - 1
    third = depth // 128 // 3 * 128
    edges = (0, third, 2 * third, depth)
    orders = [(0, ydim, wdim), (ydim, wdim, 0), (wdim, 0, ydim)]
    low = owned.bit_length() - 1
    row_bit = {0: low + bits, ydim: low, wdim: low + 1}
    first_bits = tuple(row_bit[order[0]] for order in orders)
    gown, gother, sents, keeps = back_rows(
        at, parts, logits, served, aligned, own_weight, other_weight, first_bits, edges
    )
    gots = [swap(sents[p], masks[orders[p][0]]) for p in range(3)]
    theirs = swap(gother, CORE)
    grad_head = head_gradient([hidden, x_rows, core_hidden, core_x], gown, theirs)
    grad_head, *gots = tie(grad_head, *gots)

    def folded(value, p):
        dims = [2] * (1 + bits)
        dims[orders[p][0]] = 1
        return value.reshape(*dims, owned, value.shape[-1])

    terms = [[folded(keeps[p], p), folded(gots[p], p)] for p in range(3)]
    for stage in (1, 2):
        sents = [
            sum(lax.index_in_dim(t, 1, orders[p][stage]).astype(F32) for t in terms[p]).astype(BF16)
            for p in range(3)
        ]
        gots = [swap(sents[p], masks[orders[p][stage]]) for p in range(3)]
        for p in range(3):
            terms[p] = [lax.index_in_dim(t, 0, orders[p][stage]) for t in terms[p]] + [gots[p]]
    for dim in range(1, wdim):
        for p in range(3):
            sent = sum(lax.index_in_dim(t, 1, dim).astype(F32) for t in terms[p]).astype(BF16)
            terms[p] = [lax.index_in_dim(t, 0, dim) for t in terms[p]] + [swap(sent, masks[dim])]
    total = jnp.concatenate([sum(t.astype(F32) for t in ts) for ts in terms], axis=-1)
    return (total.reshape(owned, depth), grad_head)


def solution(mesh):
    placed = (P("grp", None), P("grp"), P(), P(None, ("grp", "vocab")), P("grp", None, "vocab"))
    return jax.shard_map(
        body,
        mesh=mesh,
        in_specs=placed,
        out_specs=(P(("grp", "vocab"), None), P(None, ("grp", "vocab"))),
        check_vma=False,
    )
```

```python
import jax
import jax.numpy as jnp
from jax import lax
from jax.experimental import pallas as pl
from jax.experimental.pallas import tpu as pltpu
from jax.sharding import PartitionSpec as P

BF16 = jnp.bfloat16
F32 = jnp.float32
AXES = ("grp", "vocab")
VMEM = pl.BlockSpec(memory_space=pltpu.VMEM)
SMEM = pl.BlockSpec(memory_space=pltpu.SMEM)
STAT_ROWS = 8
MIB = 2**20


def params(mib):
    return pltpu.CompilerParams(vmem_limit_bytes=mib * MIB)


def cost(flops, nbytes, exps=0):
    return pl.CostEstimate(flops=flops, bytes_accessed=nbytes, transcendentals=exps)


def shape(dims, dtype):
    return jax.ShapeDtypeStruct(dims, dtype)


def columns_to_rows(columns):
    count = columns[0].shape[0]
    lane = lax.broadcasted_iota(jnp.int32, (count, 128), 1)
    wide = jnp.zeros((count, 128), F32)
    for k, column in enumerate(columns):
        wide = jnp.where(lane == k, column, wide)
    return wide.T[:STAT_ROWS]


def taught_kernel(kept_ref, gone_ref, out_ref):
    parts = [ref[c].astype(F32) for ref in (kept_ref, gone_ref) for c in range(2)]
    top = parts[0]
    for part in parts[1:]:
        top = jnp.maximum(top, part)
    peak = jnp.max(top, axis=1, keepdims=True)
    total = sum(jnp.exp((part - peak) * 0.5) for part in parts)
    out_ref[...] = columns_to_rows([peak, jnp.sum(total, axis=1, keepdims=True)])


def taught_stats(kept, gone):
    _, per, cols = kept.shape
    return pl.pallas_call(
        taught_kernel,
        out_shape=shape((STAT_ROWS, per), F32),
        in_specs=[VMEM] * 2,
        out_specs=VMEM,
        compiler_params=params(4),
        cost_estimate=cost(0, 4 * per * cols * 2, 4 * per * cols),
        name="taught_stats",
    )(kept, gone)


def teacher_kernel(at_ref, serving_ref, a0, a1, a2, a3, aligned_ref):
    me, core = at_ref[0], at_ref[1]
    _, per, cols = a0.shape
    for j in range(2):
        wanted = serving_ref[me ^ (2 * j)]
        sums = [0.0, 0.0]
        for k, arrived in enumerate((a0, a1, a2, a3)):
            row = lax.broadcasted_iota(jnp.int32, (per, per), 0) + (me ^ k) * per
            pick = (row == wanted).astype(BF16)
            for c in range(2):
                sums[c] += lax.dot_general(
                    pick, arrived[core ^ c], (((0,), (0,)), ((), ())), preferred_element_type=F32
                )
        for c in range(2):
            aligned_ref[j, :, c * cols : (c + 1) * cols] = sums[c].astype(BF16)


def teacher_rows(at, serving, arrived):
    _, per, cols = arrived[0].shape
    return pl.pallas_call(
        teacher_kernel,
        out_shape=shape((2, per, 2 * cols), BF16),
        in_specs=[SMEM] + [VMEM] * 5,
        out_specs=VMEM,
        compiler_params=params(5),
        cost_estimate=cost(32 * per * per * cols, 12 * per * cols * 2),
        name="teacher_rows",
    )(at, serving, *arrived)


def student_stats(logits):
    peak = jnp.max(logits, axis=1, keepdims=True)
    soft = jnp.exp((logits - peak) * 0.5)
    hard = jnp.sum(soft * soft, axis=1, keepdims=True)
    return columns_to_rows([peak, hard, jnp.sum(soft, axis=1, keepdims=True)])


def near_kernel(rows_ref, w_ref, *refs):
    logits_ref, stats_ref = refs[-2:]
    logits = jnp.dot(rows_ref[...], w_ref[...], preferred_element_type=F32)
    logits_ref[...] = logits
    stats_ref[...] = student_stats(logits)


def near_logits(rows, weight, *held):
    per, depth = rows.shape
    cols = weight.shape[1]
    return pl.pallas_call(
        near_kernel,
        out_shape=(shape((per, cols), F32), shape((STAT_ROWS, per), F32)),
        in_specs=[VMEM] * (2 + len(held)),
        out_specs=(VMEM, VMEM),
        compiler_params=params(6),
        cost_estimate=cost(2 * per * depth * cols, (per + cols) * depth * 2, per * cols),
        name="near_logits",
    )(rows, weight, *held)


NOTHING = -3.0e38


def both(a, b):
    peak = jnp.maximum(a[0:1], b[0:1])
    ea, eb = jnp.exp((a[0:1] - peak) * 0.5), jnp.exp((b[0:1] - peak) * 0.5)
    return jnp.concatenate(
        [peak, a[1:2] * (ea * ea) + b[1:2] * (eb * eb), a[2:3] * ea + b[2:3] * eb]
    )


def far_kernel(n, spots_ref, *refs):
    pieces, refs = refs[:n], refs[n:]
    own_ref, other_ref, stats_a, stats_b, taught_ref, taught_core_ref, ids_ref = refs[:7]
    a_ref, b_ref, rows_ref, out_ref = refs[7:]
    for k, piece in enumerate(pieces):
        rows_ref[pl.ds(pl.multiple_of(spots_ref[k], 16), piece.shape[0]), :] = piece[...]
    per = rows_ref.shape[0]
    a = jnp.dot(rows_ref[...], own_ref[...], preferred_element_type=F32)
    b = jnp.dot(rows_ref[...], other_ref[...], preferred_element_type=F32)
    a_ref[...] = a
    b_ref[...] = b
    out_ref[0, 0:3, :] = both(stats_a[...], stats_b[...])
    out_ref[0, 3:4, :] = ids_ref[...].astype(F32)
    out_ref[0, 4:6, :] = taught_ref[0:2, :]
    out_ref[0, 6:8, :] = taught_core_ref[0:2, :]
    out_ref[1, 0:3, :] = both(student_stats(a), student_stats(b))
    row = lax.broadcasted_iota(jnp.int32, (5, per), 0)
    out_ref[1, 3:8, :] = jnp.where((row == 1) | (row == 3), NOTHING, 0.0)


def far_logits(spots, pieces, own, other, *small):
    depth, cols = own.shape
    per = sum(piece.shape[0] for piece in pieces)
    return pl.pallas_call(
        lambda *refs: far_kernel(len(pieces), *refs),
        out_shape=(
            shape((per, cols), F32),
            shape((per, cols), F32),
            shape((per, depth), BF16),
            shape((2, STAT_ROWS, per), F32),
        ),
        in_specs=[SMEM] + [VMEM] * (len(pieces) + 2 + len(small)),
        out_specs=(VMEM, VMEM, VMEM, VMEM),
        compiler_params=params(12),
        cost_estimate=cost(4 * per * depth * cols, (per + 2 * cols) * depth * 2, 2 * per * cols),
        name="far_logits",
    )(spots, *pieces, own, other, *small)


def merged(parts):
    top = parts[0]
    for part in parts[1:]:
        top = jnp.maximum(top, part)
    hard = soft = taught0 = taught1 = 0.0
    for part in parts:
        shrink = jnp.exp((part - top) * 0.5)
        s = shrink[0:1]
        hard += part[1:2] * (s * s)
        soft += part[2:3] * s
        taught0 += part[5:6] * shrink[4:5]
        taught1 += part[7:8] * shrink[6:7]
    return top[0:1], hard, soft, top[3:4], top[4:5], taught0, top[6:7], taught1


def merge_kernel(flips, *refs):
    out_ref = refs[-1]
    for j in range(2):
        out_ref[j] = jnp.concatenate(merged([ref[j ^ f] for ref, f in zip(refs, flips)]))


def merge(parts, flips, held):
    return pl.pallas_call(
        lambda *refs: merge_kernel(flips, *refs),
        out_shape=shape(parts[0].shape, F32),
        in_specs=[VMEM] * (len(parts) + len(held)),
        out_specs=VMEM,
        compiler_params=params(6),
        cost_estimate=cost(0, 5 * parts[0].size * 4),
        name="merge_stats",
    )(*parts, *held)


def picker(bit, flip, total):
    half = total // 2
    row = lax.broadcasted_iota(jnp.int32, (total, total), 0)
    side = jnp.where(row < half, 1 << bit, 0)
    row = row & (half - 1)
    row = ((row >> bit) << (bit + 1)) + side + (row & ((1 << bit) - 1))
    return (lax.broadcasted_iota(jnp.int32, (total, total), 1) == (row ^ flip)).astype(BF16)


def grads_kernel(n, at_ref, *refs):
    stats_refs, logits_refs = refs[:n], refs[n : n + 4]
    serving_ref, aligned_ref = refs[n + 4 : n + 6]
    g_refs = refs[n + 6 :]
    me = at_ref[3]
    per, cols = logits_refs[0].shape
    stats = [merged([ref[j] for ref in stats_refs]) for j in range(2)]
    lane = lax.broadcasted_iota(jnp.int32, (per, per), 1)
    for j in range(2):
        rows = stats[j][:4] + (serving_ref[me ^ (2 * j)].astype(F32),)
        columns = jnp.concatenate(rows + (jnp.zeros((128 - len(rows), per), F32),)).T
        peak, hard, soft, ids, wanted = [columns[:, i : i + 1] for i in range(len(rows))]
        ids, wanted = ids.astype(jnp.int32), wanted.astype(jnp.int32)
        tpeak = total = 0.0
        for k in range(4):
            here = wanted - (me ^ k) * per == lane
            taught = stats[k // 2][4 + 2 * (k % 2) : 6 + 2 * (k % 2)]
            tpeak += jnp.where(here, taught[0], 0.0)
            total += jnp.where(here, taught[1], 0.0)
        tpeak = jnp.sum(tpeak, axis=1, keepdims=True)
        total = jnp.sum(total, axis=1, keepdims=True)
        hard, soft, total = 16.0 / hard, 32.0 / soft, 32.0 / total
        for c, g_ref in enumerate(g_refs):
            part = slice(c * cols, (c + 1) * cols)
            column = at_ref[1 + c] + lax.broadcasted_iota(jnp.int32, (per, cols), 1)
            half = jnp.exp((logits_refs[2 * j + c][...] - peak) * 0.5)
            taught = jnp.exp((aligned_ref[j, :, part].astype(F32) - tpeak) * 0.5)
            label = jnp.where(column == ids, 16.0, 0.0)
            grad = (half * soft - taught * total) + (half * half * hard - label)
            g_ref[j * per : (j + 1) * per, :] = grad.astype(BF16)


def push_back(bit, first, flip, g_refs, w_refs, send_ref, keep_ref):
    per, width = send_ref.shape
    pick = picker(bit, flip, 2 * per)
    back = 0.0
    for g_ref, w_ref in zip(g_refs, w_refs):
        rows = jnp.dot(pick, g_ref[...], preferred_element_type=F32).astype(BF16)
        back += lax.dot_general(
            w_ref[first : first + width, :],
            rows,
            (((1,), (1,)), ((), ())),
            preferred_element_type=F32,
        )
    back = back.T
    send_ref[...] = back[:per].astype(BF16)
    keep_ref[...] = back[per:]


def back_kernel(bit, first, n, at_ref, *refs):
    w_refs, refs = refs[:2], refs[2:]
    g_refs, (send_ref, keep_ref) = refs[-4:-2], refs[-2:]
    if n:
        grads_kernel(n, at_ref, *refs[:-2])
    push_back(bit, first, at_ref[0], g_refs, w_refs, send_ref, keep_ref)


def back_outs(own, per, first, last):
    return [shape((per, last - first), BF16), shape((per, last - first), F32)]


def grads_and_back(at, own, other, stats, logits, serving, aligned, bit, first, last):
    depth, cols = own.shape
    per = logits[0].shape[0]
    return pl.pallas_call(
        lambda *refs: back_kernel(bit, first, len(stats), *refs),
        out_shape=[shape((2 * per, cols), BF16)] * 2 + back_outs(own, per, first, last),
        in_specs=[SMEM] + [VMEM] * (2 + len(stats) + 6),
        out_specs=[VMEM] * 4,
        compiler_params=params(16),
        cost_estimate=cost(8 * per * (last - first) * cols, 2 * cols * depth * 2, 4 * per * cols),
        name="grads_and_back",
    )(at, own, other, *stats, *logits, serving, aligned)


def back_only(at, own, other, gown, gother, bit, first, last):
    depth, cols = own.shape
    per = gown.shape[0] // 2
    return pl.pallas_call(
        lambda *refs: back_kernel(bit, first, 0, *refs),
        out_shape=back_outs(own, per, first, last),
        in_specs=[SMEM] + [VMEM] * 4,
        out_specs=[VMEM] * 2,
        compiler_params=params(16),
        cost_estimate=cost(8 * per * (last - first) * cols, 2 * cols * depth * 2),
        name="back_only",
    )(at, own, other, gown, gother)


def head_kernel(r0, r1, r2, r3, mine_ref, theirs_ref, out_ref):
    rows = jnp.concatenate([r0[...], r1[...], r2[...], r3[...]])
    grads = jnp.concatenate([mine_ref[...], theirs_ref[...]])
    out_ref[...] = lax.dot_general(
        rows, grads, (((0,), (0,)), ((), ())), preferred_element_type=F32
    ).astype(BF16)


def head_gradient(rows, mine, theirs):
    per, depth = rows[0].shape
    cols = mine.shape[1]
    tile = 512 if depth % 512 == 0 else depth
    whole = pl.BlockSpec((2 * per, cols), lambda i: (0, 0))
    slab = pl.BlockSpec((per, tile), lambda i: (0, i))
    return pl.pallas_call(
        head_kernel,
        grid=(depth // tile,),
        out_shape=shape((depth, cols), BF16),
        in_specs=[slab] * 4 + [whole] * 2,
        out_specs=pl.BlockSpec((tile, cols), lambda i: (i, 0)),
        compiler_params=params(6),
        cost_estimate=cost(8 * per * depth * cols, (4 * per + cols) * depth * 2),
        name="head_gradient",
    )(*rows, mine, theirs)


def body(hidden, token_ids, serving, head_weight, teacher_logits):
    groups = lax.axis_size("grp")
    shards = lax.axis_size("vocab")
    me_g = lax.axis_index("grp")
    me_v = lax.axis_index("vocab")
    per, depth = hidden.shape
    cols = head_weight.shape[1]
    owned = per // shards
    CORE, X = shards, 2 * shards
    Y, W = 1, 2
    count = groups * shards

    def swap(value, mask):
        return lax.ppermute(value, AXES, [(i, i ^ mask) for i in range(count)])

    def tie(*values):
        return lax.optimization_barrier(values)

    def ints(*values):
        return jnp.stack([jnp.asarray(v, jnp.int32) for v in values])

    quarter_rows = per // 4
    quarter = me_v & 3
    starts = [(quarter ^ k) * quarter_rows for k in range(4)]
    chip = me_g >> 1
    spots = ints(*starts)
    at = ints(
        me_v * owned, (me_g * shards + me_v) * cols, ((me_g ^ 1) * shards + me_v) * cols, me_g
    )
    who = ints(me_g, me_g & 1)
    unsigned = [
        jnp.asarray(v, jnp.uint32)
        for v in (starts[0], starts[3], 2 * chip, 2 * (chip ^ 1))
    ]
    rows, weight, spots, at, who, *unsigned = tie(hidden, head_weight, spots, at, who, *unsigned)
    zero = jnp.uint32(0)

    def cut(value, start, size, dim):
        indices = [start if d == dim else zero for d in range(value.ndim)]
        sizes = [size if d == dim else n for d, n in enumerate(value.shape)]
        return lax.dynamic_slice(value, indices, sizes)

    other_weight = swap(weight, CORE)
    core_hidden = swap(rows, CORE)
    first = cut(rows, unsigned[0], quarter_rows, 0)
    x0 = swap(first, X)
    _, rows, teacher = tie(first, rows, teacher_logits)
    x3 = swap(cut(rows, unsigned[1], quarter_rows, 0), X)
    kept = cut(teacher, unsigned[2], 2, 1).swapaxes(0, 1)
    gone = cut(teacher, unsigned[3], 2, 1).swapaxes(0, 1)
    taught = taught_stats(kept, gone)
    near_a, stats_a = near_logits(rows, weight)
    x0, kept, gone, taught, near_a, rows = tie(x0, kept, gone, taught, near_a, rows)
    x1 = swap(x0, Y)
    x2 = swap(x0, W)
    taught_core = swap(taught, CORE)
    kept_core = swap(kept, CORE)
    near_b, stats_b = near_logits(rows, other_weight, x0)
    *pieces, gone, near_b = tie(x0, x1, x2, x3, gone, near_b)
    taught_x = swap(gone, X)
    spots, core_hidden, kept_core = tie(spots, core_hidden, kept_core)
    far_a, far_b, x_rows, stats = far_logits(
        spots,
        pieces,
        weight,
        other_weight,
        stats_a,
        stats_b,
        taught,
        taught_core,
        token_ids.reshape(1, per),
    )

    served = serving.reshape(groups, 1, per)
    logits = [near_a, near_b, far_a, far_b]
    held = logits + [weight]
    stats = merge([stats, swap(stats, X), swap(stats, Y), swap(stats, X + Y)], (0, 1, 0, 1), held)
    _, taught_x = tie(stats, taught_x)
    taught_far = swap(taught_x, CORE)
    aligned = teacher_rows(who, served, [kept, kept_core, taught_x, taught_far])
    mask = W
    while True:
        masks = [mask, 2 * mask, 3 * mask] if 2 * mask < shards else [mask]
        parts = [stats] + [swap(stats, m) for m in masks]
        mask *= 4
        if mask >= shards:
            break
        stats = merge(parts, (0,) * len(parts), held)

    bits = shards.bit_length() - 1
    masks = {0: X}
    for b in range(bits):
        masks[1 + b] = shards >> (1 + b)
    ydim, wdim = bits, bits - 1
    third = depth // 128 // 3 * 128
    edges = (0, third, 2 * third, depth)
    orders = [(0, ydim, wdim), (ydim, wdim, 0), (wdim, 0, ydim)]
    low = owned.bit_length() - 1
    row_bit = {0: low + bits, ydim: low, wdim: low + 1}
    first_bits = tuple(row_bit[order[0]] for order in orders)
    gown, gother, sent, keep = grads_and_back(
        at, weight, other_weight, parts, logits, served, aligned, first_bits[0], *edges[:2]
    )
    gots, keeps = [swap(sent, masks[orders[0][0]])], [keep]
    for p in (1, 2):
        sent, keep = back_only(
            at, weight, other_weight, gown, gother, first_bits[p], *edges[p : p + 2]
        )
        gots.append(swap(sent, masks[orders[p][0]]))
        keeps.append(keep)
    theirs = swap(gother, CORE)
    _, x_sent = tie(gother, x_rows)
    grad_head = head_gradient([hidden, x_rows, core_hidden, swap(x_sent, CORE)], gown, theirs)
    grad_head, *gots = tie(grad_head, *gots)

    def folded(value, p):
        dims = [2] * (1 + bits)
        dims[orders[p][0]] = 1
        return value.reshape(*dims, owned, value.shape[-1])

    terms = [[folded(keeps[p], p), folded(gots[p], p)] for p in range(3)]
    for stage in (1, 2):
        sents = [
            sum(lax.index_in_dim(t, 1, orders[p][stage]).astype(F32) for t in terms[p]).astype(BF16)
            for p in range(3)
        ]
        gots = [swap(sents[p], masks[orders[p][stage]]) for p in range(3)]
        for p in range(3):
            terms[p] = [lax.index_in_dim(t, 0, orders[p][stage]) for t in terms[p]] + [gots[p]]
    for dim in range(1, wdim):
        for p in range(3):
            sent = sum(lax.index_in_dim(t, 1, dim).astype(F32) for t in terms[p]).astype(BF16)
            terms[p] = [lax.index_in_dim(t, 0, dim) for t in terms[p]] + [swap(sent, masks[dim])]
    total = jnp.concatenate([sum(t.astype(F32) for t in ts) for ts in terms], axis=-1)
    return (total.reshape(owned, depth), grad_head)


def solution(mesh):
    placed = (P("grp", None), P("grp"), P(), P(None, ("grp", "vocab")), P("grp", None, "vocab"))
    return jax.shard_map(
        body,
        mesh=mesh,
        in_specs=placed,
        out_specs=(P(("grp", "vocab"), None), P(None, ("grp", "vocab"))),
        check_vma=False,
    )
```

```python
import jax
import jax.numpy as jnp
from jax import lax
from jax.experimental import pallas as pl
from jax.experimental.pallas import tpu as pltpu
from jax.sharding import PartitionSpec as P

BF16 = jnp.bfloat16
F32 = jnp.float32
AXES = ("grp", "vocab")
VMEM = pl.BlockSpec(memory_space=pltpu.VMEM)
SMEM = pl.BlockSpec(memory_space=pltpu.SMEM)
STAT_ROWS = 8
MIB = 2**20


def params(mib):
    return pltpu.CompilerParams(vmem_limit_bytes=mib * MIB)


def cost(flops, nbytes, exps=0):
    return pl.CostEstimate(flops=flops, bytes_accessed=nbytes, transcendentals=exps)


def shape(dims, dtype):
    return jax.ShapeDtypeStruct(dims, dtype)


def columns_to_rows(columns):
    count = columns[0].shape[0]
    lane = lax.broadcasted_iota(jnp.int32, (count, 128), 1)
    wide = jnp.zeros((count, 128), F32)
    for k, column in enumerate(columns):
        wide = jnp.where(lane == k, column, wide)
    return wide.T[:STAT_ROWS]


def taught_kernel(kept_ref, gone_ref, out_ref):
    parts = [ref[c].astype(F32) for ref in (kept_ref, gone_ref) for c in range(2)]
    top = parts[0]
    for part in parts[1:]:
        top = jnp.maximum(top, part)
    peak = jnp.max(top, axis=1, keepdims=True)
    total = sum(jnp.exp((part - peak) * 0.5) for part in parts)
    out_ref[...] = columns_to_rows([peak, jnp.sum(total, axis=1, keepdims=True)])


def taught_stats(kept, gone):
    _, per, cols = kept.shape
    return pl.pallas_call(
        taught_kernel,
        out_shape=shape((STAT_ROWS, per), F32),
        in_specs=[VMEM] * 2,
        out_specs=VMEM,
        compiler_params=params(4),
        cost_estimate=cost(0, 4 * per * cols * 2, 4 * per * cols),
        name="taught_stats",
    )(kept, gone)


def teacher_kernel(at_ref, serving_ref, a0, a1, a2, a3, aligned_ref):
    me, core = at_ref[0], at_ref[1]
    _, per, cols = a0.shape
    for j in range(2):
        wanted = serving_ref[me ^ (2 * j)]
        sums = [0.0, 0.0]
        for k, arrived in enumerate((a0, a1, a2, a3)):
            row = lax.broadcasted_iota(jnp.int32, (per, per), 0) + (me ^ k) * per
            pick = (row == wanted).astype(BF16)
            for c in range(2):
                sums[c] += lax.dot_general(
                    pick, arrived[core ^ c], (((0,), (0,)), ((), ())), preferred_element_type=F32
                )
        for c in range(2):
            aligned_ref[j, :, c * cols : (c + 1) * cols] = sums[c].astype(BF16)


def teacher_rows(at, serving, arrived):
    _, per, cols = arrived[0].shape
    return pl.pallas_call(
        teacher_kernel,
        out_shape=shape((2, per, 2 * cols), BF16),
        in_specs=[SMEM] + [VMEM] * 5,
        out_specs=VMEM,
        compiler_params=params(5),
        cost_estimate=cost(32 * per * per * cols, 12 * per * cols * 2),
        name="teacher_rows",
    )(at, serving, *arrived)


def student_stats(logits):
    peak = jnp.max(logits, axis=1, keepdims=True)
    soft = jnp.exp((logits - peak) * 0.5)
    hard = jnp.sum(soft * soft, axis=1, keepdims=True)
    return columns_to_rows([peak, hard, jnp.sum(soft, axis=1, keepdims=True)])


def near_kernel(rows_ref, w_ref, *refs):
    logits_ref, stats_ref = refs[-2:]
    logits = jnp.dot(rows_ref[...], w_ref[...], preferred_element_type=F32)
    logits_ref[...] = logits
    stats_ref[...] = student_stats(logits)


def near_logits(rows, weight, *held):
    per, depth = rows.shape
    cols = weight.shape[1]
    return pl.pallas_call(
        near_kernel,
        out_shape=(shape((per, cols), F32), shape((STAT_ROWS, per), F32)),
        in_specs=[VMEM] * (2 + len(held)),
        out_specs=(VMEM, VMEM),
        compiler_params=params(6),
        cost_estimate=cost(2 * per * depth * cols, (per + cols) * depth * 2, per * cols),
        name="near_logits",
    )(rows, weight, *held)


NOTHING = -3.0e38


def both(a, b):
    peak = jnp.maximum(a[0:1], b[0:1])
    ea, eb = jnp.exp((a[0:1] - peak) * 0.5), jnp.exp((b[0:1] - peak) * 0.5)
    return jnp.concatenate(
        [peak, a[1:2] * (ea * ea) + b[1:2] * (eb * eb), a[2:3] * ea + b[2:3] * eb]
    )


def far_kernel(n, spots_ref, *refs):
    pieces, refs = refs[:n], refs[n:]
    own_ref, other_ref, stats_a, stats_b, taught_ref, taught_core_ref, ids_ref = refs[:7]
    a_ref, b_ref, rows_ref, out_ref = refs[7:]
    for k, piece in enumerate(pieces):
        rows_ref[pl.ds(pl.multiple_of(spots_ref[k], 16), piece.shape[0]), :] = piece[...]
    per = rows_ref.shape[0]
    a = jnp.dot(rows_ref[...], own_ref[...], preferred_element_type=F32)
    b = jnp.dot(rows_ref[...], other_ref[...], preferred_element_type=F32)
    a_ref[...] = a
    b_ref[...] = b
    out_ref[0, 0:3, :] = both(stats_a[...], stats_b[...])
    out_ref[0, 3:4, :] = ids_ref[...].astype(F32)
    out_ref[0, 4:6, :] = taught_ref[0:2, :]
    out_ref[0, 6:8, :] = taught_core_ref[0:2, :]
    out_ref[1, 0:3, :] = both(student_stats(a), student_stats(b))
    row = lax.broadcasted_iota(jnp.int32, (5, per), 0)
    out_ref[1, 3:8, :] = jnp.where((row == 1) | (row == 3), NOTHING, 0.0)


def far_logits(spots, pieces, own, other, *small):
    depth, cols = own.shape
    per = sum(piece.shape[0] for piece in pieces)
    return pl.pallas_call(
        lambda *refs: far_kernel(len(pieces), *refs),
        out_shape=(
            shape((per, cols), F32),
            shape((per, cols), F32),
            shape((per, depth), BF16),
            shape((2, STAT_ROWS, per), F32),
        ),
        in_specs=[SMEM] + [VMEM] * (len(pieces) + 2 + len(small)),
        out_specs=(VMEM, VMEM, VMEM, VMEM),
        compiler_params=params(12),
        cost_estimate=cost(4 * per * depth * cols, (per + 2 * cols) * depth * 2, 2 * per * cols),
        name="far_logits",
    )(spots, *pieces, own, other, *small)


def merged(parts):
    top = parts[0]
    for part in parts[1:]:
        top = jnp.maximum(top, part)
    hard = soft = taught0 = taught1 = 0.0
    for part in parts:
        shrink = jnp.exp((part - top) * 0.5)
        s = shrink[0:1]
        hard += part[1:2] * (s * s)
        soft += part[2:3] * s
        taught0 += part[5:6] * shrink[4:5]
        taught1 += part[7:8] * shrink[6:7]
    return top[0:1], hard, soft, top[3:4], top[4:5], taught0, top[6:7], taught1


def merge_kernel(mine_ref, got_ref, *refs):
    out_ref = refs[-1]
    for j in range(2):
        rows = jnp.concatenate(merged([mine_ref[j], got_ref[j ^ 1]]))
        for copy in range(out_ref.shape[0]):
            out_ref[copy, j] = rows


def merge(mine, got, held, copies):
    return pl.pallas_call(
        merge_kernel,
        out_shape=shape((copies,) + mine.shape, F32),
        in_specs=[VMEM] * (2 + len(held)),
        out_specs=VMEM,
        compiler_params=params(6),
        cost_estimate=cost(0, (copies + 2) * mine.size * 4),
        name="merge_stats",
    )(mine, got, *held)


def picker(bit, flip, total):
    half = total // 2
    row = lax.broadcasted_iota(jnp.int32, (total, total), 0)
    side = jnp.where(row < half, 1 << bit, 0)
    row = row & (half - 1)
    row = ((row >> bit) << (bit + 1)) + side + (row & ((1 << bit) - 1))
    return (lax.broadcasted_iota(jnp.int32, (total, total), 1) == (row ^ flip)).astype(BF16)


def grads_kernel(at_ref, stats_ref, *refs):
    logits_refs, (serving_ref, aligned_ref), g_refs = refs[:4], refs[4:6], refs[6:]
    me = at_ref[3]
    per, cols = logits_refs[0].shape
    stats = [merged([stats_ref[i, j] for i in range(stats_ref.shape[0])]) for j in range(2)]
    lane = lax.broadcasted_iota(jnp.int32, (per, per), 1)
    for j in range(2):
        rows = stats[j][:4] + (serving_ref[me ^ (2 * j)].astype(F32),)
        columns = jnp.concatenate(rows + (jnp.zeros((128 - len(rows), per), F32),)).T
        peak, hard, soft, ids, wanted = [columns[:, i : i + 1] for i in range(len(rows))]
        ids, wanted = ids.astype(jnp.int32), wanted.astype(jnp.int32)
        tpeak = total = 0.0
        for k in range(4):
            here = wanted - (me ^ k) * per == lane
            taught = stats[k // 2][4 + 2 * (k % 2) : 6 + 2 * (k % 2)]
            tpeak += jnp.where(here, taught[0], 0.0)
            total += jnp.where(here, taught[1], 0.0)
        tpeak = jnp.sum(tpeak, axis=1, keepdims=True)
        total = jnp.sum(total, axis=1, keepdims=True)
        hard, soft, total = 16.0 / hard, 32.0 / soft, 32.0 / total
        for c, g_ref in enumerate(g_refs):
            part = slice(c * cols, (c + 1) * cols)
            column = at_ref[1 + c] + lax.broadcasted_iota(jnp.int32, (per, cols), 1)
            half = jnp.exp((logits_refs[2 * j + c][...] - peak) * 0.5)
            taught = jnp.exp((aligned_ref[j, :, part].astype(F32) - tpeak) * 0.5)
            label = jnp.where(column == ids, 16.0, 0.0)
            grad = (half * soft - taught * total) + (half * half * hard - label)
            g_ref[j * per : (j + 1) * per, :] = grad.astype(BF16)


def back_kernel(bits, edges, at_ref, *refs):
    w_refs, g_refs, send_refs, keep_refs = refs[:2], refs[-8:-6], refs[-6:-3], refs[-3:]
    grads_kernel(at_ref, *refs[2:-6])
    for p in range(3):
        per = send_refs[p].shape[0]
        pick = picker(bits[p], at_ref[0], 2 * per)
        back = 0.0
        for g_ref, w_ref in zip(g_refs, w_refs):
            rows = jnp.dot(pick, g_ref[...], preferred_element_type=F32).astype(BF16)
            back += lax.dot_general(
                w_ref[edges[p] : edges[p + 1], :],
                rows,
                (((1,), (1,)), ((), ())),
                preferred_element_type=F32,
            )
        back = back.T
        send_refs[p][...] = back[:per].astype(BF16)
        keep_refs[p][...] = back[per:]


def back_rows(at, own, other, stats, logits, serving, aligned, bits, edges):
    depth, cols = own.shape
    per = logits[0].shape[0]
    parts = [(per, edges[p + 1] - edges[p]) for p in range(3)]
    got = pl.pallas_call(
        lambda *refs: back_kernel(bits, edges, *refs),
        out_shape=[shape((2 * per, cols), BF16)] * 2
        + [shape(part, BF16) for part in parts]
        + [shape(part, F32) for part in parts],
        in_specs=[SMEM] + [VMEM] * 9,
        out_specs=[VMEM] * 8,
        compiler_params=params(20),
        cost_estimate=cost(8 * per * depth * cols, 2 * cols * depth * 2, 4 * per * cols),
        name="back_rows",
    )(at, own, other, stats, *logits, serving, aligned)
    return got[0], got[1], got[2:5], got[5:8]


def head_kernel(r0, r1, r2, r3, mine_ref, theirs_ref, out_ref):
    rows = jnp.concatenate([r0[...], r1[...], r2[...], r3[...]])
    grads = jnp.concatenate([mine_ref[...], theirs_ref[...]])
    out_ref[...] = lax.dot_general(
        rows, grads, (((0,), (0,)), ((), ())), preferred_element_type=F32
    ).astype(BF16)


def head_gradient(rows, mine, theirs):
    per, depth = rows[0].shape
    cols = mine.shape[1]
    tile = 512 if depth % 512 == 0 else depth
    whole = pl.BlockSpec((2 * per, cols), lambda i: (0, 0))
    slab = pl.BlockSpec((per, tile), lambda i: (0, i))
    return pl.pallas_call(
        head_kernel,
        grid=(depth // tile,),
        out_shape=shape((depth, cols), BF16),
        in_specs=[slab] * 4 + [whole] * 2,
        out_specs=pl.BlockSpec((tile, cols), lambda i: (i, 0)),
        compiler_params=params(6),
        cost_estimate=cost(8 * per * depth * cols, (4 * per + cols) * depth * 2),
        name="head_gradient",
    )(*rows, mine, theirs)


def body(hidden, token_ids, serving, head_weight, teacher_logits):
    groups = lax.axis_size("grp")
    shards = lax.axis_size("vocab")
    me_g = lax.axis_index("grp")
    me_v = lax.axis_index("vocab")
    per, depth = hidden.shape
    cols = head_weight.shape[1]
    owned = per // shards
    CORE, X = shards, 2 * shards
    Y, W = 1, 2
    count = groups * shards

    def swap(value, mask):
        return lax.ppermute(value, AXES, [(i, i ^ mask) for i in range(count)])

    def tie(*values):
        return lax.optimization_barrier(values)

    def ints(*values):
        return jnp.stack([jnp.asarray(v, jnp.int32) for v in values])

    quarter_rows = per // 4
    quarter = me_v & 3
    starts = [(quarter ^ k) * quarter_rows for k in range(4)]
    chip = me_g >> 1
    spots = ints(*starts)
    at = ints(
        me_v * owned, (me_g * shards + me_v) * cols, ((me_g ^ 1) * shards + me_v) * cols, me_g
    )
    who = ints(me_g, me_g & 1)
    unsigned = [
        jnp.asarray(v, jnp.uint32)
        for v in (starts[0], starts[3], 2 * chip, 2 * (chip ^ 1))
    ]
    rows, weight, spots, at, who, *unsigned = tie(hidden, head_weight, spots, at, who, *unsigned)
    zero = jnp.uint32(0)

    def cut(value, start, size, dim):
        indices = [start if d == dim else zero for d in range(value.ndim)]
        sizes = [size if d == dim else n for d, n in enumerate(value.shape)]
        return lax.dynamic_slice(value, indices, sizes)

    first = cut(rows, unsigned[0], quarter_rows, 0)
    x0 = swap(first, X)
    _, rows, weight, teacher = tie(first, rows, weight, teacher_logits)
    other_weight = swap(weight, CORE)
    core_hidden = swap(rows, CORE)
    x3 = swap(cut(rows, unsigned[1], quarter_rows, 0), X)
    kept = cut(teacher, unsigned[2], 2, 1).swapaxes(0, 1)
    gone = cut(teacher, unsigned[3], 2, 1).swapaxes(0, 1)
    taught = taught_stats(kept, gone)
    taught_core = swap(taught, CORE)
    near_a, stats_a = near_logits(rows, weight)
    x0, kept, gone, taught, taught_core, near_a, rows = tie(
        x0, kept, gone, taught, taught_core, near_a, rows
    )
    x1 = swap(x0, Y)
    x2 = swap(x0, W)
    kept_core = swap(kept, CORE)
    near_b, stats_b = near_logits(rows, other_weight, x0)
    *pieces, gone, near_b = tie(x0, x1, x2, x3, gone, near_b)
    taught_x = swap(gone, X)
    spots, core_hidden, kept_core = tie(spots, core_hidden, kept_core)
    far_a, far_b, x_rows, stats = far_logits(
        spots,
        pieces,
        weight,
        other_weight,
        stats_a,
        stats_b,
        taught,
        taught_core,
        token_ids.reshape(1, per),
    )

    served = serving.reshape(groups, 1, per)
    logits = [near_a, near_b, far_a, far_b]
    held = logits + [weight]
    stats = merge(stats, swap(stats, X), held, shards)
    _, taught_x = tie(stats, taught_x)
    taught_far = swap(taught_x, CORE)
    aligned = teacher_rows(who, served, [kept, kept_core, taught_x, taught_far])
    stats = lax.all_to_all(stats, "vocab", split_axis=0, concat_axis=0, tiled=True)

    bits = shards.bit_length() - 1
    masks = {0: X}
    for b in range(bits):
        masks[1 + b] = shards >> (1 + b)
    ydim, wdim = bits, bits - 1
    third = depth // 128 // 3 * 128
    edges = (0, third, 2 * third, depth)
    orders = [(0, ydim, wdim), (ydim, wdim, 0), (wdim, 0, ydim)]
    low = owned.bit_length() - 1
    row_bit = {0: low + bits, ydim: low, wdim: low + 1}
    first_bits = tuple(row_bit[order[0]] for order in orders)
    gown, gother, sents, keeps = back_rows(
        at, weight, other_weight, stats, logits, served, aligned, first_bits, edges
    )
    gots = [swap(sents[p], masks[orders[p][0]]) for p in range(3)]
    theirs = swap(gother, CORE)
    _, x_sent = tie(gother, x_rows)
    grad_head = head_gradient([hidden, x_rows, core_hidden, swap(x_sent, CORE)], gown, theirs)
    grad_head, *gots = tie(grad_head, *gots)

    def folded(value, p):
        dims = [2] * (1 + bits)
        dims[orders[p][0]] = 1
        return value.reshape(*dims, owned, value.shape[-1])

    terms = [[folded(keeps[p], p), folded(gots[p], p)] for p in range(3)]
    for stage in (1, 2):
        sents = [
            sum(lax.index_in_dim(t, 1, orders[p][stage]).astype(F32) for t in terms[p]).astype(BF16)
            for p in range(3)
        ]
        gots = [swap(sents[p], masks[orders[p][stage]]) for p in range(3)]
        for p in range(3):
            terms[p] = [lax.index_in_dim(t, 0, orders[p][stage]) for t in terms[p]] + [gots[p]]
    for dim in range(1, wdim):
        for p in range(3):
            sent = sum(lax.index_in_dim(t, 1, dim).astype(F32) for t in terms[p]).astype(BF16)
            terms[p] = [lax.index_in_dim(t, 0, dim) for t in terms[p]] + [swap(sent, masks[dim])]
    total = jnp.concatenate([sum(t.astype(F32) for t in ts) for ts in terms], axis=-1)
    return (total.reshape(owned, depth), grad_head)


def solution(mesh):
    placed = (P("grp", None), P("grp"), P(), P(None, ("grp", "vocab")), P("grp", None, "vocab"))
    return jax.shard_map(
        body,
        mesh=mesh,
        in_specs=placed,
        out_specs=(P(("grp", "vocab"), None), P(None, ("grp", "vocab"))),
        check_vma=False,
    )
```

```python
import jax
import jax.numpy as jnp
from jax import lax
from jax.experimental import pallas as pl
from jax.experimental.pallas import tpu as pltpu
from jax.sharding import PartitionSpec as P

BF16 = jnp.bfloat16
F32 = jnp.float32
AXES = ("grp", "vocab")
VMEM = pl.BlockSpec(memory_space=pltpu.VMEM)
SMEM = pl.BlockSpec(memory_space=pltpu.SMEM)
STAT_ROWS = 8
MIB = 2**20


def params(mib):
    return pltpu.CompilerParams(vmem_limit_bytes=mib * MIB)


def cost(flops, nbytes, exps=0):
    return pl.CostEstimate(flops=flops, bytes_accessed=nbytes, transcendentals=exps)


def shape(dims, dtype):
    return jax.ShapeDtypeStruct(dims, dtype)


def columns_to_rows(columns):
    count = columns[0].shape[0]
    lane = lax.broadcasted_iota(jnp.int32, (count, 128), 1)
    wide = jnp.zeros((count, 128), F32)
    for k, column in enumerate(columns):
        wide = jnp.where(lane == k, column, wide)
    return wide.T[:STAT_ROWS]


def taught_kernel(kept_ref, gone_ref, out_ref):
    parts = [ref[c].astype(F32) for ref in (kept_ref, gone_ref) for c in range(2)]
    top = parts[0]
    for part in parts[1:]:
        top = jnp.maximum(top, part)
    peak = jnp.max(top, axis=1, keepdims=True)
    total = sum(jnp.exp((part - peak) * 0.5) for part in parts)
    out_ref[...] = columns_to_rows([peak, jnp.sum(total, axis=1, keepdims=True)])


def taught_stats(kept, gone):
    _, per, cols = kept.shape
    return pl.pallas_call(
        taught_kernel,
        out_shape=shape((STAT_ROWS, per), F32),
        in_specs=[VMEM] * 2,
        out_specs=VMEM,
        compiler_params=params(4),
        cost_estimate=cost(0, 4 * per * cols * 2, 4 * per * cols),
        name="taught_stats",
    )(kept, gone)


def teacher_kernel(at_ref, serving_ref, a0, a1, a2, a3, aligned_ref):
    me, core = at_ref[0], at_ref[1]
    _, per, cols = a0.shape
    for j in range(2):
        wanted = serving_ref[me ^ (2 * j)]
        sums = [0.0, 0.0]
        for k, arrived in enumerate((a0, a1, a2, a3)):
            row = lax.broadcasted_iota(jnp.int32, (per, per), 0) + (me ^ k) * per
            pick = (row == wanted).astype(BF16)
            for c in range(2):
                sums[c] += lax.dot_general(
                    pick, arrived[core ^ c], (((0,), (0,)), ((), ())), preferred_element_type=F32
                )
        for c in range(2):
            aligned_ref[j, :, c * cols : (c + 1) * cols] = sums[c].astype(BF16)


def teacher_rows(at, serving, arrived):
    _, per, cols = arrived[0].shape
    return pl.pallas_call(
        teacher_kernel,
        out_shape=shape((2, per, 2 * cols), BF16),
        in_specs=[SMEM] + [VMEM] * 5,
        out_specs=VMEM,
        compiler_params=params(5),
        cost_estimate=cost(32 * per * per * cols, 12 * per * cols * 2),
        name="teacher_rows",
    )(at, serving, *arrived)


def student_stats(logits):
    peak = jnp.max(logits, axis=1, keepdims=True)
    soft = jnp.exp((logits - peak) * 0.5)
    hard = jnp.sum(soft * soft, axis=1, keepdims=True)
    return columns_to_rows([peak, hard, jnp.sum(soft, axis=1, keepdims=True)])


def near_kernel(rows_ref, w_ref, *refs):
    logits_ref, stats_ref = refs[-2:]
    logits = jnp.dot(rows_ref[...], w_ref[...], preferred_element_type=F32)
    logits_ref[...] = logits
    stats_ref[...] = student_stats(logits)


def near_logits(rows, weight, *held):
    per, depth = rows.shape
    cols = weight.shape[1]
    return pl.pallas_call(
        near_kernel,
        out_shape=(shape((per, cols), F32), shape((STAT_ROWS, per), F32)),
        in_specs=[VMEM] * (2 + len(held)),
        out_specs=(VMEM, VMEM),
        compiler_params=params(6),
        cost_estimate=cost(2 * per * depth * cols, (per + cols) * depth * 2, per * cols),
        name="near_logits",
    )(rows, weight, *held)


NOTHING = -3.0e38


def both(a, b):
    peak = jnp.maximum(a[0:1], b[0:1])
    ea, eb = jnp.exp((a[0:1] - peak) * 0.5), jnp.exp((b[0:1] - peak) * 0.5)
    return jnp.concatenate(
        [peak, a[1:2] * (ea * ea) + b[1:2] * (eb * eb), a[2:3] * ea + b[2:3] * eb]
    )


def far_kernel(n, spots_ref, *refs):
    pieces, refs = refs[:n], refs[n:]
    own_ref, other_ref, stats_a, stats_b, taught_ref, taught_core_ref, ids_ref = refs[:7]
    a_ref, b_ref, rows_ref, out_ref = refs[7:]
    for k, piece in enumerate(pieces):
        rows_ref[pl.ds(pl.multiple_of(spots_ref[k], 16), piece.shape[0]), :] = piece[...]
    per = rows_ref.shape[0]
    a = jnp.dot(rows_ref[...], own_ref[...], preferred_element_type=F32)
    b = jnp.dot(rows_ref[...], other_ref[...], preferred_element_type=F32)
    a_ref[...] = a
    b_ref[...] = b
    out_ref[0, 0:3, :] = both(stats_a[...], stats_b[...])
    out_ref[0, 3:4, :] = ids_ref[...].astype(F32)
    out_ref[0, 4:6, :] = taught_ref[0:2, :]
    out_ref[0, 6:8, :] = taught_core_ref[0:2, :]
    out_ref[1, 0:3, :] = both(student_stats(a), student_stats(b))
    row = lax.broadcasted_iota(jnp.int32, (5, per), 0)
    out_ref[1, 3:8, :] = jnp.where((row == 1) | (row == 3), NOTHING, 0.0)


def far_logits(spots, pieces, own, other, *small):
    depth, cols = own.shape
    per = sum(piece.shape[0] for piece in pieces)
    return pl.pallas_call(
        lambda *refs: far_kernel(len(pieces), *refs),
        out_shape=(
            shape((per, cols), F32),
            shape((per, cols), F32),
            shape((per, depth), BF16),
            shape((2, STAT_ROWS, per), F32),
        ),
        in_specs=[SMEM] + [VMEM] * (len(pieces) + 2 + len(small)),
        out_specs=(VMEM, VMEM, VMEM, VMEM),
        compiler_params=params(12),
        cost_estimate=cost(4 * per * depth * cols, (per + 2 * cols) * depth * 2, 2 * per * cols),
        name="far_logits",
    )(spots, *pieces, own, other, *small)


def merged(parts):
    top = parts[0]
    for part in parts[1:]:
        top = jnp.maximum(top, part)
    hard = soft = taught0 = taught1 = 0.0
    for part in parts:
        shrink = jnp.exp((part - top) * 0.5)
        s = shrink[0:1]
        hard += part[1:2] * (s * s)
        soft += part[2:3] * s
        taught0 += part[5:6] * shrink[4:5]
        taught1 += part[7:8] * shrink[6:7]
    return top[0:1], hard, soft, top[3:4], top[4:5], taught0, top[6:7], taught1


def merge_kernel(flips, *refs):
    out_ref = refs[-1]
    for j in range(2):
        out_ref[j] = jnp.concatenate(merged([ref[j ^ f] for ref, f in zip(refs, flips)]))


def merge(parts, flips, held):
    return pl.pallas_call(
        lambda *refs: merge_kernel(flips, *refs),
        out_shape=shape(parts[0].shape, F32),
        in_specs=[VMEM] * (len(parts) + len(held)),
        out_specs=VMEM,
        compiler_params=params(6),
        cost_estimate=cost(0, 5 * parts[0].size * 4),
        name="merge_stats",
    )(*parts, *held)


def picker(bit, flip, total):
    half = total // 2
    row = lax.broadcasted_iota(jnp.int32, (total, total), 0)
    side = jnp.where(row < half, 1 << bit, 0)
    row = row & (half - 1)
    row = ((row >> bit) << (bit + 1)) + side + (row & ((1 << bit) - 1))
    return (lax.broadcasted_iota(jnp.int32, (total, total), 1) == (row ^ flip)).astype(BF16)


def grads_kernel(n, at_ref, *refs):
    stats_refs, refs = refs[:n], refs[n:]
    logits_refs, (serving_ref, aligned_ref), g_refs = refs[:4], refs[4:6], refs[6:]
    me = at_ref[3]
    per, cols = logits_refs[0].shape
    stats = [merged([ref[j] for ref in stats_refs]) for j in range(2)]
    lane = lax.broadcasted_iota(jnp.int32, (per, per), 1)
    for j in range(2):
        rows = stats[j][:4] + (serving_ref[me ^ (2 * j)].astype(F32),)
        columns = jnp.concatenate(rows + (jnp.zeros((128 - len(rows), per), F32),)).T
        peak, hard, soft, ids, wanted = [columns[:, i : i + 1] for i in range(len(rows))]
        ids, wanted = ids.astype(jnp.int32), wanted.astype(jnp.int32)
        tpeak = total = 0.0
        for k in range(4):
            here = wanted - (me ^ k) * per == lane
            taught = stats[k // 2][4 + 2 * (k % 2) : 6 + 2 * (k % 2)]
            tpeak += jnp.where(here, taught[0], 0.0)
            total += jnp.where(here, taught[1], 0.0)
        tpeak = jnp.sum(tpeak, axis=1, keepdims=True)
        total = jnp.sum(total, axis=1, keepdims=True)
        hard, soft, total = 16.0 / hard, 32.0 / soft, 32.0 / total
        for c, g_ref in enumerate(g_refs):
            part = slice(c * cols, (c + 1) * cols)
            column = at_ref[1 + c] + lax.broadcasted_iota(jnp.int32, (per, cols), 1)
            half = jnp.exp((logits_refs[2 * j + c][...] - peak) * 0.5)
            taught = jnp.exp((aligned_ref[j, :, part].astype(F32) - tpeak) * 0.5)
            label = jnp.where(column == ids, 16.0, 0.0)
            grad = (half * soft - taught * total) + (half * half * hard - label)
            g_ref[j * per : (j + 1) * per, :] = grad.astype(BF16)


def back_kernel(bits, edges, n, at_ref, *refs):
    w_refs, g_refs, send_refs, keep_refs = refs[:2], refs[-8:-6], refs[-6:-3], refs[-3:]
    grads_kernel(n, at_ref, *refs[2:-6])
    for p in range(3):
        per = send_refs[p].shape[0]
        pick = picker(bits[p], at_ref[0], 2 * per)
        back = 0.0
        for g_ref, w_ref in zip(g_refs, w_refs):
            rows = jnp.dot(pick, g_ref[...], preferred_element_type=F32).astype(BF16)
            back += lax.dot_general(
                w_ref[edges[p] : edges[p + 1], :],
                rows,
                (((1,), (1,)), ((), ())),
                preferred_element_type=F32,
            )
        back = back.T
        send_refs[p][...] = back[:per].astype(BF16)
        keep_refs[p][...] = back[per:]


def back_rows(at, own, other, stats, logits, serving, aligned, bits, edges):
    depth, cols = own.shape
    per = logits[0].shape[0]
    parts = [(per, edges[p + 1] - edges[p]) for p in range(3)]
    got = pl.pallas_call(
        lambda *refs: back_kernel(bits, edges, len(stats), *refs),
        out_shape=[shape((2 * per, cols), BF16)] * 2
        + [shape(part, BF16) for part in parts]
        + [shape(part, F32) for part in parts],
        in_specs=[SMEM] + [VMEM] * (len(stats) + 8),
        out_specs=[VMEM] * 8,
        compiler_params=params(20),
        cost_estimate=cost(8 * per * depth * cols, 2 * cols * depth * 2, 4 * per * cols),
        name="back_rows",
    )(at, own, other, *stats, *logits, serving, aligned)
    return got[0], got[1], got[2:5], got[5:8]


def head_kernel(r0, r1, r2, r3, mine_ref, theirs_ref, out_ref):
    rows = jnp.concatenate([r0[...], r1[...], r2[...], r3[...]])
    grads = jnp.concatenate([mine_ref[...], theirs_ref[...]])
    out_ref[...] = lax.dot_general(
        rows, grads, (((0,), (0,)), ((), ())), preferred_element_type=F32
    ).astype(BF16)


def head_gradient(rows, mine, theirs):
    per, depth = rows[0].shape
    cols = mine.shape[1]
    tile = 512 if depth % 512 == 0 else depth
    whole = pl.BlockSpec((2 * per, cols), lambda i: (0, 0))
    slab = pl.BlockSpec((per, tile), lambda i: (0, i))
    return pl.pallas_call(
        head_kernel,
        grid=(depth // tile,),
        out_shape=shape((depth, cols), BF16),
        in_specs=[slab] * 4 + [whole] * 2,
        out_specs=pl.BlockSpec((tile, cols), lambda i: (i, 0)),
        compiler_params=params(6),
        cost_estimate=cost(8 * per * depth * cols, (4 * per + cols) * depth * 2),
        name="head_gradient",
    )(*rows, mine, theirs)


def body(hidden, token_ids, serving, head_weight, teacher_logits):
    groups = lax.axis_size("grp")
    shards = lax.axis_size("vocab")
    me_g = lax.axis_index("grp")
    me_v = lax.axis_index("vocab")
    per, depth = hidden.shape
    cols = head_weight.shape[1]
    owned = per // shards
    CORE, X = shards, 2 * shards
    Y, W = 1, 2
    count = groups * shards

    def swap(value, mask):
        return lax.ppermute(value, AXES, [(i, i ^ mask) for i in range(count)])

    def tie(*values):
        return lax.optimization_barrier(values)

    def ints(*values):
        return jnp.stack([jnp.asarray(v, jnp.int32) for v in values])

    quarter_rows = per // 4
    quarter = me_v & 3
    starts = [(quarter ^ k) * quarter_rows for k in range(4)]
    chip = me_g >> 1
    spots = ints(*starts)
    at = ints(
        me_v * owned, (me_g * shards + me_v) * cols, ((me_g ^ 1) * shards + me_v) * cols, me_g
    )
    who = ints(me_g, me_g & 1)
    unsigned = [
        jnp.asarray(v, jnp.uint32)
        for v in (starts[0], starts[3], 2 * chip, 2 * (chip ^ 1))
    ]
    rows, weight, spots, at, who, *unsigned = tie(hidden, head_weight, spots, at, who, *unsigned)
    zero = jnp.uint32(0)

    def cut(value, start, size, dim):
        indices = [start if d == dim else zero for d in range(value.ndim)]
        sizes = [size if d == dim else n for d, n in enumerate(value.shape)]
        return lax.dynamic_slice(value, indices, sizes)

    first = cut(rows, unsigned[0], quarter_rows, 0)
    x0 = swap(first, X)
    _, rows, weight, teacher = tie(first, rows, weight, teacher_logits)
    other_weight = swap(weight, CORE)
    core_hidden = swap(rows, CORE)
    x3 = swap(cut(rows, unsigned[1], quarter_rows, 0), X)
    kept = cut(teacher, unsigned[2], 2, 1).swapaxes(0, 1)
    gone = cut(teacher, unsigned[3], 2, 1).swapaxes(0, 1)
    taught = taught_stats(kept, gone)
    taught_core = swap(taught, CORE)
    near_a, stats_a = near_logits(rows, weight)
    x0, kept, gone, taught, taught_core, near_a, rows = tie(
        x0, kept, gone, taught, taught_core, near_a, rows
    )
    x1 = swap(x0, Y)
    x2 = swap(x0, W)
    kept_core = swap(kept, CORE)
    near_b, stats_b = near_logits(rows, other_weight, x0)
    *pieces, gone, near_b = tie(x0, x1, x2, x3, gone, near_b)
    taught_x = swap(gone, X)
    spots, core_hidden, kept_core = tie(spots, core_hidden, kept_core)
    far_a, far_b, x_rows, stats = far_logits(
        spots,
        pieces,
        weight,
        other_weight,
        stats_a,
        stats_b,
        taught,
        taught_core,
        token_ids.reshape(1, per),
    )

    served = serving.reshape(groups, 1, per)
    logits = [near_a, near_b, far_a, far_b]
    held = logits + [weight]
    stats = merge([stats, swap(stats, X), swap(stats, Y), swap(stats, X + Y)], (0, 1, 0, 1), held)
    _, taught_x = tie(stats, taught_x)
    taught_far = swap(taught_x, CORE)
    aligned = teacher_rows(who, served, [kept, kept_core, taught_x, taught_far])
    mask = W
    while True:
        masks = [mask, 2 * mask, 3 * mask] if 2 * mask < shards else [mask]
        parts = [stats] + [swap(stats, m) for m in masks]
        mask *= 4
        if mask >= shards:
            break
        stats = merge(parts, (0,) * len(parts), held)

    bits = shards.bit_length() - 1
    masks = {0: X}
    for b in range(bits):
        masks[1 + b] = shards >> (1 + b)
    ydim, wdim = bits, bits - 1
    third = depth // 128 // 3 * 128
    edges = (0, third, 2 * third, depth)
    orders = [(0, ydim, wdim), (ydim, wdim, 0), (wdim, 0, ydim)]
    low = owned.bit_length() - 1
    row_bit = {0: low + bits, ydim: low, wdim: low + 1}
    first_bits = tuple(row_bit[order[0]] for order in orders)
    gown, gother, sents, keeps = back_rows(
        at, weight, other_weight, parts, logits, served, aligned, first_bits, edges
    )
    gots = [swap(sents[p], masks[orders[p][0]]) for p in range(3)]
    theirs = swap(gother, CORE)
    _, x_sent = tie(gother, x_rows)
    grad_head = head_gradient([hidden, x_rows, core_hidden, swap(x_sent, CORE)], gown, theirs)
    grad_head, *gots = tie(grad_head, *gots)

    def folded(value, p):
        dims = [2] * (1 + bits)
        dims[orders[p][0]] = 1
        return value.reshape(*dims, owned, value.shape[-1])

    terms = [[folded(keeps[p], p), folded(gots[p], p)] for p in range(3)]
    for stage in (1, 2):
        sents = [
            sum(lax.index_in_dim(t, 1, orders[p][stage]).astype(F32) for t in terms[p]).astype(BF16)
            for p in range(3)
        ]
        gots = [swap(sents[p], masks[orders[p][stage]]) for p in range(3)]
        for p in range(3):
            terms[p] = [lax.index_in_dim(t, 0, orders[p][stage]) for t in terms[p]] + [gots[p]]
    for dim in range(1, wdim):
        for p in range(3):
            sent = sum(lax.index_in_dim(t, 1, dim).astype(F32) for t in terms[p]).astype(BF16)
            terms[p] = [lax.index_in_dim(t, 0, dim) for t in terms[p]] + [swap(sent, masks[dim])]
    total = jnp.concatenate([sum(t.astype(F32) for t in ts) for ts in terms], axis=-1)
    return (total.reshape(owned, depth), grad_head)


def solution(mesh):
    placed = (P("grp", None), P("grp"), P(), P(None, ("grp", "vocab")), P("grp", None, "vocab"))
    return jax.shard_map(
        body,
        mesh=mesh,
        in_specs=placed,
        out_specs=(P(("grp", "vocab"), None), P(None, ("grp", "vocab"))),
        check_vma=False,
    )
```

```python
import jax
import jax.numpy as jnp
from jax import lax
from jax.experimental import pallas as pl
from jax.experimental.pallas import tpu as pltpu
from jax.sharding import PartitionSpec as P

BF16 = jnp.bfloat16
F32 = jnp.float32
AXES = ("grp", "vocab")
VMEM = pl.BlockSpec(memory_space=pltpu.VMEM)
SMEM = pl.BlockSpec(memory_space=pltpu.SMEM)
STAT_ROWS = 8
MIB = 2**20


def params(mib):
    return pltpu.CompilerParams(vmem_limit_bytes=mib * MIB)


def cost(flops, nbytes, exps=0):
    return pl.CostEstimate(flops=flops, bytes_accessed=nbytes, transcendentals=exps)


def shape(dims, dtype):
    return jax.ShapeDtypeStruct(dims, dtype)


def columns_to_rows(columns):
    count = columns[0].shape[0]
    lane = lax.broadcasted_iota(jnp.int32, (count, 128), 1)
    wide = jnp.zeros((count, 128), F32)
    for k, column in enumerate(columns):
        wide = jnp.where(lane == k, column, wide)
    return wide.T[:STAT_ROWS]


def taught_kernel(kept_ref, gone_ref, out_ref):
    parts = [ref[c].astype(F32) for ref in (kept_ref, gone_ref) for c in range(2)]
    top = parts[0]
    for part in parts[1:]:
        top = jnp.maximum(top, part)
    peak = jnp.max(top, axis=1, keepdims=True)
    total = sum(jnp.exp((part - peak) * 0.5) for part in parts)
    out_ref[...] = columns_to_rows([peak, jnp.sum(total, axis=1, keepdims=True)])


def taught_stats(kept, gone):
    _, per, cols = kept.shape
    return pl.pallas_call(
        taught_kernel,
        out_shape=shape((STAT_ROWS, per), F32),
        in_specs=[VMEM] * 2,
        out_specs=VMEM,
        compiler_params=params(4),
        cost_estimate=cost(0, 4 * per * cols * 2, 4 * per * cols),
        name="taught_stats",
    )(kept, gone)


def teacher_kernel(at_ref, serving_ref, a0, a1, a2, a3, aligned_ref):
    me, core = at_ref[0], at_ref[1]
    _, per, cols = a0.shape
    for j in range(2):
        wanted = serving_ref[me ^ (2 * j)]
        sums = [0.0, 0.0]
        for k, arrived in enumerate((a0, a1, a2, a3)):
            row = lax.broadcasted_iota(jnp.int32, (per, per), 0) + (me ^ k) * per
            pick = (row == wanted).astype(BF16)
            for c in range(2):
                sums[c] += lax.dot_general(
                    pick, arrived[core ^ c], (((0,), (0,)), ((), ())), preferred_element_type=F32
                )
        for c in range(2):
            aligned_ref[j, :, c * cols : (c + 1) * cols] = sums[c].astype(BF16)


def teacher_rows(at, serving, arrived):
    _, per, cols = arrived[0].shape
    return pl.pallas_call(
        teacher_kernel,
        out_shape=shape((2, per, 2 * cols), BF16),
        in_specs=[SMEM] + [VMEM] * 5,
        out_specs=VMEM,
        compiler_params=params(5),
        cost_estimate=cost(32 * per * per * cols, 12 * per * cols * 2),
        name="teacher_rows",
    )(at, serving, *arrived)


def student_stats(logits):
    peak = jnp.max(logits, axis=1, keepdims=True)
    soft = jnp.exp((logits - peak) * 0.5)
    hard = jnp.sum(soft * soft, axis=1, keepdims=True)
    return columns_to_rows([peak, hard, jnp.sum(soft, axis=1, keepdims=True)])


def near_kernel(rows_ref, w_ref, *refs):
    logits_ref, stats_ref = refs[-2:]
    logits = jnp.dot(rows_ref[...], w_ref[...], preferred_element_type=F32)
    logits_ref[...] = logits
    stats_ref[...] = student_stats(logits)


def near_logits(rows, weight, *held):
    per, depth = rows.shape
    cols = weight.shape[1]
    return pl.pallas_call(
        near_kernel,
        out_shape=(shape((per, cols), F32), shape((STAT_ROWS, per), F32)),
        in_specs=[VMEM] * (2 + len(held)),
        out_specs=(VMEM, VMEM),
        compiler_params=params(6),
        cost_estimate=cost(2 * per * depth * cols, (per + cols) * depth * 2, per * cols),
        name="near_logits",
    )(rows, weight, *held)


NOTHING = -3.0e38


def both(a, b):
    peak = jnp.maximum(a[0:1], b[0:1])
    ea, eb = jnp.exp((a[0:1] - peak) * 0.5), jnp.exp((b[0:1] - peak) * 0.5)
    return jnp.concatenate(
        [peak, a[1:2] * (ea * ea) + b[1:2] * (eb * eb), a[2:3] * ea + b[2:3] * eb]
    )


def far_kernel(n, spots_ref, *refs):
    pieces, refs = refs[:n], refs[n:]
    own_ref, other_ref, stats_a, stats_b, taught_ref, taught_core_ref, ids_ref = refs[:7]
    a_ref, b_ref, rows_ref, out_ref = refs[7:]
    for k, piece in enumerate(pieces):
        rows_ref[pl.ds(pl.multiple_of(spots_ref[k], 16), piece.shape[0]), :] = piece[...]
    per = rows_ref.shape[0]
    a = jnp.dot(rows_ref[...], own_ref[...], preferred_element_type=F32)
    b = jnp.dot(rows_ref[...], other_ref[...], preferred_element_type=F32)
    a_ref[...] = a
    b_ref[...] = b
    out_ref[0, 0:3, :] = both(stats_a[...], stats_b[...])
    out_ref[0, 3:4, :] = ids_ref[...].astype(F32)
    out_ref[0, 4:6, :] = taught_ref[0:2, :]
    out_ref[0, 6:8, :] = taught_core_ref[0:2, :]
    out_ref[1, 0:3, :] = both(student_stats(a), student_stats(b))
    row = lax.broadcasted_iota(jnp.int32, (5, per), 0)
    out_ref[1, 3:8, :] = jnp.where((row == 1) | (row == 3), NOTHING, 0.0)


def far_logits(spots, pieces, own, other, *small):
    depth, cols = own.shape
    per = sum(piece.shape[0] for piece in pieces)
    return pl.pallas_call(
        lambda *refs: far_kernel(len(pieces), *refs),
        out_shape=(
            shape((per, cols), F32),
            shape((per, cols), F32),
            shape((per, depth), BF16),
            shape((2, STAT_ROWS, per), F32),
        ),
        in_specs=[SMEM] + [VMEM] * (len(pieces) + 2 + len(small)),
        out_specs=(VMEM, VMEM, VMEM, VMEM),
        compiler_params=params(12),
        cost_estimate=cost(4 * per * depth * cols, (per + 2 * cols) * depth * 2, 2 * per * cols),
        name="far_logits",
    )(spots, *pieces, own, other, *small)


def merged(parts):
    top = parts[0]
    for part in parts[1:]:
        top = jnp.maximum(top, part)
    hard = soft = taught0 = taught1 = 0.0
    for part in parts:
        shrink = jnp.exp((part - top) * 0.5)
        s = shrink[0:1]
        hard += part[1:2] * (s * s)
        soft += part[2:3] * s
        taught0 += part[5:6] * shrink[4:5]
        taught1 += part[7:8] * shrink[6:7]
    return top[0:1], hard, soft, top[3:4], top[4:5], taught0, top[6:7], taught1


def merge_kernel(flips, *refs):
    out_ref = refs[-1]
    for j in range(2):
        out_ref[j] = jnp.concatenate(merged([ref[j ^ f] for ref, f in zip(refs, flips)]))


def merge(parts, flips, held):
    return pl.pallas_call(
        lambda *refs: merge_kernel(flips, *refs),
        out_shape=shape(parts[0].shape, F32),
        in_specs=[VMEM] * (len(parts) + len(held)),
        out_specs=VMEM,
        compiler_params=params(6),
        cost_estimate=cost(0, 5 * parts[0].size * 4),
        name="merge_stats",
    )(*parts, *held)


def picker(places, low, flip, total):
    row = lax.broadcasted_iota(jnp.int32, (total, total), 0)
    top = total.bit_length() - 2
    rest = row & ((1 << (top - 2)) - 1)
    rest = ((rest >> low) << (low + 2)) | (rest & ((1 << low) - 1))
    first, second, third = [(row >> (top - k)) & 1 for k in range(3)]
    row = ((1 - first) << places[0]) | (second << places[1]) | (third << places[2]) | rest
    return (lax.broadcasted_iota(jnp.int32, (total, total), 1) == (row ^ flip)).astype(BF16)


def grads_kernel(n, at_ref, *refs):
    stats_refs, refs = refs[:n], refs[n:]
    logits_refs, (serving_ref, aligned_ref), g_refs = refs[:4], refs[4:6], refs[6:]
    me = at_ref[3]
    per, cols = logits_refs[0].shape
    stats = [merged([ref[j] for ref in stats_refs]) for j in range(2)]
    lane = lax.broadcasted_iota(jnp.int32, (per, per), 1)
    for j in range(2):
        rows = stats[j][:4] + (serving_ref[me ^ (2 * j)].astype(F32),)
        columns = jnp.concatenate(rows + (jnp.zeros((128 - len(rows), per), F32),)).T
        peak, hard, soft, ids, wanted = [columns[:, i : i + 1] for i in range(len(rows))]
        ids, wanted = ids.astype(jnp.int32), wanted.astype(jnp.int32)
        tpeak = total = 0.0
        for k in range(4):
            here = wanted - (me ^ k) * per == lane
            taught = stats[k // 2][4 + 2 * (k % 2) : 6 + 2 * (k % 2)]
            tpeak += jnp.where(here, taught[0], 0.0)
            total += jnp.where(here, taught[1], 0.0)
        tpeak = jnp.sum(tpeak, axis=1, keepdims=True)
        total = jnp.sum(total, axis=1, keepdims=True)
        hard, soft, total = 16.0 / hard, 32.0 / soft, 32.0 / total
        for c, g_ref in enumerate(g_refs):
            part = slice(c * cols, (c + 1) * cols)
            column = at_ref[1 + c] + lax.broadcasted_iota(jnp.int32, (per, cols), 1)
            half = jnp.exp((logits_refs[2 * j + c][...] - peak) * 0.5)
            taught = jnp.exp((aligned_ref[j, :, part].astype(F32) - tpeak) * 0.5)
            label = jnp.where(column == ids, 16.0, 0.0)
            grad = (half * soft - taught * total) + (half * half * hard - label)
            g_ref[j * per : (j + 1) * per, :] = grad.astype(BF16)


def back_kernel(low, edges, n, at_ref, *refs):
    w_refs, g_refs, send_refs, keep_refs = refs[:2], refs[-6:-4], refs[-4:-2], refs[-2:]
    grads_kernel(n, at_ref, *refs[2:-4])
    x, y, z = g_refs[0].shape[0].bit_length() - 2, low, low + 1
    for p, places in enumerate(([at_ref[4], at_ref[5], at_ref[6]], [y, z, x])):
        per = send_refs[p].shape[0]
        pick = picker(places, low, at_ref[0], 2 * per)
        back = 0.0
        for g_ref, w_ref in zip(g_refs, w_refs):
            rows = jnp.dot(pick, g_ref[...], preferred_element_type=F32).astype(BF16)
            back += lax.dot_general(
                w_ref[edges[p] : edges[p + 1], :],
                rows,
                (((1,), (1,)), ((), ())),
                preferred_element_type=F32,
            )
        back = back.astype(BF16).T
        send_refs[p][...] = back[:per]
        keep_refs[p][...] = back[per:]


def back_rows(at, own, other, stats, logits, serving, aligned, low, edges):
    depth, cols = own.shape
    per = logits[0].shape[0]
    parts = [shape((per, edges[p + 1] - edges[p]), BF16) for p in range(2)]
    got = pl.pallas_call(
        lambda *refs: back_kernel(low, edges, len(stats), *refs),
        out_shape=[shape((2 * per, cols), BF16)] * 2 + parts * 2,
        in_specs=[SMEM] + [VMEM] * (len(stats) + 8),
        out_specs=[VMEM] * 6,
        compiler_params=params(20),
        cost_estimate=cost(8 * per * depth * cols, 2 * cols * depth * 2, 4 * per * cols),
        name="back_rows",
    )(at, own, other, *stats, *logits, serving, aligned)
    return got[0], got[1], got[2:4], got[4:6]


def head_kernel(r0, r1, r2, r3, mine_ref, theirs_ref, out_ref):
    rows = jnp.concatenate([r0[...], r1[...], r2[...], r3[...]])
    grads = jnp.concatenate([mine_ref[...], theirs_ref[...]])
    out_ref[...] = lax.dot_general(
        rows, grads, (((0,), (0,)), ((), ())), preferred_element_type=F32
    ).astype(BF16)


def head_gradient(rows, mine, theirs):
    per, depth = rows[0].shape
    cols = mine.shape[1]
    tile = 512 if depth % 512 == 0 else depth
    whole = pl.BlockSpec((2 * per, cols), lambda i: (0, 0))
    slab = pl.BlockSpec((per, tile), lambda i: (0, i))
    return pl.pallas_call(
        head_kernel,
        grid=(depth // tile,),
        out_shape=shape((depth, cols), BF16),
        in_specs=[slab] * 4 + [whole] * 2,
        out_specs=pl.BlockSpec((tile, cols), lambda i: (i, 0)),
        compiler_params=params(6),
        cost_estimate=cost(8 * per * depth * cols, (4 * per + cols) * depth * 2),
        name="head_gradient",
    )(*rows, mine, theirs)


def body(hidden, token_ids, serving, head_weight, teacher_logits):
    groups = lax.axis_size("grp")
    shards = lax.axis_size("vocab")
    me_g = lax.axis_index("grp")
    me_v = lax.axis_index("vocab")
    per, depth = hidden.shape
    cols = head_weight.shape[1]
    owned = per // shards
    CORE, X = shards, 2 * shards
    Y, W = 1, 2
    count = groups * shards

    def swap(value, mask):
        return lax.ppermute(value, AXES, [(i, i ^ mask) for i in range(count)])

    def tie(*values):
        return lax.optimization_barrier(values)

    def ints(*values):
        return jnp.stack([jnp.asarray(v, jnp.int32) for v in values])

    quarter_rows = per // 4
    quarter = me_v & 3
    starts = [(quarter ^ k) * quarter_rows for k in range(4)]
    chip = me_g >> 1
    spots = ints(*starts)
    low = owned.bit_length() - 1
    turn = [per.bit_length() - 1, low, low + 1]
    odd = (me_g & 1) == 1
    at = ints(
        me_v * owned,
        (me_g * shards + me_v) * cols,
        ((me_g ^ 1) * shards + me_v) * cols,
        me_g,
        *[jnp.where(odd, turn[k - 1], turn[k]) for k in range(3)],
    )
    who = ints(me_g, me_g & 1)
    unsigned = [
        jnp.asarray(v, jnp.uint32)
        for v in (starts[0], starts[3], 2 * chip, 2 * (chip ^ 1))
    ]
    rows, weight, spots, at, who, *unsigned = tie(hidden, head_weight, spots, at, who, *unsigned)
    zero = jnp.uint32(0)

    def cut(value, start, size, dim):
        indices = [start if d == dim else zero for d in range(value.ndim)]
        sizes = [size if d == dim else n for d, n in enumerate(value.shape)]
        return lax.dynamic_slice(value, indices, sizes)

    first = cut(rows, unsigned[0], quarter_rows, 0)
    x0 = swap(first, X)
    _, rows, weight, teacher = tie(first, rows, weight, teacher_logits)
    other_weight = swap(weight, CORE)
    core_hidden = swap(rows, CORE)
    x3 = swap(cut(rows, unsigned[1], quarter_rows, 0), X)
    kept = cut(teacher, unsigned[2], 2, 1).swapaxes(0, 1)
    gone = cut(teacher, unsigned[3], 2, 1).swapaxes(0, 1)
    taught = taught_stats(kept, gone)
    taught_core = swap(taught, CORE)
    near_a, stats_a = near_logits(rows, weight)
    x0, kept, gone, taught, taught_core, near_a, rows = tie(
        x0, kept, gone, taught, taught_core, near_a, rows
    )
    x1 = swap(x0, Y)
    x2 = swap(x0, W)
    kept_core = swap(kept, CORE)
    near_b, stats_b = near_logits(rows, other_weight, x0)
    *pieces, gone, near_b = tie(x0, x1, x2, x3, gone, near_b)
    taught_x = swap(gone, X)
    spots, core_hidden, kept_core = tie(spots, core_hidden, kept_core)
    far_a, far_b, x_rows, stats = far_logits(
        spots,
        pieces,
        weight,
        other_weight,
        stats_a,
        stats_b,
        taught,
        taught_core,
        token_ids.reshape(1, per),
    )

    served = serving.reshape(groups, 1, per)
    logits = [near_a, near_b, far_a, far_b]
    held = logits + [weight]
    stats = merge([stats, swap(stats, X), swap(stats, Y), swap(stats, X + Y)], (0, 1, 0, 1), held)
    _, taught_x = tie(stats, taught_x)
    taught_far = swap(taught_x, CORE)
    aligned = teacher_rows(who, served, [kept, kept_core, taught_x, taught_far])
    mask = W
    while True:
        masks = [mask, 2 * mask, 3 * mask] if 2 * mask < shards else [mask]
        parts = [stats] + [swap(stats, m) for m in masks]
        mask *= 4
        if mask >= shards:
            break
        stats = merge(parts, (0,) * len(parts), held)

    units = depth // 128
    edges = (0, units * 19 // 28 * 128, depth)
    orders = [([X, Y, W], [W, X, Y]), ([Y, W, X], [Y, W, X])]

    def step(value, even, odd):
        masks = [odd if (i // shards) & 1 else even for i in range(count)]
        return lax.ppermute(value, AXES, [(i, i ^ masks[i]) for i in range(count)])

    gown, gother, sents, keeps = back_rows(
        at, weight, other_weight, parts, logits, served, aligned, low, edges
    )
    gots = [step(sents[p], orders[p][0][0], orders[p][1][0]) for p in range(2)]
    theirs = swap(gother, CORE)
    _, x_sent = tie(gother, x_rows)
    grad_head = head_gradient([hidden, x_rows, core_hidden, swap(x_sent, CORE)], gown, theirs)
    for p in range(2):
        grad_head, gots[p] = tie(grad_head, gots[p])
    terms = [[keeps[p], gots[p]] for p in range(2)]
    masks = [(orders[p][0][k], orders[p][1][k]) for k in (1, 2) for p in range(2)]
    mask = shards // 2
    while mask > W:
        masks += [(mask, mask)] * 2
        mask //= 2
    for k, pair in enumerate(masks):
        ours = terms[k % 2]
        kept = ours[0].shape[0] // 2
        sent = sum(t[kept:].astype(F32) for t in ours).astype(BF16)
        terms[k % 2] = [t[:kept] for t in ours] + [step(sent, *pair)]
    total = jnp.concatenate([sum(t.astype(F32) for t in ours) for ours in terms], axis=-1)
    return (total, grad_head)


def solution(mesh):
    placed = (P("grp", None), P("grp"), P(), P(None, ("grp", "vocab")), P("grp", None, "vocab"))
    return jax.shard_map(
        body,
        mesh=mesh,
        in_specs=placed,
        out_specs=(P(("grp", "vocab"), None), P(None, ("grp", "vocab"))),
        check_vma=False,
    )
```

```python
import jax
import jax.numpy as jnp
from jax import lax
from jax.experimental import pallas as pl
from jax.experimental.pallas import tpu as pltpu
from jax.sharding import PartitionSpec as P

BF16 = jnp.bfloat16
F32 = jnp.float32
AXES = ("grp", "vocab")
VMEM = pl.BlockSpec(memory_space=pltpu.VMEM)
SMEM = pl.BlockSpec(memory_space=pltpu.SMEM)
STAT_ROWS = 8
MIB = 2**20


def params(mib):
    return pltpu.CompilerParams(vmem_limit_bytes=mib * MIB)


def cost(flops, nbytes, exps=0):
    return pl.CostEstimate(flops=flops, bytes_accessed=nbytes, transcendentals=exps)


def shape(dims, dtype):
    return jax.ShapeDtypeStruct(dims, dtype)


def columns_to_rows(columns):
    count = columns[0].shape[0]
    lane = lax.broadcasted_iota(jnp.int32, (count, 128), 1)
    wide = jnp.zeros((count, 128), F32)
    for k, column in enumerate(columns):
        wide = jnp.where(lane == k, column, wide)
    return wide.T[:STAT_ROWS]


def taught_kernel(kept_ref, gone_ref, out_ref):
    parts = [ref[c].astype(F32) for ref in (kept_ref, gone_ref) for c in range(2)]
    top = parts[0]
    for part in parts[1:]:
        top = jnp.maximum(top, part)
    peak = jnp.max(top, axis=1, keepdims=True)
    total = sum(jnp.exp((part - peak) * 0.5) for part in parts)
    out_ref[...] = columns_to_rows([peak, jnp.sum(total, axis=1, keepdims=True)])


def taught_stats(kept, gone):
    _, per, cols = kept.shape
    return pl.pallas_call(
        taught_kernel,
        out_shape=shape((STAT_ROWS, per), F32),
        in_specs=[VMEM] * 2,
        out_specs=VMEM,
        compiler_params=params(4),
        cost_estimate=cost(0, 4 * per * cols * 2, 4 * per * cols),
        name="taught_stats",
    )(kept, gone)


def teacher_kernel(at_ref, serving_ref, a0, a1, a2, a3, aligned_ref):
    me, core = at_ref[0], at_ref[1]
    _, per, cols = a0.shape
    for j in range(2):
        wanted = serving_ref[me ^ (2 * j)]
        sums = [0.0, 0.0]
        for k, arrived in enumerate((a0, a1, a2, a3)):
            row = lax.broadcasted_iota(jnp.int32, (per, per), 0) + (me ^ k) * per
            pick = (row == wanted).astype(BF16)
            for c in range(2):
                sums[c] += lax.dot_general(
                    pick, arrived[core ^ c], (((0,), (0,)), ((), ())), preferred_element_type=F32
                )
        for c in range(2):
            aligned_ref[j, :, c * cols : (c + 1) * cols] = sums[c].astype(BF16)


def teacher_rows(at, serving, arrived):
    _, per, cols = arrived[0].shape
    return pl.pallas_call(
        teacher_kernel,
        out_shape=shape((2, per, 2 * cols), BF16),
        in_specs=[SMEM] + [VMEM] * 5,
        out_specs=VMEM,
        compiler_params=params(5),
        cost_estimate=cost(32 * per * per * cols, 12 * per * cols * 2),
        name="teacher_rows",
    )(at, serving, *arrived)


def student_stats(logits):
    peak = jnp.max(logits, axis=1, keepdims=True)
    soft = jnp.exp((logits - peak) * 0.5)
    hard = jnp.sum(soft * soft, axis=1, keepdims=True)
    return columns_to_rows([peak, hard, jnp.sum(soft, axis=1, keepdims=True)])


def near_kernel(rows_ref, w_ref, *refs):
    logits_ref, stats_ref = refs[-2:]
    logits = jnp.dot(rows_ref[...], w_ref[...], preferred_element_type=F32)
    logits_ref[...] = logits
    stats_ref[...] = student_stats(logits)


def near_logits(rows, weight, *held):
    per, depth = rows.shape
    cols = weight.shape[1]
    return pl.pallas_call(
        near_kernel,
        out_shape=(shape((per, cols), F32), shape((STAT_ROWS, per), F32)),
        in_specs=[VMEM] * (2 + len(held)),
        out_specs=(VMEM, VMEM),
        compiler_params=params(6),
        cost_estimate=cost(2 * per * depth * cols, (per + cols) * depth * 2, per * cols),
        name="near_logits",
    )(rows, weight, *held)


NOTHING = -3.0e38


def both(a, b):
    peak = jnp.maximum(a[0:1], b[0:1])
    ea, eb = jnp.exp((a[0:1] - peak) * 0.5), jnp.exp((b[0:1] - peak) * 0.5)
    return jnp.concatenate(
        [peak, a[1:2] * (ea * ea) + b[1:2] * (eb * eb), a[2:3] * ea + b[2:3] * eb]
    )


def far_kernel(n, spots_ref, *refs):
    pieces, refs = refs[:n], refs[n:]
    own_ref, other_ref, stats_a, stats_b, taught_ref, taught_core_ref, ids_ref = refs[:7]
    a_ref, b_ref, rows_ref, out_ref = refs[7:]
    for k, piece in enumerate(pieces):
        rows_ref[pl.ds(pl.multiple_of(spots_ref[k], 16), piece.shape[0]), :] = piece[...]
    per = rows_ref.shape[0]
    a = jnp.dot(rows_ref[...], own_ref[...], preferred_element_type=F32)
    b = jnp.dot(rows_ref[...], other_ref[...], preferred_element_type=F32)
    a_ref[...] = a
    b_ref[...] = b
    out_ref[0, 0:3, :] = both(stats_a[...], stats_b[...])
    out_ref[0, 3:4, :] = ids_ref[...].astype(F32)
    out_ref[0, 4:6, :] = taught_ref[0:2, :]
    out_ref[0, 6:8, :] = taught_core_ref[0:2, :]
    out_ref[1, 0:3, :] = both(student_stats(a), student_stats(b))
    row = lax.broadcasted_iota(jnp.int32, (5, per), 0)
    out_ref[1, 3:8, :] = jnp.where((row == 1) | (row == 3), NOTHING, 0.0)


def far_logits(spots, pieces, own, other, *small):
    depth, cols = own.shape
    per = sum(piece.shape[0] for piece in pieces)
    return pl.pallas_call(
        lambda *refs: far_kernel(len(pieces), *refs),
        out_shape=(
            shape((per, cols), F32),
            shape((per, cols), F32),
            shape((per, depth), BF16),
            shape((2, STAT_ROWS, per), F32),
        ),
        in_specs=[SMEM] + [VMEM] * (len(pieces) + 2 + len(small)),
        out_specs=(VMEM, VMEM, VMEM, VMEM),
        compiler_params=params(12),
        cost_estimate=cost(4 * per * depth * cols, (per + 2 * cols) * depth * 2, 2 * per * cols),
        name="far_logits",
    )(spots, *pieces, own, other, *small)


def merged(parts):
    top = parts[0]
    for part in parts[1:]:
        top = jnp.maximum(top, part)
    hard = soft = taught0 = taught1 = 0.0
    for part in parts:
        shrink = jnp.exp((part - top) * 0.5)
        s = shrink[0:1]
        hard += part[1:2] * (s * s)
        soft += part[2:3] * s
        taught0 += part[5:6] * shrink[4:5]
        taught1 += part[7:8] * shrink[6:7]
    return top[0:1], hard, soft, top[3:4], top[4:5], taught0, top[6:7], taught1


def merge_kernel(n, *refs):
    out_ref = refs[-1]
    for j in range(2):
        out_ref[j] = jnp.concatenate(merged([ref[j] for ref in refs[:n]]))


def merge(parts, held):
    return pl.pallas_call(
        lambda *refs: merge_kernel(len(parts), *refs),
        out_shape=shape(parts[0].shape, F32),
        in_specs=[VMEM] * (len(parts) + len(held)),
        out_specs=VMEM,
        compiler_params=params(6),
        cost_estimate=cost(0, 5 * parts[0].size * 4),
        name="merge_stats",
    )(*parts, *held)


def picker(bit, flip, total):
    half = total // 2
    row = lax.broadcasted_iota(jnp.int32, (total, total), 0)
    side = jnp.where(row < half, 1 << bit, 0)
    row = row & (half - 1)
    row = ((row >> bit) << (bit + 1)) + side + (row & ((1 << bit) - 1))
    return (lax.broadcasted_iota(jnp.int32, (total, total), 1) == (row ^ flip)).astype(BF16)


def grads_kernel(n, at_ref, *refs):
    stats_refs, refs = refs[:n], refs[n:]
    logits_refs, (serving_ref, aligned_ref), g_refs = refs[:4], refs[4:6], refs[6:]
    me = at_ref[3]
    per, cols = logits_refs[0].shape
    stats = [merged([ref[j ^ (i & 1)] for i, ref in enumerate(stats_refs)]) for j in range(2)]
    lane = lax.broadcasted_iota(jnp.int32, (per, per), 1)
    for j in range(2):
        rows = stats[j][:4] + (serving_ref[me ^ (2 * j)].astype(F32),)
        columns = jnp.concatenate(rows + (jnp.zeros((128 - len(rows), per), F32),)).T
        peak, hard, soft, ids, wanted = [columns[:, i : i + 1] for i in range(len(rows))]
        ids, wanted = ids.astype(jnp.int32), wanted.astype(jnp.int32)
        tpeak = total = 0.0
        for k in range(4):
            here = wanted - (me ^ k) * per == lane
            taught = stats[k // 2][4 + 2 * (k % 2) : 6 + 2 * (k % 2)]
            tpeak += jnp.where(here, taught[0], 0.0)
            total += jnp.where(here, taught[1], 0.0)
        tpeak = jnp.sum(tpeak, axis=1, keepdims=True)
        total = jnp.sum(total, axis=1, keepdims=True)
        hard, soft, total = 16.0 / hard, 32.0 / soft, 32.0 / total
        for c, g_ref in enumerate(g_refs):
            part = slice(c * cols, (c + 1) * cols)
            column = at_ref[1 + c] + lax.broadcasted_iota(jnp.int32, (per, cols), 1)
            half = jnp.exp((logits_refs[2 * j + c][...] - peak) * 0.5)
            taught = jnp.exp((aligned_ref[j, :, part].astype(F32) - tpeak) * 0.5)
            label = jnp.where(column == ids, 16.0, 0.0)
            grad = (half * soft - taught * total) + (half * half * hard - label)
            g_ref[j * per : (j + 1) * per, :] = grad.astype(BF16)


def back_kernel(bits, edges, n, at_ref, *refs):
    w_refs, g_refs, send_refs, keep_refs = refs[:2], refs[-8:-6], refs[-6:-3], refs[-3:]
    grads_kernel(n, at_ref, *refs[2:-6])
    for p in range(3):
        per = send_refs[p].shape[0]
        pick = picker(bits[p], at_ref[0], 2 * per)
        back = 0.0
        for g_ref, w_ref in zip(g_refs, w_refs):
            rows = jnp.dot(pick, g_ref[...], preferred_element_type=F32).astype(BF16)
            back += lax.dot_general(
                w_ref[edges[p] : edges[p + 1], :],
                rows,
                (((1,), (1,)), ((), ())),
                preferred_element_type=F32,
            )
        back = back.T
        send_refs[p][...] = back[:per].astype(BF16)
        keep_refs[p][...] = back[per:]


def back_rows(at, own, other, stats, logits, serving, aligned, bits, edges):
    depth, cols = own.shape
    per = logits[0].shape[0]
    parts = [(per, edges[p + 1] - edges[p]) for p in range(3)]
    got = pl.pallas_call(
        lambda *refs: back_kernel(bits, edges, len(stats), *refs),
        out_shape=[shape((2 * per, cols), BF16)] * 2
        + [shape(part, BF16) for part in parts]
        + [shape(part, F32) for part in parts],
        in_specs=[SMEM] + [VMEM] * (len(stats) + 8),
        out_specs=[VMEM] * 8,
        compiler_params=params(20),
        cost_estimate=cost(8 * per * depth * cols, 2 * cols * depth * 2, 4 * per * cols),
        name="back_rows",
    )(at, own, other, *stats, *logits, serving, aligned)
    return got[0], got[1], got[2:5], got[5:8]


def head_kernel(r0, r1, r2, r3, mine_ref, theirs_ref, out_ref):
    rows = jnp.concatenate([r0[...], r1[...], r2[...], r3[...]])
    grads = jnp.concatenate([mine_ref[...], theirs_ref[...]])
    out_ref[...] = lax.dot_general(
        rows, grads, (((0,), (0,)), ((), ())), preferred_element_type=F32
    ).astype(BF16)


def head_gradient(rows, mine, theirs):
    per, depth = rows[0].shape
    cols = mine.shape[1]
    tile = 512 if depth % 512 == 0 else depth
    whole = pl.BlockSpec((2 * per, cols), lambda i: (0, 0))
    slab = pl.BlockSpec((per, tile), lambda i: (0, i))
    return pl.pallas_call(
        head_kernel,
        grid=(depth // tile,),
        out_shape=shape((depth, cols), BF16),
        in_specs=[slab] * 4 + [whole] * 2,
        out_specs=pl.BlockSpec((tile, cols), lambda i: (i, 0)),
        compiler_params=params(6),
        cost_estimate=cost(8 * per * depth * cols, (4 * per + cols) * depth * 2),
        name="head_gradient",
    )(*rows, mine, theirs)


def body(hidden, token_ids, serving, head_weight, teacher_logits):
    groups = lax.axis_size("grp")
    shards = lax.axis_size("vocab")
    me_g = lax.axis_index("grp")
    me_v = lax.axis_index("vocab")
    per, depth = hidden.shape
    cols = head_weight.shape[1]
    owned = per // shards
    CORE, X = shards, 2 * shards
    Y, W = 1, 2
    count = groups * shards

    def swap(value, mask):
        return lax.ppermute(value, AXES, [(i, i ^ mask) for i in range(count)])

    def tie(*values):
        return lax.optimization_barrier(values)

    def ints(*values):
        return jnp.stack([jnp.asarray(v, jnp.int32) for v in values])

    quarter_rows = per // 4
    quarter = me_v & 3
    starts = [(quarter ^ k) * quarter_rows for k in range(4)]
    chip = me_g >> 1
    spots = ints(*starts)
    at = ints(
        me_v * owned, (me_g * shards + me_v) * cols, ((me_g ^ 1) * shards + me_v) * cols, me_g
    )
    who = ints(me_g, me_g & 1)
    unsigned = [
        jnp.asarray(v, jnp.uint32)
        for v in (starts[0], starts[3], 2 * chip, 2 * (chip ^ 1))
    ]
    rows, weight, spots, at, who, *unsigned = tie(hidden, head_weight, spots, at, who, *unsigned)
    zero = jnp.uint32(0)

    def cut(value, start, size, dim):
        indices = [start if d == dim else zero for d in range(value.ndim)]
        sizes = [size if d == dim else n for d, n in enumerate(value.shape)]
        return lax.dynamic_slice(value, indices, sizes)

    first = cut(rows, unsigned[0], quarter_rows, 0)
    x0 = swap(first, X)
    _, rows, weight, teacher = tie(first, rows, weight, teacher_logits)
    other_weight = swap(weight, CORE)
    core_hidden = swap(rows, CORE)
    x3 = swap(cut(rows, unsigned[1], quarter_rows, 0), X)
    kept = cut(teacher, unsigned[2], 2, 1).swapaxes(0, 1)
    gone = cut(teacher, unsigned[3], 2, 1).swapaxes(0, 1)
    taught = taught_stats(kept, gone)
    taught_core = swap(taught, CORE)
    near_a, stats_a = near_logits(rows, weight)
    x0, kept, gone, taught, taught_core, near_a, rows = tie(
        x0, kept, gone, taught, taught_core, near_a, rows
    )
    x1 = swap(x0, Y)
    x2 = swap(x0, W)
    kept_core = swap(kept, CORE)
    near_b, stats_b = near_logits(rows, other_weight, x0)
    *pieces, gone, near_b = tie(x0, x1, x2, x3, gone, near_b)
    taught_x = swap(gone, X)
    spots, core_hidden, kept_core = tie(spots, core_hidden, kept_core)
    far_a, far_b, x_rows, stats = far_logits(
        spots,
        pieces,
        weight,
        other_weight,
        stats_a,
        stats_b,
        taught,
        taught_core,
        token_ids.reshape(1, per),
    )

    served = serving.reshape(groups, 1, per)
    logits = [near_a, near_b, far_a, far_b]
    held = logits + [weight]
    mask = W
    while mask < shards:
        masks = [mask, 2 * mask, 3 * mask] if 2 * mask < shards else [mask]
        stats = merge([stats] + [swap(stats, m) for m in masks], held)
        mask *= 4
    _, taught_x = tie(stats, taught_x)
    taught_far = swap(taught_x, CORE)
    aligned = teacher_rows(who, served, [kept, kept_core, taught_x, taught_far])
    parts = [stats] + [swap(stats, mask) for mask in (X, Y, X + Y)]

    bits = shards.bit_length() - 1
    masks = {0: X}
    for b in range(bits):
        masks[1 + b] = shards >> (1 + b)
    ydim, wdim = bits, bits - 1
    third = depth // 128 // 3 * 128
    edges = (0, third, 2 * third, depth)
    orders = [(0, ydim, wdim), (ydim, wdim, 0), (wdim, 0, ydim)]
    low = owned.bit_length() - 1
    row_bit = {0: low + bits, ydim: low, wdim: low + 1}
    first_bits = tuple(row_bit[order[0]] for order in orders)
    gown, gother, sents, keeps = back_rows(
        at, weight, other_weight, parts, logits, served, aligned, first_bits, edges
    )
    gots = [swap(sents[p], masks[orders[p][0]]) for p in range(3)]
    theirs = swap(gother, CORE)
    _, x_sent = tie(gother, x_rows)
    grad_head = head_gradient([hidden, x_rows, core_hidden, swap(x_sent, CORE)], gown, theirs)
    for p in range(3):
        grad_head, gots[p] = tie(grad_head, gots[p])

    def folded(value, p):
        dims = [2] * (1 + bits)
        dims[orders[p][0]] = 1
        return value.reshape(*dims, owned, value.shape[-1])

    terms = [[folded(keeps[p], p), folded(gots[p], p)] for p in range(3)]
    for stage in (1, 2):
        sents = [
            sum(lax.index_in_dim(t, 1, orders[p][stage]).astype(F32) for t in terms[p]).astype(BF16)
            for p in range(3)
        ]
        gots = [swap(sents[p], masks[orders[p][stage]]) for p in range(3)]
        for p in range(3):
            terms[p] = [lax.index_in_dim(t, 0, orders[p][stage]) for t in terms[p]] + [gots[p]]
    for dim in range(1, wdim):
        for p in range(3):
            sent = sum(lax.index_in_dim(t, 1, dim).astype(F32) for t in terms[p]).astype(BF16)
            terms[p] = [lax.index_in_dim(t, 0, dim) for t in terms[p]] + [swap(sent, masks[dim])]
    total = jnp.concatenate([sum(t.astype(F32) for t in ts) for ts in terms], axis=-1)
    return (total.reshape(owned, depth), grad_head)


def solution(mesh):
    placed = (P("grp", None), P("grp"), P(), P(None, ("grp", "vocab")), P("grp", None, "vocab"))
    return jax.shard_map(
        body,
        mesh=mesh,
        in_specs=placed,
        out_specs=(P(("grp", "vocab"), None), P(None, ("grp", "vocab"))),
        check_vma=False,
    )
```

```python
import jax
import jax.numpy as jnp
from jax import lax
from jax.experimental import pallas as pl
from jax.experimental.pallas import tpu as pltpu
from jax.sharding import PartitionSpec as P

BF16 = jnp.bfloat16
F32 = jnp.float32
AXES = ("grp", "vocab")
VMEM = pl.BlockSpec(memory_space=pltpu.VMEM)
SMEM = pl.BlockSpec(memory_space=pltpu.SMEM)
STAT_ROWS = 8
MIB = 2**20


def params(mib):
    return pltpu.CompilerParams(vmem_limit_bytes=mib * MIB)


def cost(flops, nbytes, exps=0):
    return pl.CostEstimate(flops=flops, bytes_accessed=nbytes, transcendentals=exps)


def shape(dims, dtype):
    return jax.ShapeDtypeStruct(dims, dtype)


def columns_to_rows(columns):
    count = columns[0].shape[0]
    lane = lax.broadcasted_iota(jnp.int32, (count, 128), 1)
    wide = jnp.zeros((count, 128), F32)
    for k, column in enumerate(columns):
        wide = jnp.where(lane == k, column, wide)
    return wide.T[:STAT_ROWS]


def taught_kernel(kept_ref, gone_ref, out_ref):
    parts = [ref[c].astype(F32) for ref in (kept_ref, gone_ref) for c in range(2)]
    top = parts[0]
    for part in parts[1:]:
        top = jnp.maximum(top, part)
    peak = jnp.max(top, axis=1, keepdims=True)
    total = sum(jnp.exp((part - peak) * 0.5) for part in parts)
    out_ref[...] = columns_to_rows([peak, jnp.sum(total, axis=1, keepdims=True)])


def taught_stats(kept, gone):
    _, per, cols = kept.shape
    return pl.pallas_call(
        taught_kernel,
        out_shape=shape((STAT_ROWS, per), F32),
        in_specs=[VMEM] * 2,
        out_specs=VMEM,
        compiler_params=params(4),
        cost_estimate=cost(0, 4 * per * cols * 2, 4 * per * cols),
        name="taught_stats",
    )(kept, gone)


def teacher_kernel(at_ref, serving_ref, a0, a1, a2, a3, aligned_ref):
    me, core = at_ref[0], at_ref[1]
    _, per, cols = a0.shape
    for j in range(2):
        wanted = serving_ref[me ^ (2 * j)]
        sums = [0.0, 0.0]
        for k, arrived in enumerate((a0, a1, a2, a3)):
            row = lax.broadcasted_iota(jnp.int32, (per, per), 0) + (me ^ k) * per
            pick = (row == wanted).astype(BF16)
            for c in range(2):
                sums[c] += lax.dot_general(
                    pick, arrived[core ^ c], (((0,), (0,)), ((), ())), preferred_element_type=F32
                )
        for c in range(2):
            aligned_ref[j, :, c * cols : (c + 1) * cols] = sums[c].astype(BF16)


def teacher_rows(at, serving, arrived):
    _, per, cols = arrived[0].shape
    return pl.pallas_call(
        teacher_kernel,
        out_shape=shape((2, per, 2 * cols), BF16),
        in_specs=[SMEM] + [VMEM] * 5,
        out_specs=VMEM,
        compiler_params=params(5),
        cost_estimate=cost(32 * per * per * cols, 12 * per * cols * 2),
        name="teacher_rows",
    )(at, serving, *arrived)


def student_stats(logits):
    peak = jnp.max(logits, axis=1, keepdims=True)
    soft = jnp.exp((logits - peak) * 0.5)
    hard = jnp.sum(soft * soft, axis=1, keepdims=True)
    return columns_to_rows([peak, hard, jnp.sum(soft, axis=1, keepdims=True)])


def near_kernel(rows_ref, w_ref, *refs):
    logits_ref, stats_ref = refs[-2:]
    logits = jnp.dot(rows_ref[...], w_ref[...], preferred_element_type=F32)
    logits_ref[...] = logits
    stats_ref[...] = student_stats(logits)


def near_logits(rows, weight, *held):
    per, depth = rows.shape
    cols = weight.shape[1]
    return pl.pallas_call(
        near_kernel,
        out_shape=(shape((per, cols), F32), shape((STAT_ROWS, per), F32)),
        in_specs=[VMEM] * (2 + len(held)),
        out_specs=(VMEM, VMEM),
        compiler_params=params(6),
        cost_estimate=cost(2 * per * depth * cols, (per + cols) * depth * 2, per * cols),
        name="near_logits",
    )(rows, weight, *held)


NOTHING = -3.0e38


def both(a, b):
    peak = jnp.maximum(a[0:1], b[0:1])
    ea, eb = jnp.exp((a[0:1] - peak) * 0.5), jnp.exp((b[0:1] - peak) * 0.5)
    return jnp.concatenate(
        [peak, a[1:2] * (ea * ea) + b[1:2] * (eb * eb), a[2:3] * ea + b[2:3] * eb]
    )


def far_kernel(n, spots_ref, *refs):
    pieces, refs = refs[:n], refs[n:]
    own_ref, other_ref, stats_a, stats_b, taught_ref, taught_core_ref, ids_ref = refs[:7]
    a_ref, b_ref, rows_ref, out_ref = refs[7:]
    for k, piece in enumerate(pieces):
        rows_ref[pl.ds(pl.multiple_of(spots_ref[k], 16), piece.shape[0]), :] = piece[...]
    per = rows_ref.shape[0]
    a = jnp.dot(rows_ref[...], own_ref[...], preferred_element_type=F32)
    b = jnp.dot(rows_ref[...], other_ref[...], preferred_element_type=F32)
    a_ref[...] = a
    b_ref[...] = b
    out_ref[0, 0:3, :] = both(stats_a[...], stats_b[...])
    out_ref[0, 3:4, :] = ids_ref[...].astype(F32)
    out_ref[0, 4:6, :] = taught_ref[0:2, :]
    out_ref[0, 6:8, :] = taught_core_ref[0:2, :]
    out_ref[1, 0:3, :] = both(student_stats(a), student_stats(b))
    row = lax.broadcasted_iota(jnp.int32, (5, per), 0)
    out_ref[1, 3:8, :] = jnp.where((row == 1) | (row == 3), NOTHING, 0.0)


def far_logits(spots, pieces, own, other, *small):
    depth, cols = own.shape
    per = sum(piece.shape[0] for piece in pieces)
    return pl.pallas_call(
        lambda *refs: far_kernel(len(pieces), *refs),
        out_shape=(
            shape((per, cols), F32),
            shape((per, cols), F32),
            shape((per, depth), BF16),
            shape((2, STAT_ROWS, per), F32),
        ),
        in_specs=[SMEM] + [VMEM] * (len(pieces) + 2 + len(small)),
        out_specs=(VMEM, VMEM, VMEM, VMEM),
        compiler_params=params(12),
        cost_estimate=cost(4 * per * depth * cols, (per + 2 * cols) * depth * 2, 2 * per * cols),
        name="far_logits",
    )(spots, *pieces, own, other, *small)


def merged(parts):
    top = parts[0]
    for part in parts[1:]:
        top = jnp.maximum(top, part)
    hard = soft = taught0 = taught1 = 0.0
    for part in parts:
        shrink = jnp.exp((part - top) * 0.5)
        s = shrink[0:1]
        hard += part[1:2] * (s * s)
        soft += part[2:3] * s
        taught0 += part[5:6] * shrink[4:5]
        taught1 += part[7:8] * shrink[6:7]
    return top[0:1], hard, soft, top[3:4], top[4:5], taught0, top[6:7], taught1


def merge_kernel(n, *refs):
    out_ref = refs[-1]
    for j in range(2):
        out_ref[j] = jnp.concatenate(merged([ref[j] for ref in refs[:n]]))


def merge(parts, held):
    return pl.pallas_call(
        lambda *refs: merge_kernel(len(parts), *refs),
        out_shape=shape(parts[0].shape, F32),
        in_specs=[VMEM] * (len(parts) + len(held)),
        out_specs=VMEM,
        compiler_params=params(6),
        cost_estimate=cost(0, 5 * parts[0].size * 4),
        name="merge_stats",
    )(*parts, *held)


def picker(bit, flip, total):
    half = total // 2
    row = lax.broadcasted_iota(jnp.int32, (total, total), 0)
    side = jnp.where(row < half, 1 << bit, 0)
    row = row & (half - 1)
    row = ((row >> bit) << (bit + 1)) + side + (row & ((1 << bit) - 1))
    return (lax.broadcasted_iota(jnp.int32, (total, total), 1) == (row ^ flip)).astype(BF16)


def grads_kernel(n, at_ref, *refs):
    stats_refs, refs = refs[:n], refs[n:]
    logits_refs, (serving_ref, aligned_ref), g_refs = refs[:4], refs[4:6], refs[6:]
    me = at_ref[3]
    per, cols = logits_refs[0].shape
    stats = [merged([ref[j ^ (i & 1)] for i, ref in enumerate(stats_refs)]) for j in range(2)]
    lane = lax.broadcasted_iota(jnp.int32, (per, per), 1)
    for j in range(2):
        rows = stats[j][:4] + (serving_ref[me ^ (2 * j)].astype(F32),)
        columns = jnp.concatenate(rows + (jnp.zeros((128 - len(rows), per), F32),)).T
        peak, hard, soft, ids, wanted = [columns[:, i : i + 1] for i in range(len(rows))]
        ids, wanted = ids.astype(jnp.int32), wanted.astype(jnp.int32)
        tpeak = total = 0.0
        for k in range(4):
            here = wanted - (me ^ k) * per == lane
            taught = stats[k // 2][4 + 2 * (k % 2) : 6 + 2 * (k % 2)]
            tpeak += jnp.where(here, taught[0], 0.0)
            total += jnp.where(here, taught[1], 0.0)
        tpeak = jnp.sum(tpeak, axis=1, keepdims=True)
        total = jnp.sum(total, axis=1, keepdims=True)
        hard, soft, total = 16.0 / hard, 32.0 / soft, 32.0 / total
        for c, g_ref in enumerate(g_refs):
            part = slice(c * cols, (c + 1) * cols)
            column = at_ref[1 + c] + lax.broadcasted_iota(jnp.int32, (per, cols), 1)
            half = jnp.exp((logits_refs[2 * j + c][...] - peak) * 0.5)
            taught = jnp.exp((aligned_ref[j, :, part].astype(F32) - tpeak) * 0.5)
            label = jnp.where(column == ids, 16.0, 0.0)
            grad = (half * soft - taught * total) + (half * half * hard - label)
            g_ref[j * per : (j + 1) * per, :] = grad.astype(BF16)


def back_kernel(bits, edges, n, at_ref, *refs):
    w_refs, g_refs, send_refs, keep_refs, both_ref = refs[:2], refs[-7:-5], refs[-5:-3], refs[-3:-1], refs[-1]
    grads_kernel(n, at_ref, *refs[2:-5])
    for p in range(3):
        per = g_refs[0].shape[0] // 2
        pick = picker(bits[p], at_ref[0], 2 * per)
        back = 0.0
        for g_ref, w_ref in zip(g_refs, w_refs):
            rows = jnp.dot(pick, g_ref[...], preferred_element_type=F32).astype(BF16)
            back += lax.dot_general(
                w_ref[edges[p] : edges[p + 1], :],
                rows,
                (((1,), (1,)), ((), ())),
                preferred_element_type=F32,
            )
        back = back.T
        if p < 2:
            send_refs[p][...] = back[:per].astype(BF16)
            keep_refs[p][...] = back[per:]
        else:
            both_ref[...] = back.astype(BF16)


def back_rows(at, own, other, stats, logits, serving, aligned, bits, edges):
    depth, cols = own.shape
    per = logits[0].shape[0]
    parts = [(per, edges[p + 1] - edges[p]) for p in range(2)]
    got = pl.pallas_call(
        lambda *refs: back_kernel(bits, edges, len(stats), *refs),
        out_shape=[shape((2 * per, cols), BF16)] * 2
        + [shape(part, BF16) for part in parts]
        + [shape(part, F32) for part in parts]
        + [shape((2 * per, edges[3] - edges[2]), BF16)],
        in_specs=[SMEM] + [VMEM] * (len(stats) + 8),
        out_specs=[VMEM] * 7,
        compiler_params=params(20),
        cost_estimate=cost(8 * per * depth * cols, 2 * cols * depth * 2, 4 * per * cols),
        name="back_rows",
    )(at, own, other, *stats, *logits, serving, aligned)
    return got[0], got[1], list(got[2:4]), list(got[4:6]), got[6]


def head_kernel(r0, r1, r2, r3, mine_ref, theirs_ref, out_ref):
    rows = jnp.concatenate([r0[...], r1[...], r2[...], r3[...]])
    grads = jnp.concatenate([mine_ref[...], theirs_ref[...]])
    out_ref[...] = lax.dot_general(
        rows, grads, (((0,), (0,)), ((), ())), preferred_element_type=F32
    ).astype(BF16)


def head_gradient(rows, mine, theirs):
    per, depth = rows[0].shape
    cols = mine.shape[1]
    tile = 512 if depth % 512 == 0 else depth
    whole = pl.BlockSpec((2 * per, cols), lambda i: (0, 0))
    slab = pl.BlockSpec((per, tile), lambda i: (0, i))
    return pl.pallas_call(
        head_kernel,
        grid=(depth // tile,),
        out_shape=shape((depth, cols), BF16),
        in_specs=[slab] * 4 + [whole] * 2,
        out_specs=pl.BlockSpec((tile, cols), lambda i: (i, 0)),
        compiler_params=params(6),
        cost_estimate=cost(8 * per * depth * cols, (4 * per + cols) * depth * 2),
        name="head_gradient",
    )(*rows, mine, theirs)


def body(hidden, token_ids, serving, head_weight, teacher_logits):
    groups = lax.axis_size("grp")
    shards = lax.axis_size("vocab")
    me_g = lax.axis_index("grp")
    me_v = lax.axis_index("vocab")
    per, depth = hidden.shape
    cols = head_weight.shape[1]
    owned = per // shards
    CORE, X = shards, 2 * shards
    Y, W = 1, 2
    count = groups * shards

    def swap(value, mask):
        return lax.ppermute(value, AXES, [(i, i ^ mask) for i in range(count)])

    def tie(*values):
        return lax.optimization_barrier(values)

    def ints(*values):
        return jnp.stack([jnp.asarray(v, jnp.int32) for v in values])

    quarter_rows = per // 4
    quarter = me_v & 3
    starts = [(quarter ^ k) * quarter_rows for k in range(4)]
    chip = me_g >> 1
    spots = ints(*starts)
    at = ints(
        me_v * owned, (me_g * shards + me_v) * cols, ((me_g ^ 1) * shards + me_v) * cols, me_g
    )
    who = ints(me_g, me_g & 1)
    unsigned = [
        jnp.asarray(v, jnp.uint32)
        for v in (starts[0], starts[3], 2 * chip, 2 * (chip ^ 1))
    ]
    odd = jnp.broadcast_to((me_g & 1).astype(F32), (owned, depth - depth // 384 * 256))
    rows, weight, spots, at, who, odd, *unsigned = tie(
        hidden, head_weight, spots, at, who, odd, *unsigned
    )
    zero = jnp.uint32(0)

    def cut(value, start, size, dim):
        indices = [start if d == dim else zero for d in range(value.ndim)]
        sizes = [size if d == dim else n for d, n in enumerate(value.shape)]
        return lax.dynamic_slice(value, indices, sizes)

    first = cut(rows, unsigned[0], quarter_rows, 0)
    x0 = swap(first, X)
    _, rows, weight, teacher = tie(first, rows, weight, teacher_logits)
    other_weight = swap(weight, CORE)
    core_hidden = swap(rows, CORE)
    x3 = swap(cut(rows, unsigned[1], quarter_rows, 0), X)
    kept = cut(teacher, unsigned[2], 2, 1).swapaxes(0, 1)
    gone = cut(teacher, unsigned[3], 2, 1).swapaxes(0, 1)
    taught = taught_stats(kept, gone)
    taught_core = swap(taught, CORE)
    near_a, stats_a = near_logits(rows, weight)
    x0, kept, gone, taught, taught_core, near_a, rows = tie(
        x0, kept, gone, taught, taught_core, near_a, rows
    )
    x1 = swap(x0, Y)
    x2 = swap(x0, W)
    kept_core = swap(kept, CORE)
    near_b, stats_b = near_logits(rows, other_weight, x0)
    *pieces, gone, near_b = tie(x0, x1, x2, x3, gone, near_b)
    taught_x = swap(gone, X)
    spots, core_hidden, kept_core = tie(spots, core_hidden, kept_core)
    far_a, far_b, x_rows, stats = far_logits(
        spots,
        pieces,
        weight,
        other_weight,
        stats_a,
        stats_b,
        taught,
        taught_core,
        token_ids.reshape(1, per),
    )

    served = serving.reshape(groups, 1, per)
    logits = [near_a, near_b, far_a, far_b]
    held = logits + [weight]
    mask = W
    while mask < shards:
        masks = [mask, 2 * mask, 3 * mask] if 2 * mask < shards else [mask]
        stats = merge([stats] + [swap(stats, m) for m in masks], held)
        mask *= 4
    _, taught_x = tie(stats, taught_x)
    taught_far = swap(taught_x, CORE)
    aligned = teacher_rows(who, served, [kept, kept_core, taught_x, taught_far])
    parts = [stats] + [swap(stats, mask) for mask in (X, Y, X + Y)]

    bits = shards.bit_length() - 1
    masks = {1: X}
    for b in range(bits):
        masks[2 + b] = shards >> (1 + b)
    xdim, ydim, wdim = 1, 1 + bits, bits
    units = depth // 128
    edges = (0, units // 3 * 128, units // 3 * 256, depth)
    orders = [(xdim, ydim, wdim), (ydim, wdim, xdim), (wdim, xdim, ydim)]
    orders = [order + tuple(range(2, wdim)) for order in orders]
    low = owned.bit_length() - 1
    row_bit = {xdim: low + bits, ydim: low, wdim: low + 1}
    first_bits = tuple(row_bit[order[0]] for order in orders)
    gown, gother, sents, keeps, third = back_rows(
        at, weight, other_weight, parts, logits, served, aligned, first_bits, edges
    )

    def step(value, p, dim):
        movers = [i for i in range(count) if p < 2 or (i // shards) & 1]
        return lax.ppermute(value, AXES, [(i, i ^ masks[dim]) for i in movers])

    def folded(value, p):
        dims = [2] * (1 + bits)
        dims[orders[p][0] - 1] = 1
        return value.reshape(-1, *dims, owned, value.shape[-1])

    gots = [step(sents[p], p, orders[p][0]) for p in range(2)]
    third_core = swap(third, CORE)
    sents = sents + [jnp.stack([third[:per], third_core[:per]])]
    keeps = keeps + [jnp.stack([third[per:], third_core[per:]])]
    gots.append(step(sents[2], 2, orders[2][0]))
    theirs = swap(gother, CORE)
    _, x_sent = tie(gother, x_rows)
    grad_head = head_gradient([hidden, x_rows, core_hidden, swap(x_sent, CORE)], gown, theirs)
    for p in range(3):
        grad_head, gots[p] = tie(grad_head, gots[p])
    terms = [[folded(keeps[p], p), folded(gots[p], p)] for p in range(3)]
    for stage in range(1, 1 + bits):
        for p in (2, 0, 1):
            dim = orders[p][stage]
            sent = sum(lax.index_in_dim(t, 1, dim).astype(F32) for t in terms[p]).astype(BF16)
            terms[p] = [lax.index_in_dim(t, 0, dim) for t in terms[p]] + [step(sent, p, dim)]
    totals = [sum(t.astype(F32) for t in terms[p]) for p in range(3)]
    totals = [total.reshape(-1, owned, total.shape[-1]) for total in totals]
    back = swap(totals[2][1], CORE)
    total = jnp.concatenate(
        [totals[0][0], totals[1][0], jnp.where(odd > 0.5, totals[2][0], back)], axis=-1
    )
    return (total, grad_head)


def solution(mesh):
    placed = (P("grp", None), P("grp"), P(), P(None, ("grp", "vocab")), P("grp", None, "vocab"))
    return jax.shard_map(
        body,
        mesh=mesh,
        in_specs=placed,
        out_specs=(P(("grp", "vocab"), None), P(None, ("grp", "vocab"))),
        check_vma=False,
    )
```

```python
import jax
import jax.numpy as jnp
from jax import lax
from jax.experimental import pallas as pl
from jax.experimental.pallas import tpu as pltpu
from jax.sharding import PartitionSpec as P

BF16 = jnp.bfloat16
F32 = jnp.float32
AXES = ("grp", "vocab")
VMEM = pl.BlockSpec(memory_space=pltpu.VMEM)
SMEM = pl.BlockSpec(memory_space=pltpu.SMEM)
STAT_ROWS = 8
MIB = 2**20


def params(mib):
    return pltpu.CompilerParams(vmem_limit_bytes=mib * MIB)


def cost(flops, nbytes, exps=0):
    return pl.CostEstimate(flops=flops, bytes_accessed=nbytes, transcendentals=exps)


def shape(dims, dtype):
    return jax.ShapeDtypeStruct(dims, dtype)


def columns_to_rows(columns):
    count = columns[0].shape[0]
    lane = lax.broadcasted_iota(jnp.int32, (count, 128), 1)
    wide = jnp.zeros((count, 128), F32)
    for k, column in enumerate(columns):
        wide = jnp.where(lane == k, column, wide)
    return wide.T[:STAT_ROWS]


def taught_kernel(kept_ref, gone_ref, out_ref):
    parts = [ref[c].astype(F32) for ref in (kept_ref, gone_ref) for c in range(2)]
    top = parts[0]
    for part in parts[1:]:
        top = jnp.maximum(top, part)
    peak = jnp.max(top, axis=1, keepdims=True)
    total = sum(jnp.exp((part - peak) * 0.5) for part in parts)
    out_ref[...] = columns_to_rows([peak, jnp.sum(total, axis=1, keepdims=True)])


def taught_stats(kept, gone):
    _, per, cols = kept.shape
    return pl.pallas_call(
        taught_kernel,
        out_shape=shape((STAT_ROWS, per), F32),
        in_specs=[VMEM] * 2,
        out_specs=VMEM,
        compiler_params=params(4),
        cost_estimate=cost(0, 4 * per * cols * 2, 4 * per * cols),
        name="taught_stats",
    )(kept, gone)


def teacher_kernel(at_ref, serving_ref, a0, a1, a2, a3, aligned_ref):
    me, core = at_ref[0], at_ref[1]
    _, per, cols = a0.shape
    for j in range(2):
        wanted = serving_ref[me ^ (2 * j)]
        sums = [0.0, 0.0]
        for k, arrived in enumerate((a0, a1, a2, a3)):
            row = lax.broadcasted_iota(jnp.int32, (per, per), 0) + (me ^ k) * per
            pick = (row == wanted).astype(BF16)
            for c in range(2):
                sums[c] += lax.dot_general(
                    pick, arrived[core ^ c], (((0,), (0,)), ((), ())), preferred_element_type=F32
                )
        for c in range(2):
            aligned_ref[j, :, c * cols : (c + 1) * cols] = sums[c].astype(BF16)


def teacher_rows(at, serving, arrived):
    _, per, cols = arrived[0].shape
    return pl.pallas_call(
        teacher_kernel,
        out_shape=shape((2, per, 2 * cols), BF16),
        in_specs=[SMEM] + [VMEM] * 5,
        out_specs=VMEM,
        compiler_params=params(5),
        cost_estimate=cost(32 * per * per * cols, 12 * per * cols * 2),
        name="teacher_rows",
    )(at, serving, *arrived)


def student_stats(logits):
    peak = jnp.max(logits, axis=1, keepdims=True)
    soft = jnp.exp((logits - peak) * 0.5)
    hard = jnp.sum(soft * soft, axis=1, keepdims=True)
    return columns_to_rows([peak, hard, jnp.sum(soft, axis=1, keepdims=True)])


def near_kernel(rows_ref, w_ref, *refs):
    logits_ref, stats_ref = refs[-2:]
    logits = jnp.dot(rows_ref[...], w_ref[...], preferred_element_type=F32)
    logits_ref[...] = logits
    stats_ref[...] = student_stats(logits)


def near_logits(rows, weight, *held):
    per, depth = rows.shape
    cols = weight.shape[1]
    return pl.pallas_call(
        near_kernel,
        out_shape=(shape((per, cols), F32), shape((STAT_ROWS, per), F32)),
        in_specs=[VMEM] * (2 + len(held)),
        out_specs=(VMEM, VMEM),
        compiler_params=params(6),
        cost_estimate=cost(2 * per * depth * cols, (per + cols) * depth * 2, per * cols),
        name="near_logits",
    )(rows, weight, *held)


NOTHING = -3.0e38


def both(a, b):
    peak = jnp.maximum(a[0:1], b[0:1])
    ea, eb = jnp.exp((a[0:1] - peak) * 0.5), jnp.exp((b[0:1] - peak) * 0.5)
    return jnp.concatenate(
        [peak, a[1:2] * (ea * ea) + b[1:2] * (eb * eb), a[2:3] * ea + b[2:3] * eb]
    )


def far_kernel(n, spots_ref, *refs):
    pieces, refs = refs[:n], refs[n:]
    own_ref, other_ref, near_ref, stats_a, stats_b, taught_ref, taught_core_ref, ids_ref = refs[:8]
    a_ref, b_ref, rows_ref, out_ref, full = refs[8:]
    share = pieces[0].shape[0]
    for k, piece in enumerate(pieces[:-1]):
        full[pl.ds(pl.multiple_of(spots_ref[k], 8), share), :] = piece[...].astype(F32)
    full[4 * share :, :] = pieces[-1][...].astype(F32)
    rows_ref[0] = near_ref[...]
    rows_ref[1] = full[...].astype(BF16)
    per = rows_ref.shape[1]
    a = jnp.dot(rows_ref[1], own_ref[...], preferred_element_type=F32)
    b = jnp.dot(rows_ref[1], other_ref[...], preferred_element_type=F32)
    a_ref[...] = a
    b_ref[...] = b
    out_ref[0, 0:3, :] = both(stats_a[...], stats_b[...])
    out_ref[0, 3:4, :] = ids_ref[...].astype(F32)
    out_ref[0, 4:6, :] = taught_ref[0:2, :]
    out_ref[0, 6:8, :] = taught_core_ref[0:2, :]
    out_ref[1, 0:3, :] = both(student_stats(a), student_stats(b))
    row = lax.broadcasted_iota(jnp.int32, (5, per), 0)
    out_ref[1, 3:8, :] = jnp.where((row == 1) | (row == 3), NOTHING, 0.0)


def far_logits(spots, pieces, own, other, *small):
    depth, cols = own.shape
    per = sum(piece.shape[0] for piece in pieces)
    return pl.pallas_call(
        lambda *refs: far_kernel(len(pieces), *refs),
        out_shape=(
            shape((per, cols), F32),
            shape((per, cols), F32),
            shape((2, per, depth), BF16),
            shape((2, STAT_ROWS, per), F32),
        ),
        in_specs=[SMEM] + [VMEM] * (len(pieces) + 2 + len(small)),
        out_specs=(VMEM, VMEM, VMEM, VMEM),
        scratch_shapes=[pltpu.VMEM((per, depth), F32)],
        compiler_params=params(16),
        cost_estimate=cost(4 * per * depth * cols, (per + 2 * cols) * depth * 2, 2 * per * cols),
        name="far_logits",
    )(spots, *pieces, own, other, *small)


def merged(parts):
    top = parts[0]
    for part in parts[1:]:
        top = jnp.maximum(top, part)
    hard = soft = taught0 = taught1 = 0.0
    for part in parts:
        shrink = jnp.exp((part - top) * 0.5)
        s = shrink[0:1]
        hard += part[1:2] * (s * s)
        soft += part[2:3] * s
        taught0 += part[5:6] * shrink[4:5]
        taught1 += part[7:8] * shrink[6:7]
    return top[0:1], hard, soft, top[3:4], top[4:5], taught0, top[6:7], taught1


def merge_kernel(n, *refs):
    out_ref = refs[-1]
    for j in range(2):
        out_ref[j] = jnp.concatenate(merged([ref[j] for ref in refs[:n]]))


def merge(parts, held):
    return pl.pallas_call(
        lambda *refs: merge_kernel(len(parts), *refs),
        out_shape=shape(parts[0].shape, F32),
        in_specs=[VMEM] * (len(parts) + len(held)),
        out_specs=VMEM,
        compiler_params=params(6),
        cost_estimate=cost(0, 5 * parts[0].size * 4),
        name="merge_stats",
    )(*parts, *held)


def picker(bit, flip, total):
    half = total // 2
    row = lax.broadcasted_iota(jnp.int32, (total, total), 0)
    side = jnp.where(row < half, 1 << bit, 0)
    row = row & (half - 1)
    row = ((row >> bit) << (bit + 1)) + side + (row & ((1 << bit) - 1))
    return (lax.broadcasted_iota(jnp.int32, (total, total), 1) == (row ^ flip)).astype(BF16)


def grads_kernel(n, at_ref, *refs):
    stats_refs, refs = refs[:n], refs[n:]
    logits_refs, (serving_ref, aligned_ref), g_refs = refs[:4], refs[4:6], refs[6:]
    me = at_ref[3]
    per, cols = logits_refs[0].shape
    stats = [merged([ref[j ^ (i & 1)] for i, ref in enumerate(stats_refs)]) for j in range(2)]
    lane = lax.broadcasted_iota(jnp.int32, (per, per), 1)
    for j in range(2):
        rows = stats[j][:4] + (serving_ref[me ^ (2 * j)].astype(F32),)
        columns = jnp.concatenate(rows + (jnp.zeros((128 - len(rows), per), F32),)).T
        peak, hard, soft, ids, wanted = [columns[:, i : i + 1] for i in range(len(rows))]
        ids, wanted = ids.astype(jnp.int32), wanted.astype(jnp.int32)
        tpeak = total = 0.0
        for k in range(4):
            here = wanted - (me ^ k) * per == lane
            taught = stats[k // 2][4 + 2 * (k % 2) : 6 + 2 * (k % 2)]
            tpeak += jnp.where(here, taught[0], 0.0)
            total += jnp.where(here, taught[1], 0.0)
        tpeak = jnp.sum(tpeak, axis=1, keepdims=True)
        total = jnp.sum(total, axis=1, keepdims=True)
        hard, soft, total = 16.0 / hard, 32.0 / soft, 32.0 / total
        for c, g_ref in enumerate(g_refs):
            part = slice(c * cols, (c + 1) * cols)
            column = at_ref[1 + c] + lax.broadcasted_iota(jnp.int32, (per, cols), 1)
            half = jnp.exp((logits_refs[2 * j + c][...] - peak) * 0.5)
            taught = jnp.exp((aligned_ref[j, :, part].astype(F32) - tpeak) * 0.5)
            label = jnp.where(column == ids, 16.0, 0.0)
            grad = (half * soft - taught * total) + (half * half * hard - label)
            g_ref[j * per : (j + 1) * per, :] = grad.astype(BF16)


def back_kernel(bits, edges, n, at_ref, *refs):
    w_refs, g_refs, send_refs, keep_refs = refs[:2], refs[-8:-6], refs[-6:-3], refs[-3:]
    grads_kernel(n, at_ref, *refs[2:-6])
    for p in range(3):
        per = send_refs[p].shape[0]
        pick = picker(bits[p], at_ref[0], 2 * per)
        back = 0.0
        for g_ref, w_ref in zip(g_refs, w_refs):
            rows = jnp.dot(pick, g_ref[...], preferred_element_type=F32).astype(BF16)
            back += lax.dot_general(
                w_ref[edges[p] : edges[p + 1], :],
                rows,
                (((1,), (1,)), ((), ())),
                preferred_element_type=F32,
            )
        back = back.T
        send_refs[p][...] = back[:per].astype(BF16)
        keep_refs[p][...] = back[per:]


def back_rows(at, own, other, stats, logits, serving, aligned, bits, edges):
    depth, cols = own.shape
    per = logits[0].shape[0]
    parts = [(per, edges[p + 1] - edges[p]) for p in range(3)]
    got = pl.pallas_call(
        lambda *refs: back_kernel(bits, edges, len(stats), *refs),
        out_shape=[shape((2 * per, cols), BF16)] * 2
        + [shape(part, BF16) for part in parts]
        + [shape(part, F32) for part in parts],
        in_specs=[SMEM] + [VMEM] * (len(stats) + 8),
        out_specs=[VMEM] * 8,
        compiler_params=params(20),
        cost_estimate=cost(8 * per * depth * cols, 2 * cols * depth * 2, 4 * per * cols),
        name="back_rows",
    )(at, own, other, *stats, *logits, serving, aligned)
    return got[0], got[1], got[2:5], got[5:8]


def head_kernel(rows_ref, core_ref, mine_ref, theirs_ref, out_ref):
    rows = jnp.concatenate([rows_ref[0], rows_ref[1], core_ref[0], core_ref[1]])
    grads = jnp.concatenate([mine_ref[...], theirs_ref[...]])
    out_ref[...] = lax.dot_general(
        rows, grads, (((0,), (0,)), ((), ())), preferred_element_type=F32
    ).astype(BF16)


def head_gradient(rows, core_rows, mine, theirs):
    _, per, depth = rows.shape
    cols = mine.shape[1]
    tile = 512 if depth % 512 == 0 else depth
    whole = pl.BlockSpec((2 * per, cols), lambda i: (0, 0))
    slab = pl.BlockSpec((2, per, tile), lambda i: (0, 0, i))
    return pl.pallas_call(
        head_kernel,
        grid=(depth // tile,),
        out_shape=shape((depth, cols), BF16),
        in_specs=[slab] * 2 + [whole] * 2,
        out_specs=pl.BlockSpec((tile, cols), lambda i: (i, 0)),
        compiler_params=params(6),
        cost_estimate=cost(8 * per * depth * cols, (4 * per + cols) * depth * 2),
        name="head_gradient",
    )(rows, core_rows, mine, theirs)


def body(hidden, token_ids, serving, head_weight, teacher_logits):
    groups = lax.axis_size("grp")
    shards = lax.axis_size("vocab")
    me_g = lax.axis_index("grp")
    me_v = lax.axis_index("vocab")
    per, depth = hidden.shape
    cols = head_weight.shape[1]
    owned = per // shards
    CORE, X = shards, 2 * shards
    Y, W = 1, 2
    count = groups * shards

    def swap(value, mask):
        return lax.ppermute(value, AXES, [(i, i ^ mask) for i in range(count)])

    def tie(*values):
        return lax.optimization_barrier(values)

    def ints(*values):
        return jnp.stack([jnp.asarray(v, jnp.int32) for v in values])

    quarter_rows = per * 3 // 16
    quarter = me_v & 3
    starts = [(quarter ^ k) * quarter_rows for k in range(4)]
    chip = me_g >> 1
    spots = ints(*starts)
    at = ints(
        me_v * owned, (me_g * shards + me_v) * cols, ((me_g ^ 1) * shards + me_v) * cols, me_g
    )
    who = ints(me_g, me_g & 1)
    unsigned = [
        jnp.asarray(v, jnp.uint32)
        for v in (starts[0], starts[3], 2 * chip, 2 * (chip ^ 1))
    ]
    rows, weight, spots, at, who, *unsigned = tie(hidden, head_weight, spots, at, who, *unsigned)
    zero = jnp.uint32(0)

    def cut(value, start, size, dim):
        indices = [start if d == dim else zero for d in range(value.ndim)]
        sizes = [size if d == dim else n for d, n in enumerate(value.shape)]
        return lax.dynamic_slice(value, indices, sizes)

    first = cut(rows, unsigned[0], quarter_rows, 0)
    x0 = swap(first, X)
    _, rows, weight, teacher = tie(first, rows, weight, teacher_logits)
    other_weight = swap(weight, CORE)
    x3 = swap(cut(rows, unsigned[1], quarter_rows, 0), X)
    rest = swap(rows[4 * quarter_rows :], X)
    kept = cut(teacher, unsigned[2], 2, 1).swapaxes(0, 1)
    gone = cut(teacher, unsigned[3], 2, 1).swapaxes(0, 1)
    taught = taught_stats(kept, gone)
    taught_core = swap(taught, CORE)
    x0, kept, gone, taught, taught_core, rows = tie(x0, kept, gone, taught, taught_core, rows)
    x1 = swap(x0, Y)
    x2 = swap(x0, W)
    kept_core = swap(kept, CORE)
    near_a, stats_a = near_logits(rows, weight, x0)
    near_b, stats_b = near_logits(rows, other_weight, x0)
    *pieces, gone, near_a, near_b = tie(x0, x1, x2, x3, rest, gone, near_a, near_b)
    taught_x = swap(gone, X)
    far_a, far_b, both_rows, stats = far_logits(
        spots,
        pieces,
        weight,
        other_weight,
        rows,
        stats_a,
        stats_b,
        taught,
        taught_core,
        token_ids.reshape(1, per),
    )

    served = serving.reshape(groups, 1, per)
    logits = [near_a, near_b, far_a, far_b]
    held = logits + [weight]
    mask = W
    while mask < shards:
        masks = [mask, 2 * mask, 3 * mask] if 2 * mask < shards else [mask]
        stats = merge([stats] + [swap(stats, m) for m in masks], held)
        mask *= 4
    _, taught_x = tie(stats, taught_x)
    taught_far = swap(taught_x, CORE)
    aligned = teacher_rows(who, served, [kept, kept_core, taught_x, taught_far])
    parts = [stats] + [swap(stats, mask) for mask in (X, Y, X + Y)]

    bits = shards.bit_length() - 1
    masks = {0: X}
    for b in range(bits):
        masks[1 + b] = shards >> (1 + b)
    ydim, wdim = bits, bits - 1
    third = depth // 128 // 3 * 128
    edges = (0, third, 2 * third, depth)
    orders = [(0, ydim, wdim), (ydim, wdim, 0), (wdim, 0, ydim)]
    low = owned.bit_length() - 1
    row_bit = {0: low + bits, ydim: low, wdim: low + 1}
    first_bits = tuple(row_bit[order[0]] for order in orders)
    gown, gother, sents, keeps = back_rows(
        at, weight, other_weight, parts, logits, served, aligned, first_bits, edges
    )
    gots = [swap(sents[p], masks[orders[p][0]]) for p in range(3)]
    theirs = swap(gother, CORE)
    _, rows_sent = tie(gother, both_rows)
    grad_head = head_gradient(both_rows, swap(rows_sent, CORE), gown, theirs)
    for p in range(3):
        grad_head, gots[p] = tie(grad_head, gots[p])

    def folded(value, p):
        dims = [2] * (1 + bits)
        dims[orders[p][0]] = 1
        return value.reshape(*dims, owned, value.shape[-1])

    terms = [[folded(keeps[p], p), folded(gots[p], p)] for p in range(3)]
    for stage in (1, 2):
        sents = [
            sum(lax.index_in_dim(t, 1, orders[p][stage]).astype(F32) for t in terms[p]).astype(BF16)
            for p in range(3)
        ]
        gots = [swap(sents[p], masks[orders[p][stage]]) for p in range(3)]
        for p in range(3):
            terms[p] = [lax.index_in_dim(t, 0, orders[p][stage]) for t in terms[p]] + [gots[p]]
    for dim in range(1, wdim):
        for p in range(3):
            sent = sum(lax.index_in_dim(t, 1, dim).astype(F32) for t in terms[p]).astype(BF16)
            terms[p] = [lax.index_in_dim(t, 0, dim) for t in terms[p]] + [swap(sent, masks[dim])]
    total = jnp.concatenate([sum(t.astype(F32) for t in ts) for ts in terms], axis=-1)
    return (total.reshape(owned, depth), grad_head)


def solution(mesh):
    placed = (P("grp", None), P("grp"), P(), P(None, ("grp", "vocab")), P("grp", None, "vocab"))
    return jax.shard_map(
        body,
        mesh=mesh,
        in_specs=placed,
        out_specs=(P(("grp", "vocab"), None), P(None, ("grp", "vocab"))),
        check_vma=False,
    )
```

```python
import jax
import jax.numpy as jnp
from jax import lax
from jax.experimental import pallas as pl
from jax.experimental.pallas import tpu as pltpu
from jax.sharding import PartitionSpec as P

BF16 = jnp.bfloat16
F32 = jnp.float32
AXES = ("grp", "vocab")
VMEM = pl.BlockSpec(memory_space=pltpu.VMEM)
SMEM = pl.BlockSpec(memory_space=pltpu.SMEM)
STAT_ROWS = 8
MIB = 2**20


def params(mib):
    return pltpu.CompilerParams(vmem_limit_bytes=mib * MIB)


def cost(flops, nbytes, exps=0):
    return pl.CostEstimate(flops=flops, bytes_accessed=nbytes, transcendentals=exps)


def shape(dims, dtype):
    return jax.ShapeDtypeStruct(dims, dtype)


def columns_to_rows(columns):
    count = columns[0].shape[0]
    lane = lax.broadcasted_iota(jnp.int32, (count, 128), 1)
    wide = jnp.zeros((count, 128), F32)
    for k, column in enumerate(columns):
        wide = jnp.where(lane == k, column, wide)
    return wide.T[:STAT_ROWS]


def taught_kernel(kept_ref, gone_ref, out_ref):
    parts = [ref[c].astype(F32) for ref in (kept_ref, gone_ref) for c in range(2)]
    top = parts[0]
    for part in parts[1:]:
        top = jnp.maximum(top, part)
    peak = jnp.max(top, axis=1, keepdims=True)
    total = sum(jnp.exp((part - peak) * 0.5) for part in parts)
    out_ref[...] = columns_to_rows([peak, jnp.sum(total, axis=1, keepdims=True)])


def taught_stats(kept, gone):
    _, per, cols = kept.shape
    return pl.pallas_call(
        taught_kernel,
        out_shape=shape((STAT_ROWS, per), F32),
        in_specs=[VMEM] * 2,
        out_specs=VMEM,
        compiler_params=params(4),
        cost_estimate=cost(0, 4 * per * cols * 2, 4 * per * cols),
        name="taught_stats",
    )(kept, gone)


def teacher_kernel(at_ref, serving_ref, a0, a1, a2, a3, soft_ref, peaks_ref):
    me, core = at_ref[0], at_ref[1]
    _, per, cols = a0.shape
    for j in range(2):
        wanted = serving_ref[me ^ (2 * j)]
        sums = [0.0, 0.0]
        for k, arrived in enumerate((a0, a1, a2, a3)):
            row = lax.broadcasted_iota(jnp.int32, (per, per), 0) + (me ^ k) * per
            pick = (row == wanted).astype(BF16)
            for c in range(2):
                sums[c] += lax.dot_general(
                    pick, arrived[core ^ c], (((0,), (0,)), ((), ())), preferred_element_type=F32
                )
        peak = jnp.max(jnp.maximum(*sums), axis=1, keepdims=True)
        for c in range(2):
            soft_ref[j, :, c * cols : (c + 1) * cols] = jnp.exp((sums[c] - peak) * 0.5)
        peaks_ref[j] = columns_to_rows([peak])


def teacher_rows(at, serving, arrived):
    _, per, cols = arrived[0].shape
    return pl.pallas_call(
        teacher_kernel,
        out_shape=(shape((2, per, 2 * cols), F32), shape((2, STAT_ROWS, per), F32)),
        in_specs=[SMEM] + [VMEM] * 5,
        out_specs=(VMEM, VMEM),
        compiler_params=params(8),
        cost_estimate=cost(32 * per * per * cols, 12 * per * cols * 2, 4 * per * cols),
        name="teacher_rows",
    )(at, serving, *arrived)


def student_stats(logits):
    peak = jnp.max(logits, axis=1, keepdims=True)
    soft = jnp.exp((logits - peak) * 0.5)
    hard = jnp.sum(soft * soft, axis=1, keepdims=True)
    return soft, columns_to_rows([peak, hard, jnp.sum(soft, axis=1, keepdims=True)])


def near_kernel(rows_ref, w_ref, *refs):
    logits_ref, stats_ref = refs[-2:]
    logits = jnp.dot(rows_ref[...], w_ref[...], preferred_element_type=F32)
    logits_ref[...], stats_ref[...] = student_stats(logits)


def near_logits(rows, weight, *held):
    per, depth = rows.shape
    cols = weight.shape[1]
    return pl.pallas_call(
        near_kernel,
        out_shape=(shape((per, cols), F32), shape((STAT_ROWS, per), F32)),
        in_specs=[VMEM] * (2 + len(held)),
        out_specs=(VMEM, VMEM),
        compiler_params=params(6),
        cost_estimate=cost(2 * per * depth * cols, (per + cols) * depth * 2, per * cols),
        name="near_logits",
    )(rows, weight, *held)


NOTHING = -3.0e38


def both(a, b):
    peak = jnp.maximum(a[0:1], b[0:1])
    ea, eb = jnp.exp((a[0:1] - peak) * 0.5), jnp.exp((b[0:1] - peak) * 0.5)
    return jnp.concatenate(
        [peak, a[1:2] * (ea * ea) + b[1:2] * (eb * eb), a[2:3] * ea + b[2:3] * eb]
    )


def far_kernel(n, spots_ref, *refs):
    pieces, refs = refs[:n], refs[n:]
    own_ref, other_ref, near_ref, stats_a, stats_b, taught_ref, taught_core_ref, ids_ref = refs[:8]
    a_ref, b_ref, rows_ref, out_ref, peaks_ref, full = refs[8:]
    share = pieces[0].shape[0]
    for k, piece in enumerate(pieces[:-1]):
        full[pl.ds(pl.multiple_of(spots_ref[k], 8), share), :] = piece[...].astype(F32)
    full[4 * share :, :] = pieces[-1][...].astype(F32)
    rows_ref[0] = near_ref[...]
    rows_ref[1] = full[...].astype(BF16)
    per = rows_ref.shape[1]
    a = jnp.dot(rows_ref[1], own_ref[...], preferred_element_type=F32)
    b = jnp.dot(rows_ref[1], other_ref[...], preferred_element_type=F32)
    a_ref[...], a = student_stats(a)
    b_ref[...], b = student_stats(b)
    peaks_ref[...] = jnp.concatenate(
        [stats_a[0:1], stats_b[0:1], a[0:1], b[0:1], jnp.zeros((STAT_ROWS - 4, per), F32)]
    )
    out_ref[0, 0:3, :] = both(stats_a[...], stats_b[...])
    out_ref[0, 3:4, :] = ids_ref[...].astype(F32)
    out_ref[0, 4:6, :] = taught_ref[0:2, :]
    out_ref[0, 6:8, :] = taught_core_ref[0:2, :]
    out_ref[1, 0:3, :] = both(a, b)
    row = lax.broadcasted_iota(jnp.int32, (5, per), 0)
    out_ref[1, 3:8, :] = jnp.where((row == 1) | (row == 3), NOTHING, 0.0)


def far_logits(spots, pieces, own, other, *small):
    depth, cols = own.shape
    per = sum(piece.shape[0] for piece in pieces)
    return pl.pallas_call(
        lambda *refs: far_kernel(len(pieces), *refs),
        out_shape=(
            shape((per, cols), F32),
            shape((per, cols), F32),
            shape((2, per, depth), BF16),
            shape((2, STAT_ROWS, per), F32),
            shape((STAT_ROWS, per), F32),
        ),
        in_specs=[SMEM] + [VMEM] * (len(pieces) + 2 + len(small)),
        out_specs=(VMEM,) * 5,
        scratch_shapes=[pltpu.VMEM((per, depth), F32)],
        compiler_params=params(16),
        cost_estimate=cost(4 * per * depth * cols, (per + 2 * cols) * depth * 2, 2 * per * cols),
        name="far_logits",
    )(spots, *pieces, own, other, *small)


def merged(parts):
    top = parts[0]
    for part in parts[1:]:
        top = jnp.maximum(top, part)
    hard = soft = taught0 = taught1 = 0.0
    for part in parts:
        shrink = jnp.exp((part - top) * 0.5)
        s = shrink[0:1]
        hard += part[1:2] * (s * s)
        soft += part[2:3] * s
        taught0 += part[5:6] * shrink[4:5]
        taught1 += part[7:8] * shrink[6:7]
    return top[0:1], hard, soft, top[3:4], top[4:5], taught0, top[6:7], taught1


def merge_kernel(n, *refs):
    out_ref = refs[-1]
    for j in range(2):
        out_ref[j] = jnp.concatenate(merged([ref[j] for ref in refs[:n]]))


def merge(parts, held):
    return pl.pallas_call(
        lambda *refs: merge_kernel(len(parts), *refs),
        out_shape=shape(parts[0].shape, F32),
        in_specs=[VMEM] * (len(parts) + len(held)),
        out_specs=VMEM,
        compiler_params=params(6),
        cost_estimate=cost(0, 5 * parts[0].size * 4),
        name="merge_stats",
    )(*parts, *held)


def picker(bit, flip, total):
    half = total // 2
    row = lax.broadcasted_iota(jnp.int32, (total, total), 0)
    side = jnp.where(row < half, 1 << bit, 0)
    row = row & (half - 1)
    row = ((row >> bit) << (bit + 1)) + side + (row & ((1 << bit) - 1))
    return (lax.broadcasted_iota(jnp.int32, (total, total), 1) == (row ^ flip)).astype(BF16)


def grads_kernel(n, at_ref, *refs):
    stats_refs, refs = refs[:n], refs[n:]
    soft_refs, (peaks_ref, serving_ref, taught_ref, tpeaks_ref), g_refs = refs[:4], refs[4:8], refs[8:]
    me = at_ref[3]
    per, cols = soft_refs[0].shape
    stats = [merged([ref[j ^ (i & 1)] for i, ref in enumerate(stats_refs)]) for j in range(2)]
    lane = lax.broadcasted_iota(jnp.int32, (per, per), 1)
    for j in range(2):
        rows = stats[j][:4] + (
            serving_ref[me ^ (2 * j)].astype(F32),
            tpeaks_ref[j, 0:1, :],
            peaks_ref[2 * j : 2 * j + 2, :],
        )
        columns = jnp.concatenate(rows + (jnp.zeros((128 - 8, per), F32),)).T
        peak, hard, soft, ids, wanted, tlocal, *local = [columns[:, i : i + 1] for i in range(8)]
        ids, wanted = ids.astype(jnp.int32), wanted.astype(jnp.int32)
        tpeak = total = 0.0
        for k in range(4):
            here = wanted - (me ^ k) * per == lane
            taught = stats[k // 2][4 + 2 * (k % 2) : 6 + 2 * (k % 2)]
            tpeak += jnp.where(here, taught[0], 0.0)
            total += jnp.where(here, taught[1], 0.0)
        tpeak = jnp.sum(tpeak, axis=1, keepdims=True)
        total = jnp.sum(total, axis=1, keepdims=True)
        teach = jnp.exp((tlocal - tpeak) * 0.5) * (32.0 / total)
        hard, soft = 16.0 / hard, 32.0 / soft
        for c, g_ref in enumerate(g_refs):
            part = slice(c * cols, (c + 1) * cols)
            column = at_ref[1 + c] + lax.broadcasted_iota(jnp.int32, (per, cols), 1)
            scale = jnp.exp((local[c] - peak) * 0.5)
            own = soft_refs[2 * j + c][...]
            label = jnp.where(column == ids, 16.0, 0.0)
            grad = own * (scale * soft + own * (scale * scale * hard)) - taught_ref[j, :, part] * teach
            g_ref[j * per : (j + 1) * per, :] = (grad - label).astype(BF16)


def back_kernel(bits, edges, low, n, at_ref, *refs):
    w_refs, refs, mixed = refs[:2], refs[2:-1], refs[-1]
    g_refs, send_refs, keep_refs = refs[-8:-6], refs[-6:-3], refs[-3:]
    grads_kernel(n, at_ref, *refs[:-6])
    total = mixed.shape[1]
    per = total // 2
    aligned = (1 << low) % 16 == 0
    if aligned:
        row = lax.broadcasted_iota(jnp.int32, (total, total), 0)
        turn = lax.broadcasted_iota(jnp.int32, (total, total), 1) == (row ^ at_ref[0])
        for c, g_ref in enumerate(g_refs):
            mixed[c] = jnp.dot(turn.astype(BF16), g_ref[...], preferred_element_type=F32).astype(BF16)
    for p in range(3):
        back = 0.0
        for c, (g_ref, w_ref) in enumerate(zip(g_refs, w_refs)):
            if aligned:
                run = 1 << bits[p]
                starts = [i for side in (run, 0) for i in range(side, total, 2 * run)]
                rows = jnp.concatenate([mixed[c, i : i + run, :] for i in starts])
            else:
                pick = picker(bits[p], at_ref[0], total)
                rows = jnp.dot(pick, g_ref[...], preferred_element_type=F32).astype(BF16)
            back += lax.dot_general(
                w_ref[edges[p] : edges[p + 1], :],
                rows,
                (((1,), (1,)), ((), ())),
                preferred_element_type=F32,
            )
        back = back.T
        send_refs[p][...] = back[:per].astype(BF16)
        keep_refs[p][...] = back[per:]


def back_rows(at, own, other, stats, soft, small, bits, edges, low):
    depth, cols = own.shape
    per = soft[0].shape[0]
    parts = [(per, edges[p + 1] - edges[p]) for p in range(3)]
    got = pl.pallas_call(
        lambda *refs: back_kernel(bits, edges, low, len(stats), *refs),
        out_shape=[shape((2 * per, cols), BF16)] * 2
        + [shape(part, BF16) for part in parts]
        + [shape(part, F32) for part in parts],
        in_specs=[SMEM] + [VMEM] * (len(stats) + 6 + len(small)),
        out_specs=[VMEM] * 8,
        scratch_shapes=[pltpu.VMEM((2, 2 * per, cols), BF16)],
        compiler_params=params(20),
        cost_estimate=cost(8 * per * depth * cols, 2 * cols * depth * 2),
        name="back_rows",
    )(at, own, other, *stats, *soft, *small)
    return got[0], got[1], got[2:5], got[5:8]


def head_kernel(rows_ref, core_ref, mine_ref, theirs_ref, out_ref):
    rows = jnp.concatenate([rows_ref[0], rows_ref[1], core_ref[0], core_ref[1]])
    grads = jnp.concatenate([mine_ref[...], theirs_ref[...]])
    out_ref[...] = lax.dot_general(
        rows, grads, (((0,), (0,)), ((), ())), preferred_element_type=F32
    ).astype(BF16)


def head_gradient(rows, core_rows, mine, theirs):
    _, per, depth = rows.shape
    cols = mine.shape[1]
    tile = 512 if depth % 512 == 0 else depth
    whole = pl.BlockSpec((2 * per, cols), lambda i: (0, 0))
    slab = pl.BlockSpec((2, per, tile), lambda i: (0, 0, i))
    return pl.pallas_call(
        head_kernel,
        grid=(depth // tile,),
        out_shape=shape((depth, cols), BF16),
        in_specs=[slab] * 2 + [whole] * 2,
        out_specs=pl.BlockSpec((tile, cols), lambda i: (i, 0)),
        compiler_params=params(6),
        cost_estimate=cost(8 * per * depth * cols, (4 * per + cols) * depth * 2),
        name="head_gradient",
    )(rows, core_rows, mine, theirs)


def body(hidden, token_ids, serving, head_weight, teacher_logits):
    groups = lax.axis_size("grp")
    shards = lax.axis_size("vocab")
    me_g = lax.axis_index("grp")
    me_v = lax.axis_index("vocab")
    per, depth = hidden.shape
    cols = head_weight.shape[1]
    owned = per // shards
    CORE, X = shards, 2 * shards
    Y, W = 1, 2
    count = groups * shards

    def swap(value, mask):
        return lax.ppermute(value, AXES, [(i, i ^ mask) for i in range(count)])

    def tie(*values):
        return lax.optimization_barrier(values)

    def ints(*values):
        return jnp.stack([jnp.asarray(v, jnp.int32) for v in values])

    quarter_rows = per * 3 // 16
    quarter = me_v & 3
    starts = [(quarter ^ k) * quarter_rows for k in range(4)]
    chip = me_g >> 1
    spots = ints(*starts)
    at = ints(
        me_v * owned, (me_g * shards + me_v) * cols, ((me_g ^ 1) * shards + me_v) * cols, me_g
    )
    who = ints(me_g, me_g & 1)
    unsigned = [
        jnp.asarray(v, jnp.uint32)
        for v in (starts[0], starts[3], 2 * chip, 2 * (chip ^ 1))
    ]
    rows, weight, spots, at, who, *unsigned = tie(hidden, head_weight, spots, at, who, *unsigned)
    zero = jnp.uint32(0)

    def cut(value, start, size, dim):
        indices = [start if d == dim else zero for d in range(value.ndim)]
        sizes = [size if d == dim else n for d, n in enumerate(value.shape)]
        return lax.dynamic_slice(value, indices, sizes)

    first = cut(rows, unsigned[0], quarter_rows, 0)
    x0 = swap(first, X)
    _, rows, weight, teacher = tie(first, rows, weight, teacher_logits)
    other_weight = swap(weight, CORE)
    x3 = swap(cut(rows, unsigned[1], quarter_rows, 0), X)
    rest = swap(rows[4 * quarter_rows :], X)
    kept = cut(teacher, unsigned[2], 2, 1).swapaxes(0, 1)
    gone = cut(teacher, unsigned[3], 2, 1).swapaxes(0, 1)
    taught = taught_stats(kept, gone)
    taught_core = swap(taught, CORE)
    x0, kept, gone, taught, taught_core, rows = tie(x0, kept, gone, taught, taught_core, rows)
    x1 = swap(x0, Y)
    x2 = swap(x0, W)
    kept_core = swap(kept, CORE)
    near_a, stats_a = near_logits(rows, weight, x0)
    near_b, stats_b = near_logits(rows, other_weight, x0)
    *pieces, gone, near_a, near_b = tie(x0, x1, x2, x3, rest, gone, near_a, near_b)
    taught_x = swap(gone, X)
    far_a, far_b, both_rows, stats, peaks = far_logits(
        spots,
        pieces,
        weight,
        other_weight,
        rows,
        stats_a,
        stats_b,
        taught,
        taught_core,
        token_ids.reshape(1, per),
    )

    served = serving.reshape(groups, 1, per)
    logits = [near_a, near_b, far_a, far_b]
    held = logits + [weight]
    mask = W
    while mask < shards:
        masks = [mask, 2 * mask, 3 * mask] if 2 * mask < shards else [mask]
        stats = merge([stats] + [swap(stats, m) for m in masks], held)
        mask *= 4
    _, taught_x = tie(stats, taught_x)
    taught_far = swap(taught_x, CORE)
    taught_soft, taught_peaks = teacher_rows(
        who, served, [kept, kept_core, taught_x, taught_far]
    )
    parts = [stats] + [swap(stats, mask) for mask in (X, Y, X + Y)]

    bits = shards.bit_length() - 1
    masks = {0: X}
    for b in range(bits):
        masks[1 + b] = shards >> (1 + b)
    ydim, wdim = bits, bits - 1
    third = depth // 128 // 3 * 128
    edges = (0, third, 2 * third, depth)
    orders = [(0, ydim, wdim), (ydim, wdim, 0), (wdim, 0, ydim)]
    low = owned.bit_length() - 1
    row_bit = {0: low + bits, ydim: low, wdim: low + 1}
    first_bits = tuple(row_bit[order[0]] for order in orders)
    small = (peaks, served, taught_soft, taught_peaks)
    gown, gother, sents, keeps = back_rows(
        at, weight, other_weight, parts, logits, small, first_bits, edges, low
    )
    gots = [swap(sents[p], masks[orders[p][0]]) for p in range(3)]
    theirs = swap(gother, CORE)
    _, rows_sent = tie(gother, both_rows)
    grad_head = head_gradient(both_rows, swap(rows_sent, CORE), gown, theirs)
    for p in range(3):
        grad_head, gots[p] = tie(grad_head, gots[p])

    def folded(value, p):
        dims = [2] * (1 + bits)
        dims[orders[p][0]] = 1
        return value.reshape(*dims, owned, value.shape[-1])

    terms = [[folded(keeps[p], p), folded(gots[p], p)] for p in range(3)]
    for stage in (1, 2):
        sents = [
            sum(lax.index_in_dim(t, 1, orders[p][stage]).astype(F32) for t in terms[p]).astype(BF16)
            for p in range(3)
        ]
        gots = [swap(sents[p], masks[orders[p][stage]]) for p in range(3)]
        for p in range(3):
            terms[p] = [lax.index_in_dim(t, 0, orders[p][stage]) for t in terms[p]] + [gots[p]]
    for dim in range(1, wdim):
        for p in range(3):
            sent = sum(lax.index_in_dim(t, 1, dim).astype(F32) for t in terms[p]).astype(BF16)
            terms[p] = [lax.index_in_dim(t, 0, dim) for t in terms[p]] + [swap(sent, masks[dim])]
    total = jnp.concatenate([sum(t.astype(F32) for t in ts) for ts in terms], axis=-1)
    return (total.reshape(owned, depth), grad_head)


def solution(mesh):
    placed = (P("grp", None), P("grp"), P(), P(None, ("grp", "vocab")), P("grp", None, "vocab"))
    return jax.shard_map(
        body,
        mesh=mesh,
        in_specs=placed,
        out_specs=(P(("grp", "vocab"), None), P(None, ("grp", "vocab"))),
        check_vma=False,
    )
```

```python
import jax
import jax.numpy as jnp
from jax import lax
from jax.experimental import pallas as pl
from jax.experimental.pallas import tpu as pltpu
from jax.sharding import PartitionSpec as P

BF16 = jnp.bfloat16
F32 = jnp.float32
AXES = ("grp", "vocab")
VMEM = pl.BlockSpec(memory_space=pltpu.VMEM)
SMEM = pl.BlockSpec(memory_space=pltpu.SMEM)
STAT_ROWS = 8
MIB = 2**20


def params(mib):
    return pltpu.CompilerParams(vmem_limit_bytes=mib * MIB)


def cost(flops, nbytes, exps=0):
    return pl.CostEstimate(flops=flops, bytes_accessed=nbytes, transcendentals=exps)


def shape(dims, dtype):
    return jax.ShapeDtypeStruct(dims, dtype)


def columns_to_rows(columns):
    count = columns[0].shape[0]
    lane = lax.broadcasted_iota(jnp.int32, (count, 128), 1)
    wide = jnp.zeros((count, 128), F32)
    for k, column in enumerate(columns):
        wide = jnp.where(lane == k, column, wide)
    return wide.T[:STAT_ROWS]


def taught_kernel(kept_ref, gone_ref, out_ref):
    parts = [ref[c].astype(F32) for ref in (kept_ref, gone_ref) for c in range(2)]
    top = parts[0]
    for part in parts[1:]:
        top = jnp.maximum(top, part)
    peak = jnp.max(top, axis=1, keepdims=True)
    total = sum(jnp.exp((part - peak) * 0.5) for part in parts)
    out_ref[...] = columns_to_rows([peak, jnp.sum(total, axis=1, keepdims=True)])


def taught_stats(kept, gone):
    _, per, cols = kept.shape
    return pl.pallas_call(
        taught_kernel,
        out_shape=shape((STAT_ROWS, per), F32),
        in_specs=[VMEM] * 2,
        out_specs=VMEM,
        compiler_params=params(4),
        cost_estimate=cost(0, 4 * per * cols * 2, 4 * per * cols),
        name="taught_stats",
    )(kept, gone)


def teacher_kernel(at_ref, serving_ref, a0, a1, a2, a3, soft_ref, peaks_ref):
    me, core = at_ref[0], at_ref[1]
    _, per, cols = a0.shape
    for j in range(2):
        wanted = serving_ref[me ^ (2 * j)]
        sums = [0.0, 0.0]
        for k, arrived in enumerate((a0, a1, a2, a3)):
            row = lax.broadcasted_iota(jnp.int32, (per, per), 0) + (me ^ k) * per
            pick = (row == wanted).astype(BF16)
            for c in range(2):
                sums[c] += lax.dot_general(
                    pick, arrived[core ^ c], (((0,), (0,)), ((), ())), preferred_element_type=F32
                )
        peak = jnp.max(jnp.maximum(*sums), axis=1, keepdims=True)
        for c in range(2):
            soft_ref[j, :, c * cols : (c + 1) * cols] = jnp.exp((sums[c] - peak) * 0.5)
        peaks_ref[j] = columns_to_rows([peak])


def teacher_rows(at, serving, arrived):
    _, per, cols = arrived[0].shape
    return pl.pallas_call(
        teacher_kernel,
        out_shape=(shape((2, per, 2 * cols), F32), shape((2, STAT_ROWS, per), F32)),
        in_specs=[SMEM] + [VMEM] * 5,
        out_specs=(VMEM, VMEM),
        compiler_params=params(8),
        cost_estimate=cost(32 * per * per * cols, 12 * per * cols * 2, 4 * per * cols),
        name="teacher_rows",
    )(at, serving, *arrived)


def student_stats(logits):
    peak = jnp.max(logits, axis=1, keepdims=True)
    soft = jnp.exp((logits - peak) * 0.5)
    hard = jnp.sum(soft * soft, axis=1, keepdims=True)
    return soft, columns_to_rows([peak, hard, jnp.sum(soft, axis=1, keepdims=True)])


def near_kernel(rows_ref, w_ref, *refs):
    logits_ref, stats_ref = refs[-2:]
    logits = jnp.dot(rows_ref[...], w_ref[...], preferred_element_type=F32)
    logits_ref[...], stats_ref[...] = student_stats(logits)


def near_logits(rows, weight, *held):
    per, depth = rows.shape
    cols = weight.shape[1]
    return pl.pallas_call(
        near_kernel,
        out_shape=(shape((per, cols), F32), shape((STAT_ROWS, per), F32)),
        in_specs=[VMEM] * (2 + len(held)),
        out_specs=(VMEM, VMEM),
        compiler_params=params(6),
        cost_estimate=cost(2 * per * depth * cols, (per + cols) * depth * 2, per * cols),
        name="near_logits",
    )(rows, weight, *held)


NOTHING = -3.0e38


def both(a, b):
    peak = jnp.maximum(a[0:1], b[0:1])
    ea, eb = jnp.exp((a[0:1] - peak) * 0.5), jnp.exp((b[0:1] - peak) * 0.5)
    return jnp.concatenate(
        [peak, a[1:2] * (ea * ea) + b[1:2] * (eb * eb), a[2:3] * ea + b[2:3] * eb]
    )


def far_kernel(n, spots_ref, *refs):
    pieces, refs = refs[:n], refs[n:]
    own_ref, other_ref, near_ref, stats_a, stats_b, taught_ref, taught_core_ref, ids_ref = refs[:8]
    a_ref, b_ref, rows_ref, out_ref, peaks_ref, full = refs[8:]
    share = pieces[0].shape[0]
    for k, piece in enumerate(pieces[:-1]):
        full[pl.ds(pl.multiple_of(spots_ref[k], 8), share), :] = piece[...].astype(F32)
    full[4 * share :, :] = pieces[-1][...].astype(F32)
    rows_ref[0] = near_ref[...]
    rows_ref[1] = full[...].astype(BF16)
    per = rows_ref.shape[1]
    a = jnp.dot(rows_ref[1], own_ref[...], preferred_element_type=F32)
    b = jnp.dot(rows_ref[1], other_ref[...], preferred_element_type=F32)
    a_ref[...], a = student_stats(a)
    b_ref[...], b = student_stats(b)
    peaks_ref[...] = jnp.concatenate(
        [stats_a[0:1], stats_b[0:1], a[0:1], b[0:1], jnp.zeros((STAT_ROWS - 4, per), F32)]
    )
    out_ref[0, 0:3, :] = both(stats_a[...], stats_b[...])
    out_ref[0, 3:4, :] = ids_ref[...].astype(F32)
    out_ref[0, 4:6, :] = taught_ref[0:2, :]
    out_ref[0, 6:8, :] = taught_core_ref[0:2, :]
    out_ref[1, 0:3, :] = both(a, b)
    row = lax.broadcasted_iota(jnp.int32, (5, per), 0)
    out_ref[1, 3:8, :] = jnp.where((row == 1) | (row == 3), NOTHING, 0.0)


def far_logits(spots, pieces, own, other, *small):
    depth, cols = own.shape
    per = sum(piece.shape[0] for piece in pieces)
    return pl.pallas_call(
        lambda *refs: far_kernel(len(pieces), *refs),
        out_shape=(
            shape((per, cols), F32),
            shape((per, cols), F32),
            shape((2, per, depth), BF16),
            shape((2, STAT_ROWS, per), F32),
            shape((STAT_ROWS, per), F32),
        ),
        in_specs=[SMEM] + [VMEM] * (len(pieces) + 2 + len(small)),
        out_specs=(VMEM,) * 5,
        scratch_shapes=[pltpu.VMEM((per, depth), F32)],
        compiler_params=params(16),
        cost_estimate=cost(4 * per * depth * cols, (per + 2 * cols) * depth * 2, 2 * per * cols),
        name="far_logits",
    )(spots, *pieces, own, other, *small)


def merged(parts):
    top = parts[0]
    for part in parts[1:]:
        top = jnp.maximum(top, part)
    hard = soft = taught0 = taught1 = 0.0
    for part in parts:
        shrink = jnp.exp((part - top) * 0.5)
        s = shrink[0:1]
        hard += part[1:2] * (s * s)
        soft += part[2:3] * s
        taught0 += part[5:6] * shrink[4:5]
        taught1 += part[7:8] * shrink[6:7]
    return top[0:1], hard, soft, top[3:4], top[4:5], taught0, top[6:7], taught1


def merge_kernel(n, *refs):
    out_ref = refs[-1]
    for j in range(2):
        out_ref[j] = jnp.concatenate(merged([ref[j] for ref in refs[:n]]))


def merge(parts, held):
    return pl.pallas_call(
        lambda *refs: merge_kernel(len(parts), *refs),
        out_shape=shape(parts[0].shape, F32),
        in_specs=[VMEM] * (len(parts) + len(held)),
        out_specs=VMEM,
        compiler_params=params(6),
        cost_estimate=cost(0, 5 * parts[0].size * 4),
        name="merge_stats",
    )(*parts, *held)


def picker(bit, flip, total):
    half = total // 2
    row = lax.broadcasted_iota(jnp.int32, (total, total), 0)
    side = jnp.where(row < half, 1 << bit, 0)
    row = row & (half - 1)
    row = ((row >> bit) << (bit + 1)) + side + (row & ((1 << bit) - 1))
    return (lax.broadcasted_iota(jnp.int32, (total, total), 1) == (row ^ flip)).astype(BF16)


def grads_kernel(n, at_ref, *refs):
    stats_refs, refs = refs[:n], refs[n:]
    soft_refs, (peaks_ref, serving_ref, taught_ref, tpeaks_ref), g_refs = refs[:4], refs[4:8], refs[8:]
    me = at_ref[3]
    per, cols = soft_refs[0].shape
    stats = [merged([ref[j ^ (i & 1)] for i, ref in enumerate(stats_refs)]) for j in range(2)]
    lane = lax.broadcasted_iota(jnp.int32, (per, per), 1)
    for j in range(2):
        rows = stats[j][:4] + (
            serving_ref[me ^ (2 * j)].astype(F32),
            tpeaks_ref[j, 0:1, :],
            peaks_ref[2 * j : 2 * j + 2, :],
        )
        columns = jnp.concatenate(rows + (jnp.zeros((128 - 8, per), F32),)).T
        peak, hard, soft, ids, wanted, tlocal, *local = [columns[:, i : i + 1] for i in range(8)]
        ids, wanted = ids.astype(jnp.int32), wanted.astype(jnp.int32)
        tpeak = total = 0.0
        for k in range(4):
            here = wanted - (me ^ k) * per == lane
            taught = stats[k // 2][4 + 2 * (k % 2) : 6 + 2 * (k % 2)]
            tpeak += jnp.where(here, taught[0], 0.0)
            total += jnp.where(here, taught[1], 0.0)
        tpeak = jnp.sum(tpeak, axis=1, keepdims=True)
        total = jnp.sum(total, axis=1, keepdims=True)
        teach = jnp.exp((tlocal - tpeak) * 0.5) * (32.0 / total)
        hard, soft = 16.0 / hard, 32.0 / soft
        for c, g_ref in enumerate(g_refs):
            part = slice(c * cols, (c + 1) * cols)
            column = at_ref[1 + c] + lax.broadcasted_iota(jnp.int32, (per, cols), 1)
            scale = jnp.exp((local[c] - peak) * 0.5)
            own = soft_refs[2 * j + c][...]
            label = jnp.where(column == ids, 16.0, 0.0)
            grad = own * (scale * soft + own * (scale * scale * hard)) - taught_ref[j, :, part] * teach
            g_ref[j * per : (j + 1) * per, :] = (grad - label).astype(BF16)


def back_kernel(bits, edges, low, n, at_ref, *refs):
    w_refs, refs, mixed = refs[:2], refs[2:-1], refs[-1]
    g_refs, send_refs, keep_refs = refs[-8:-6], refs[-6:-3], refs[-3:]
    grads_kernel(n, at_ref, *refs[:-6])
    total = mixed.shape[1]
    per = total // 2
    aligned = (1 << low) % 16 == 0
    if aligned:
        row = lax.broadcasted_iota(jnp.int32, (total, total), 0)
        turn = lax.broadcasted_iota(jnp.int32, (total, total), 1) == (row ^ at_ref[0])
        for c, g_ref in enumerate(g_refs):
            mixed[c] = jnp.dot(turn.astype(BF16), g_ref[...], preferred_element_type=F32).astype(BF16)
    for p in range(3):
        back = 0.0
        for c, (g_ref, w_ref) in enumerate(zip(g_refs, w_refs)):
            if aligned:
                run = 1 << bits[p]
                starts = [i for side in (run, 0) for i in range(side, total, 2 * run)]
                rows = jnp.concatenate([mixed[c, i : i + run, :] for i in starts])
            else:
                pick = picker(bits[p], at_ref[0], total)
                rows = jnp.dot(pick, g_ref[...], preferred_element_type=F32).astype(BF16)
            back += lax.dot_general(
                w_ref[edges[p] : edges[p + 1], :],
                rows,
                (((1,), (1,)), ((), ())),
                preferred_element_type=F32,
            )
        back = back.T
        send_refs[p][...] = back[:per].astype(BF16)
        keep_refs[p][...] = back[per:]


def back_rows(at, own, other, stats, soft, small, bits, edges, low):
    depth, cols = own.shape
    per = soft[0].shape[0]
    parts = [(per, edges[p + 1] - edges[p]) for p in range(3)]
    got = pl.pallas_call(
        lambda *refs: back_kernel(bits, edges, low, len(stats), *refs),
        out_shape=[shape((2 * per, cols), BF16)] * 2
        + [shape(part, BF16) for part in parts]
        + [shape(part, F32) for part in parts],
        in_specs=[SMEM] + [VMEM] * (len(stats) + 6 + len(small)),
        out_specs=[VMEM] * 8,
        scratch_shapes=[pltpu.VMEM((2, 2 * per, cols), BF16)],
        compiler_params=params(20),
        cost_estimate=cost(8 * per * depth * cols, 2 * cols * depth * 2),
        name="back_rows",
    )(at, own, other, *stats, *soft, *small)
    return got[0], got[1], got[2:5], got[5:8]


def head_kernel(rows_ref, core_ref, mine_ref, theirs_ref, out_ref):
    rows = jnp.concatenate([rows_ref[0], rows_ref[1], core_ref[0], core_ref[1]])
    grads = jnp.concatenate([mine_ref[...], theirs_ref[...]])
    out_ref[...] = lax.dot_general(
        rows, grads, (((0,), (0,)), ((), ())), preferred_element_type=F32
    ).astype(BF16)


def head_gradient(rows, core_rows, mine, theirs):
    _, per, depth = rows.shape
    cols = mine.shape[1]
    tile = 512 if depth % 512 == 0 else depth
    whole = pl.BlockSpec((2 * per, cols), lambda i: (0, 0))
    slab = pl.BlockSpec((2, per, tile), lambda i: (0, 0, i))
    return pl.pallas_call(
        head_kernel,
        grid=(depth // tile,),
        out_shape=shape((depth, cols), BF16),
        in_specs=[slab] * 2 + [whole] * 2,
        out_specs=pl.BlockSpec((tile, cols), lambda i: (i, 0)),
        compiler_params=pltpu.CompilerParams(
            vmem_limit_bytes=6 * MIB, fuse_transposed_lhs_in_matmul=True
        ),
        cost_estimate=cost(8 * per * depth * cols, (4 * per + cols) * depth * 2),
        name="head_gradient",
    )(rows, core_rows, mine, theirs)


def body(hidden, token_ids, serving, head_weight, teacher_logits):
    groups = lax.axis_size("grp")
    shards = lax.axis_size("vocab")
    me_g = lax.axis_index("grp")
    me_v = lax.axis_index("vocab")
    per, depth = hidden.shape
    cols = head_weight.shape[1]
    owned = per // shards
    CORE, X = shards, 2 * shards
    Y, W = 1, 2
    count = groups * shards

    def swap(value, mask):
        return lax.ppermute(value, AXES, [(i, i ^ mask) for i in range(count)])

    def tie(*values):
        return lax.optimization_barrier(values)

    def ints(*values):
        return jnp.stack([jnp.asarray(v, jnp.int32) for v in values])

    quarter_rows = per * 3 // 16
    quarter = me_v & 3
    starts = [(quarter ^ k) * quarter_rows for k in range(4)]
    chip = me_g >> 1
    spots = ints(*starts)
    at = ints(
        me_v * owned, (me_g * shards + me_v) * cols, ((me_g ^ 1) * shards + me_v) * cols, me_g
    )
    who = ints(me_g, me_g & 1)
    unsigned = [
        jnp.asarray(v, jnp.uint32)
        for v in (starts[0], starts[3], 2 * chip, 2 * (chip ^ 1))
    ]
    rows, weight, spots, at, who, *unsigned = tie(hidden, head_weight, spots, at, who, *unsigned)
    zero = jnp.uint32(0)

    def cut(value, start, size, dim):
        indices = [start if d == dim else zero for d in range(value.ndim)]
        sizes = [size if d == dim else n for d, n in enumerate(value.shape)]
        return lax.dynamic_slice(value, indices, sizes)

    first = cut(rows, unsigned[0], quarter_rows, 0)
    x0 = swap(first, X)
    _, rows, weight, teacher = tie(first, rows, weight, teacher_logits)
    other_weight = swap(weight, CORE)
    x3 = swap(cut(rows, unsigned[1], quarter_rows, 0), X)
    rest = swap(rows[4 * quarter_rows :], X)
    kept = cut(teacher, unsigned[2], 2, 1).swapaxes(0, 1)
    gone = cut(teacher, unsigned[3], 2, 1).swapaxes(0, 1)
    taught = taught_stats(kept, gone)
    taught_core = swap(taught, CORE)
    x0, kept, gone, taught, taught_core, rows = tie(x0, kept, gone, taught, taught_core, rows)
    x1 = swap(x0, Y)
    x2 = swap(x0, W)
    kept_core = swap(kept, CORE)
    near_a, stats_a = near_logits(rows, weight, x0)
    near_b, stats_b = near_logits(rows, other_weight, x0)
    *pieces, gone, near_a, near_b = tie(x0, x1, x2, x3, rest, gone, near_a, near_b)
    taught_x = swap(gone, X)
    far_a, far_b, both_rows, stats, peaks = far_logits(
        spots,
        pieces,
        weight,
        other_weight,
        rows,
        stats_a,
        stats_b,
        taught,
        taught_core,
        token_ids.reshape(1, per),
    )

    served = serving.reshape(groups, 1, per)
    logits = [near_a, near_b, far_a, far_b]
    held = logits + [weight]
    mask = W
    while mask < shards:
        masks = [mask, 2 * mask, 3 * mask] if 2 * mask < shards else [mask]
        stats = merge([stats] + [swap(stats, m) for m in masks], held)
        mask *= 4
    _, taught_x = tie(stats, taught_x)
    taught_far = swap(taught_x, CORE)
    taught_soft, taught_peaks = teacher_rows(
        who, served, [kept, kept_core, taught_x, taught_far]
    )
    parts = [stats] + [swap(stats, mask) for mask in (X, Y, X + Y)]

    bits = shards.bit_length() - 1
    masks = {0: X}
    for b in range(bits):
        masks[1 + b] = shards >> (1 + b)
    ydim, wdim = bits, bits - 1
    third = depth // 128 // 3 * 128
    edges = (0, third, 2 * third, depth)
    orders = [(0, ydim, wdim), (ydim, wdim, 0), (wdim, 0, ydim)]
    low = owned.bit_length() - 1
    row_bit = {0: low + bits, ydim: low, wdim: low + 1}
    first_bits = tuple(row_bit[order[0]] for order in orders)
    small = (peaks, served, taught_soft, taught_peaks)
    gown, gother, sents, keeps = back_rows(
        at, weight, other_weight, parts, logits, small, first_bits, edges, low
    )
    gots = [swap(sents[p], masks[orders[p][0]]) for p in range(3)]
    theirs = swap(gother, CORE)
    _, rows_sent = tie(gother, both_rows)
    grad_head = head_gradient(both_rows, swap(rows_sent, CORE), gown, theirs)
    for p in range(3):
        grad_head, gots[p] = tie(grad_head, gots[p])

    def folded(value, p):
        dims = [2] * (1 + bits)
        dims[orders[p][0]] = 1
        return value.reshape(*dims, owned, value.shape[-1])

    terms = [[folded(keeps[p], p), folded(gots[p], p)] for p in range(3)]
    for stage in (1, 2):
        sents = [
            sum(lax.index_in_dim(t, 1, orders[p][stage]).astype(F32) for t in terms[p]).astype(BF16)
            for p in range(3)
        ]
        gots = [swap(sents[p], masks[orders[p][stage]]) for p in range(3)]
        for p in range(3):
            terms[p] = [lax.index_in_dim(t, 0, orders[p][stage]) for t in terms[p]] + [gots[p]]
    for dim in range(1, wdim):
        for p in range(3):
            sent = sum(lax.index_in_dim(t, 1, dim).astype(F32) for t in terms[p]).astype(BF16)
            terms[p] = [lax.index_in_dim(t, 0, dim) for t in terms[p]] + [swap(sent, masks[dim])]
    total = jnp.concatenate([sum(t.astype(F32) for t in ts) for ts in terms], axis=-1)
    return (total.reshape(owned, depth), grad_head)


def solution(mesh):
    placed = (P("grp", None), P("grp"), P(), P(None, ("grp", "vocab")), P("grp", None, "vocab"))
    return jax.shard_map(
        body,
        mesh=mesh,
        in_specs=placed,
        out_specs=(P(("grp", "vocab"), None), P(None, ("grp", "vocab"))),
        check_vma=False,
    )
```

```python
import jax
import jax.numpy as jnp
from jax import lax
from jax.experimental import pallas as pl
from jax.experimental.pallas import tpu as pltpu
from jax.sharding import PartitionSpec as P

BF16 = jnp.bfloat16
F32 = jnp.float32
AXES = ("grp", "vocab")
VMEM = pl.BlockSpec(memory_space=pltpu.VMEM)
SMEM = pl.BlockSpec(memory_space=pltpu.SMEM)
STAT_ROWS = 8
MIB = 2**20


def params(mib):
    return pltpu.CompilerParams(vmem_limit_bytes=mib * MIB)


def cost(flops, nbytes, exps=0):
    return pl.CostEstimate(flops=flops, bytes_accessed=nbytes, transcendentals=exps)


def shape(dims, dtype):
    return jax.ShapeDtypeStruct(dims, dtype)


def columns_to_rows(columns):
    count = columns[0].shape[0]
    lane = lax.broadcasted_iota(jnp.int32, (count, 128), 1)
    wide = jnp.zeros((count, 128), F32)
    for k, column in enumerate(columns):
        wide = jnp.where(lane == k, column, wide)
    return wide.T[:STAT_ROWS]


def taught_kernel(kept_ref, gone_ref, out_ref):
    parts = [ref[c].astype(F32) for ref in (kept_ref, gone_ref) for c in range(2)]
    top = parts[0]
    for part in parts[1:]:
        top = jnp.maximum(top, part)
    peak = jnp.max(top, axis=1, keepdims=True)
    total = sum(jnp.exp((part - peak) * 0.5) for part in parts)
    out_ref[...] = columns_to_rows([peak, jnp.sum(total, axis=1, keepdims=True)])


def taught_stats(kept, gone):
    _, per, cols = kept.shape
    return pl.pallas_call(
        taught_kernel,
        out_shape=shape((STAT_ROWS, per), F32),
        in_specs=[VMEM] * 2,
        out_specs=VMEM,
        compiler_params=params(4),
        cost_estimate=cost(0, 4 * per * cols * 2, 4 * per * cols),
        name="taught_stats",
    )(kept, gone)


def teacher_kernel(at_ref, serving_ref, a0, a1, a2, a3, soft_ref, peaks_ref):
    me, core = at_ref[0], at_ref[1]
    _, per, cols = a0.shape
    for j in range(2):
        wanted = serving_ref[me ^ (2 * j)]
        sums = [0.0, 0.0]
        for k, arrived in enumerate((a0, a1, a2, a3)):
            row = lax.broadcasted_iota(jnp.int32, (per, per), 0) + (me ^ k) * per
            pick = (row == wanted).astype(BF16)
            for c in range(2):
                sums[c] += lax.dot_general(
                    pick, arrived[core ^ c], (((0,), (0,)), ((), ())), preferred_element_type=F32
                )
        peak = jnp.max(jnp.maximum(*sums), axis=1, keepdims=True)
        for c in range(2):
            soft_ref[j, :, c * cols : (c + 1) * cols] = jnp.exp((sums[c] - peak) * 0.5)
        peaks_ref[j] = columns_to_rows([peak])


def teacher_rows(at, serving, arrived):
    _, per, cols = arrived[0].shape
    return pl.pallas_call(
        teacher_kernel,
        out_shape=(shape((2, per, 2 * cols), F32), shape((2, STAT_ROWS, per), F32)),
        in_specs=[SMEM] + [VMEM] * 5,
        out_specs=(VMEM, VMEM),
        compiler_params=params(8),
        cost_estimate=cost(32 * per * per * cols, 12 * per * cols * 2, 4 * per * cols),
        name="teacher_rows",
    )(at, serving, *arrived)


def student_stats(logits):
    peak = jnp.max(logits, axis=1, keepdims=True)
    soft = jnp.exp((logits - peak) * 0.5)
    hard = jnp.sum(soft * soft, axis=1, keepdims=True)
    return soft, columns_to_rows([peak, hard, jnp.sum(soft, axis=1, keepdims=True)])


def near_kernel(rows_ref, w_ref, *refs):
    logits_ref, stats_ref = refs[-2:]
    logits = jnp.dot(rows_ref[...], w_ref[...], preferred_element_type=F32)
    logits_ref[...], stats_ref[...] = student_stats(logits)


def near_logits(rows, weight, *held):
    per, depth = rows.shape
    cols = weight.shape[1]
    return pl.pallas_call(
        near_kernel,
        out_shape=(shape((per, cols), F32), shape((STAT_ROWS, per), F32)),
        in_specs=[VMEM] * (2 + len(held)),
        out_specs=(VMEM, VMEM),
        compiler_params=params(6),
        cost_estimate=cost(2 * per * depth * cols, (per + cols) * depth * 2, per * cols),
        name="near_logits",
    )(rows, weight, *held)


NOTHING = -3.0e38


def both(a, b):
    peak = jnp.maximum(a[0:1], b[0:1])
    ea, eb = jnp.exp((a[0:1] - peak) * 0.5), jnp.exp((b[0:1] - peak) * 0.5)
    return jnp.concatenate(
        [peak, a[1:2] * (ea * ea) + b[1:2] * (eb * eb), a[2:3] * ea + b[2:3] * eb]
    )


def far_kernel(n, spots_ref, *refs):
    pieces, refs = refs[:n], refs[n:]
    own_ref, other_ref, near_ref, stats_a, stats_b, taught_ref, taught_core_ref, ids_ref = refs[:8]
    a_ref, b_ref, rows_ref, out_ref, peaks_ref, full = refs[8:]
    share = pieces[0].shape[0]
    for k, piece in enumerate(pieces[:-1]):
        full[pl.ds(pl.multiple_of(spots_ref[k], 8), share), :] = piece[...].astype(F32)
    full[4 * share :, :] = pieces[-1][...].astype(F32)
    rows_ref[0] = near_ref[...]
    rows_ref[1] = full[...].astype(BF16)
    per = rows_ref.shape[1]
    a = jnp.dot(rows_ref[1], own_ref[...], preferred_element_type=F32)
    b = jnp.dot(rows_ref[1], other_ref[...], preferred_element_type=F32)
    a_ref[...], a = student_stats(a)
    b_ref[...], b = student_stats(b)
    peaks_ref[...] = jnp.concatenate(
        [stats_a[0:1], stats_b[0:1], a[0:1], b[0:1], jnp.zeros((STAT_ROWS - 4, per), F32)]
    )
    out_ref[0, 0:3, :] = both(stats_a[...], stats_b[...])
    out_ref[0, 3:4, :] = ids_ref[...].astype(F32)
    out_ref[0, 4:6, :] = taught_ref[0:2, :]
    out_ref[0, 6:8, :] = taught_core_ref[0:2, :]
    out_ref[1, 0:3, :] = both(a, b)
    row = lax.broadcasted_iota(jnp.int32, (5, per), 0)
    out_ref[1, 3:8, :] = jnp.where((row == 1) | (row == 3), NOTHING, 0.0)


def far_logits(spots, pieces, own, other, *small):
    depth, cols = own.shape
    per = sum(piece.shape[0] for piece in pieces)
    return pl.pallas_call(
        lambda *refs: far_kernel(len(pieces), *refs),
        out_shape=(
            shape((per, cols), F32),
            shape((per, cols), F32),
            shape((2, per, depth), BF16),
            shape((2, STAT_ROWS, per), F32),
            shape((STAT_ROWS, per), F32),
        ),
        in_specs=[SMEM] + [VMEM] * (len(pieces) + 2 + len(small)),
        out_specs=(VMEM,) * 5,
        scratch_shapes=[pltpu.VMEM((per, depth), F32)],
        compiler_params=params(16),
        cost_estimate=cost(4 * per * depth * cols, (per + 2 * cols) * depth * 2, 2 * per * cols),
        name="far_logits",
    )(spots, *pieces, own, other, *small)


def merged(parts):
    top = parts[0]
    for part in parts[1:]:
        top = jnp.maximum(top, part)
    hard = soft = taught0 = taught1 = 0.0
    for part in parts:
        shrink = jnp.exp((part - top) * 0.5)
        s = shrink[0:1]
        hard += part[1:2] * (s * s)
        soft += part[2:3] * s
        taught0 += part[5:6] * shrink[4:5]
        taught1 += part[7:8] * shrink[6:7]
    return top[0:1], hard, soft, top[3:4], top[4:5], taught0, top[6:7], taught1


def merge_kernel(n, *refs):
    out_ref = refs[-1]
    for j in range(2):
        out_ref[j] = jnp.concatenate(merged([ref[j] for ref in refs[:n]]))


def merge(parts, held):
    return pl.pallas_call(
        lambda *refs: merge_kernel(len(parts), *refs),
        out_shape=shape(parts[0].shape, F32),
        in_specs=[VMEM] * (len(parts) + len(held)),
        out_specs=VMEM,
        compiler_params=params(6),
        cost_estimate=cost(0, 5 * parts[0].size * 4),
        name="merge_stats",
    )(*parts, *held)


def picker(bit, flip, total):
    half = total // 2
    row = lax.broadcasted_iota(jnp.int32, (total, total), 0)
    side = jnp.where(row < half, 1 << bit, 0)
    row = row & (half - 1)
    row = ((row >> bit) << (bit + 1)) + side + (row & ((1 << bit) - 1))
    return (lax.broadcasted_iota(jnp.int32, (total, total), 1) == (row ^ flip)).astype(BF16)


def grads_kernel(n, at_ref, *refs):
    stats_refs, refs = refs[:n], refs[n:]
    soft_refs, (peaks_ref, serving_ref, taught_ref, tpeaks_ref), g_refs = refs[:4], refs[4:8], refs[8:]
    me = at_ref[3]
    per, cols = soft_refs[0].shape
    stats = [merged([ref[j ^ (i & 1)] for i, ref in enumerate(stats_refs)]) for j in range(2)]
    lane = lax.broadcasted_iota(jnp.int32, (per, per), 1)
    for j in range(2):
        rows = stats[j][:4] + (
            serving_ref[me ^ (2 * j)].astype(F32),
            tpeaks_ref[j, 0:1, :],
            peaks_ref[2 * j : 2 * j + 2, :],
        )
        columns = jnp.concatenate(rows + (jnp.zeros((128 - 8, per), F32),)).T
        peak, hard, soft, ids, wanted, tlocal, *local = [columns[:, i : i + 1] for i in range(8)]
        ids, wanted = ids.astype(jnp.int32), wanted.astype(jnp.int32)
        tpeak = total = 0.0
        for k in range(4):
            here = wanted - (me ^ k) * per == lane
            taught = stats[k // 2][4 + 2 * (k % 2) : 6 + 2 * (k % 2)]
            tpeak += jnp.where(here, taught[0], 0.0)
            total += jnp.where(here, taught[1], 0.0)
        tpeak = jnp.sum(tpeak, axis=1, keepdims=True)
        total = jnp.sum(total, axis=1, keepdims=True)
        teach = jnp.exp((tlocal - tpeak) * 0.5) * (32.0 / total)
        hard, soft = 16.0 / hard, 32.0 / soft
        for c, g_ref in enumerate(g_refs):
            part = slice(c * cols, (c + 1) * cols)
            column = at_ref[1 + c] + lax.broadcasted_iota(jnp.int32, (per, cols), 1)
            scale = jnp.exp((local[c] - peak) * 0.5)
            own = soft_refs[2 * j + c][...]
            label = jnp.where(column == ids, 16.0, 0.0)
            grad = own * (scale * soft + own * (scale * scale * hard)) - taught_ref[j, :, part] * teach
            g_ref[j * per : (j + 1) * per, :] = (grad - label).astype(BF16)


def back_kernel(bits, edges, low, n, at_ref, *refs):
    w_refs, refs, mixed = refs[:2], refs[2:-1], refs[-1]
    g_refs, send_refs, keep_refs = refs[-8:-6], refs[-6:-3], refs[-3:]
    grads_kernel(n, at_ref, *refs[:-6])
    total = mixed.shape[1]
    per = total // 2
    aligned = (1 << low) % 16 == 0
    if aligned:
        row = lax.broadcasted_iota(jnp.int32, (total, total), 0)
        turn = lax.broadcasted_iota(jnp.int32, (total, total), 1) == (row ^ at_ref[0])
        for c, g_ref in enumerate(g_refs):
            mixed[c] = jnp.dot(turn.astype(BF16), g_ref[...], preferred_element_type=F32).astype(BF16)
    for p in range(3):
        back = 0.0
        for c, (g_ref, w_ref) in enumerate(zip(g_refs, w_refs)):
            if aligned:
                run = 1 << bits[p]
                starts = [i for side in (run, 0) for i in range(side, total, 2 * run)]
                rows = jnp.concatenate([mixed[c, i : i + run, :] for i in starts])
            else:
                pick = picker(bits[p], at_ref[0], total)
                rows = jnp.dot(pick, g_ref[...], preferred_element_type=F32).astype(BF16)
            back += lax.dot_general(
                w_ref[edges[p] : edges[p + 1], :],
                rows,
                (((1,), (1,)), ((), ())),
                preferred_element_type=F32,
            )
        back = back.T
        send_refs[p][...] = back[:per].astype(BF16)
        keep_refs[p][...] = back[per:]


def back_rows(at, own, other, stats, soft, small, bits, edges, low):
    depth, cols = own.shape
    per = soft[0].shape[0]
    parts = [(per, edges[p + 1] - edges[p]) for p in range(3)]
    got = pl.pallas_call(
        lambda *refs: back_kernel(bits, edges, low, len(stats), *refs),
        out_shape=[shape((2 * per, cols), BF16)] * 2
        + [shape(part, BF16) for part in parts]
        + [shape(part, F32) for part in parts],
        in_specs=[SMEM] + [VMEM] * (len(stats) + 6 + len(small)),
        out_specs=[VMEM] * 8,
        scratch_shapes=[pltpu.VMEM((2, 2 * per, cols), BF16)],
        compiler_params=params(20),
        cost_estimate=cost(8 * per * depth * cols, 2 * cols * depth * 2),
        name="back_rows",
    )(at, own, other, *stats, *soft, *small)
    return got[0], got[1], got[2:5], got[5:8]


def head_kernel(rows_ref, core_ref, mine_ref, theirs_ref, out_ref):
    rows = jnp.concatenate([rows_ref[0], rows_ref[1], core_ref[0], core_ref[1]])
    grads = jnp.concatenate([mine_ref[...], theirs_ref[...]])
    out_ref[...] = lax.dot_general(
        rows, grads, (((0,), (0,)), ((), ())), preferred_element_type=F32
    ).astype(BF16)


def head_gradient(rows, core_rows, mine, theirs):
    _, per, depth = rows.shape
    cols = mine.shape[1]
    tile = 512 if depth % 512 == 0 else depth
    whole = pl.BlockSpec((2 * per, cols), lambda i: (0, 0))
    slab = pl.BlockSpec((2, per, tile), lambda i: (0, 0, i))
    return pl.pallas_call(
        head_kernel,
        grid=(depth // tile,),
        out_shape=shape((depth, cols), BF16),
        in_specs=[slab] * 2 + [whole] * 2,
        out_specs=pl.BlockSpec((tile, cols), lambda i: (i, 0)),
        compiler_params=params(6),
        cost_estimate=cost(8 * per * depth * cols, (4 * per + cols) * depth * 2),
        name="head_gradient",
    )(rows, core_rows, mine, theirs)


def body(hidden, token_ids, serving, head_weight, teacher_logits):
    groups = lax.axis_size("grp")
    shards = lax.axis_size("vocab")
    me_g = lax.axis_index("grp")
    me_v = lax.axis_index("vocab")
    per, depth = hidden.shape
    cols = head_weight.shape[1]
    owned = per // shards
    CORE, X = shards, 2 * shards
    Y, W = 1, 2
    count = groups * shards

    def swap(value, mask):
        return lax.ppermute(value, AXES, [(i, i ^ mask) for i in range(count)])

    def tie(*values):
        return lax.optimization_barrier(values)

    def ints(*values):
        return jnp.stack([jnp.asarray(v, jnp.int32) for v in values])

    quarter_rows = per * 3 // 16
    quarter = me_v & 3
    starts = [(quarter ^ k) * quarter_rows for k in range(4)]
    chip = me_g >> 1
    spots = ints(*starts)
    at = ints(
        me_v * owned, (me_g * shards + me_v) * cols, ((me_g ^ 1) * shards + me_v) * cols, me_g
    )
    who = ints(me_g, me_g & 1)
    unsigned = [
        jnp.asarray(v, jnp.uint32)
        for v in (starts[0], starts[3], 2 * chip, 2 * (chip ^ 1))
    ]
    rows, weight, spots, at, who, *unsigned = tie(hidden, head_weight, spots, at, who, *unsigned)
    zero = jnp.uint32(0)

    def cut(value, start, size, dim):
        indices = [start if d == dim else zero for d in range(value.ndim)]
        sizes = [size if d == dim else n for d, n in enumerate(value.shape)]
        return lax.dynamic_slice(value, indices, sizes)

    first = cut(rows, unsigned[0], quarter_rows, 0)
    x0 = swap(first, X)
    _, rows, weight, teacher = tie(first, rows, weight, teacher_logits)
    other_weight = swap(weight, CORE)
    x3 = swap(cut(rows, unsigned[1], quarter_rows, 0), X)
    rest = swap(rows[4 * quarter_rows :], X)
    kept = cut(teacher, unsigned[2], 2, 1).swapaxes(0, 1)
    gone = cut(teacher, unsigned[3], 2, 1).swapaxes(0, 1)
    taught = taught_stats(kept, gone)
    taught_core = swap(taught, CORE)
    x0, kept, gone, taught, taught_core, rows = tie(x0, kept, gone, taught, taught_core, rows)
    x1 = swap(x0, Y)
    x2 = swap(x0, W)
    kept_core = swap(kept, CORE)
    near_a, stats_a = near_logits(rows, weight, x0)
    near_b, stats_b = near_logits(rows, other_weight, x0)
    *pieces, gone, near_a, near_b = tie(x0, x1, x2, x3, rest, gone, near_a, near_b)
    taught_x = swap(gone, X)
    far_a, far_b, both_rows, stats, peaks = far_logits(
        spots,
        pieces,
        weight,
        other_weight,
        rows,
        stats_a,
        stats_b,
        taught,
        taught_core,
        token_ids.reshape(1, per),
    )

    served = serving.reshape(groups, 1, per)
    logits = [near_a, near_b, far_a, far_b]
    held = logits + [weight]
    mask = W
    while mask < shards:
        masks = [mask, 2 * mask, 3 * mask] if 2 * mask < shards else [mask]
        stats = merge([stats] + [swap(stats, m) for m in masks], held)
        mask *= 4
    _, taught_x = tie(stats, taught_x)
    taught_far = swap(taught_x, CORE)
    taught_soft, taught_peaks = teacher_rows(
        who, served, [kept, kept_core, taught_x, taught_far]
    )
    parts = [stats] + [swap(stats, mask) for mask in (X, Y, X + Y)]
    *parts, taught_soft, rows_sent = tie(*parts, taught_soft, both_rows)
    core_rows = swap(rows_sent, CORE)

    bits = shards.bit_length() - 1
    masks = {0: X}
    for b in range(bits):
        masks[1 + b] = shards >> (1 + b)
    ydim, wdim = bits, bits - 1
    units = depth // 128
    edges = (0, units // 3 * 128, units // 3 * 256, depth)
    orders = [(0, ydim, wdim), (ydim, wdim, 0), (wdim, 0, ydim)]
    low = owned.bit_length() - 1
    row_bit = {0: low + bits, ydim: low, wdim: low + 1}
    first_bits = tuple(row_bit[order[0]] for order in orders)
    small = (peaks, served, taught_soft, taught_peaks)
    gown, gother, sents, keeps = back_rows(
        at, weight, other_weight, parts, logits, small, first_bits, edges, low
    )
    gots = [swap(sents[p], masks[orders[p][0]]) for p in range(3)]
    theirs = swap(gother, CORE)
    grad_head = head_gradient(both_rows, core_rows, gown, theirs)
    for p in range(3):
        grad_head, gots[p] = tie(grad_head, gots[p])

    def folded(value, p):
        dims = [2] * (1 + bits)
        dims[orders[p][0]] = 1
        return value.reshape(*dims, owned, value.shape[-1])

    terms = [[folded(keeps[p], p), folded(gots[p], p)] for p in range(3)]
    for stage in (1, 2):
        sents = [
            sum(lax.index_in_dim(t, 1, orders[p][stage]).astype(F32) for t in terms[p]).astype(BF16)
            for p in range(3)
        ]
        gots = [swap(sents[p], masks[orders[p][stage]]) for p in range(3)]
        for p in range(3):
            terms[p] = [lax.index_in_dim(t, 0, orders[p][stage]) for t in terms[p]] + [gots[p]]
    for dim in range(1, wdim):
        for p in range(3):
            sent = sum(lax.index_in_dim(t, 1, dim).astype(F32) for t in terms[p]).astype(BF16)
            terms[p] = [lax.index_in_dim(t, 0, dim) for t in terms[p]] + [swap(sent, masks[dim])]
    total = jnp.concatenate([sum(t.astype(F32) for t in ts) for ts in terms], axis=-1)
    return (total.reshape(owned, depth), grad_head)


def solution(mesh):
    placed = (P("grp", None), P("grp"), P(), P(None, ("grp", "vocab")), P("grp", None, "vocab"))
    return jax.shard_map(
        body,
        mesh=mesh,
        in_specs=placed,
        out_specs=(P(("grp", "vocab"), None), P(None, ("grp", "vocab"))),
        check_vma=False,
    )
```

```python
import jax
import jax.numpy as jnp
from jax import lax
from jax.experimental import pallas as pl
from jax.experimental.pallas import tpu as pltpu
from jax.sharding import PartitionSpec as P

BF16 = jnp.bfloat16
F32 = jnp.float32
AXES = ("grp", "vocab")
VMEM = pl.BlockSpec(memory_space=pltpu.VMEM)
SMEM = pl.BlockSpec(memory_space=pltpu.SMEM)
STAT_ROWS = 8
MIB = 2**20


def params(mib):
    return pltpu.CompilerParams(vmem_limit_bytes=mib * MIB)


def cost(flops, nbytes, exps=0):
    return pl.CostEstimate(flops=flops, bytes_accessed=nbytes, transcendentals=exps)


def shape(dims, dtype):
    return jax.ShapeDtypeStruct(dims, dtype)


def columns_to_rows(columns):
    count = columns[0].shape[0]
    lane = lax.broadcasted_iota(jnp.int32, (count, 128), 1)
    wide = jnp.zeros((count, 128), F32)
    for k, column in enumerate(columns):
        wide = jnp.where(lane == k, column, wide)
    return wide.T[:STAT_ROWS]


def taught_kernel(kept_ref, gone_ref, out_ref):
    parts = [ref[c].astype(F32) for ref in (kept_ref, gone_ref) for c in range(2)]
    top = parts[0]
    for part in parts[1:]:
        top = jnp.maximum(top, part)
    peak = jnp.max(top, axis=1, keepdims=True)
    total = sum(jnp.exp((part - peak) * 0.5) for part in parts)
    out_ref[...] = columns_to_rows([peak, jnp.sum(total, axis=1, keepdims=True)])


def taught_stats(kept, gone):
    _, per, cols = kept.shape
    return pl.pallas_call(
        taught_kernel,
        out_shape=shape((STAT_ROWS, per), F32),
        in_specs=[VMEM] * 2,
        out_specs=VMEM,
        compiler_params=params(4),
        cost_estimate=cost(0, 4 * per * cols * 2, 4 * per * cols),
        name="taught_stats",
    )(kept, gone)


def teacher_kernel(at_ref, serving_ref, a0, a1, a2, a3, soft_ref, peaks_ref):
    me, core = at_ref[0], at_ref[1]
    _, per, cols = a0.shape
    for j in range(2):
        wanted = serving_ref[me ^ (2 * j)]
        sums = [0.0, 0.0]
        for k, arrived in enumerate((a0, a1, a2, a3)):
            row = lax.broadcasted_iota(jnp.int32, (per, per), 0) + (me ^ k) * per
            pick = (row == wanted).astype(BF16)
            for c in range(2):
                sums[c] += lax.dot_general(
                    pick, arrived[core ^ c], (((0,), (0,)), ((), ())), preferred_element_type=F32
                )
        peak = jnp.max(jnp.maximum(*sums), axis=1, keepdims=True)
        for c in range(2):
            soft_ref[j, :, c * cols : (c + 1) * cols] = jnp.exp((sums[c] - peak) * 0.5)
        peaks_ref[j] = columns_to_rows([peak])


def teacher_rows(at, serving, arrived):
    _, per, cols = arrived[0].shape
    return pl.pallas_call(
        teacher_kernel,
        out_shape=(shape((2, per, 2 * cols), F32), shape((2, STAT_ROWS, per), F32)),
        in_specs=[SMEM] + [VMEM] * 5,
        out_specs=(VMEM, VMEM),
        compiler_params=params(8),
        cost_estimate=cost(32 * per * per * cols, 12 * per * cols * 2, 4 * per * cols),
        name="teacher_rows",
    )(at, serving, *arrived)


def student_stats(logits):
    peak = jnp.max(logits, axis=1, keepdims=True)
    soft = jnp.exp((logits - peak) * 0.5)
    hard = jnp.sum(soft * soft, axis=1, keepdims=True)
    return soft, columns_to_rows([peak, hard, jnp.sum(soft, axis=1, keepdims=True)])


def near_kernel(rows_ref, w_ref, *refs):
    logits_ref, stats_ref = refs[-2:]
    logits = jnp.dot(rows_ref[...], w_ref[...], preferred_element_type=F32)
    logits_ref[...], stats_ref[...] = student_stats(logits)


def near_logits(rows, weight, *held):
    per, depth = rows.shape
    cols = weight.shape[1]
    return pl.pallas_call(
        near_kernel,
        out_shape=(shape((per, cols), F32), shape((STAT_ROWS, per), F32)),
        in_specs=[VMEM] * (2 + len(held)),
        out_specs=(VMEM, VMEM),
        compiler_params=params(6),
        cost_estimate=cost(2 * per * depth * cols, (per + cols) * depth * 2, per * cols),
        name="near_logits",
    )(rows, weight, *held)


NOTHING = -3.0e38


def both(a, b):
    peak = jnp.maximum(a[0:1], b[0:1])
    ea, eb = jnp.exp((a[0:1] - peak) * 0.5), jnp.exp((b[0:1] - peak) * 0.5)
    return jnp.concatenate(
        [peak, a[1:2] * (ea * ea) + b[1:2] * (eb * eb), a[2:3] * ea + b[2:3] * eb]
    )


def far_kernel(n, spots_ref, *refs):
    pieces, refs = refs[:n], refs[n:]
    own_ref, other_ref, near_ref, stats_a, stats_b, taught_ref, taught_core_ref, ids_ref = refs[:8]
    a_ref, b_ref, rows_ref, out_ref, peaks_ref, full = refs[8:]
    share = pieces[0].shape[0]
    for k, piece in enumerate(pieces[:-1]):
        full[pl.ds(pl.multiple_of(spots_ref[k], 8), share), :] = piece[...].astype(F32)
    full[4 * share :, :] = pieces[-1][...].astype(F32)
    rows_ref[0] = near_ref[...]
    rows_ref[1] = full[...].astype(BF16)
    per = rows_ref.shape[1]
    a = jnp.dot(rows_ref[1], own_ref[...], preferred_element_type=F32)
    b = jnp.dot(rows_ref[1], other_ref[...], preferred_element_type=F32)
    a_ref[...], a = student_stats(a)
    b_ref[...], b = student_stats(b)
    peaks_ref[...] = jnp.concatenate(
        [stats_a[0:1], stats_b[0:1], a[0:1], b[0:1], jnp.zeros((STAT_ROWS - 4, per), F32)]
    )
    out_ref[0, 0:3, :] = both(stats_a[...], stats_b[...])
    out_ref[0, 3:4, :] = ids_ref[...].astype(F32)
    out_ref[0, 4:6, :] = taught_ref[0:2, :]
    out_ref[0, 6:8, :] = taught_core_ref[0:2, :]
    out_ref[1, 0:3, :] = both(a, b)
    row = lax.broadcasted_iota(jnp.int32, (5, per), 0)
    out_ref[1, 3:8, :] = jnp.where((row == 1) | (row == 3), NOTHING, 0.0)


def far_logits(spots, pieces, own, other, *small):
    depth, cols = own.shape
    per = sum(piece.shape[0] for piece in pieces)
    return pl.pallas_call(
        lambda *refs: far_kernel(len(pieces), *refs),
        out_shape=(
            shape((per, cols), F32),
            shape((per, cols), F32),
            shape((2, per, depth), BF16),
            shape((2, STAT_ROWS, per), F32),
            shape((STAT_ROWS, per), F32),
        ),
        in_specs=[SMEM] + [VMEM] * (len(pieces) + 2 + len(small)),
        out_specs=(VMEM,) * 5,
        scratch_shapes=[pltpu.VMEM((per, depth), F32)],
        compiler_params=params(16),
        cost_estimate=cost(4 * per * depth * cols, (per + 2 * cols) * depth * 2, 2 * per * cols),
        name="far_logits",
    )(spots, *pieces, own, other, *small)


def merged(parts):
    top = parts[0]
    for part in parts[1:]:
        top = jnp.maximum(top, part)
    hard = soft = taught0 = taught1 = 0.0
    for part in parts:
        shrink = jnp.exp((part - top) * 0.5)
        s = shrink[0:1]
        hard += part[1:2] * (s * s)
        soft += part[2:3] * s
        taught0 += part[5:6] * shrink[4:5]
        taught1 += part[7:8] * shrink[6:7]
    return top[0:1], hard, soft, top[3:4], top[4:5], taught0, top[6:7], taught1


def merge_kernel(n, *refs):
    out_ref = refs[-1]
    for j in range(2):
        out_ref[j] = jnp.concatenate(merged([ref[j] for ref in refs[:n]]))


def merge(parts, held):
    return pl.pallas_call(
        lambda *refs: merge_kernel(len(parts), *refs),
        out_shape=shape(parts[0].shape, F32),
        in_specs=[VMEM] * (len(parts) + len(held)),
        out_specs=VMEM,
        compiler_params=params(6),
        cost_estimate=cost(0, 5 * parts[0].size * 4),
        name="merge_stats",
    )(*parts, *held)


def picker(bit, flip, total):
    half = total // 2
    row = lax.broadcasted_iota(jnp.int32, (total, total), 0)
    side = jnp.where(row < half, 1 << bit, 0)
    row = row & (half - 1)
    row = ((row >> bit) << (bit + 1)) + side + (row & ((1 << bit) - 1))
    return (lax.broadcasted_iota(jnp.int32, (total, total), 1) == (row ^ flip)).astype(BF16)


def grads_kernel(n, at_ref, *refs):
    stats_refs, refs = refs[:n], refs[n:]
    soft_refs, (peaks_ref, serving_ref, taught_ref, tpeaks_ref), g_refs = refs[:4], refs[4:8], refs[8:]
    me = at_ref[3]
    per, cols = soft_refs[0].shape
    stats = [merged([ref[j ^ (i & 1)] for i, ref in enumerate(stats_refs)]) for j in range(2)]
    lane = lax.broadcasted_iota(jnp.int32, (per, per), 1)
    for j in range(2):
        rows = stats[j][:4] + (
            serving_ref[me ^ (2 * j)].astype(F32),
            tpeaks_ref[j, 0:1, :],
            peaks_ref[2 * j : 2 * j + 2, :],
        )
        columns = jnp.concatenate(rows + (jnp.zeros((128 - 8, per), F32),)).T
        peak, hard, soft, ids, wanted, tlocal, *local = [columns[:, i : i + 1] for i in range(8)]
        ids, wanted = ids.astype(jnp.int32), wanted.astype(jnp.int32)
        tpeak = total = 0.0
        for k in range(4):
            here = wanted - (me ^ k) * per == lane
            taught = stats[k // 2][4 + 2 * (k % 2) : 6 + 2 * (k % 2)]
            tpeak += jnp.where(here, taught[0], 0.0)
            total += jnp.where(here, taught[1], 0.0)
        tpeak = jnp.sum(tpeak, axis=1, keepdims=True)
        total = jnp.sum(total, axis=1, keepdims=True)
        teach = jnp.exp((tlocal - tpeak) * 0.5) * (32.0 / total)
        hard, soft = 16.0 / hard, 32.0 / soft
        for c, g_ref in enumerate(g_refs):
            part = slice(c * cols, (c + 1) * cols)
            column = at_ref[1 + c] + lax.broadcasted_iota(jnp.int32, (per, cols), 1)
            scale = jnp.exp((local[c] - peak) * 0.5)
            own = soft_refs[2 * j + c][...]
            label = jnp.where(column == ids, 16.0, 0.0)
            grad = own * (scale * soft + own * (scale * scale * hard)) - taught_ref[j, :, part] * teach
            g_ref[j * per : (j + 1) * per, :] = (grad - label).astype(BF16)


def back_kernel(bits, edges, low, n, at_ref, *refs):
    w_refs, refs, mixed = refs[:2], refs[2:-1], refs[-1]
    g_refs, send_refs, keep_refs = refs[-8:-6], refs[-6:-3], refs[-3:]
    grads_kernel(n, at_ref, *refs[:-6])
    total = mixed.shape[1]
    per = total // 2
    aligned = (1 << low) % 16 == 0
    if aligned:
        row = lax.broadcasted_iota(jnp.int32, (total, total), 0)
        turn = lax.broadcasted_iota(jnp.int32, (total, total), 1) == (row ^ at_ref[0])
        for c, g_ref in enumerate(g_refs):
            mixed[c] = jnp.dot(turn.astype(BF16), g_ref[...], preferred_element_type=F32).astype(BF16)
    for p in range(3):
        back = 0.0
        for c, (g_ref, w_ref) in enumerate(zip(g_refs, w_refs)):
            if aligned:
                run = 1 << bits[p]
                starts = [i for side in (run, 0) for i in range(side, total, 2 * run)]
                rows = jnp.concatenate([mixed[c, i : i + run, :] for i in starts])
            else:
                pick = picker(bits[p], at_ref[0], total)
                rows = jnp.dot(pick, g_ref[...], preferred_element_type=F32).astype(BF16)
            back += lax.dot_general(
                w_ref[edges[p] : edges[p + 1], :],
                rows,
                (((1,), (1,)), ((), ())),
                preferred_element_type=F32,
            )
        back = back.T
        send_refs[p][...] = back[:per].astype(BF16)
        keep_refs[p][...] = back[per:]


def back_rows(at, own, other, stats, soft, small, bits, edges, low):
    depth, cols = own.shape
    per = soft[0].shape[0]
    parts = [(per, edges[p + 1] - edges[p]) for p in range(3)]
    got = pl.pallas_call(
        lambda *refs: back_kernel(bits, edges, low, len(stats), *refs),
        out_shape=[shape((2 * per, cols), BF16)] * 2
        + [shape(part, BF16) for part in parts]
        + [shape(part, F32) for part in parts],
        in_specs=[SMEM] + [VMEM] * (len(stats) + 6 + len(small)),
        out_specs=[VMEM] * 8,
        scratch_shapes=[pltpu.VMEM((2, 2 * per, cols), BF16)],
        compiler_params=params(20),
        cost_estimate=cost(8 * per * depth * cols, 2 * cols * depth * 2),
        name="back_rows",
    )(at, own, other, *stats, *soft, *small)
    return got[0], got[1], got[2:5], got[5:8]


def head_kernel(rows_ref, core_ref, mine_ref, theirs_ref, out_ref):
    rows = jnp.concatenate([rows_ref[0], rows_ref[1], core_ref[0], core_ref[1]])
    grads = jnp.concatenate([mine_ref[...], theirs_ref[...]])
    out_ref[...] = lax.dot_general(
        rows, grads, (((0,), (0,)), ((), ())), preferred_element_type=F32
    ).astype(BF16)


def head_gradient(rows, core_rows, mine, theirs):
    _, per, depth = rows.shape
    cols = mine.shape[1]
    tile = 512 if depth % 512 == 0 else depth
    whole = pl.BlockSpec((2 * per, cols), lambda i: (0, 0))
    slab = pl.BlockSpec((2, per, tile), lambda i: (0, 0, i))
    return pl.pallas_call(
        head_kernel,
        grid=(depth // tile,),
        out_shape=shape((depth, cols), BF16),
        in_specs=[slab] * 2 + [whole] * 2,
        out_specs=pl.BlockSpec((tile, cols), lambda i: (i, 0)),
        compiler_params=params(6),
        cost_estimate=cost(8 * per * depth * cols, (4 * per + cols) * depth * 2),
        name="head_gradient",
    )(rows, core_rows, mine, theirs)


def body(hidden, token_ids, serving, head_weight, teacher_logits):
    groups = lax.axis_size("grp")
    shards = lax.axis_size("vocab")
    me_g = lax.axis_index("grp")
    me_v = lax.axis_index("vocab")
    per, depth = hidden.shape
    cols = head_weight.shape[1]
    owned = per // shards
    CORE, X = shards, 2 * shards
    Y, W = 1, 2
    count = groups * shards

    def swap(value, mask):
        return lax.ppermute(value, AXES, [(i, i ^ mask) for i in range(count)])

    def tie(*values):
        return lax.optimization_barrier(values)

    def ints(*values):
        return jnp.stack([jnp.asarray(v, jnp.int32) for v in values])

    quarter_rows = per * 3 // 16
    quarter = me_v & 3
    starts = [(quarter ^ k) * quarter_rows for k in range(4)]
    chip = me_g >> 1
    spots = ints(*starts)
    at = ints(
        me_v * owned, (me_g * shards + me_v) * cols, ((me_g ^ 1) * shards + me_v) * cols, me_g
    )
    who = ints(me_g, me_g & 1)
    unsigned = [
        jnp.asarray(v, jnp.uint32)
        for v in (starts[0], starts[3], 2 * chip, 2 * (chip ^ 1))
    ]
    rows, weight, spots, at, who, *unsigned = tie(hidden, head_weight, spots, at, who, *unsigned)
    zero = jnp.uint32(0)

    def cut(value, start, size, dim):
        indices = [start if d == dim else zero for d in range(value.ndim)]
        sizes = [size if d == dim else n for d, n in enumerate(value.shape)]
        return lax.dynamic_slice(value, indices, sizes)

    first = cut(rows, unsigned[0], quarter_rows, 0)
    x0 = swap(first, X)
    _, rows, weight, teacher = tie(first, rows, weight, teacher_logits)
    other_weight = swap(weight, CORE)
    x3 = swap(cut(rows, unsigned[1], quarter_rows, 0), X)
    rest = swap(rows[4 * quarter_rows :], X)
    kept = cut(teacher, unsigned[2], 2, 1).swapaxes(0, 1)
    gone = cut(teacher, unsigned[3], 2, 1).swapaxes(0, 1)
    taught = taught_stats(kept, gone)
    taught_core = swap(taught, CORE)
    x0, kept, gone, taught, taught_core, rows = tie(x0, kept, gone, taught, taught_core, rows)
    x1 = swap(x0, Y)
    x2 = swap(x0, W)
    kept_core = swap(kept, CORE)
    near_a, stats_a = near_logits(rows, weight, x0)
    near_b, stats_b = near_logits(rows, other_weight, x0)
    *pieces, gone, near_a, near_b = tie(x0, x1, x2, x3, rest, gone, near_a, near_b)
    taught_x = swap(gone, X)
    far_a, far_b, both_rows, stats, peaks = far_logits(
        spots,
        pieces,
        weight,
        other_weight,
        rows,
        stats_a,
        stats_b,
        taught,
        taught_core,
        token_ids.reshape(1, per),
    )

    served = serving.reshape(groups, 1, per)
    logits = [near_a, near_b, far_a, far_b]
    held = logits + [weight]
    mask = W
    while mask < shards:
        masks = [mask, 2 * mask, 3 * mask] if 2 * mask < shards else [mask]
        stats = merge([stats] + [swap(stats, m) for m in masks], held)
        mask *= 4
    _, taught_x = tie(stats, taught_x)
    taught_far = swap(taught_x, CORE)
    taught_soft, taught_peaks = teacher_rows(
        who, served, [kept, kept_core, taught_x, taught_far]
    )
    parts = [stats] + [swap(stats, mask) for mask in (X, Y, X + Y)]

    bits = shards.bit_length() - 1
    masks = {0: X}
    for b in range(bits):
        masks[1 + b] = shards >> (1 + b)
    ydim, wdim = bits, bits - 1
    third = depth // 128 // 3 * 128
    edges = (0, third, 2 * third, depth)
    rest = tuple(range(1, wdim))
    orders = [(0, ydim, wdim) + rest, (ydim, wdim, 0) + rest, (wdim, 0) + rest + (ydim,)]
    low = owned.bit_length() - 1
    row_bit = {0: low + bits, ydim: low, wdim: low + 1}
    first_bits = tuple(row_bit[order[0]] for order in orders)
    small = (peaks, served, taught_soft, taught_peaks)
    gown, gother, sents, keeps = back_rows(
        at, weight, other_weight, parts, logits, small, first_bits, edges, low
    )
    gots = [swap(sents[p], masks[orders[p][0]]) for p in range(3)]
    theirs = swap(gother, CORE)
    _, rows_sent = tie(gother, both_rows)
    grad_head = head_gradient(both_rows, swap(rows_sent, CORE), gown, theirs)
    for p in range(3):
        grad_head, gots[p] = tie(grad_head, gots[p])

    def folded(value, p):
        dims = [2] * (1 + bits)
        dims[orders[p][0]] = 1
        return value.reshape(*dims, owned, value.shape[-1])

    terms = [[folded(keeps[p], p), folded(gots[p], p)] for p in range(3)]
    for stage in range(1, 1 + bits):
        for p in range(3):
            dim = orders[p][stage]
            sent = sum(lax.index_in_dim(t, 1, dim).astype(F32) for t in terms[p]).astype(BF16)
            terms[p] = [lax.index_in_dim(t, 0, dim) for t in terms[p]] + [swap(sent, masks[dim])]
    total = jnp.concatenate([sum(t.astype(F32) for t in ts) for ts in terms], axis=-1)
    return (total.reshape(owned, depth), grad_head)


def solution(mesh):
    placed = (P("grp", None), P("grp"), P(), P(None, ("grp", "vocab")), P("grp", None, "vocab"))
    return jax.shard_map(
        body,
        mesh=mesh,
        in_specs=placed,
        out_specs=(P(("grp", "vocab"), None), P(None, ("grp", "vocab"))),
        check_vma=False,
    )
```

```python
import jax
import jax.numpy as jnp
from jax import lax
from jax.experimental import pallas as pl
from jax.experimental.pallas import tpu as pltpu
from jax.sharding import PartitionSpec as P

BF16 = jnp.bfloat16
F32 = jnp.float32
AXES = ("grp", "vocab")
VMEM = pl.BlockSpec(memory_space=pltpu.VMEM)
SMEM = pl.BlockSpec(memory_space=pltpu.SMEM)
STAT_ROWS = 8
MIB = 2**20


def params(mib):
    return pltpu.CompilerParams(vmem_limit_bytes=mib * MIB)


def cost(flops, nbytes, exps=0):
    return pl.CostEstimate(flops=flops, bytes_accessed=nbytes, transcendentals=exps)


def shape(dims, dtype):
    return jax.ShapeDtypeStruct(dims, dtype)


def columns_to_rows(columns):
    count = columns[0].shape[0]
    lane = lax.broadcasted_iota(jnp.int32, (count, 128), 1)
    wide = jnp.zeros((count, 128), F32)
    for k, column in enumerate(columns):
        wide = jnp.where(lane == k, column, wide)
    return wide.T[:STAT_ROWS]


def taught_kernel(kept_ref, gone_ref, out_ref):
    parts = [ref[c].astype(F32) for ref in (kept_ref, gone_ref) for c in range(2)]
    top = parts[0]
    for part in parts[1:]:
        top = jnp.maximum(top, part)
    peak = jnp.max(top, axis=1, keepdims=True)
    total = sum(jnp.exp((part - peak) * 0.5) for part in parts)
    out_ref[...] = columns_to_rows([peak, jnp.sum(total, axis=1, keepdims=True)])


def taught_stats(kept, gone):
    _, per, cols = kept.shape
    return pl.pallas_call(
        taught_kernel,
        out_shape=shape((STAT_ROWS, per), F32),
        in_specs=[VMEM] * 2,
        out_specs=VMEM,
        compiler_params=params(4),
        cost_estimate=cost(0, 4 * per * cols * 2, 4 * per * cols),
        name="taught_stats",
    )(kept, gone)


def teacher_kernel(at_ref, serving_ref, a0, a1, a2, a3, soft_ref, peaks_ref):
    me, core = at_ref[0], at_ref[1]
    _, per, cols = a0.shape
    for j in range(2):
        wanted = serving_ref[me ^ (2 * j)]
        sums = [0.0, 0.0]
        for k, arrived in enumerate((a0, a1, a2, a3)):
            row = lax.broadcasted_iota(jnp.int32, (per, per), 0) + (me ^ k) * per
            pick = (row == wanted).astype(BF16)
            for c in range(2):
                sums[c] += lax.dot_general(
                    pick, arrived[core ^ c], (((0,), (0,)), ((), ())), preferred_element_type=F32
                )
        peak = jnp.max(jnp.maximum(*sums), axis=1, keepdims=True)
        for c in range(2):
            soft_ref[j, :, c * cols : (c + 1) * cols] = jnp.exp((sums[c] - peak) * 0.5)
        peaks_ref[j] = columns_to_rows([peak])


def teacher_rows(at, serving, arrived):
    _, per, cols = arrived[0].shape
    return pl.pallas_call(
        teacher_kernel,
        out_shape=(shape((2, per, 2 * cols), F32), shape((2, STAT_ROWS, per), F32)),
        in_specs=[SMEM] + [VMEM] * 5,
        out_specs=(VMEM, VMEM),
        compiler_params=params(8),
        cost_estimate=cost(32 * per * per * cols, 12 * per * cols * 2, 4 * per * cols),
        name="teacher_rows",
    )(at, serving, *arrived)


def student_stats(logits):
    peak = jnp.max(logits, axis=1, keepdims=True)
    soft = jnp.exp((logits - peak) * 0.5)
    hard = jnp.sum(soft * soft, axis=1, keepdims=True)
    return soft, columns_to_rows([peak, hard, jnp.sum(soft, axis=1, keepdims=True)])


def near_kernel(rows_ref, w_ref, *refs):
    logits_ref, stats_ref = refs[-2:]
    logits = jnp.dot(rows_ref[...], w_ref[...], preferred_element_type=F32)
    logits_ref[...], stats_ref[...] = student_stats(logits)


def near_logits(rows, weight, *held):
    per, depth = rows.shape
    cols = weight.shape[1]
    return pl.pallas_call(
        near_kernel,
        out_shape=(shape((per, cols), F32), shape((STAT_ROWS, per), F32)),
        in_specs=[VMEM] * (2 + len(held)),
        out_specs=(VMEM, VMEM),
        compiler_params=params(6),
        cost_estimate=cost(2 * per * depth * cols, (per + cols) * depth * 2, per * cols),
        name="near_logits",
    )(rows, weight, *held)


NOTHING = -3.0e38


def both(a, b):
    peak = jnp.maximum(a[0:1], b[0:1])
    ea, eb = jnp.exp((a[0:1] - peak) * 0.5), jnp.exp((b[0:1] - peak) * 0.5)
    return jnp.concatenate(
        [peak, a[1:2] * (ea * ea) + b[1:2] * (eb * eb), a[2:3] * ea + b[2:3] * eb]
    )


def far_kernel(n, spots_ref, *refs):
    pieces, refs = refs[:n], refs[n:]
    own_ref, other_ref, near_ref, stats_a, stats_b, taught_ref, taught_core_ref, ids_ref = refs[:8]
    a_ref, b_ref, rows_ref, out_ref, peaks_ref, full = refs[8:]
    share = pieces[0].shape[0]
    for k, piece in enumerate(pieces[:-1]):
        full[pl.ds(pl.multiple_of(spots_ref[k], 8), share), :] = piece[...].astype(F32)
    full[4 * share :, :] = pieces[-1][...].astype(F32)
    rows_ref[0] = near_ref[...]
    rows_ref[1] = full[...].astype(BF16)
    per = rows_ref.shape[1]
    a = jnp.dot(rows_ref[1], own_ref[...], preferred_element_type=F32)
    b = jnp.dot(rows_ref[1], other_ref[...], preferred_element_type=F32)
    a_ref[...], a = student_stats(a)
    b_ref[...], b = student_stats(b)
    peaks_ref[...] = jnp.concatenate(
        [stats_a[0:1], stats_b[0:1], a[0:1], b[0:1], jnp.zeros((STAT_ROWS - 4, per), F32)]
    )
    out_ref[0, 0:3, :] = both(stats_a[...], stats_b[...])
    out_ref[0, 3:4, :] = ids_ref[...].astype(F32)
    out_ref[0, 4:6, :] = taught_ref[0:2, :]
    out_ref[0, 6:8, :] = taught_core_ref[0:2, :]
    out_ref[1, 0:3, :] = both(a, b)
    row = lax.broadcasted_iota(jnp.int32, (5, per), 0)
    out_ref[1, 3:8, :] = jnp.where((row == 1) | (row == 3), NOTHING, 0.0)


def far_logits(spots, pieces, own, other, *small):
    depth, cols = own.shape
    per = sum(piece.shape[0] for piece in pieces)
    return pl.pallas_call(
        lambda *refs: far_kernel(len(pieces), *refs),
        out_shape=(
            shape((per, cols), F32),
            shape((per, cols), F32),
            shape((2, per, depth), BF16),
            shape((2, STAT_ROWS, per), F32),
            shape((STAT_ROWS, per), F32),
        ),
        in_specs=[SMEM] + [VMEM] * (len(pieces) + 2 + len(small)),
        out_specs=(VMEM,) * 5,
        scratch_shapes=[pltpu.VMEM((per, depth), F32)],
        compiler_params=params(16),
        cost_estimate=cost(4 * per * depth * cols, (per + 2 * cols) * depth * 2, 2 * per * cols),
        name="far_logits",
    )(spots, *pieces, own, other, *small)


def merged(parts):
    top = parts[0]
    for part in parts[1:]:
        top = jnp.maximum(top, part)
    hard = soft = taught0 = taught1 = 0.0
    for part in parts:
        shrink = jnp.exp((part - top) * 0.5)
        s = shrink[0:1]
        hard += part[1:2] * (s * s)
        soft += part[2:3] * s
        taught0 += part[5:6] * shrink[4:5]
        taught1 += part[7:8] * shrink[6:7]
    return top[0:1], hard, soft, top[3:4], top[4:5], taught0, top[6:7], taught1


def merge_kernel(n, *refs):
    out_ref = refs[-1]
    for j in range(2):
        out_ref[j] = jnp.concatenate(merged([ref[j] for ref in refs[:n]]))


def merge(parts, held):
    return pl.pallas_call(
        lambda *refs: merge_kernel(len(parts), *refs),
        out_shape=shape(parts[0].shape, F32),
        in_specs=[VMEM] * (len(parts) + len(held)),
        out_specs=VMEM,
        compiler_params=params(6),
        cost_estimate=cost(0, 5 * parts[0].size * 4),
        name="merge_stats",
    )(*parts, *held)


def picker(bit, flip, total):
    half = total // 2
    row = lax.broadcasted_iota(jnp.int32, (total, total), 0)
    side = jnp.where(row < half, 1 << bit, 0)
    row = row & (half - 1)
    row = ((row >> bit) << (bit + 1)) + side + (row & ((1 << bit) - 1))
    return (lax.broadcasted_iota(jnp.int32, (total, total), 1) == (row ^ flip)).astype(BF16)


def grads_kernel(n, at_ref, *refs):
    stats_refs, refs = refs[:n], refs[n:]
    soft_refs, (peaks_ref, serving_ref, taught_ref, tpeaks_ref), g_refs = refs[:4], refs[4:8], refs[8:]
    me = at_ref[3]
    per, cols = soft_refs[0].shape
    stats = [merged([ref[j ^ (i & 1)] for i, ref in enumerate(stats_refs)]) for j in range(2)]
    lane = lax.broadcasted_iota(jnp.int32, (per, per), 1)
    for j in range(2):
        rows = stats[j][:4] + (
            serving_ref[me ^ (2 * j)].astype(F32),
            tpeaks_ref[j, 0:1, :],
            peaks_ref[2 * j : 2 * j + 2, :],
        )
        columns = jnp.concatenate(rows + (jnp.zeros((128 - 8, per), F32),)).T
        peak, hard, soft, ids, wanted, tlocal, *local = [columns[:, i : i + 1] for i in range(8)]
        ids, wanted = ids.astype(jnp.int32), wanted.astype(jnp.int32)
        tpeak = total = 0.0
        for k in range(4):
            here = wanted - (me ^ k) * per == lane
            taught = stats[k // 2][4 + 2 * (k % 2) : 6 + 2 * (k % 2)]
            tpeak += jnp.where(here, taught[0], 0.0)
            total += jnp.where(here, taught[1], 0.0)
        tpeak = jnp.sum(tpeak, axis=1, keepdims=True)
        total = jnp.sum(total, axis=1, keepdims=True)
        teach = jnp.exp((tlocal - tpeak) * 0.5) * (32.0 / total)
        hard, soft = 16.0 / hard, 32.0 / soft
        for c, g_ref in enumerate(g_refs):
            part = slice(c * cols, (c + 1) * cols)
            column = at_ref[1 + c] + lax.broadcasted_iota(jnp.int32, (per, cols), 1)
            scale = jnp.exp((local[c] - peak) * 0.5)
            own = soft_refs[2 * j + c][...]
            label = jnp.where(column == ids, 16.0, 0.0)
            grad = own * (scale * soft + own * (scale * scale * hard)) - taught_ref[j, :, part] * teach
            g_ref[j * per : (j + 1) * per, :] = (grad - label).astype(BF16)


def back_kernel(bits, edges, low, n, at_ref, *refs):
    w_refs, refs, mixed = refs[:2], refs[2:-1], refs[-1]
    g_refs, send_refs, keep_refs = refs[-8:-6], refs[-6:-3], refs[-3:]
    grads_kernel(n, at_ref, *refs[:-6])
    total = mixed.shape[1]
    per = total // 2
    aligned = (1 << low) % 16 == 0
    if aligned:
        row = lax.broadcasted_iota(jnp.int32, (total, total), 0)
        turn = lax.broadcasted_iota(jnp.int32, (total, total), 1) == (row ^ at_ref[0])
        for c, g_ref in enumerate(g_refs):
            mixed[c] = jnp.dot(turn.astype(BF16), g_ref[...], preferred_element_type=F32).astype(BF16)
    for p in range(3):
        back = 0.0
        for c, (g_ref, w_ref) in enumerate(zip(g_refs, w_refs)):
            if aligned:
                run = 1 << bits[p]
                starts = [i for side in (run, 0) for i in range(side, total, 2 * run)]
                rows = jnp.concatenate([mixed[c, i : i + run, :] for i in starts])
            else:
                pick = picker(bits[p], at_ref[0], total)
                rows = jnp.dot(pick, g_ref[...], preferred_element_type=F32).astype(BF16)
            back += lax.dot_general(
                w_ref[edges[p] : edges[p + 1], :],
                rows,
                (((1,), (1,)), ((), ())),
                preferred_element_type=F32,
            )
        back = back.T
        send_refs[p][...] = back[:per].astype(BF16)
        keep_refs[p][...] = back[per:]


def back_rows(at, own, other, stats, soft, small, bits, edges, low):
    depth, cols = own.shape
    per = soft[0].shape[0]
    parts = [(per, edges[p + 1] - edges[p]) for p in range(3)]
    got = pl.pallas_call(
        lambda *refs: back_kernel(bits, edges, low, len(stats), *refs),
        out_shape=[shape((2 * per, cols), BF16)] * 2
        + [shape(part, BF16) for part in parts]
        + [shape(part, F32) for part in parts],
        in_specs=[SMEM] + [VMEM] * (len(stats) + 6 + len(small)),
        out_specs=[VMEM] * 8,
        scratch_shapes=[pltpu.VMEM((2, 2 * per, cols), BF16)],
        compiler_params=params(20),
        cost_estimate=cost(8 * per * depth * cols, 2 * cols * depth * 2),
        name="back_rows",
    )(at, own, other, *stats, *soft, *small)
    return got[0], got[1], got[2:5], got[5:8]


def head_kernel(rows_ref, core_ref, mine_ref, theirs_ref, out_ref):
    rows = jnp.concatenate([rows_ref[0], rows_ref[1], core_ref[0], core_ref[1]])
    grads = jnp.concatenate([mine_ref[...], theirs_ref[...]])
    out_ref[...] = lax.dot_general(
        rows, grads, (((0,), (0,)), ((), ())), preferred_element_type=F32
    ).astype(BF16)


def head_gradient(rows, core_rows, mine, theirs):
    _, per, depth = rows.shape
    cols = mine.shape[1]
    tile = 512 if depth % 512 == 0 else depth
    whole = pl.BlockSpec((2 * per, cols), lambda i: (0, 0))
    slab = pl.BlockSpec((2, per, tile), lambda i: (0, 0, i))
    return pl.pallas_call(
        head_kernel,
        grid=(depth // tile,),
        out_shape=shape((depth, cols), BF16),
        in_specs=[slab] * 2 + [whole] * 2,
        out_specs=pl.BlockSpec((tile, cols), lambda i: (i, 0)),
        compiler_params=pltpu.CompilerParams(
            vmem_limit_bytes=6 * MIB, fuse_transposed_lhs_in_matmul=True
        ),
        cost_estimate=cost(8 * per * depth * cols, (4 * per + cols) * depth * 2),
        name="head_gradient",
    )(rows, core_rows, mine, theirs)


def body(hidden, token_ids, serving, head_weight, teacher_logits):
    groups = lax.axis_size("grp")
    shards = lax.axis_size("vocab")
    me_g = lax.axis_index("grp")
    me_v = lax.axis_index("vocab")
    per, depth = hidden.shape
    cols = head_weight.shape[1]
    owned = per // shards
    CORE, X = shards, 2 * shards
    Y, W = 1, 2
    count = groups * shards

    def swap(value, mask):
        return lax.ppermute(value, AXES, [(i, i ^ mask) for i in range(count)])

    def tie(*values):
        return lax.optimization_barrier(values)

    def ints(*values):
        return jnp.stack([jnp.asarray(v, jnp.int32) for v in values])

    quarter_rows = per * 3 // 16
    quarter = me_v & 3
    starts = [(quarter ^ k) * quarter_rows for k in range(4)]
    chip = me_g >> 1
    spots = ints(*starts)
    at = ints(
        me_v * owned, (me_g * shards + me_v) * cols, ((me_g ^ 1) * shards + me_v) * cols, me_g
    )
    who = ints(me_g, me_g & 1)
    unsigned = [
        jnp.asarray(v, jnp.uint32)
        for v in (starts[0], starts[3], 2 * chip, 2 * (chip ^ 1))
    ]
    rows, weight, spots, at, who, *unsigned = tie(hidden, head_weight, spots, at, who, *unsigned)
    zero = jnp.uint32(0)

    def cut(value, start, size, dim):
        indices = [start if d == dim else zero for d in range(value.ndim)]
        sizes = [size if d == dim else n for d, n in enumerate(value.shape)]
        return lax.dynamic_slice(value, indices, sizes)

    first = cut(rows, unsigned[0], quarter_rows, 0)
    x0 = swap(first, X)
    _, rows, weight, teacher = tie(first, rows, weight, teacher_logits)
    other_weight = swap(weight, CORE)
    x3 = swap(cut(rows, unsigned[1], quarter_rows, 0), X)
    rest = swap(rows[4 * quarter_rows :], X)
    kept = cut(teacher, unsigned[2], 2, 1).swapaxes(0, 1)
    gone = cut(teacher, unsigned[3], 2, 1).swapaxes(0, 1)
    taught = taught_stats(kept, gone)
    taught_core = swap(taught, CORE)
    x0, kept, gone, taught, taught_core, rows = tie(x0, kept, gone, taught, taught_core, rows)
    x1 = swap(x0, Y)
    x2 = swap(x0, W)
    kept_core = swap(kept, CORE)
    near_a, stats_a = near_logits(rows, weight, x0)
    near_b, stats_b = near_logits(rows, other_weight, x0)
    *pieces, gone, near_a, near_b = tie(x0, x1, x2, x3, rest, gone, near_a, near_b)
    taught_x = swap(gone, X)
    far_a, far_b, both_rows, stats, peaks = far_logits(
        spots,
        pieces,
        weight,
        other_weight,
        rows,
        stats_a,
        stats_b,
        taught,
        taught_core,
        token_ids.reshape(1, per),
    )

    served = serving.reshape(groups, 1, per)
    logits = [near_a, near_b, far_a, far_b]
    held = logits + [weight]
    mask = W
    while mask < shards:
        masks = [mask, 2 * mask, 3 * mask] if 2 * mask < shards else [mask]
        stats = merge([stats] + [swap(stats, m) for m in masks], held)
        mask *= 4
    _, taught_x = tie(stats, taught_x)
    taught_far = swap(taught_x, CORE)
    taught_soft, taught_peaks = teacher_rows(
        who, served, [kept, kept_core, taught_x, taught_far]
    )
    parts = [stats] + [swap(stats, mask) for mask in (X, Y, X + Y)]

    bits = shards.bit_length() - 1
    masks = {0: X}
    for b in range(bits):
        masks[1 + b] = shards >> (1 + b)
    ydim, wdim = bits, bits - 1
    third = depth // 128 // 3 * 128
    edges = (0, depth - 2 * third, depth - third, depth)
    orders = [(0, ydim, wdim), (ydim, wdim, 0), (wdim, 0, ydim)]
    low = owned.bit_length() - 1
    row_bit = {0: low + bits, ydim: low, wdim: low + 1}
    first_bits = tuple(row_bit[order[0]] for order in orders)
    small = (peaks, served, taught_soft, taught_peaks)
    gown, gother, sents, keeps = back_rows(
        at, weight, other_weight, parts, logits, small, first_bits, edges, low
    )
    gots = [swap(sents[p], masks[orders[p][0]]) for p in range(3)]
    theirs = swap(gother, CORE)
    _, rows_sent = tie(gother, both_rows)
    grad_head = head_gradient(both_rows, swap(rows_sent, CORE), gown, theirs)
    for p in range(3):
        grad_head, gots[p] = tie(grad_head, gots[p])

    def folded(value, p):
        dims = [2] * (1 + bits)
        dims[orders[p][0]] = 1
        return value.reshape(*dims, owned, value.shape[-1])

    terms = [[folded(keeps[p], p), folded(gots[p], p)] for p in range(3)]
    for stage in (1, 2):
        sents = [
            sum(lax.index_in_dim(t, 1, orders[p][stage]).astype(F32) for t in terms[p]).astype(BF16)
            for p in range(3)
        ]
        gots = [swap(sents[p], masks[orders[p][stage]]) for p in range(3)]
        for p in range(3):
            terms[p] = [lax.index_in_dim(t, 0, orders[p][stage]) for t in terms[p]] + [gots[p]]
    for dim in range(1, wdim):
        for p in range(3):
            sent = sum(lax.index_in_dim(t, 1, dim).astype(F32) for t in terms[p]).astype(BF16)
            terms[p] = [lax.index_in_dim(t, 0, dim) for t in terms[p]] + [swap(sent, masks[dim])]
    total = jnp.concatenate([sum(t.astype(F32) for t in ts) for ts in terms], axis=-1)
    return (total.reshape(owned, depth), grad_head)


def solution(mesh):
    placed = (P("grp", None), P("grp"), P(), P(None, ("grp", "vocab")), P("grp", None, "vocab"))
    return jax.shard_map(
        body,
        mesh=mesh,
        in_specs=placed,
        out_specs=(P(("grp", "vocab"), None), P(None, ("grp", "vocab"))),
        check_vma=False,
    )
```

```python
import jax
import jax.numpy as jnp
from jax import lax
from jax.experimental import pallas as pl
from jax.experimental.pallas import tpu as pltpu
from jax.sharding import PartitionSpec as P

BF16 = jnp.bfloat16
F32 = jnp.float32
AXES = ("grp", "vocab")
VMEM = pl.BlockSpec(memory_space=pltpu.VMEM)
SMEM = pl.BlockSpec(memory_space=pltpu.SMEM)
STAT_ROWS = 8
MIB = 2**20


def params(mib):
    return pltpu.CompilerParams(vmem_limit_bytes=mib * MIB)


def cost(flops, nbytes, exps=0):
    return pl.CostEstimate(flops=flops, bytes_accessed=nbytes, transcendentals=exps)


def shape(dims, dtype):
    return jax.ShapeDtypeStruct(dims, dtype)


def columns_to_rows(columns):
    count = columns[0].shape[0]
    lane = lax.broadcasted_iota(jnp.int32, (count, 128), 1)
    wide = jnp.zeros((count, 128), F32)
    for k, column in enumerate(columns):
        wide = jnp.where(lane == k, column, wide)
    return wide.T[:STAT_ROWS]


def taught_kernel(kept_ref, gone_ref, out_ref):
    parts = [ref[c].astype(F32) for ref in (kept_ref, gone_ref) for c in range(2)]
    top = parts[0]
    for part in parts[1:]:
        top = jnp.maximum(top, part)
    peak = jnp.max(top, axis=1, keepdims=True)
    total = sum(jnp.exp((part - peak) * 0.5) for part in parts)
    out_ref[...] = columns_to_rows([peak, jnp.sum(total, axis=1, keepdims=True)])


def taught_stats(kept, gone):
    _, per, cols = kept.shape
    return pl.pallas_call(
        taught_kernel,
        out_shape=shape((STAT_ROWS, per), F32),
        in_specs=[VMEM] * 2,
        out_specs=VMEM,
        compiler_params=params(4),
        cost_estimate=cost(0, 4 * per * cols * 2, 4 * per * cols),
        name="taught_stats",
    )(kept, gone)


def teacher_kernel(at_ref, serving_ref, a0, a1, a2, a3, soft_ref, peaks_ref):
    me, core = at_ref[0], at_ref[1]
    _, per, cols = a0.shape
    for j in range(2):
        wanted = serving_ref[me ^ (2 * j)]
        sums = [0.0, 0.0]
        for k, arrived in enumerate((a0, a1, a2, a3)):
            row = lax.broadcasted_iota(jnp.int32, (per, per), 0) + (me ^ k) * per
            pick = (row == wanted).astype(BF16)
            for c in range(2):
                sums[c] += lax.dot_general(
                    pick, arrived[core ^ c], (((0,), (0,)), ((), ())), preferred_element_type=F32
                )
        peak = jnp.max(jnp.maximum(*sums), axis=1, keepdims=True)
        for c in range(2):
            soft_ref[j, :, c * cols : (c + 1) * cols] = jnp.exp((sums[c] - peak) * 0.5)
        peaks_ref[j] = columns_to_rows([peak])


def teacher_rows(at, serving, arrived):
    _, per, cols = arrived[0].shape
    return pl.pallas_call(
        teacher_kernel,
        out_shape=(shape((2, per, 2 * cols), F32), shape((2, STAT_ROWS, per), F32)),
        in_specs=[SMEM] + [VMEM] * 5,
        out_specs=(VMEM, VMEM),
        compiler_params=params(8),
        cost_estimate=cost(32 * per * per * cols, 12 * per * cols * 2, 4 * per * cols),
        name="teacher_rows",
    )(at, serving, *arrived)


def student_stats(logits):
    peak = jnp.max(logits, axis=1, keepdims=True)
    soft = jnp.exp((logits - peak) * 0.5)
    hard = jnp.sum(soft * soft, axis=1, keepdims=True)
    return soft, columns_to_rows([peak, hard, jnp.sum(soft, axis=1, keepdims=True)])


def near_kernel(rows_ref, w_ref, *refs):
    logits_ref, stats_ref = refs[-2:]
    logits = jnp.dot(rows_ref[...], w_ref[...], preferred_element_type=F32)
    logits_ref[...], stats_ref[...] = student_stats(logits)


def near_logits(rows, weight, *held):
    per, depth = rows.shape
    cols = weight.shape[1]
    return pl.pallas_call(
        near_kernel,
        out_shape=(shape((per, cols), F32), shape((STAT_ROWS, per), F32)),
        in_specs=[VMEM] * (2 + len(held)),
        out_specs=(VMEM, VMEM),
        compiler_params=params(6),
        cost_estimate=cost(2 * per * depth * cols, (per + cols) * depth * 2, per * cols),
        name="near_logits",
    )(rows, weight, *held)


NOTHING = -3.0e38


def both(a, b):
    peak = jnp.maximum(a[0:1], b[0:1])
    ea, eb = jnp.exp((a[0:1] - peak) * 0.5), jnp.exp((b[0:1] - peak) * 0.5)
    return jnp.concatenate(
        [peak, a[1:2] * (ea * ea) + b[1:2] * (eb * eb), a[2:3] * ea + b[2:3] * eb]
    )


def far_kernel(n, spots_ref, *refs):
    pieces, refs = refs[:n], refs[n:]
    own_ref, other_ref, near_ref, stats_a, stats_b, taught_ref, taught_core_ref, ids_ref = refs[:8]
    a_ref, b_ref, rows_ref, out_ref, peaks_ref, full = refs[8:]
    share = pieces[0].shape[0]
    for k, piece in enumerate(pieces[:-1]):
        full[pl.ds(pl.multiple_of(spots_ref[k], 8), share), :] = piece[...].astype(F32)
    full[4 * share :, :] = pieces[-1][...].astype(F32)
    rows_ref[0] = near_ref[...]
    rows_ref[1] = full[...].astype(BF16)
    per = rows_ref.shape[1]
    a = jnp.dot(rows_ref[1], own_ref[...], preferred_element_type=F32)
    b = jnp.dot(rows_ref[1], other_ref[...], preferred_element_type=F32)
    a_ref[...], a = student_stats(a)
    b_ref[...], b = student_stats(b)
    peaks_ref[...] = jnp.concatenate(
        [stats_a[0:1], stats_b[0:1], a[0:1], b[0:1], jnp.zeros((STAT_ROWS - 4, per), F32)]
    )
    out_ref[0, 0:3, :] = both(stats_a[...], stats_b[...])
    out_ref[0, 3:4, :] = ids_ref[...].astype(F32)
    out_ref[0, 4:6, :] = taught_ref[0:2, :]
    out_ref[0, 6:8, :] = taught_core_ref[0:2, :]
    out_ref[1, 0:3, :] = both(a, b)
    row = lax.broadcasted_iota(jnp.int32, (5, per), 0)
    out_ref[1, 3:8, :] = jnp.where((row == 1) | (row == 3), NOTHING, 0.0)


def far_logits(spots, pieces, own, other, *small):
    depth, cols = own.shape
    per = sum(piece.shape[0] for piece in pieces)
    return pl.pallas_call(
        lambda *refs: far_kernel(len(pieces), *refs),
        out_shape=(
            shape((per, cols), F32),
            shape((per, cols), F32),
            shape((2, per, depth), BF16),
            shape((2, STAT_ROWS, per), F32),
            shape((STAT_ROWS, per), F32),
        ),
        in_specs=[SMEM] + [VMEM] * (len(pieces) + 2 + len(small)),
        out_specs=(VMEM,) * 5,
        scratch_shapes=[pltpu.VMEM((per, depth), F32)],
        compiler_params=params(16),
        cost_estimate=cost(4 * per * depth * cols, (per + 2 * cols) * depth * 2, 2 * per * cols),
        name="far_logits",
    )(spots, *pieces, own, other, *small)


def merged(parts):
    top = parts[0]
    for part in parts[1:]:
        top = jnp.maximum(top, part)
    hard = soft = taught0 = taught1 = 0.0
    for part in parts:
        shrink = jnp.exp((part - top) * 0.5)
        s = shrink[0:1]
        hard += part[1:2] * (s * s)
        soft += part[2:3] * s
        taught0 += part[5:6] * shrink[4:5]
        taught1 += part[7:8] * shrink[6:7]
    return top[0:1], hard, soft, top[3:4], top[4:5], taught0, top[6:7], taught1


def merge_kernel(n, *refs):
    out_ref = refs[-1]
    for j in range(2):
        out_ref[j] = jnp.concatenate(merged([ref[j] for ref in refs[:n]]))


def merge(parts, held):
    return pl.pallas_call(
        lambda *refs: merge_kernel(len(parts), *refs),
        out_shape=shape(parts[0].shape, F32),
        in_specs=[VMEM] * (len(parts) + len(held)),
        out_specs=VMEM,
        compiler_params=params(6),
        cost_estimate=cost(0, 5 * parts[0].size * 4),
        name="merge_stats",
    )(*parts, *held)


def picker(bit, flip, total):
    half = total // 2
    row = lax.broadcasted_iota(jnp.int32, (total, total), 0)
    side = jnp.where(row < half, 1 << bit, 0)
    row = row & (half - 1)
    row = ((row >> bit) << (bit + 1)) + side + (row & ((1 << bit) - 1))
    return (lax.broadcasted_iota(jnp.int32, (total, total), 1) == (row ^ flip)).astype(BF16)


def grads_kernel(n, at_ref, *refs):
    stats_refs, refs = refs[:n], refs[n:]
    soft_refs, (peaks_ref, serving_ref, taught_ref, tpeaks_ref), g_refs = refs[:4], refs[4:8], refs[8:]
    me = at_ref[3]
    per, cols = soft_refs[0].shape
    stats = [merged([ref[j ^ (i & 1)] for i, ref in enumerate(stats_refs)]) for j in range(2)]
    lane = lax.broadcasted_iota(jnp.int32, (per, per), 1)
    for j in range(2):
        rows = stats[j][:4] + (
            serving_ref[me ^ (2 * j)].astype(F32),
            tpeaks_ref[j, 0:1, :],
            peaks_ref[2 * j : 2 * j + 2, :],
        )
        columns = jnp.concatenate(rows + (jnp.zeros((128 - 8, per), F32),)).T
        peak, hard, soft, ids, wanted, tlocal, *local = [columns[:, i : i + 1] for i in range(8)]
        ids, wanted = ids.astype(jnp.int32), wanted.astype(jnp.int32)
        tpeak = total = 0.0
        for k in range(4):
            here = wanted - (me ^ k) * per == lane
            taught = stats[k // 2][4 + 2 * (k % 2) : 6 + 2 * (k % 2)]
            tpeak += jnp.where(here, taught[0], 0.0)
            total += jnp.where(here, taught[1], 0.0)
        tpeak = jnp.sum(tpeak, axis=1, keepdims=True)
        total = jnp.sum(total, axis=1, keepdims=True)
        teach = jnp.exp((tlocal - tpeak) * 0.5) * (32.0 / total)
        hard, soft = 16.0 / hard, 32.0 / soft
        for c, g_ref in enumerate(g_refs):
            part = slice(c * cols, (c + 1) * cols)
            column = at_ref[1 + c] + lax.broadcasted_iota(jnp.int32, (per, cols), 1)
            scale = jnp.exp((local[c] - peak) * 0.5)
            own = soft_refs[2 * j + c][...]
            label = jnp.where(column == ids, 16.0, 0.0)
            grad = own * (scale * soft + own * (scale * scale * hard)) - taught_ref[j, :, part] * teach
            g_ref[j * per : (j + 1) * per, :] = (grad - label).astype(BF16)


def back_kernel(bits, edges, low, n, at_ref, *refs):
    w_refs, refs, mixed = refs[:2], refs[2:-1], refs[-1]
    g_refs, send_refs, keep_refs = refs[-8:-6], refs[-6:-3], refs[-3:]
    grads_kernel(n, at_ref, *refs[:-6])
    total = mixed.shape[1]
    per = total // 2
    aligned = (1 << low) % 16 == 0
    if aligned:
        row = lax.broadcasted_iota(jnp.int32, (total, total), 0)
        turn = lax.broadcasted_iota(jnp.int32, (total, total), 1) == (row ^ at_ref[0])
        for c, g_ref in enumerate(g_refs):
            mixed[c] = jnp.dot(turn.astype(BF16), g_ref[...], preferred_element_type=F32).astype(BF16)
    for p in range(3):
        back = 0.0
        for c, (g_ref, w_ref) in enumerate(zip(g_refs, w_refs)):
            if aligned:
                run = 1 << bits[p]
                starts = [i for side in (run, 0) for i in range(side, total, 2 * run)]
                rows = jnp.concatenate([mixed[c, i : i + run, :] for i in starts])
            else:
                pick = picker(bits[p], at_ref[0], total)
                rows = jnp.dot(pick, g_ref[...], preferred_element_type=F32).astype(BF16)
            back += lax.dot_general(
                w_ref[edges[p] : edges[p + 1], :],
                rows,
                (((1,), (1,)), ((), ())),
                preferred_element_type=F32,
            )
        back = back.astype(BF16).T
        send_refs[p][...] = back[:per]
        keep_refs[p][...] = back[per:]


def back_rows(at, own, other, stats, soft, small, bits, edges, low):
    depth, cols = own.shape
    per = soft[0].shape[0]
    parts = [(per, edges[p + 1] - edges[p]) for p in range(3)]
    got = pl.pallas_call(
        lambda *refs: back_kernel(bits, edges, low, len(stats), *refs),
        out_shape=[shape((2 * per, cols), BF16)] * 2
        + [shape(part, BF16) for part in parts] * 2,
        in_specs=[SMEM] + [VMEM] * (len(stats) + 6 + len(small)),
        out_specs=[VMEM] * 8,
        scratch_shapes=[pltpu.VMEM((2, 2 * per, cols), BF16)],
        compiler_params=params(20),
        cost_estimate=cost(8 * per * depth * cols, 2 * cols * depth * 2),
        name="back_rows",
    )(at, own, other, *stats, *soft, *small)
    return got[0], got[1], got[2:5], got[5:8]


def head_kernel(rows_ref, core_ref, mine_ref, theirs_ref, out_ref):
    rows = jnp.concatenate([rows_ref[0], rows_ref[1], core_ref[0], core_ref[1]])
    grads = jnp.concatenate([mine_ref[...], theirs_ref[...]])
    out_ref[...] = lax.dot_general(
        rows, grads, (((0,), (0,)), ((), ())), preferred_element_type=F32
    ).astype(BF16)


def head_gradient(rows, core_rows, mine, theirs):
    _, per, depth = rows.shape
    cols = mine.shape[1]
    tile = 512 if depth % 512 == 0 else depth
    whole = pl.BlockSpec((2 * per, cols), lambda i: (0, 0))
    slab = pl.BlockSpec((2, per, tile), lambda i: (0, 0, i))
    return pl.pallas_call(
        head_kernel,
        grid=(depth // tile,),
        out_shape=shape((depth, cols), BF16),
        in_specs=[slab] * 2 + [whole] * 2,
        out_specs=pl.BlockSpec((tile, cols), lambda i: (i, 0)),
        compiler_params=pltpu.CompilerParams(
            vmem_limit_bytes=6 * MIB, fuse_transposed_lhs_in_matmul=True
        ),
        cost_estimate=cost(8 * per * depth * cols, (4 * per + cols) * depth * 2),
        name="head_gradient",
    )(rows, core_rows, mine, theirs)


def body(hidden, token_ids, serving, head_weight, teacher_logits):
    groups = lax.axis_size("grp")
    shards = lax.axis_size("vocab")
    me_g = lax.axis_index("grp")
    me_v = lax.axis_index("vocab")
    per, depth = hidden.shape
    cols = head_weight.shape[1]
    owned = per // shards
    CORE, X = shards, 2 * shards
    Y, W = 1, 2
    count = groups * shards

    def swap(value, mask):
        return lax.ppermute(value, AXES, [(i, i ^ mask) for i in range(count)])

    def tie(*values):
        return lax.optimization_barrier(values)

    def ints(*values):
        return jnp.stack([jnp.asarray(v, jnp.int32) for v in values])

    quarter_rows = per * 3 // 16
    quarter = me_v & 3
    starts = [(quarter ^ k) * quarter_rows for k in range(4)]
    chip = me_g >> 1
    spots = ints(*starts)
    at = ints(
        me_v * owned, (me_g * shards + me_v) * cols, ((me_g ^ 1) * shards + me_v) * cols, me_g
    )
    who = ints(me_g, me_g & 1)
    unsigned = [
        jnp.asarray(v, jnp.uint32)
        for v in (starts[0], starts[3], 2 * chip, 2 * (chip ^ 1))
    ]
    rows, weight, spots, at, who, *unsigned = tie(hidden, head_weight, spots, at, who, *unsigned)
    zero = jnp.uint32(0)

    def cut(value, start, size, dim):
        indices = [start if d == dim else zero for d in range(value.ndim)]
        sizes = [size if d == dim else n for d, n in enumerate(value.shape)]
        return lax.dynamic_slice(value, indices, sizes)

    first = cut(rows, unsigned[0], quarter_rows, 0)
    x0 = swap(first, X)
    _, rows, weight, teacher = tie(first, rows, weight, teacher_logits)
    other_weight = swap(weight, CORE)
    x3 = swap(cut(rows, unsigned[1], quarter_rows, 0), X)
    rest = swap(rows[4 * quarter_rows :], X)
    kept = cut(teacher, unsigned[2], 2, 1).swapaxes(0, 1)
    gone = cut(teacher, unsigned[3], 2, 1).swapaxes(0, 1)
    taught = taught_stats(kept, gone)
    taught_core = swap(taught, CORE)
    x0, kept, gone, taught, taught_core, rows = tie(x0, kept, gone, taught, taught_core, rows)
    x1 = swap(x0, Y)
    x2 = swap(x0, W)
    kept_core = swap(kept, CORE)
    near_a, stats_a = near_logits(rows, weight, x0)
    near_b, stats_b = near_logits(rows, other_weight, x0)
    *pieces, gone, near_a, near_b = tie(x0, x1, x2, x3, rest, gone, near_a, near_b)
    taught_x = swap(gone, X)
    far_a, far_b, both_rows, stats, peaks = far_logits(
        spots,
        pieces,
        weight,
        other_weight,
        rows,
        stats_a,
        stats_b,
        taught,
        taught_core,
        token_ids.reshape(1, per),
    )

    served = serving.reshape(groups, 1, per)
    logits = [near_a, near_b, far_a, far_b]
    held = logits + [weight]
    mask = W
    while mask < shards:
        masks = [mask, 2 * mask, 3 * mask] if 2 * mask < shards else [mask]
        stats = merge([stats] + [swap(stats, m) for m in masks], held)
        mask *= 4
    _, taught_x = tie(stats, taught_x)
    taught_far = swap(taught_x, CORE)
    taught_soft, taught_peaks = teacher_rows(
        who, served, [kept, kept_core, taught_x, taught_far]
    )
    parts = [stats] + [swap(stats, mask) for mask in (X, Y, X + Y)]

    bits = shards.bit_length() - 1
    masks = {0: X}
    for b in range(bits):
        masks[1 + b] = shards >> (1 + b)
    ydim, wdim = bits, bits - 1
    third = depth // 128 // 3 * 128
    edges = (0, third, 2 * third, depth)
    orders = [(0, ydim, wdim), (ydim, wdim, 0), (wdim, 0, ydim)]
    low = owned.bit_length() - 1
    row_bit = {0: low + bits, ydim: low, wdim: low + 1}
    first_bits = tuple(row_bit[order[0]] for order in orders)
    small = (peaks, served, taught_soft, taught_peaks)
    gown, gother, sents, keeps = back_rows(
        at, weight, other_weight, parts, logits, small, first_bits, edges, low
    )
    gots = [swap(sents[p], masks[orders[p][0]]) for p in range(3)]
    theirs = swap(gother, CORE)
    _, rows_sent = tie(gother, both_rows)
    grad_head = head_gradient(both_rows, swap(rows_sent, CORE), gown, theirs)
    for p in range(3):
        grad_head, gots[p] = tie(grad_head, gots[p])

    def folded(value, p):
        dims = [2] * (1 + bits)
        dims[orders[p][0]] = 1
        return value.reshape(*dims, owned, value.shape[-1])

    terms = [[folded(keeps[p], p), folded(gots[p], p)] for p in range(3)]
    for stage in (1, 2):
        sents = [
            sum(lax.index_in_dim(t, 1, orders[p][stage]).astype(F32) for t in terms[p]).astype(BF16)
            for p in range(3)
        ]
        gots = [swap(sents[p], masks[orders[p][stage]]) for p in range(3)]
        for p in range(3):
            terms[p] = [lax.index_in_dim(t, 0, orders[p][stage]) for t in terms[p]] + [gots[p]]
    for dim in range(1, wdim):
        for p in range(3):
            sent = sum(lax.index_in_dim(t, 1, dim).astype(F32) for t in terms[p]).astype(BF16)
            terms[p] = [lax.index_in_dim(t, 0, dim) for t in terms[p]] + [swap(sent, masks[dim])]
    total = jnp.concatenate([sum(t.astype(F32) for t in ts) for ts in terms], axis=-1)
    return (total.reshape(owned, depth), grad_head)


def solution(mesh):
    placed = (P("grp", None), P("grp"), P(), P(None, ("grp", "vocab")), P("grp", None, "vocab"))
    return jax.shard_map(
        body,
        mesh=mesh,
        in_specs=placed,
        out_specs=(P(("grp", "vocab"), None), P(None, ("grp", "vocab"))),
        check_vma=False,
    )
```
